32 devices in a mesh: batch: 8 (over z, x), seq: 4 (over y, core).
Axes of the slice: x: 2, y: 2, z: 4, core: 2. Of those that a mesh axis runs over, the one named last changes fastest.
Arguments:
- hidden_in: bfloat16 [24, 512, 768], P('batch', 'seq'), may hold values from -6 to 6
- cotangent: bfloat16 [24, 512, 768], P('batch', 'seq'), may hold values from -6 to 6
- span_mask: int32 [24, 512], P('batch', 'seq'), may hold values from 0 to 1, as said below
- lengths: int32 [24], P('batch'), may hold values from 128 to 512, as said below
- repeats: int32 [24], P('batch'), may hold values from 1 to 4
- mask_embedding: bfloat16 [768], replicated, may hold values from -6 to 6
- query_weight: bfloat16 [768, 768], replicated, may hold values from -0.21875 to 0.21875
- query_bias: bfloat16 [768], replicated, may hold values from -2 to 2
- key_weight: bfloat16 [768, 768], replicated, may hold values from -0.21875 to 0.21875
- value_weight: bfloat16 [768, 768], replicated, may hold values from -0.21875 to 0.21875
- value_bias: bfloat16 [768], replicated, may hold values from -2 to 2
- output_weight: bfloat16 [768, 768], replicated, may hold values from -2.5 to 2.5
- output_bias: bfloat16 [768], replicated, may hold values from -2 to 2
- mixing_gain: bfloat16 [768], replicated, may hold values from 0.25 to 1.75
- mixing_shift: bfloat16 [768], replicated, may hold values from -2 to 2
- inner_weight: bfloat16 [768, 3072], replicated, may hold values from -0.21875 to 0.21875
- inner_bias: bfloat16 [3072], replicated, may hold values from -2 to 2
- outer_weight: bfloat16 [3072, 768], replicated, may hold values from -0.21875 to 0.21875
- outer_bias: bfloat16 [768], replicated, may hold values from -2 to 2
- final_gain: bfloat16 [768], replicated, may hold values from 0.25 to 1.75
- final_shift: bfloat16 [768], replicated, may hold values from -2 to 2
Outputs:
- layer_out: bfloat16 [24, 512, 768], P('batch', 'seq')
- grad_input: bfloat16 [24, 512, 768], P('batch', 'seq')
- gradient_mask_embedding: float32 [768], replicated
- gradient_query_weight: float32 [768, 768], P('batch', 'seq')
- gradient_query_bias: float32 [768], replicated
- gradient_key_weight: float32 [768, 768], P('batch', 'seq')
- gradient_value_weight: float32 [768, 768], P('batch', 'seq')
- gradient_value_bias: float32 [768], replicated
- gradient_output_weight: float32 [768, 768], P('batch', 'seq')
- gradient_output_bias: float32 [768], replicated
- gradient_mixing_gain: float32 [768], replicated
- gradient_mixing_shift: float32 [768], replicated
- gradient_inner_weight: float32 [768, 3072], P('batch', 'seq')
- gradient_inner_bias: float32 [3072], replicated
- gradient_outer_weight: float32 [3072, 768], P('batch', 'seq')
- gradient_outer_bias: float32 [768], replicated
- gradient_final_gain: float32 [768], replicated
- gradient_final_shift: float32 [768], replicated
The draws below stay inside these ranges and needn't reach their ends.
Inputs may be any that keep to these rules, and one draw needn't show every extreme that they name: `lengths`: in every aligned block of 3 rows, at least one row has length 512. `span_mask`: A union of runs of 6 positions; each row has a run that ends or starts within two positions of a multiple of 128 without crossing it.
All inputs are finite; a program needn't handle non-finite values.
Results may differ from the reference program's by a relative error of at most 0.015.
Values may be sent and summed in bfloat16 or wider, within the bound.
A program may use at most 128 MiB of HBM per device.

```python
import jax
import jax.numpy as jnp
from jax import lax

D = 768
HEADS = 12
HEAD_DIM = 64
FF = 3072
LEN = 512
WIDEN = 5
SPAN = 6
ROWS_DEV = 3
STRETCH = 128
ROWS = 24


def draw_lengths(key, part):
    key = jax.random.fold_in(key, 11)
    first_key, second_key = jax.random.split(key)
    ragged = jax.random.randint(first_key, (ROWS,), LEN // 4, LEN + 1)
    chosen = jax.random.randint(second_key, (ROWS // ROWS_DEV,), 0, ROWS_DEV)
    within = jnp.arange(ROWS, dtype=jnp.int32) % ROWS_DEV
    longest = within == jnp.repeat(chosen, ROWS_DEV)
    return jnp.where(longest, LEN, ragged).astype(jnp.int32)


def draw_span_mask(key, part):
    key = jax.random.fold_in(key, 23)
    random_key, bound_key, side_key, shift_key = jax.random.split(key, 4)
    starts = (jax.random.randint(random_key, (ROWS, LEN), 0, 60) == 0).astype(jnp.int32)
    pieces = LEN // STRETCH
    boundary = jax.random.randint(bound_key, (ROWS,), 1, pieces) * STRETCH
    side = jax.random.randint(side_key, (ROWS,), 0, 2)
    nudge = jax.random.randint(shift_key, (ROWS,), 0, 2)
    placed = jnp.where(side == 0, boundary - SPAN - nudge, boundary + nudge).astype(jnp.int32)
    positions = jnp.arange(LEN, dtype=jnp.int32)
    forced = (positions[None, :] == placed[:, None]).astype(jnp.int32)
    limit = (positions <= LEN - SPAN).astype(jnp.int32)
    starts = jnp.maximum(starts * limit[None, :], forced)
    padded = jnp.pad(starts, ((0, 0), (SPAN - 1, 0)))
    covered = padded[:, 0:LEN]
    for offset in range(1, SPAN):
        covered = covered + padded[:, offset:offset + LEN]
    return (covered > 0).astype(jnp.int32)


def set_ends(result, stream_key, least, top_value):
    shape = result.shape
    place = [jax.random.randint(jax.random.fold_in(stream_key, axis), (), 0, shape[axis]) for axis in range(len(shape))]
    result = result.at[tuple(place)].set(least)
    longest = shape.index(max(shape))
    place[longest] = (place[longest] + 1) % shape[longest]
    return result.at[tuple(place)].set(top_value)


def steps_of(rng, extent, cuts, low, top_value):
    level = 1.0
    for position, parts in cuts:
        steps = jax.random.uniform(jax.random.fold_in(jax.random.fold_in(rng, 6), position), (parts,), jnp.float32, low / len(cuts), top_value / len(cuts))
        level = level * jnp.repeat(jnp.exp(steps), extent[position] // parts).reshape((-1,) + (1,) * (len(extent) - 1 - position))
    return level


def normal_values(key, dims, scale, reach, cuts=(), held_as=jnp.bfloat16):
    loudness = steps_of(key, dims, cuts, -0.22, 0.18) if cuts else 1.0
    array = jax.random.normal(key, dims, jnp.float32) * scale * loudness
    return jnp.minimum(jnp.maximum(array, -reach), reach).astype(held_as)


def setup_inputs(seed: int = 0) -> dict:
    seeds = jax.random.split(jax.random.key(seed), 22)
    return {
        "hidden_in": normal_values(seeds[0], (ROWS, LEN, D), 1.0, 6.0, ((0, 8), (1, 4))),
        "cotangent": normal_values(seeds[1], (ROWS, LEN, D), 1.0, 6.0, ((0, 8), (1, 4))),
        "span_mask": draw_span_mask(jax.random.fold_in(seeds[21], 71), 0),
        "lengths": draw_lengths(jax.random.fold_in(seeds[21], 71), 0),
        "repeats": set_ends(jax.random.randint(seeds[4], (ROWS,), 1, 5), jax.random.fold_in(seeds[4], 1), 1, 4).astype(jnp.int32),
        "mask_embedding": normal_values(seeds[5], (D,), 1.0, 6.0),
        "query_weight": normal_values(seeds[6], (D, D), D ** -0.5, 0.21875),
        "query_bias": normal_values(seeds[7], (D,), 0.3, 2.0),
        "key_weight": normal_values(seeds[8], (D, D), D ** -0.5, 0.21875),
        "value_weight": normal_values(seeds[9], (D, D), D ** -0.5, 0.21875),
        "value_bias": normal_values(seeds[10], (D,), 0.3, 2.0),
        "output_weight": normal_values(seeds[11], (D, D), (max(D // 128, 1)) ** -0.5, 2.5),
        "output_bias": normal_values(seeds[12], (D,), 0.3, 2.0),
        "mixing_gain": jnp.clip(1.0 + 0.15 * jax.random.normal(seeds[13], (D,), jnp.float32), 0.25, 1.75).astype(jnp.bfloat16),
        "mixing_shift": normal_values(seeds[14], (D,), 0.3, 2.0),
        "inner_weight": normal_values(seeds[15], (D, FF), D ** -0.5, 0.21875),
        "inner_bias": normal_values(seeds[16], (FF,), 0.3, 2.0),
        "outer_weight": normal_values(seeds[17], (FF, D), (FF // 4) ** -0.5, 0.21875),
        "outer_bias": normal_values(seeds[18], (D,), 0.3, 2.0),
        "final_gain": jnp.clip(1.0 + 0.15 * jax.random.normal(seeds[19], (D,), jnp.float32), 0.25, 1.75).astype(jnp.bfloat16),
        "final_shift": normal_values(seeds[20], (D,), 0.3, 2.0),
    }


@jax.custom_vjp
def low(v):
    return lax.optimization_barrier(v.astype(jnp.bfloat16)).astype(jnp.float32)

@jax.custom_vjp
def low_back(v):
    return v

def low_keep(v):
    return (low(v), None)

def low_pass(kept, grad):
    return (grad,)

def back_keep(v):
    return (v, None)

def back_low(kept, grad):
    return (low(grad),)
low.defvjp(low_keep, low_pass)
low_back.defvjp(back_keep, back_low)

def layer_norm(inputs, gain, shift):
    center = inputs - lax.optimization_barrier(jnp.mean(inputs, -1, keepdims=True))
    spread = lax.optimization_barrier(jnp.mean(center * center, -1, keepdims=True))
    return center * lax.rsqrt(spread + 1e-05) * gain + shift

def project(inputs, weight):
    return jnp.einsum('bld,de->ble', inputs, weight, precision=lax.Precision.HIGHEST)

def forward(params, inputs, widened, live):
    mask_vec, query_w, query_b, key_w, value_w, value_b, output_w, output_b, mixing_g, mixing_s, inner_w, inner_b, outer_w, outer_b, final_g, final_s = params
    blocks = inputs.shape[0]
    masked_in = jnp.where(widened[..., None], mask_vec[None, None, :], inputs)
    heads_shape = (blocks, LEN, HEADS, HEAD_DIM)
    queries = low(low_back(project(masked_in, query_w) + query_b)).reshape(heads_shape)
    keys = low(low_back(project(masked_in, key_w))).reshape(heads_shape)
    values = low(low_back(project(masked_in, value_w) + value_b)).reshape(heads_shape)
    raw = low_back(jnp.einsum('bqhd,bkhd->bhqk', queries, keys, precision=lax.Precision.HIGHEST))
    logits = jnp.where(live[:, None, None, :], raw * HEAD_DIM ** (-0.5), -1e+30)
    highest = lax.optimization_barrier(jnp.max(logits, -1, keepdims=True))
    expd = jnp.exp(logits - highest)
    probs = expd / lax.optimization_barrier(jnp.sum(expd, -1, keepdims=True))
    mixed = jnp.einsum('bhqk,bkhd->bqhd', low(probs), values, precision=lax.Precision.HIGHEST)
    mixed = low(low_back(mixed.reshape(blocks, LEN, D)))
    attended = low_back(project(mixed, output_w) + output_b)
    first = layer_norm(masked_in + attended, mixing_g, mixing_s)
    inner = low_back(project(low(first), inner_w) + inner_b)
    activated = low(jax.nn.gelu(inner, approximate=False))
    outer = low_back(project(activated, outer_w) + outer_b)
    return layer_norm(first + outer, final_g, final_s)

def reference(hidden_in, cotangent, span_mask, lengths, repeats, mask_embedding, query_weight, query_bias, key_weight, value_weight, value_bias, output_weight, output_bias, mixing_gain, mixing_shift, inner_weight, inner_bias, outer_weight, outer_bias, final_gain, final_shift):
    params = tuple((tensor.astype(jnp.float32) for tensor in (mask_embedding, query_weight, query_bias, key_weight, value_weight, value_bias, output_weight, output_bias, mixing_gain, mixing_shift, inner_weight, inner_bias, outer_weight, outer_bias, final_gain, final_shift)))
    padded = jnp.pad(span_mask, ((0, 0), (WIDEN, WIDEN)))
    window = padded[:, 0:LEN]
    for offset in range(1, 2 * WIDEN + 1):
        window = window + padded[:, offset:offset + LEN]
    widened = window > 0
    positions = jnp.arange(LEN, dtype=jnp.int32)
    live = positions[None, :] < lengths[:, None]
    weighted = cotangent.astype(jnp.float32) * repeats.astype(jnp.float32)[:, None, None]
    weighted = weighted * live.astype(jnp.float32)[:, :, None]
    groups = ROWS // ROWS_DEV
    inputs = hidden_in.astype(jnp.float32).reshape(groups, ROWS_DEV, LEN, D)
    stacked = (inputs, weighted.reshape(groups, ROWS_DEV, LEN, D), widened.reshape(groups, ROWS_DEV, LEN), live.reshape(groups, ROWS_DEV, LEN))

    def one_block(totals, block):
        block_in, block_cot, block_wide, block_live = block
        outputs, pullback = jax.vjp(lambda prm, xin: forward(prm, xin, block_wide, block_live), params, block_in)
        param_grads, input_grad = pullback(block_cot)
        totals = jax.tree.map(lambda left, right: left + right, totals, param_grads)
        return (totals, (outputs.astype(jnp.bfloat16), input_grad.astype(jnp.bfloat16)))
    zeros = jax.tree.map(jnp.zeros_like, params)
    totals, (layer_out, grad_input) = lax.scan(one_block, zeros, stacked)
    layer_out = layer_out.reshape(ROWS, LEN, D)
    grad_input = grad_input.reshape(ROWS, LEN, D)
    return (layer_out, grad_input, totals[0], totals[1], totals[2], totals[3], totals[4], totals[5], totals[6], totals[7], totals[8], totals[9], totals[10], totals[11], totals[12], totals[13], totals[14], totals[15])
```

```python
import functools

import jax
import jax.numpy as jnp
from jax import lax
from jax.experimental import pallas as pl
from jax.experimental.pallas import tpu as pltpu
from jax.sharding import PartitionSpec as P

HEADS = 12
HEAD_DIM = 64
WIDEN = 5


def with_halo(x, sides, width):
    for axis, dim in sides:
        count, length = (lax.axis_size(axis), x.shape[dim])
        up = [(i, (i + 1) % count) for i in range(count - 1)]
        down = [(j, i) for i, j in up]
        last = lax.slice_in_dim(x, length - width, length, axis=dim)
        initial = lax.slice_in_dim(x, 0, width, axis=dim)
        before = lax.ppermute(last, axis, up)
        after = lax.ppermute(initial, axis, down)
        x = jnp.concatenate([before, x, after], axis=dim)
    return x


def layer_norm(inputs, gain, shift):
    center = inputs - jnp.mean(inputs, -1, keepdims=True)
    spread = jnp.mean(center * center, -1, keepdims=True)
    return center * lax.rsqrt(spread + 1e-05) * gain + shift


def linear(inputs, weight):
    return jnp.dot(inputs, weight, preferred_element_type=jnp.float32)


def linear_back(grads, weight):
    return lax.dot_general(
        grads, weight, (((1,), (1,)), ((), ())), preferred_element_type=jnp.float32
    )


def contract_rows(left, right):
    return lax.dot_general(
        left, right, (((0,), (0,)), ((), ())), preferred_element_type=jnp.float32
    )


def gelu_exact(inputs):
    return jax.nn.gelu(inputs, approximate=False)


MESH = pl.DeviceIdType.MESH
PHASES = 5


def places():
    b, s = lax.axis_index("batch"), lax.axis_index("seq")
    x, zlo, zhi = lax.rem(b, 2), lax.rem(b // 2, 2), b // 4
    core, y = lax.rem(s, 2), s // 2
    spot = {"core": core, "x": x, "y": y, "zlo": zlo, "zhi": zhi}
    peer = {
        "core": (b, s + 1 - 2 * core),
        "y": (b, s + 2 - 4 * y),
        "x": (b + 1 - 2 * x, s),
        "zlo": (b + 2 - 4 * zlo, s),
        "zhi": (b + 4 - 8 * zhi, s),
    }
    return spot, peer


def each_block(shape, body):
    count = 1
    for size in shape:
        count *= size

    def step(n, carry):
        place = []
        for size in reversed(shape):
            place.append(lax.rem(n, size))
            n = n // size
        body(tuple(reversed(place)))
        return carry

    lax.fori_loop(0, count, step, 0)


class Unit:
    def __init__(self, number, order, own, inbox, sends, recvs, spot, peer):
        self.number, self.order, self.own, self.inbox = number, order, own, inbox
        self.sends, self.recvs, self.spot, self.peer = sends, recvs, spot, peer

    def axis(self, phase):
        return ("core", *self.order, "zlo", "zhi")[phase]

    def where(self, phase, stays):
        spot = self.spot
        first = self.order[0]
        here = lambda name: spot[name] if stays else 1 - spot[name]
        if phase == 1 and first == "x":
            return (slice(None), slice(None), slice(None), here("x"))
        if phase == 1:
            return (here("y"),)
        if phase == 2 and first == "x":
            return (here("y"), slice(None), slice(None), spot["x"])
        if phase == 2:
            return (spot["y"], slice(None), slice(None), here("x"))
        if phase == 3:
            return (spot["y"], slice(None), here("zlo"), spot["x"])
        return (spot["y"], here("zhi"), spot["zlo"], spot["x"])

    def copy(self, phase):
        return pltpu.make_async_remote_copy(
            src_ref=self.own.at[self.where(phase, False)],
            dst_ref=self.inbox[phase],
            send_sem=self.sends.at[self.number, phase],
            recv_sem=self.recvs.at[self.number, phase],
            device_id=self.peer[self.axis(phase)],
            device_id_type=MESH,
        )

    def start(self, phase):
        self.copy(phase).start()

    def add(self, phase):
        came = self.inbox[phase]
        if phase == 0:
            target = self.own
        else:
            target = self.own.at[self.where(phase, True)]
        lead = came.shape[:-2]

        def body(place):
            target[place] = target[place] + came[place]

        if lead:
            each_block(lead, body)
        else:
            target[...] = target[...] + came[...]


GRAINS = ((192, 384), (96, 768), (48, 384), (48, 384), (48, 384), (48, 384))
ORDERS = (("x", "y"), ("y", "x"), ("x", "y"), ("y", "x"), ("x", "y"), ("y", "x"))


def inbox_shapes(order, grain):
    return (
        (2, 2, 2, 2) + grain,
        ((2, 2, 2) if order[0] == "x" else (2, 2, 2)) + grain,
        (2, 2) + grain,
        (2,) + grain,
        grain,
        grain,
    )


def reduce_body(*refs):
    mats, vec_in = refs[:6], refs[6]
    outs, vec_out = refs[7:13], refs[13]
    rest = list(refs[14:])
    owns = [rest.pop(0) for _ in range(6)]
    inboxes = [[rest.pop(0) for _ in range(6)] for _ in range(6)]
    final = [rest.pop(0) for _ in range(6)]
    vec, vec_came = rest.pop(0), rest.pop(0)
    sends, recvs, local = rest
    spot, peer = places()
    core = spot["core"]
    names = ("core", "x", "y", "zlo", "zhi")
    barrier = pltpu.get_barrier_semaphore()
    for name in names:
        pl.semaphore_signal(barrier, inc=1, device_id=peer[name], device_id_type=MESH)
    pl.semaphore_wait(barrier, len(names))

    def piece(u, y, side):
        if u == 1:
            start = pl.multiple_of((2 * y + side) * 768, 128)
            return mats[u].at[:, :, :, :, pl.ds(start, 768)]
        return mats[u].at[:, :, :, side, :, pl.ds(y * 384, 384)]

    first_sends, first_locals = [], []
    for u in range(6):
        for y in range(2):
            go = pltpu.make_async_remote_copy(
                src_ref=piece(u, y, 1 - core),
                dst_ref=inboxes[u][0].at[y],
                send_sem=sends.at[u, 6 + y],
                recv_sem=recvs.at[u, 6 + y],
                device_id=peer["core"],
                device_id_type=MESH,
            )
            go.start()
            keep = pltpu.make_async_copy(piece(u, y, core), owns[u].at[y], local.at[u, y])
            keep.start()
            first_sends.append(go)
            first_locals.append(keep)
    units = [
        Unit(u, ORDERS[u], owns[u], inboxes[u], sends, recvs, spot, peer) for u in range(6)
    ]

    def vector_copy(phase):
        return pltpu.make_async_remote_copy(
            src_ref=vec.at[phase],
            dst_ref=vec_came.at[phase],
            send_sem=sends.at[6, phase],
            recv_sem=recvs.at[6, phase],
            device_id=peer[names[phase]],
            device_id_type=MESH,
        )

    vec[0] = vec_in[...]
    vector_copy(0).start()
    for phase in range(PHASES):
        for u, unit in enumerate(units):
            if phase == 0:
                for y in range(2):
                    first_sends[2 * u + y].wait()
                    first_locals[2 * u + y].wait()
            else:
                unit.copy(phase).wait()
            if phase < 4:
                unit.add(phase)
                unit.start(phase + 1)
        vector_copy(phase).wait()
        vec[phase + 1] = vec[phase] + vec_came[phase]
        if phase < 4:
            vector_copy(phase + 1).start()
    vec_out[...] = vec[5]
    swaps = []
    for u, unit in enumerate(units):
        mine = (spot["y"], spot["zhi"], spot["zlo"], spot["x"])
        total = owns[u][mine].astype(jnp.float32) + inboxes[u][4][...].astype(jnp.float32)
        if u == 1:
            outs[u][...] = total
            continue
        final[u][...] = total.astype(jnp.bfloat16)
        swap = pltpu.make_async_remote_copy(
            src_ref=final[u],
            dst_ref=inboxes[u][5],
            send_sem=sends.at[u, 5],
            recv_sem=recvs.at[u, 5],
            device_id=peer["core"],
            device_id_type=MESH,
        )
        swap.start()
        swaps.append((u, swap, total))
    for u, swap, total in swaps:
        rows = total.shape[0]
        swap.wait()
        pick = lambda v: jnp.where(core == 0, v[:, :192], pltpu.roll(v, 192, 1)[:, :192])
        outs[u][pl.ds(core * rows, rows), :] = pick(total)
        outs[u][pl.ds((1 - core) * rows, rows), :] = pick(inboxes[u][5][...].astype(jnp.float32))


def reduce_plain(mats, vectors):
    summed = []
    for mat in mats:
        part = lax.psum_scatter(
            mat.astype(jnp.float32), "seq", scatter_dimension=1, tiled=True
        )
        summed.append(lax.psum_scatter(part, "batch", scatter_dimension=0, tiled=True))
    return summed, lax.psum(vectors, ("batch", "seq"))


def reduce_gradients(mats, vectors):
    if lax.axis_size("batch") != 8 or lax.axis_size("seq") != 4:
        return reduce_plain(mats, vectors)
    split = []
    for u, mat in enumerate(mats):
        rows, cols = GRAINS[u]
        lead = (2, 2, 2) if u == 1 else (2, 2, 2, 2)
        split.append(mat.reshape(lead + (rows, mat.shape[1])))
    outs = [jax.ShapeDtypeStruct((2 * r, 192), jnp.float32) for r, _ in GRAINS]
    outs[1] = jax.ShapeDtypeStruct((96, 768), jnp.float32)
    outs.append(jax.ShapeDtypeStruct(vectors.shape, jnp.float32))
    bf = lambda shape: pltpu.VMEM(shape, jnp.bfloat16)
    scratch = [bf((2, 2, 2, 2) + grain) for grain in GRAINS]
    for order, grain in zip(ORDERS, GRAINS):
        scratch += [bf(shape) for shape in inbox_shapes(order, grain)]
    scratch += [bf(grain) for grain in GRAINS]
    scratch += [
        pltpu.VMEM((6,) + vectors.shape, jnp.float32),
        pltpu.VMEM((5,) + vectors.shape, jnp.float32),
        pltpu.SemaphoreType.DMA((7, 8)),
        pltpu.SemaphoreType.DMA((7, 8)),
        pltpu.SemaphoreType.DMA((6, 2)),
    ]
    vmem = pl.BlockSpec(memory_space=pltpu.VMEM)
    result = pl.pallas_call(
        reduce_body,
        out_shape=outs,
        in_specs=[pl.BlockSpec(memory_space=pl.ANY)] * 6 + [vmem],
        out_specs=[vmem] * 7,
        scratch_shapes=scratch,
        compiler_params=pltpu.CompilerParams(
            collective_id=1, has_side_effects=True, vmem_limit_bytes=56 * 2**20
        ),
        name="reduce_gradients",
    )(*split, vectors)
    return result[:6], result[6]


def shards(
    hidden_in,
    cotangent,
    span_mask,
    lengths,
    repeats,
    mask_embedding,
    query_weight,
    query_bias,
    key_weight,
    value_weight,
    value_bias,
    output_weight,
    output_bias,
    mixing_gain,
    mixing_shift,
    inner_weight,
    inner_bias,
    outer_weight,
    outer_bias,
    final_gain,
    final_shift,
):
    rows, stretch, width = hidden_in.shape
    whole = stretch * lax.axis_size("seq")
    scale = HEAD_DIM ** (-0.5)
    offset = lax.axis_index("seq") * stretch
    rim = with_halo(span_mask, (("seq", 1),), WIDEN)
    window = rim[:, 0:stretch]
    for shifted in range(1, 2 * WIDEN + 1):
        window = window + rim[:, shifted : shifted + stretch]
    widened = window > 0
    positions = offset + jnp.arange(stretch, dtype=jnp.int32)
    live = positions[None, :] < lengths[:, None]
    key_live = jnp.arange(whole, dtype=jnp.int32)[None, :] < lengths[:, None]
    masked_in = jnp.where(widened[..., None], mask_embedding[None, None, :], hidden_in)
    flat_in = masked_in.reshape(rows * stretch, width)
    queries = (linear(flat_in, query_weight) + query_bias.astype(jnp.float32)).astype(jnp.bfloat16)
    key_rows = linear(flat_in, key_weight).astype(jnp.bfloat16).reshape(rows, stretch, width)
    value_rows = (linear(flat_in, value_weight) + value_bias.astype(jnp.float32)).astype(
        jnp.bfloat16
    )
    value_rows = value_rows.reshape(rows, stretch, width)
    key_all, value_all = (
        lax.all_gather(key_rows, "seq", axis=1, tiled=True),
        lax.all_gather(value_rows, "seq", axis=1, tiled=True),
    )
    query_heads = queries.reshape(rows, stretch, HEADS, HEAD_DIM)

    def scores_of(key_full):
        key_heads = key_full.reshape(rows, whole, HEADS, HEAD_DIM)
        raw = jnp.einsum(
            "rqhd,rkhd->rhqk", query_heads, key_heads, preferred_element_type=jnp.float32
        )
        return jnp.where(key_live[:, None, None, :], raw * scale, -1e30)

    logits = scores_of(key_all)
    highest = jnp.max(logits, -1, keepdims=True)
    expd = jnp.exp(logits - highest)
    totals = jnp.sum(expd, -1, keepdims=True)
    log_total = highest + jnp.log(totals)
    probs_low = (expd / totals).astype(jnp.bfloat16)
    value_heads = value_all.reshape(rows, whole, HEADS, HEAD_DIM)
    mixed = jnp.einsum(
        "rhqk,rkhd->rqhd", probs_low, value_heads, preferred_element_type=jnp.float32
    )
    mixed = mixed.reshape(rows * stretch, width).astype(jnp.bfloat16)
    attended = linear(mixed, output_weight) + output_bias.astype(jnp.float32)
    residual_one = flat_in.astype(jnp.float32) + attended
    first, norm_back_one = jax.vjp(
        layer_norm, residual_one, mixing_gain.astype(jnp.float32), mixing_shift.astype(jnp.float32)
    )
    first_low = first.astype(jnp.bfloat16)
    inner = linear(first_low, inner_weight) + inner_bias.astype(jnp.float32)
    activated, gelu_back = jax.vjp(gelu_exact, inner)
    activated_low = activated.astype(jnp.bfloat16)
    outer = linear(activated_low, outer_weight) + outer_bias.astype(jnp.float32)
    final, norm_back_two = jax.vjp(
        layer_norm, first + outer, final_gain.astype(jnp.float32), final_shift.astype(jnp.float32)
    )
    layer_out = final.astype(jnp.bfloat16).reshape(rows, stretch, width)
    weighting = repeats.astype(jnp.float32)[:, None] * live.astype(jnp.float32)
    d_final = (cotangent.astype(jnp.float32) * weighting[:, :, None]).reshape(rows * stretch, width)
    d_two, d_final_gain, d_final_shift = norm_back_two(d_final)
    d_outer = d_two.astype(jnp.bfloat16)
    g_outer_weight = contract_rows(activated_low, d_outer)
    g_outer_bias = jnp.sum(d_outer.astype(jnp.float32), 0)
    (d_inner,) = gelu_back(linear_back(d_outer, outer_weight))
    d_inner = d_inner.astype(jnp.bfloat16)
    g_inner_weight = contract_rows(first_low, d_inner)
    g_inner_bias = jnp.sum(d_inner.astype(jnp.float32), 0)
    d_first = linear_back(d_inner, inner_weight) + d_two
    d_one, d_mixing_gain, d_mixing_shift = norm_back_one(d_first)
    d_attended = d_one.astype(jnp.bfloat16)
    g_output_weight = contract_rows(mixed, d_attended)
    g_output_bias = jnp.sum(d_attended.astype(jnp.float32), 0)
    d_mixed = linear_back(d_attended, output_weight).astype(jnp.bfloat16)
    d_mixed_heads = d_mixed.reshape(rows, stretch, HEADS, HEAD_DIM)
    key_back, value_back = (
        lax.all_gather(key_rows, "seq", axis=1, tiled=True),
        lax.all_gather(value_rows, "seq", axis=1, tiled=True),
    )
    probs = jnp.exp(scores_of(key_back) - log_total)
    probs_again = probs.astype(jnp.bfloat16)
    key_heads = key_back.reshape(rows, whole, HEADS, HEAD_DIM)
    value_heads = value_back.reshape(rows, whole, HEADS, HEAD_DIM)
    d_probs = jnp.einsum(
        "rqhd,rkhd->rhqk", d_mixed_heads, value_heads, preferred_element_type=jnp.float32
    )
    centered = d_probs - jnp.sum(probs * d_probs, -1, keepdims=True)
    d_raw = (probs * centered * scale).astype(jnp.bfloat16)
    d_queries = jnp.einsum("rhqk,rkhd->rqhd", d_raw, key_heads, preferred_element_type=jnp.float32)
    d_queries = d_queries.reshape(rows * stretch, width).astype(jnp.bfloat16)
    d_key_part = jnp.einsum(
        "rhqk,rqhd->rkhd", d_raw, query_heads, preferred_element_type=jnp.float32
    )
    d_value_part = jnp.einsum(
        "rhqk,rqhd->rkhd", probs_again, d_mixed_heads, preferred_element_type=jnp.float32
    )
    d_key_sum, d_value_sum = (
        lax.psum_scatter(
            d_key_part.reshape(rows, whole, width), "seq", scatter_dimension=1, tiled=True
        ),
        lax.psum_scatter(
            d_value_part.reshape(rows, whole, width), "seq", scatter_dimension=1, tiled=True
        ),
    )
    d_keys = d_key_sum.astype(jnp.bfloat16).reshape(rows * stretch, width)
    d_values = d_value_sum.astype(jnp.bfloat16).reshape(rows * stretch, width)
    g_query_weight = contract_rows(flat_in, d_queries)
    g_key_weight = contract_rows(flat_in, d_keys)
    g_value_weight = contract_rows(flat_in, d_values)
    g_query_bias = jnp.sum(d_queries.astype(jnp.float32), 0)
    g_value_bias = jnp.sum(d_values.astype(jnp.float32), 0)
    d_input = (
        d_one
        + linear_back(d_queries, query_weight)
        + linear_back(d_keys, key_weight)
        + linear_back(d_values, value_weight)
    ).reshape(rows, stretch, width)
    grad_input = jnp.where(widened[..., None], 0.0, d_input).astype(jnp.bfloat16)
    g_mask = jnp.sum(jnp.where(widened[..., None], d_input, 0.0), (0, 1))
    small_vectors = jnp.stack(
        [g_mask, g_query_bias, g_value_bias, g_output_bias, d_mixing_gain, d_mixing_shift]
        + [g_inner_bias[i * width : (i + 1) * width] for i in range(4)]
        + [g_outer_bias, d_final_gain, d_final_shift]
    )
    small_vectors = jnp.pad(small_vectors, ((0, 3), (0, 0)))
    summed, vectors = reduce_gradients(
        [g.astype(jnp.bfloat16) for g in (g_outer_weight, g_inner_weight, g_query_weight, g_key_weight, g_value_weight, g_output_weight)],
        small_vectors,
    )
    summed = (summed[2], summed[3], summed[4], summed[5], summed[1], summed[0])
    vectors = [vectors[i] for i in range(6)] + [vectors[6:10].reshape(-1)] + [vectors[i] for i in range(10, 13)]
    return (
        layer_out,
        grad_input,
        vectors[0],
        summed[0],
        vectors[1],
        summed[1],
        summed[2],
        vectors[2],
        summed[3],
        vectors[3],
        vectors[4],
        vectors[5],
        summed[4],
        vectors[6],
        summed[5],
        vectors[7],
        vectors[8],
        vectors[9],
    )


def solution(mesh):
    return jax.shard_map(
        shards,
        mesh=mesh,
        in_specs=(
            P("batch", "seq", None),
            P("batch", "seq", None),
            P("batch", "seq"),
            P("batch"),
            P("batch"),
            P(),
            P(),
            P(),
            P(),
            P(),
            P(),
            P(),
            P(),
            P(),
            P(),
            P(),
            P(),
            P(),
            P(),
            P(),
            P(),
        ),
        out_specs=(
            P("batch", "seq", None),
            P("batch", "seq", None),
            P(),
            P("batch", "seq"),
            P(),
            P("batch", "seq"),
            P("batch", "seq"),
            P(),
            P("batch", "seq"),
            P(),
            P(),
            P(),
            P("batch", "seq"),
            P(),
            P("batch", "seq"),
            P(),
            P(),
            P(),
        ),
        check_vma=False,
    )
```

```python
import jax
import jax.numpy as jnp
from jax import lax
from jax.experimental import pallas as pl
from jax.experimental.pallas import tpu as pltpu
from jax.sharding import PartitionSpec as P

HEADS = 12
HEAD_DIM = 64
WIDEN = 5

MESH = pl.DeviceIdType.MESH
F32 = jnp.float32
BF16 = jnp.bfloat16
ROOT_HALF = 0.7071067811865476
DENSITY = 0.3989422804014327


def mm(a, b):
    return jnp.dot(a, b, preferred_element_type=F32)


def mm_t(a, b):
    return lax.dot_general(a, b, (((1,), (1,)), ((), ())), preferred_element_type=F32)


def mm_tl(a, b):
    return lax.dot_general(a, b, (((0,), (0,)), ((), ())), preferred_element_type=F32)


def fold(v):
    return jnp.sum(v.reshape(v.shape[0] // 8, 8, v.shape[1]), 0)


def loop(count, body):
    def step(i, carry):
        body(i)
        return carry

    lax.fori_loop(0, count, step, 0)


def aligned(i, size):
    return pl.ds(pl.multiple_of(i * size, size), size)


def places():
    b, s = lax.axis_index("batch"), lax.axis_index("seq")
    x, zlo, zhi = lax.rem(b, 2), lax.rem(b // 2, 2), b // 4
    core, y = lax.rem(s, 2), s // 2
    spot = {"core": core, "x": x, "y": y, "zlo": zlo, "zhi": zhi}
    peer = {
        "core": (b, s + 1 - 2 * core),
        "y": (b, s + 2 - 4 * y),
        "x": (b + 1 - 2 * x, s),
        "zlo": (b + 2 - 4 * zlo, s),
        "zhi": (b + 4 - 8 * zhi, s),
        "far": (b, 3 - s),
    }
    return spot, peer


class Unit:
    def __init__(self, number, order, both, inbox, sends, recvs, spot, peer):
        self.number, self.order, self.both, self.inbox = number, order, both, inbox
        self.sends, self.recvs, self.spot, self.peer = sends, recvs, spot, peer
        self.own = both.at[spot["core"]]

    def axis(self, phase):
        return ("core", *self.order, "zlo", "zhi")[phase]

    def where(self, phase, stays):
        spot = self.spot
        first = self.order[0]
        here = lambda name: spot[name] if stays else 1 - spot[name]
        if phase == 1 and first == "x":
            return (slice(None), slice(None), slice(None), here("x"))
        if phase == 1:
            return (here("y"),)
        if phase == 2 and first == "x":
            return (here("y"), slice(None), slice(None), spot["x"])
        if phase == 2:
            return (spot["y"], slice(None), slice(None), here("x"))
        if phase == 3:
            return (spot["y"], slice(None), here("zlo"), spot["x"])
        return (spot["y"], here("zhi"), spot["zlo"], spot["x"])

    def copy(self, phase):
        if phase == 0:
            source = self.both.at[1 - self.spot["core"]]
        else:
            source = self.own.at[self.where(phase, False)]
        return pltpu.make_async_remote_copy(
            src_ref=source,
            dst_ref=self.inbox[phase],
            send_sem=self.sends.at[self.number, phase],
            recv_sem=self.recvs.at[self.number, phase],
            device_id=self.peer[self.axis(phase)],
            device_id_type=MESH,
        )

    def start(self, phase):
        self.copy(phase).start()

    def finish(self, phase):
        self.copy(phase).wait()
        came = self.inbox[phase]
        target = self.own if phase == 0 else self.own.at[self.where(phase, True)]
        lead = came.shape[:-2]
        count = 1
        for size in lead:
            count *= size

        def body(n):
            place = []
            for size in reversed(lead):
                place.append(lax.rem(n, size))
                n = n // size
            place = tuple(reversed(place))
            target[place] = target[place] + came[place]

        loop(count, body)

    def step(self, phase):
        self.finish(phase)
        self.start(phase + 1)


ORDERS = (("x", "y"), ("y", "x"), ("x", "y"), ("y", "x"), ("x", "y"), ("y", "x"))
SLOTS = 3


def layer_body(
    hidden,
    cotangent,
    query_weight,
    key_weight,
    value_weight,
    output_weight,
    inner_weight,
    outer_weight,
    span,
    params,
    lengths,
    repeats,
    layer_out,
    grad_input,
    probs_out,
    out_query,
    out_key,
    out_value,
    out_output,
    out_inner,
    out_outer,
    out_vectors,
    wi,
    wf,
    wq,
    wk,
    wv,
    wo,
    x_all,
    k_all,
    v_all,
    q_own,
    mixed,
    region,
    first_low,
    norm_one,
    spread_one,
    total,
    d_res,
    d_outer,
    d_att,
    masks,
    wide,
    inner_sums,
    grads,
    in0,
    in1,
    in2,
    in3,
    in4,
    in5,
    d_in0,
    d_in1,
    vec,
    vec_came,
    sends,
    recvs,
    x_send,
    x_recv,
    m_send,
    m_recv,
    v_send,
    v_recv,
    local,
    credit,
):
    spot, peer = places()
    core, y = spot["core"], spot["y"]
    me = 2 * y + core
    sibling = 2 * y + 1 - core
    across = 2 * (1 - y) + core

    weight_loads = {}

    def load(name, number, source, target):
        copy = pltpu.make_async_copy(source, target, local.at[number])
        copy.start()
        weight_loads[name] = copy

    load("hidden", 0, hidden, x_all.at[:, aligned(me, 128)])
    load("key", 1, key_weight, wk)
    load("value", 2, value_weight, wv)
    load("query", 3, query_weight, wq)
    load("output", 4, output_weight, wo)
    for j in range(4):
        load(f"inner{j}", 5 + j, inner_weight.at[:, pl.ds(768 * j, 768)], wi.at[pl.ds(768 * j, 768)])
    load("outer", 9, outer_weight, wf)
    load("cotangent", 10, cotangent, d_outer)

    names = ("core", "x", "y", "zlo", "zhi", "far")
    barrier = pltpu.get_barrier_semaphore()
    for name in names:
        pl.semaphore_signal(barrier, inc=1, device_id=peer[name], device_id_type=MESH)
    pl.semaphore_wait(barrier, len(names))

    masks[me] = jnp.zeros((8, 128), jnp.int32)
    masks[me, 0:3] = span[...]
    mask_copies = []
    for i, name in enumerate(("core", "y", "far")):
        copy = pltpu.make_async_remote_copy(
            src_ref=masks.at[me],
            dst_ref=masks.at[me],
            send_sem=m_send.at[i],
            recv_sem=m_recv.at[i],
            device_id=peer[name],
            device_id_type=MESH,
        )
        copy.start()
        mask_copies.append(copy)

    def x_copy(kind, r):
        source = hidden.at[r] if kind < 2 else x_all.at[r, aligned(across, 128)]
        slot = me if kind < 2 else across
        return pltpu.make_async_remote_copy(
            src_ref=source,
            dst_ref=x_all.at[r, aligned(slot, 128)],
            send_sem=x_send.at[kind, r],
            recv_sem=x_recv.at[kind, r],
            device_id=peer["y" if kind == 0 else "core"],
            device_id_type=MESH,
        )

    for r in range(3):
        x_copy(0, r).start()
        x_copy(1, r).start()

    for copy in mask_copies:
        copy.wait()
    span_all = jnp.concatenate([masks[s].astype(F32) for s in range(4)], axis=1)
    lane = lax.broadcasted_iota(jnp.int32, span_all.shape, 1)
    window = span_all
    for d in range(1, WIDEN + 1):
        window = jnp.maximum(window, jnp.where(lane >= d, pltpu.roll(span_all, d, 1), 0.0))
        window = jnp.maximum(
            window, jnp.where(lane < 512 - d, pltpu.roll(span_all, 512 - d, 1), 0.0)
        )
    wide[...] = window.T

    weight_loads["hidden"].wait()
    weight_loads["key"].wait()
    weight_loads["value"].wait()
    weight_loads["query"].wait()
    half = lax.broadcasted_iota(jnp.int32, (128, 128), 1) < HEAD_DIM
    zero = jnp.zeros((128, 128), BF16)

    def stacked(pair):
        return jnp.concatenate([jnp.where(half, pair, zero), jnp.where(half, zero, pair)], 0)

    def unstacked(both):
        return jnp.where(half, both[:128], both[128:])

    mask_row = params[0:1]
    spills = []
    for r in range(3):
        x_copy(0, r).wait_recv()
        x_copy(2, r).start()
        x_copy(1, r).wait_recv()
        x_copy(2, r).wait()
        x_copy(0, r).wait_send()
        x_copy(1, r).wait_send()

        def put_mask(i):
            rows = aligned(i, 128)
            chosen = wide[rows, r : r + 1] > 0.5
            kept = x_all[r, rows].astype(F32)
            x_all[r, rows] = jnp.where(chosen, mask_row, kept).astype(BF16)

        loop(4, put_mask)

        def project(n):
            cols = aligned(n, 256)
            x_row = x_all[r]
            k_all[r, :, cols] = mm(x_row, wk[:, cols]).astype(BF16)
            v_all[r, :, cols] = (mm(x_row, wv[:, cols]) + params[2:3, cols]).astype(BF16)
            x_own = x_all[r, aligned(me, 128)]
            q_own[pl.ds(128 * r, 128), cols] = (
                mm(x_own, wq[:, cols]) + params[1:2, cols]
            ).astype(BF16)

        loop(3, project)
        key_live = lax.broadcasted_iota(jnp.int32, (1, 512), 1) < lengths[r]

        def attend(p):
            cols = aligned(p, 128)
            queries = stacked(q_own[pl.ds(128 * r, 128), cols] * BF16(HEAD_DIM**-0.5))
            logits = mm_t(queries, k_all[r, :, cols])
            logits = jnp.where(key_live, logits, -1e30)
            expd = jnp.exp(logits - jnp.max(logits, -1, keepdims=True))
            probs = (expd / jnp.sum(expd, -1, keepdims=True)).astype(BF16)
            base = r * 6 + p
            region[aligned(2 * base, 256)] = probs[:, :256]
            region[aligned(2 * base + 1, 256)] = probs[:, 256:]
            out = mm(probs, v_all[r, :, cols])
            mixed[pl.ds(128 * r, 128), cols] = unstacked(out).astype(BF16)

        loop(6, attend)
        rows = pl.ds(3072 * r, 3072)
        spill = pltpu.make_async_copy(region.at[rows], probs_out.at[rows], local.at[11 + r])
        spill.start()
        spills.append(spill)

    weight_loads["output"].wait()

    def first_norm(i):
        rows = aligned(i, 128)
        attended = mm(mixed[rows], wo[...]) + params[3:4]
        value = x_all[i, aligned(me, 128)].astype(F32) + attended
        center = value - jnp.mean(value, -1, keepdims=True)
        scale = lax.rsqrt(jnp.mean(center * center, -1, keepdims=True) + 1e-5)
        norm = center * scale
        norm_one[rows] = norm
        spread_one[rows] = scale
        first_low[rows] = (norm * params[4:5] + params[5:6]).astype(BF16)

    loop(3, first_norm)
    for spill in spills:
        spill.wait()
    for j in range(4):
        weight_loads[f"inner{j}"].wait()

    def hidden_units(j):
        inner = mm(
            first_low[...], wi[pl.ds((j // 3) * 768, 768), aligned(lax.rem(j, 3), 256)]
        ) + params[pl.ds(6 + j // 3, 1), aligned(lax.rem(j, 3), 256)]
        below = 0.5 * (1.0 + lax.erf(inner * ROOT_HALF))
        slope = below + inner * (DENSITY * jnp.exp(-0.5 * inner * inner))
        region[aligned(j, 384)] = (inner * below).astype(BF16)
        region[aligned(12 + j, 384)] = slope.astype(BF16)

    loop(12, hidden_units)
    weight_loads["outer"].wait()
    weight_loads["cotangent"].wait()

    def panels(first, count):
        return jnp.concatenate(
            [region[pl.ds(384 * j, 384)] for j in range(first, first + count)], axis=1
        )

    def project_out(n):
        cols = aligned(n, 256)
        total[:, cols] = mm(panels(0, 12), wf[:, cols])

    loop(3, project_out)

    def last_norm(i, sums):
        rows = aligned(i, 64)
        first = norm_one[rows] * params[4:5] + params[5:6]
        value = first + (total[rows] + params[10:11])
        center = value - jnp.mean(value, -1, keepdims=True)
        scale = lax.rsqrt(jnp.mean(center * center, -1, keepdims=True) + 1e-5)
        norm = center * scale
        d_att[rows] = (norm * params[11:12] + params[12:13]).astype(BF16)
        r = i // 2
        position = lax.broadcasted_iota(jnp.int32, (64, 1), 0) + lax.rem(i, 2) * 64 + me * 128
        weight = jnp.where(position < lengths[r], repeats[r].astype(F32), 0.0)
        d_final = d_outer[rows].astype(F32) * weight
        d_norm = d_final * params[11:12]
        d_two = scale * (
            d_norm
            - jnp.mean(d_norm, -1, keepdims=True)
            - norm * jnp.mean(d_norm * norm, -1, keepdims=True)
        )
        d_res[rows] = d_two
        low = d_two.astype(BF16)
        d_outer[rows] = low
        return (
            sums[0] + fold(d_final * norm),
            sums[1] + fold(d_final),
            sums[2] + fold(low.astype(F32)),
        )

    nothing = jnp.zeros((8, 768), F32)

    def put_sum(row, value):
        vec[0, row : row + 1] = jnp.sum(value, 0, keepdims=True)

    vec[0] = jnp.zeros((16, 768), F32)
    sums = lax.fori_loop(0, 6, last_norm, (nothing, nothing, nothing))
    put_sum(11, sums[0])
    put_sum(12, sums[1])
    put_sum(10, sums[2])
    out_copy = pltpu.make_async_copy(
        d_att, layer_out, local.at[14]
    )
    out_copy.start()

    units = []
    for u in range(6):
        inbox = [in0.at[u % SLOTS], in1.at[u], in2.at[u], in3.at[u], in4.at[u]]
        units.append(Unit(u, ORDERS[u], grads.at[u], inbox, sends, recvs, spot, peer))

    def free_slot():
        pl.semaphore_signal(credit, inc=1, device_id=peer["core"], device_id_type=MESH)

    def claim_slot():
        pl.semaphore_wait(credit, 1)

    def outer_grads(z):
        for x in range(2):
            cols = [region[pl.ds(pl.multiple_of((3 * z + j) * 384, 384), 384)] for j in range(3)]
            part = jnp.concatenate(cols, axis=1)[:, 384 * x : 384 * x + 384]
            grad = mm_tl(part, d_outer[...]).astype(BF16)
            for h in range(2):
                for i in range(2):
                    for side in range(2):
                        rows = (h * 2 + i) * 96
                        grads[i, h, side, z // 2, lax.rem(z, 2), x] = grad[
                            rows : rows + 96, side * 384 : side * 384 + 384
                        ]

    loop(4, outer_grads)
    units[0].start(0)
    units[1].start(0)

    def d_hidden_units(j):
        d_act = mm_t(d_outer[...], wf[aligned(j, 256)])
        place = aligned(12 + j, 384)
        low = (d_act * region[place].astype(F32)).astype(BF16)
        region[place] = low
        inner_sums[j] = fold(low.astype(F32))

    loop(12, d_hidden_units)

    def inner_grads(s):
        cols = [region[pl.ds(pl.multiple_of((12 + 3 * s + j) * 384, 384), 384)] for j in range(3)]
        grad = mm_tl(first_low[...], jnp.concatenate(cols, axis=1)).astype(BF16)
        for b in range(8):
            for i in range(2):
                grads[2 + i, lax.rem(s, 2), s // 2, b // 4, (b // 2) % 2, b % 2] = grad[
                    96 * b : 96 * b + 96, 384 * i : 384 * i + 384
                ]

    loop(4, inner_grads)
    units[2].start(0)
    for u in range(2):
        units[u].step(0)
        if u == 0:
            free_slot()
            claim_slot()
            units[3].start(0)
        else:
            free_slot()

    def d_first_part(n):
        cols = aligned(n, 256)
        acc = None
        for s in range(4):
            d_inner = panels(12 + 3 * s, 3)
            term = mm_t(d_inner, wi[pl.ds(pl.multiple_of(s * 768 + n * 256, 256), 256)])
            acc = term if acc is None else acc + term
        total[:, cols] = acc

    loop(3, d_first_part)
    for j in range(12):
        vec[0, 6 + j // 3 : 7 + j // 3, (j % 3) * 256 : (j % 3) * 256 + 256] = jnp.sum(
            inner_sums[j], 0, keepdims=True
        )
    refills = []
    for r in range(3):
        rows = pl.ds(3072 * r, 3072)
        refill = pltpu.make_async_copy(probs_out.at[rows], region.at[rows], local.at[15 + r])
        refill.start()
        refills.append(refill)
    out_copy.wait()

    def first_norm_back(i, sums):
        rows = aligned(i, 64)
        d_first = total[rows] + d_res[rows]
        norm = norm_one[rows]
        d_norm = d_first * params[4:5]
        d_one = spread_one[rows] * (
            d_norm
            - jnp.mean(d_norm, -1, keepdims=True)
            - norm * jnp.mean(d_norm * norm, -1, keepdims=True)
        )
        d_res[rows] = d_one
        low = d_one.astype(BF16)
        d_att[rows] = low
        return (
            sums[0] + fold(d_first * norm),
            sums[1] + fold(d_first),
            sums[2] + fold(low.astype(F32)),
        )

    sums = lax.fori_loop(0, 6, first_norm_back, (nothing, nothing, nothing))
    put_sum(4, sums[0])
    put_sum(5, sums[1])
    put_sum(3, sums[2])

    def square_grads(u, lower, left, right):
        for m in range(2):
            grad = mm_tl(left(m), right).astype(BF16)
            for b in range(4):
                for h in range(2):
                    for side in range(2):
                        rows = b * 96 + h * 48
                        grads[u, h, side, m, b // 2, b % 2, pl.ds(lower * 48, 48)] = grad[
                            rows : rows + 48, side * 384 : side * 384 + 384
                        ]

    square_grads(4, 0, lambda m: mixed[:, 384 * m : 384 * m + 384], d_att[...])

    def d_mixed_part(i):
        rows = aligned(i, 128)
        mixed[rows] = mm_t(d_att[rows], wo[...]).astype(BF16)

    loop(3, d_mixed_part)
    units[2].step(0)
    free_slot()
    units[3].step(0)

    for r in range(3):
        refills[r].wait()

        def attend_back(p):
            cols = aligned(p, 128)
            own_rows = pl.ds(128 * r, 128)
            base = r * 6 + p
            queries = stacked(q_own[own_rows, cols] * BF16(HEAD_DIM**-0.5))
            d_mix = stacked(mixed[own_rows, cols])
            low_probs = jnp.concatenate(
                [region[aligned(2 * base, 256)], region[aligned(2 * base + 1, 256)]], axis=1
            )
            d_probs = mm_t(d_mix, v_all[r, :, cols])
            probs = low_probs.astype(F32)
            weighted = probs * d_probs
            d_raw = (weighted - probs * jnp.sum(weighted, -1, keepdims=True)).astype(BF16)
            d_query = mm(d_raw, k_all[r, :, cols]) * HEAD_DIM**-0.5
            q_own[own_rows, cols] = unstacked(d_query).astype(BF16)
            wi[pl.ds(512 * r, 512), cols] = mm_tl(d_raw, queries).astype(BF16)
            wi[pl.ds(1536 + 512 * r, 512), cols] = mm_tl(low_probs, d_mix).astype(BF16)

        loop(6, attend_back)
        if r == 0:
            units[0].step(1)
            units[1].step(1)
        elif r == 1:
            units[0].step(2)
            units[1].step(2)
        else:
            units[2].step(1)
            units[3].step(1)

    def own_inputs(m):
        return jnp.concatenate(
            [x_all[r, aligned(me, 128), pl.ds(384 * m, 384)] for r in range(3)], 0
        )

    def all_inputs(m):
        return jnp.concatenate([x_all[r, :, pl.ds(384 * m, 384)] for r in range(3)], 0)

    square_grads(4, 1, own_inputs, q_own[...])
    claim_slot()
    units[4].start(0)
    square_grads(5, 0, all_inputs, wi[pl.ds(0, 1536)])
    square_grads(5, 1, all_inputs, wi[pl.ds(1536, 1536)])
    claim_slot()
    units[5].start(0)
    put_sum(1, fold(q_own[...].astype(F32)))

    def value_sum(i, acc):
        return acc + fold(wi[pl.ds(pl.multiple_of(1536 + i * 128, 128), 128)].astype(F32))

    put_sum(2, lax.fori_loop(0, 12, value_sum, nothing))
    units[0].step(3)
    units[1].step(3)

    mask_sum = nothing
    for r in range(3):

        def d_in_part(s, acc):
            part = mm_t(wi[pl.ds(pl.multiple_of(512 * r + s * 128, 128), 128)], wk[...]) + mm_t(
                wi[pl.ds(pl.multiple_of(1536 + 512 * r + s * 128, 128), 128)], wv[...]
            )
            chosen = wide[aligned(s, 128), r : r + 1]
            wf[pl.ds(pl.multiple_of(s * 384 + r * 128, 128), 128)] = part.astype(BF16)
            return acc + fold(part * chosen)

        mask_sum = lax.fori_loop(0, 4, d_in_part, mask_sum)

    def d_in_copy(i):
        if i < 2:
            piece, target, name = 2 * i + 1 - core, d_in0.at[i], "core"
        else:
            piece, target, name = across, d_in1, "y"
        return pltpu.make_async_remote_copy(
            src_ref=wf.at[aligned(piece, 384)],
            dst_ref=target,
            send_sem=x_send.at[3, i],
            recv_sem=x_recv.at[3, i],
            device_id=peer[name],
            device_id_type=MESH,
        )

    d_in_copy(0).start()
    d_in_copy(1).start()

    def own_part(i, acc):
        rows = aligned(i, 128)
        part = d_res[rows] + mm_t(q_own[rows], wq[...])
        d_res[rows] = part
        chosen = wide[aligned(me, 128)]
        chosen = jnp.where(i == 0, chosen[:, 0:1], jnp.where(i == 1, chosen[:, 1:2], chosen[:, 2:3]))
        return acc + fold(part * chosen)

    put_sum(0, lax.fori_loop(0, 3, own_part, mask_sum))

    def vector_copy(phase):
        return pltpu.make_async_remote_copy(
            src_ref=vec.at[phase],
            dst_ref=vec_came.at[phase],
            send_sem=v_send.at[phase],
            recv_sem=v_recv.at[phase],
            device_id=peer[names[phase]],
            device_id_type=MESH,
        )

    def vector_step(phase):
        vector_copy(phase).wait()
        vec[phase + 1] = vec[phase] + vec_came[phase]
        if phase < 4:
            vector_copy(phase + 1).start()

    vector_copy(0).start()
    d_in_copy(0).wait()
    d_in_copy(1).wait()

    def add_across(i):
        rows = pl.ds(pl.multiple_of(across * 384 + i * 128, 128), 128)
        wf[rows] = wf[rows] + d_in0[1 - y, aligned(i, 128)]

    loop(3, add_across)
    d_in_copy(2).start()
    units[4].step(0)
    units[5].step(0)
    vector_step(0)
    units[2].step(2)
    units[3].step(2)
    vector_step(1)
    units[4].step(1)
    units[5].step(1)
    vector_step(2)
    units[2].step(3)
    units[3].step(3)
    units[4].step(2)
    units[5].step(2)
    vector_step(3)

    mine = (y, spot["zhi"], spot["zlo"], spot["x"])

    def swap_copy(u):
        return pltpu.make_async_remote_copy(
            src_ref=units[u].own.at[mine],
            dst_ref=in5.at[u],
            send_sem=sends.at[u, 5],
            recv_sem=recvs.at[u, 5],
            device_id=peer["core"],
            device_id_type=MESH,
        )

    def close(u):
        units[u].copy(4).wait()
        result = units[u].own[mine].astype(F32) + in4[u].astype(F32)
        if u == 2 or u == 3:
            out_inner[:, pl.ds(384 * (u - 2), 384)] = result
            return
        units[u].own[mine] = result.astype(BF16)
        swap_copy(u).start()
        put_half(u, core, result)

    def put_half(u, side, value):
        value = jnp.where(core == 0, value[:, :192], pltpu.roll(value, 192, 1)[:, :192])
        if u < 2:
            out_outer[pl.ds(pl.multiple_of(side * 192 + u * 96, 96), 96)] = value
            return
        targets = (out_output, out_query) if u == 4 else (out_key, out_value)
        for i, target in enumerate(targets):
            target[pl.ds(pl.multiple_of(side * 48, 48), 48)] = value[48 * i : 48 * i + 48]

    for u in range(4):
        close(u)
    units[4].step(3)
    units[5].step(3)

    d_in_copy(2).wait()

    def finish_input(i):
        rows = aligned(i, 128)
        mine = pl.ds(pl.multiple_of(me * 384 + i * 128, 128), 128)
        value = (
            d_res[rows]
            + wf[mine].astype(F32)
            + d_in0[y, rows].astype(F32)
            + d_in1[rows].astype(F32)
        )
        chosen = wide[aligned(me, 128)]
        chosen = jnp.where(i == 0, chosen[:, 0:1], jnp.where(i == 1, chosen[:, 1:2], chosen[:, 2:3]))
        d_att[rows] = jnp.where(chosen > 0.5, 0.0, value).astype(BF16)

    loop(3, finish_input)
    grad_copy = pltpu.make_async_copy(d_att, grad_input, local.at[18])
    grad_copy.start()
    close(4)
    close(5)
    vector_step(4)
    out_vectors[...] = vec[5]
    for u in (0, 1, 4, 5):
        swap_copy(u).wait()
        put_half(u, 1 - core, in5[u].astype(F32))
    grad_copy.wait()


def fused_layer(
    hidden_in,
    cotangent,
    span_mask,
    lengths,
    repeats,
    mask_embedding,
    query_weight,
    query_bias,
    key_weight,
    value_weight,
    value_bias,
    output_weight,
    output_bias,
    mixing_gain,
    mixing_shift,
    inner_weight,
    inner_bias,
    outer_weight,
    outer_bias,
    final_gain,
    final_shift,
):
    params = jnp.concatenate(
        [
            v.astype(F32)
            for v in (
                mask_embedding,
                query_bias,
                value_bias,
                output_bias,
                mixing_gain,
                mixing_shift,
                inner_bias,
                outer_bias,
                final_gain,
                final_shift,
            )
        ]
    ).reshape(13, 768)
    vmem = pl.BlockSpec(memory_space=pltpu.VMEM)
    anywhere = pl.BlockSpec(memory_space=pl.ANY)
    scalars = pl.BlockSpec(memory_space=pltpu.SMEM)
    bf = lambda *shape: pltpu.VMEM(shape, BF16)
    fl = lambda *shape: pltpu.VMEM(shape, F32)
    dma = lambda *shape: pltpu.SemaphoreType.DMA(shape)
    shape = lambda dims, dtype: jax.ShapeDtypeStruct(dims, dtype)
    result = pl.pallas_call(
        layer_body,
        out_shape=[
            shape((384, 768), BF16),
            shape((384, 768), BF16),
            shape((9216, 256), BF16),
            shape((96, 192), F32),
            shape((96, 192), F32),
            shape((96, 192), F32),
            shape((96, 192), F32),
            shape((96, 768), F32),
            shape((384, 192), F32),
            shape((16, 768), F32),
        ],
        in_specs=[anywhere] * 8 + [vmem, vmem, scalars, scalars],
        out_specs=[anywhere] * 3 + [vmem] * 7,
        scratch_shapes=[
            bf(3072, 768),
            bf(3072, 768),
            bf(768, 768),
            bf(768, 768),
            bf(768, 768),
            bf(768, 768),
            bf(3, 512, 768),
            bf(3, 512, 768),
            bf(3, 512, 768),
            bf(384, 768),
            bf(384, 768),
            bf(9216, 256),
            bf(384, 768),
            fl(384, 768),
            fl(384, 1),
            fl(384, 768),
            fl(384, 768),
            bf(384, 768),
            bf(384, 768),
            pltpu.VMEM((4, 8, 128), jnp.int32),
            fl(512, 8),
            fl(12, 8, 256),
            bf(6, 2, 2, 2, 2, 2, 96, 384),
            bf(SLOTS, 2, 2, 2, 2, 96, 384),
            bf(6, 2, 2, 2, 96, 384),
            bf(6, 2, 2, 96, 384),
            bf(6, 2, 96, 384),
            bf(6, 96, 384),
            bf(6, 96, 384),
            bf(2, 384, 768),
            bf(384, 768),
            fl(6, 16, 768),
            fl(5, 16, 768),
            dma(6, 6),
            dma(6, 6),
            dma(4, 3),
            dma(4, 3),
            dma(3),
            dma(3),
            dma(5),
            dma(5),
            dma(19),
            pltpu.SemaphoreType.REGULAR,
        ],
        compiler_params=pltpu.CompilerParams(
            collective_id=1, has_side_effects=True, vmem_limit_bytes=63 * 2**20
        ),
        name="fused_layer",
    )(
        hidden_in,
        cotangent.reshape(384, 768),
        query_weight,
        key_weight,
        value_weight,
        output_weight,
        inner_weight,
        outer_weight,
        span_mask,
        params,
        lengths,
        repeats,
    )
    layer_out, grad_input, _, g_query, g_key, g_value, g_output, g_inner, g_outer, vectors = result
    return (
        layer_out.reshape(3, 128, 768),
        grad_input.reshape(3, 128, 768),
        vectors[0],
        g_query,
        vectors[1],
        g_key,
        g_value,
        vectors[2],
        g_output,
        vectors[3],
        vectors[4],
        vectors[5],
        g_inner,
        vectors[6:10].reshape(-1),
        g_outer,
        vectors[10],
        vectors[11],
        vectors[12],
    )


def with_halo(x, sides, width):
    for axis, dim in sides:
        count, length = (lax.axis_size(axis), x.shape[dim])
        up = [(i, (i + 1) % count) for i in range(count - 1)]
        down = [(j, i) for i, j in up]
        last = lax.slice_in_dim(x, length - width, length, axis=dim)
        initial = lax.slice_in_dim(x, 0, width, axis=dim)
        before = lax.ppermute(last, axis, up)
        after = lax.ppermute(initial, axis, down)
        x = jnp.concatenate([before, x, after], axis=dim)
    return x


def layer_norm(inputs, gain, shift):
    center = inputs - jnp.mean(inputs, -1, keepdims=True)
    spread = jnp.mean(center * center, -1, keepdims=True)
    return center * lax.rsqrt(spread + 1e-05) * gain + shift


def linear(inputs, weight):
    return jnp.dot(inputs, weight, preferred_element_type=jnp.float32)


def linear_back(grads, weight):
    return lax.dot_general(
        grads, weight, (((1,), (1,)), ((), ())), preferred_element_type=jnp.float32
    )


def contract_rows(left, right):
    return lax.dot_general(
        left, right, (((0,), (0,)), ((), ())), preferred_element_type=jnp.float32
    )


def gelu_exact(inputs):
    return jax.nn.gelu(inputs, approximate=False)


def plain_layer(
    hidden_in,
    cotangent,
    span_mask,
    lengths,
    repeats,
    mask_embedding,
    query_weight,
    query_bias,
    key_weight,
    value_weight,
    value_bias,
    output_weight,
    output_bias,
    mixing_gain,
    mixing_shift,
    inner_weight,
    inner_bias,
    outer_weight,
    outer_bias,
    final_gain,
    final_shift,
):
    rows, stretch, width = hidden_in.shape
    whole = stretch * lax.axis_size("seq")
    scale = HEAD_DIM ** (-0.5)
    offset = lax.axis_index("seq") * stretch
    rim = with_halo(span_mask, (("seq", 1),), WIDEN)
    window = rim[:, 0:stretch]
    for shifted in range(1, 2 * WIDEN + 1):
        window = window + rim[:, shifted : shifted + stretch]
    widened = window > 0
    positions = offset + jnp.arange(stretch, dtype=jnp.int32)
    live = positions[None, :] < lengths[:, None]
    key_live = jnp.arange(whole, dtype=jnp.int32)[None, :] < lengths[:, None]
    masked_in = jnp.where(widened[..., None], mask_embedding[None, None, :], hidden_in)
    flat_in = masked_in.reshape(rows * stretch, width)
    queries = (linear(flat_in, query_weight) + query_bias.astype(jnp.float32)).astype(jnp.bfloat16)
    key_rows = linear(flat_in, key_weight).astype(jnp.bfloat16).reshape(rows, stretch, width)
    value_rows = (linear(flat_in, value_weight) + value_bias.astype(jnp.float32)).astype(
        jnp.bfloat16
    )
    value_rows = value_rows.reshape(rows, stretch, width)
    key_all, value_all = (
        lax.all_gather(key_rows, "seq", axis=1, tiled=True),
        lax.all_gather(value_rows, "seq", axis=1, tiled=True),
    )
    query_heads = queries.reshape(rows, stretch, HEADS, HEAD_DIM)

    def scores_of(key_full):
        key_heads = key_full.reshape(rows, whole, HEADS, HEAD_DIM)
        raw = jnp.einsum(
            "rqhd,rkhd->rhqk", query_heads, key_heads, preferred_element_type=jnp.float32
        )
        return jnp.where(key_live[:, None, None, :], raw * scale, -1e30)

    logits = scores_of(key_all)
    highest = jnp.max(logits, -1, keepdims=True)
    expd = jnp.exp(logits - highest)
    totals = jnp.sum(expd, -1, keepdims=True)
    log_total = highest + jnp.log(totals)
    probs_low = (expd / totals).astype(jnp.bfloat16)
    value_heads = value_all.reshape(rows, whole, HEADS, HEAD_DIM)
    mixed = jnp.einsum(
        "rhqk,rkhd->rqhd", probs_low, value_heads, preferred_element_type=jnp.float32
    )
    mixed = mixed.reshape(rows * stretch, width).astype(jnp.bfloat16)
    attended = linear(mixed, output_weight) + output_bias.astype(jnp.float32)
    residual_one = flat_in.astype(jnp.float32) + attended
    first, norm_back_one = jax.vjp(
        layer_norm, residual_one, mixing_gain.astype(jnp.float32), mixing_shift.astype(jnp.float32)
    )
    first_low = first.astype(jnp.bfloat16)
    inner = linear(first_low, inner_weight) + inner_bias.astype(jnp.float32)
    activated, gelu_back = jax.vjp(gelu_exact, inner)
    activated_low = activated.astype(jnp.bfloat16)
    outer = linear(activated_low, outer_weight) + outer_bias.astype(jnp.float32)
    final, norm_back_two = jax.vjp(
        layer_norm, first + outer, final_gain.astype(jnp.float32), final_shift.astype(jnp.float32)
    )
    layer_out = final.astype(jnp.bfloat16).reshape(rows, stretch, width)
    weighting = repeats.astype(jnp.float32)[:, None] * live.astype(jnp.float32)
    d_final = (cotangent.astype(jnp.float32) * weighting[:, :, None]).reshape(rows * stretch, width)
    d_two, d_final_gain, d_final_shift = norm_back_two(d_final)
    d_outer = d_two.astype(jnp.bfloat16)
    g_outer_weight = contract_rows(activated_low, d_outer)
    g_outer_bias = jnp.sum(d_outer.astype(jnp.float32), 0)
    (d_inner,) = gelu_back(linear_back(d_outer, outer_weight))
    d_inner = d_inner.astype(jnp.bfloat16)
    g_inner_weight = contract_rows(first_low, d_inner)
    g_inner_bias = jnp.sum(d_inner.astype(jnp.float32), 0)
    d_first = linear_back(d_inner, inner_weight) + d_two
    d_one, d_mixing_gain, d_mixing_shift = norm_back_one(d_first)
    d_attended = d_one.astype(jnp.bfloat16)
    g_output_weight = contract_rows(mixed, d_attended)
    g_output_bias = jnp.sum(d_attended.astype(jnp.float32), 0)
    d_mixed = linear_back(d_attended, output_weight).astype(jnp.bfloat16)
    d_mixed_heads = d_mixed.reshape(rows, stretch, HEADS, HEAD_DIM)
    key_back, value_back = (
        lax.all_gather(key_rows, "seq", axis=1, tiled=True),
        lax.all_gather(value_rows, "seq", axis=1, tiled=True),
    )
    probs = jnp.exp(scores_of(key_back) - log_total)
    probs_again = probs.astype(jnp.bfloat16)
    key_heads = key_back.reshape(rows, whole, HEADS, HEAD_DIM)
    value_heads = value_back.reshape(rows, whole, HEADS, HEAD_DIM)
    d_probs = jnp.einsum(
        "rqhd,rkhd->rhqk", d_mixed_heads, value_heads, preferred_element_type=jnp.float32
    )
    centered = d_probs - jnp.sum(probs * d_probs, -1, keepdims=True)
    d_raw = (probs * centered * scale).astype(jnp.bfloat16)
    d_queries = jnp.einsum("rhqk,rkhd->rqhd", d_raw, key_heads, preferred_element_type=jnp.float32)
    d_queries = d_queries.reshape(rows * stretch, width).astype(jnp.bfloat16)
    d_key_part = jnp.einsum(
        "rhqk,rqhd->rkhd", d_raw, query_heads, preferred_element_type=jnp.float32
    )
    d_value_part = jnp.einsum(
        "rhqk,rqhd->rkhd", probs_again, d_mixed_heads, preferred_element_type=jnp.float32
    )
    d_key_sum, d_value_sum = (
        lax.psum_scatter(
            d_key_part.reshape(rows, whole, width), "seq", scatter_dimension=1, tiled=True
        ),
        lax.psum_scatter(
            d_value_part.reshape(rows, whole, width), "seq", scatter_dimension=1, tiled=True
        ),
    )
    d_keys = d_key_sum.astype(jnp.bfloat16).reshape(rows * stretch, width)
    d_values = d_value_sum.astype(jnp.bfloat16).reshape(rows * stretch, width)
    g_query_weight = contract_rows(flat_in, d_queries)
    g_key_weight = contract_rows(flat_in, d_keys)
    g_value_weight = contract_rows(flat_in, d_values)
    g_query_bias = jnp.sum(d_queries.astype(jnp.float32), 0)
    g_value_bias = jnp.sum(d_values.astype(jnp.float32), 0)
    d_input = (
        d_one
        + linear_back(d_queries, query_weight)
        + linear_back(d_keys, key_weight)
        + linear_back(d_values, value_weight)
    ).reshape(rows, stretch, width)
    grad_input = jnp.where(widened[..., None], 0.0, d_input).astype(jnp.bfloat16)
    g_mask = jnp.sum(jnp.where(widened[..., None], d_input, 0.0), (0, 1))
    matrices = (
        g_query_weight,
        g_key_weight,
        g_value_weight,
        g_output_weight,
        g_inner_weight,
        g_outer_weight,
    )
    partial_sums = (
        lax.psum_scatter(matrices[0], "batch", scatter_dimension=0, tiled=True),
        lax.psum_scatter(matrices[1], "batch", scatter_dimension=0, tiled=True),
        lax.psum_scatter(matrices[2], "batch", scatter_dimension=0, tiled=True),
        lax.psum_scatter(matrices[3], "batch", scatter_dimension=0, tiled=True),
        lax.psum_scatter(matrices[4], "batch", scatter_dimension=0, tiled=True),
        lax.psum_scatter(matrices[5], "batch", scatter_dimension=0, tiled=True),
    )
    summed = (
        lax.psum_scatter(partial_sums[0], "seq", scatter_dimension=1, tiled=True),
        lax.psum_scatter(partial_sums[1], "seq", scatter_dimension=1, tiled=True),
        lax.psum_scatter(partial_sums[2], "seq", scatter_dimension=1, tiled=True),
        lax.psum_scatter(partial_sums[3], "seq", scatter_dimension=1, tiled=True),
        lax.psum_scatter(partial_sums[4], "seq", scatter_dimension=1, tiled=True),
        lax.psum_scatter(partial_sums[5], "seq", scatter_dimension=1, tiled=True),
    )
    vectors = lax.psum(
        (
            g_mask,
            g_query_bias,
            g_value_bias,
            g_output_bias,
            d_mixing_gain,
            d_mixing_shift,
            g_inner_bias,
            g_outer_bias,
            d_final_gain,
            d_final_shift,
        ),
        ("batch", "seq"),
    )
    return (
        layer_out,
        grad_input,
        vectors[0],
        summed[0],
        vectors[1],
        summed[1],
        summed[2],
        vectors[2],
        summed[3],
        vectors[3],
        vectors[4],
        vectors[5],
        summed[4],
        vectors[6],
        summed[5],
        vectors[7],
        vectors[8],
        vectors[9],
    )


def solution(mesh):
    fused = mesh.shape["batch"] == 8 and mesh.shape["seq"] == 4
    return jax.shard_map(
        fused_layer if fused else plain_layer,
        mesh=mesh,
        in_specs=(
            P("batch", "seq", None),
            P("batch", "seq", None),
            P("batch", "seq"),
            P("batch"),
            P("batch"),
            P(),
            P(),
            P(),
            P(),
            P(),
            P(),
            P(),
            P(),
            P(),
            P(),
            P(),
            P(),
            P(),
            P(),
            P(),
            P(),
        ),
        out_specs=(
            P("batch", "seq", None),
            P("batch", "seq", None),
            P(),
            P("batch", "seq"),
            P(),
            P("batch", "seq"),
            P("batch", "seq"),
            P(),
            P("batch", "seq"),
            P(),
            P(),
            P(),
            P("batch", "seq"),
            P(),
            P("batch", "seq"),
            P(),
            P(),
            P(),
        ),
        check_vma=False,
    )
```

```python
import jax
import jax.numpy as jnp
from jax import lax
from jax.experimental import pallas as pl
from jax.experimental.pallas import tpu as pltpu
from jax.sharding import PartitionSpec as P

HEADS = 12
HEAD_DIM = 64
WIDEN = 5

MESH = pl.DeviceIdType.MESH
F32 = jnp.float32
BF16 = jnp.bfloat16
ROOT_HALF = 0.7071067811865476
DENSITY = 0.3989422804014327


def mm(a, b):
    return jnp.dot(a, b, preferred_element_type=F32)


def mm_t(a, b):
    return lax.dot_general(a, b, (((1,), (1,)), ((), ())), preferred_element_type=F32)


def mm_tl(a, b):
    return lax.dot_general(a, b, (((0,), (0,)), ((), ())), preferred_element_type=F32)


def fold(v):
    return jnp.sum(v.reshape(v.shape[0] // 8, 8, v.shape[1]), 0)


def loop(count, body):
    def step(i, carry):
        body(i)
        return carry

    lax.fori_loop(0, count, step, 0)


def aligned(i, size):
    return pl.ds(pl.multiple_of(i * size, size), size)


def places():
    b, s = lax.axis_index("batch"), lax.axis_index("seq")
    x, zlo, zhi = lax.rem(b, 2), lax.rem(b // 2, 2), b // 4
    core, y = lax.rem(s, 2), s // 2
    spot = {"core": core, "x": x, "y": y, "zlo": zlo, "zhi": zhi}
    peer = {
        "core": (b, s + 1 - 2 * core),
        "y": (b, s + 2 - 4 * y),
        "x": (b + 1 - 2 * x, s),
        "zlo": (b + 2 - 4 * zlo, s),
        "zhi": (b + 4 - 8 * zhi, s),
        "far": (b, 3 - s),
    }
    return spot, peer


class Unit:
    def __init__(self, order, both, inbox, sends, recvs, spot, peer):
        self.order, self.both, self.inbox = order, both, inbox
        self.sends, self.recvs, self.spot, self.peer = sends, recvs, spot, peer
        self.own = both.at[spot["core"]]
        self.phase = 0

    def where(self, phase, stays):
        done, axis = self.order[: phase - 1], self.order[phase - 1]
        place = []
        for name in ("y", "zhi", "zlo", "x"):
            side = self.spot[name]
            if name == axis:
                place.append(side if stays else 1 - side)
            else:
                place.append(side if name in done else slice(None))
        return tuple(place)

    def copy(self, phase):
        if phase == 0:
            axis, source = "core", self.both.at[1 - self.spot["core"]]
        else:
            axis, source = self.order[phase - 1], self.own.at[self.where(phase, False)]
        return pltpu.make_async_remote_copy(
            src_ref=source,
            dst_ref=self.inbox[phase],
            send_sem=self.sends.at[phase],
            recv_sem=self.recvs.at[phase],
            device_id=self.peer[axis],
            device_id_type=MESH,
        )

    def start(self):
        self.copy(0).start()

    def step(self):
        phase = self.phase
        self.copy(phase).wait()
        came = self.inbox[phase]
        target = self.own if phase == 0 else self.own.at[self.where(phase, True)]
        lead = 4 - phase

        def body(n):
            place = tuple(lax.rem(n // 2 ** (lead - 1 - i), 2) for i in range(lead))
            target[place] = target[place] + came[place]

        loop(2**lead, body)
        self.phase = phase + 1
        self.copy(self.phase).start()


NAMES = ("outer0", "outer1", "inner0", "inner1", "output", "query", "key", "value")
ORDERS = {
    "outer0": ("x", "y", "zlo", "zhi"),
    "outer1": ("y", "x", "zlo", "zhi"),
    "inner0": ("x", "y", "zlo", "zhi"),
    "inner1": ("zlo", "y", "x", "zhi"),
    "output": ("y", "x", "zlo", "zhi"),
    "query": ("x", "y", "zlo", "zhi"),
    "key": ("x", "zlo", "zhi", "y"),
    "value": ("zlo", "zhi", "x", "y"),
}
SLOTS = 3


def layer_body(
    hidden,
    cotangent,
    query_weight,
    key_weight,
    value_weight,
    output_weight,
    inner_weight,
    outer_weight,
    span,
    mask_embedding,
    query_bias,
    value_bias,
    output_bias,
    mixing_gain,
    mixing_shift,
    inner_bias,
    outer_bias,
    final_gain,
    final_shift,
    lengths,
    repeats,
    layer_out,
    grad_input,
    probs_out,
    out_query,
    out_key,
    out_value,
    out_output,
    out_inner,
    out_outer,
    out_vectors,
    wi,
    wf,
    wq,
    wk,
    wv,
    wo,
    params,
    x_all,
    k_all,
    v_all,
    q_own,
    mixed,
    region,
    first_low,
    norm_one,
    spread_one,
    total,
    d_res,
    d_outer,
    d_att,
    masks,
    wide,
    inner_sums,
    mask_sums,
    big_grads,
    small_grads,
    in0,
    big1,
    big2,
    big3,
    big4,
    big5,
    small1,
    small2,
    small3,
    small4,
    small5,
    d_in0,
    d_in1,
    vec,
    vec_came,
    sends,
    recvs,
    x_send,
    x_recv,
    m_send,
    m_recv,
    v_send,
    v_recv,
    local,
    credit,
):
    spot, peer = places()
    core, y = spot["core"], spot["y"]
    me = 2 * y + core
    sibling = 2 * y + 1 - core
    across = 2 * (1 - y) + core

    weight_loads = {}

    def load(name, number, source, target):
        copy = pltpu.make_async_copy(source, target, local.at[number])
        copy.start()
        weight_loads[name] = copy

    load("hidden", 0, hidden, x_all.at[:, aligned(me, 128)])
    load("key", 1, key_weight, wk)
    load("value", 2, value_weight, wv)
    load("query", 3, query_weight, wq)
    load("output", 4, output_weight, wo)
    for j in range(4):
        load(f"inner{j}", 5 + j, inner_weight.at[:, pl.ds(768 * j, 768)], wi.at[pl.ds(768 * j, 768)])
    load("outer", 9, outer_weight, wf)
    load("cotangent", 10, cotangent, d_outer)

    names = ("core", "x", "y", "zlo", "zhi", "far")
    barrier = pltpu.get_barrier_semaphore()
    for name in names:
        pl.semaphore_signal(barrier, inc=1, device_id=peer[name], device_id_type=MESH)
    pl.semaphore_wait(barrier, len(names))

    vectors = [mask_embedding, query_bias, value_bias, output_bias, mixing_gain, mixing_shift]
    vectors += [inner_bias.at[pl.ds(768 * i, 768)] for i in range(4)]
    vectors += [outer_bias, final_gain, final_shift]
    for i, vector in enumerate(vectors):
        params[i : i + 1] = vector[...].astype(F32).reshape(1, 768)

    masks[me] = jnp.zeros((8, 128), jnp.int32)
    masks[me, 0:3] = span[...]
    mask_copies = []
    for i, name in enumerate(("core", "y", "far")):
        copy = pltpu.make_async_remote_copy(
            src_ref=masks.at[me],
            dst_ref=masks.at[me],
            send_sem=m_send.at[i],
            recv_sem=m_recv.at[i],
            device_id=peer[name],
            device_id_type=MESH,
        )
        copy.start()
        mask_copies.append(copy)

    def x_copy(kind, r):
        source = hidden.at[r] if kind < 2 else x_all.at[r, aligned(across, 128)]
        slot = me if kind < 2 else across
        return pltpu.make_async_remote_copy(
            src_ref=source,
            dst_ref=x_all.at[r, aligned(slot, 128)],
            send_sem=x_send.at[kind, r],
            recv_sem=x_recv.at[kind, r],
            device_id=peer["y" if kind == 0 else "core"],
            device_id_type=MESH,
        )

    for r in range(3):
        x_copy(0, r).start()
        x_copy(1, r).start()

    for copy in mask_copies:
        copy.wait()
    span_all = jnp.concatenate([masks[s].astype(F32) for s in range(4)], axis=1)
    lane = lax.broadcasted_iota(jnp.int32, span_all.shape, 1)
    window = span_all
    for d in range(1, WIDEN + 1):
        window = jnp.maximum(window, jnp.where(lane >= d, pltpu.roll(span_all, d, 1), 0.0))
        window = jnp.maximum(
            window, jnp.where(lane < 512 - d, pltpu.roll(span_all, 512 - d, 1), 0.0)
        )
    wide[...] = window.T

    weight_loads["hidden"].wait()
    weight_loads["key"].wait()
    weight_loads["value"].wait()
    weight_loads["query"].wait()
    half = lax.broadcasted_iota(jnp.int32, (128, 128), 1) < HEAD_DIM
    zero = jnp.zeros((128, 128), BF16)

    def stacked(pair):
        return jnp.concatenate([jnp.where(half, pair, zero), jnp.where(half, zero, pair)], 0)

    def unstacked(both):
        return jnp.where(half, both[:128], both[128:])

    mask_row = params[0:1]
    spills = []
    for r in range(3):
        x_copy(0, r).wait_recv()
        x_copy(2, r).start()
        x_copy(1, r).wait_recv()
        x_copy(2, r).wait()
        x_copy(0, r).wait_send()
        x_copy(1, r).wait_send()

        def put_mask(i):
            rows = aligned(i, 128)
            chosen = wide[rows, r : r + 1] > 0.5
            kept = x_all[r, rows].astype(F32)
            x_all[r, rows] = jnp.where(chosen, mask_row, kept).astype(BF16)

        loop(4, put_mask)

        def project(n):
            cols = aligned(n, 256)
            x_row = x_all[r]
            k_all[r, :, cols] = mm(x_row, wk[:, cols]).astype(BF16)
            v_all[r, :, cols] = (mm(x_row, wv[:, cols]) + params[2:3, cols]).astype(BF16)
            x_own = x_all[r, aligned(me, 128)]
            q_own[pl.ds(128 * r, 128), cols] = (
                mm(x_own, wq[:, cols]) + params[1:2, cols]
            ).astype(BF16)

        loop(3, project)
        key_live = lax.broadcasted_iota(jnp.int32, (1, 512), 1) < lengths[r]

        def attend(p):
            cols = aligned(p, 128)
            queries = stacked(q_own[pl.ds(128 * r, 128), cols] * BF16(HEAD_DIM**-0.5))
            logits = mm_t(queries, k_all[r, :, cols])
            logits = jnp.where(key_live, logits, -1e30)
            expd = jnp.exp(logits - jnp.max(logits, -1, keepdims=True))
            probs = (expd / jnp.sum(expd, -1, keepdims=True)).astype(BF16)
            base = r * 6 + p
            region[aligned(2 * base, 256)] = probs[:, :256]
            region[aligned(2 * base + 1, 256)] = probs[:, 256:]
            out = mm(probs, v_all[r, :, cols])
            mixed[pl.ds(128 * r, 128), cols] = unstacked(out).astype(BF16)

        loop(6, attend)
        rows = pl.ds(3072 * r, 3072)
        spill = pltpu.make_async_copy(region.at[rows], probs_out.at[rows], local.at[11 + r])
        spill.start()
        spills.append(spill)

    weight_loads["output"].wait()

    def first_norm(i):
        rows = aligned(i, 128)
        attended = mm(mixed[rows], wo[...]) + params[3:4]
        value = x_all[i, aligned(me, 128)].astype(F32) + attended
        center = value - jnp.mean(value, -1, keepdims=True)
        scale = lax.rsqrt(jnp.mean(center * center, -1, keepdims=True) + 1e-5)
        norm = center * scale
        norm_one[rows] = norm
        spread_one[rows] = scale
        first_low[rows] = (norm * params[4:5] + params[5:6]).astype(BF16)

    loop(3, first_norm)
    for spill in spills:
        spill.wait()
    for j in range(4):
        weight_loads[f"inner{j}"].wait()

    def hidden_units(j):
        inner = mm(
            first_low[...], wi[pl.ds((j // 3) * 768, 768), aligned(lax.rem(j, 3), 256)]
        ) + params[pl.ds(6 + j // 3, 1), aligned(lax.rem(j, 3), 256)]
        below = 0.5 * (1.0 + lax.erf(inner * ROOT_HALF))
        slope = below + inner * (DENSITY * jnp.exp(-0.5 * inner * inner))
        region[aligned(j, 384)] = (inner * below).astype(BF16)
        region[aligned(12 + j, 384)] = slope.astype(BF16)

    loop(12, hidden_units)
    weight_loads["outer"].wait()
    weight_loads["cotangent"].wait()

    def panels(first, count):
        return jnp.concatenate(
            [region[pl.ds(384 * j, 384)] for j in range(first, first + count)], axis=1
        )

    def project_out(n):
        cols = aligned(n, 256)
        total[:, cols] = mm(panels(0, 12), wf[:, cols])

    loop(3, project_out)

    def last_norm(i, sums):
        rows = aligned(i, 64)
        first = norm_one[rows] * params[4:5] + params[5:6]
        value = first + (total[rows] + params[10:11])
        center = value - jnp.mean(value, -1, keepdims=True)
        scale = lax.rsqrt(jnp.mean(center * center, -1, keepdims=True) + 1e-5)
        norm = center * scale
        d_att[rows] = (norm * params[11:12] + params[12:13]).astype(BF16)
        r = i // 2
        position = lax.broadcasted_iota(jnp.int32, (64, 1), 0) + lax.rem(i, 2) * 64 + me * 128
        weight = jnp.where(position < lengths[r], repeats[r].astype(F32), 0.0)
        d_final = d_outer[rows].astype(F32) * weight
        d_norm = d_final * params[11:12]
        d_two = scale * (
            d_norm
            - jnp.mean(d_norm, -1, keepdims=True)
            - norm * jnp.mean(d_norm * norm, -1, keepdims=True)
        )
        d_res[rows] = d_two
        low = d_two.astype(BF16)
        d_outer[rows] = low
        return (
            sums[0] + fold(d_final * norm),
            sums[1] + fold(d_final),
            sums[2] + fold(low.astype(F32)),
        )

    nothing = jnp.zeros((8, 768), F32)

    def put_sum(row, value):
        vec[0, row : row + 1] = jnp.sum(value, 0, keepdims=True)

    vec[0] = jnp.zeros((16, 768), F32)
    sums = lax.fori_loop(0, 6, last_norm, (nothing, nothing, nothing))
    put_sum(11, sums[0])
    put_sum(12, sums[1])
    put_sum(10, sums[2])
    out_copy = pltpu.make_async_copy(
        d_att, layer_out, local.at[14]
    )
    out_copy.start()

    units = {}
    for u, name in enumerate(NAMES):
        if u < 4:
            both = big_grads.at[u]
            inbox = [in0.at[u % SLOTS], big1.at[u], big2.at[u], big3.at[u], big4.at[u]]
        else:
            n = u - 4
            both = small_grads.at[n]
            first = in0.at[1 + n // 2, :, :, :, :, pl.ds(48 * (n % 2), 48)]
            inbox = [first, small1.at[n], small2.at[n], small3.at[n], small4.at[n]]
        units[name] = Unit(ORDERS[name], both, inbox, sends.at[u], recvs.at[u], spot, peer)

    def step(*which):
        for name in which:
            units[name].step()

    def free_slot(count):
        pl.semaphore_signal(credit, inc=count, device_id=peer["core"], device_id_type=MESH)

    def claim_slot():
        pl.semaphore_wait(credit, 1)

    def outer_grads(z):
        for x in range(2):
            cols = [region[pl.ds(pl.multiple_of((3 * z + j) * 384, 384), 384)] for j in range(3)]
            part = jnp.concatenate(cols, axis=1)[:, 384 * x : 384 * x + 384]
            grad = mm_tl(part, d_outer[...]).astype(BF16)
            for h in range(2):
                for i in range(2):
                    for side in range(2):
                        rows = (h * 2 + i) * 96
                        big_grads[i, h, side, z // 2, lax.rem(z, 2), x] = grad[
                            rows : rows + 96, side * 384 : side * 384 + 384
                        ]

    loop(4, outer_grads)
    units["outer0"].start()
    units["outer1"].start()

    def d_hidden_units(j):
        d_act = mm_t(d_outer[...], wf[aligned(j, 256)])
        place = aligned(12 + j, 384)
        low = (d_act * region[place].astype(F32)).astype(BF16)
        region[place] = low
        inner_sums[j] = fold(low.astype(F32))

    loop(12, d_hidden_units)
    step("outer0")
    free_slot(1)
    step("outer1")
    free_slot(2)

    def inner_grads(s):
        cols = [region[pl.ds(pl.multiple_of((12 + 3 * s + j) * 384, 384), 384)] for j in range(3)]
        grad = mm_tl(first_low[...], jnp.concatenate(cols, axis=1)).astype(BF16)
        for b in range(8):
            for i in range(2):
                big_grads[2 + i, lax.rem(s, 2), s // 2, b // 4, (b // 2) % 2, b % 2] = grad[
                    96 * b : 96 * b + 96, 384 * i : 384 * i + 384
                ]

    loop(4, inner_grads)
    units["inner0"].start()
    claim_slot()
    units["inner1"].start()

    def d_first_part(n):
        cols = aligned(n, 256)
        acc = None
        for s in range(4):
            d_inner = panels(12 + 3 * s, 3)
            term = mm_t(d_inner, wi[pl.ds(pl.multiple_of(s * 768 + n * 256, 256), 256)])
            acc = term if acc is None else acc + term
        total[:, cols] = acc

    loop(3, d_first_part)
    for j in range(12):
        vec[0, 6 + j // 3 : 7 + j // 3, (j % 3) * 256 : (j % 3) * 256 + 256] = jnp.sum(
            inner_sums[j], 0, keepdims=True
        )
    refills = []
    for r in range(3):
        rows = pl.ds(3072 * r, 3072)
        refill = pltpu.make_async_copy(probs_out.at[rows], region.at[rows], local.at[15 + r])
        refill.start()
        refills.append(refill)
    out_copy.wait()

    def first_norm_back(i, sums):
        rows = aligned(i, 64)
        d_first = total[rows] + d_res[rows]
        norm = norm_one[rows]
        d_norm = d_first * params[4:5]
        d_one = spread_one[rows] * (
            d_norm
            - jnp.mean(d_norm, -1, keepdims=True)
            - norm * jnp.mean(d_norm * norm, -1, keepdims=True)
        )
        d_res[rows] = d_one
        low = d_one.astype(BF16)
        d_att[rows] = low
        return (
            sums[0] + fold(d_first * norm),
            sums[1] + fold(d_first),
            sums[2] + fold(low.astype(F32)),
        )

    sums = lax.fori_loop(0, 6, first_norm_back, (nothing, nothing, nothing))
    put_sum(4, sums[0])
    put_sum(5, sums[1])
    put_sum(3, sums[2])

    def square_grads(name, left, right):
        u = NAMES.index(name) - 4
        for m in range(2):
            grad = mm_tl(left(m), right).astype(BF16)
            for b in range(4):
                for h in range(2):
                    for side in range(2):
                        rows = b * 96 + h * 48
                        small_grads[u, h, side, m, b // 2, b % 2] = grad[
                            rows : rows + 48, side * 384 : side * 384 + 384
                        ]
        claim_slot()
        units[name].start()

    step("inner0")
    free_slot(2)
    step("inner1")
    square_grads("output", lambda m: mixed[:, 384 * m : 384 * m + 384], d_att[...])

    def d_mixed_part(i):
        rows = aligned(i, 128)
        mixed[rows] = mm_t(d_att[rows], wo[...]).astype(BF16)

    loop(3, d_mixed_part)
    step("outer0", "outer1")

    for r in range(3):
        refills[r].wait()

        def attend_back(p):
            cols = aligned(p, 128)
            own_rows = pl.ds(128 * r, 128)
            base = r * 6 + p
            queries = stacked(q_own[own_rows, cols] * BF16(HEAD_DIM**-0.5))
            d_mix = stacked(mixed[own_rows, cols])
            low_probs = jnp.concatenate(
                [region[aligned(2 * base, 256)], region[aligned(2 * base + 1, 256)]], axis=1
            )
            d_probs = mm_t(d_mix, v_all[r, :, cols])
            probs = low_probs.astype(F32)
            weighted = probs * d_probs
            d_raw = (weighted - probs * jnp.sum(weighted, -1, keepdims=True)).astype(BF16)
            d_query = mm(d_raw, k_all[r, :, cols]) * HEAD_DIM**-0.5
            q_own[own_rows, cols] = unstacked(d_query).astype(BF16)
            wi[pl.ds(512 * r, 512), cols] = mm_tl(d_raw, queries).astype(BF16)
            wi[pl.ds(1536 + 512 * r, 512), cols] = mm_tl(low_probs, d_mix).astype(BF16)

        loop(6, attend_back)
        if r == 0:
            step("output")
        elif r == 1:
            step("inner1")
        else:
            step("outer0", "outer1", "output")

    def own_inputs(m):
        return jnp.concatenate(
            [x_all[r, aligned(me, 128), pl.ds(384 * m, 384)] for r in range(3)], 0
        )

    def all_inputs(m):
        return jnp.concatenate([x_all[r, :, pl.ds(384 * m, 384)] for r in range(3)], 0)

    square_grads("query", own_inputs, q_own[...])
    square_grads("key", all_inputs, wi[pl.ds(0, 1536)])
    step("inner0", "query")
    square_grads("value", all_inputs, wi[pl.ds(1536, 1536)])
    step("outer0", "outer1", "inner1", "key")
    put_sum(1, fold(q_own[...].astype(F32)))

    def value_sum(i, acc):
        return acc + fold(wi[pl.ds(pl.multiple_of(1536 + i * 128, 128), 128)].astype(F32))

    put_sum(2, lax.fori_loop(0, 12, value_sum, nothing))
    mask_sums[...] = jnp.zeros((3, 8, 256), F32)
    for r in range(3):

        def d_in_part(n, carry):
            cols = aligned(n, 256)
            part = mm_t(wi[pl.ds(512 * r, 512)], wk[cols]) + mm_t(
                wi[pl.ds(1536 + 512 * r, 512)], wv[cols]
            )
            for s in range(4):
                piece = part[128 * s : 128 * s + 128]
                wf[pl.ds(s * 384 + r * 128, 128), cols] = piece.astype(BF16)
            mask_sums[n] = mask_sums[n] + fold(part * wide[:, r : r + 1])
            return carry

        lax.fori_loop(0, 3, d_in_part, 0)
        if r == 0:
            step("value")
        elif r == 1:
            step("output")

    def d_in_copy(i):
        if i < 2:
            piece, target, name = 2 * i + 1 - core, d_in0.at[i], "core"
        else:
            piece, target, name = across, d_in1, "y"
        return pltpu.make_async_remote_copy(
            src_ref=wf.at[aligned(piece, 384)],
            dst_ref=target,
            send_sem=x_send.at[3, i],
            recv_sem=x_recv.at[3, i],
            device_id=peer[name],
            device_id_type=MESH,
        )

    d_in_copy(0).start()
    d_in_copy(1).start()

    def own_part(i, acc):
        rows = aligned(i, 128)
        part = d_res[rows] + mm_t(q_own[rows], wq[...])
        d_res[rows] = part
        chosen = wide[aligned(me, 128)]
        chosen = jnp.where(i == 0, chosen[:, 0:1], jnp.where(i == 1, chosen[:, 1:2], chosen[:, 2:3]))
        return acc + fold(part * chosen)

    mask_sum = jnp.concatenate([mask_sums[n] for n in range(3)], axis=1)
    put_sum(0, lax.fori_loop(0, 3, own_part, mask_sum))

    def vector_copy(phase):
        return pltpu.make_async_remote_copy(
            src_ref=vec.at[phase],
            dst_ref=vec_came.at[phase],
            send_sem=v_send.at[phase],
            recv_sem=v_recv.at[phase],
            device_id=peer[names[phase]],
            device_id_type=MESH,
        )

    def vector_step(phase):
        vector_copy(phase).wait()
        vec[phase + 1] = vec[phase] + vec_came[phase]
        if phase < 4:
            vector_copy(phase + 1).start()

    vector_copy(0).start()
    d_in_copy(0).wait()
    d_in_copy(1).wait()

    def add_across(i):
        rows = pl.ds(pl.multiple_of(across * 384 + i * 128, 128), 128)
        wf[rows] = wf[rows] + d_in0[1 - y, aligned(i, 128)]

    loop(3, add_across)
    d_in_copy(2).start()
    step("inner0")
    vector_step(0)
    step("query", "key")
    vector_step(1)
    mine = (y, spot["zhi"], spot["zlo"], spot["x"])

    def swap_copy(u):
        return pltpu.make_async_remote_copy(
            src_ref=units[NAMES[u]].own.at[mine],
            dst_ref=big5.at[u] if u < 2 else small5.at[u - 4],
            send_sem=sends.at[u, 5],
            recv_sem=recvs.at[u, 5],
            device_id=peer["core"],
            device_id_type=MESH,
        )

    def close(name):
        u, unit = NAMES.index(name), units[name]
        unit.copy(4).wait()
        result = unit.own[mine].astype(F32) + unit.inbox[4][...].astype(F32)
        if u == 2 or u == 3:
            out_inner[:, pl.ds(384 * (u - 2), 384)] = result
            return
        unit.own[mine] = result.astype(BF16)
        swap_copy(u).start()
        put_half(u, core, result)

    def put_half(u, side, value):
        value = jnp.where(core == 0, value[:, :192], pltpu.roll(value, 192, 1)[:, :192])
        if u < 2:
            out_outer[pl.ds(pl.multiple_of(side * 192 + u * 96, 96), 96)] = value
        else:
            target = (out_output, out_query, out_key, out_value)[u - 4]
            target[pl.ds(pl.multiple_of(side * 48, 48), 48)] = value

    def open_half(name):
        u = NAMES.index(name)
        swap_copy(u).wait()
        put_half(u, 1 - core, (big5[u] if u < 2 else small5[u - 4]).astype(F32))

    close("outer0")
    close("outer1")
    step("output", "value")
    vector_step(2)
    step("query", "key")
    vector_step(3)
    step("inner0", "inner1")
    open_half("outer0")
    open_half("outer1")
    close("output")
    step("value", "query", "key")
    vector_step(4)
    open_half("output")
    close("inner0")
    close("inner1")

    d_in_copy(2).wait()

    def finish_input(i):
        rows = aligned(i, 128)
        mine = pl.ds(pl.multiple_of(me * 384 + i * 128, 128), 128)
        value = (
            d_res[rows]
            + wf[mine].astype(F32)
            + d_in0[y, rows].astype(F32)
            + d_in1[rows].astype(F32)
        )
        chosen = wide[aligned(me, 128)]
        chosen = jnp.where(i == 0, chosen[:, 0:1], jnp.where(i == 1, chosen[:, 1:2], chosen[:, 2:3]))
        d_att[rows] = jnp.where(chosen > 0.5, 0.0, value).astype(BF16)

    loop(3, finish_input)
    grad_copy = pltpu.make_async_copy(d_att, grad_input, local.at[18])
    grad_copy.start()
    out_vectors[...] = vec[5]
    step("value")
    close("query")
    close("key")
    close("value")
    open_half("query")
    open_half("key")
    open_half("value")
    grad_copy.wait()


def hand_out(*refs):
    sources, vectors, targets, rows = refs[:8], refs[8], refs[9:17], refs[17:27]
    for source, target in zip(sources, targets):
        target[...] = source[...]
    for i, place in enumerate((0, 1, 2, 3, 4, 5, None, 10, 11, 12)):
        if place is not None:
            rows[i][...] = vectors[place]
    for j in range(4):
        rows[6][pl.ds(768 * j, 768)] = vectors[6 + j]


def fused_layer(
    hidden_in,
    cotangent,
    span_mask,
    lengths,
    repeats,
    mask_embedding,
    query_weight,
    query_bias,
    key_weight,
    value_weight,
    value_bias,
    output_weight,
    output_bias,
    mixing_gain,
    mixing_shift,
    inner_weight,
    inner_bias,
    outer_weight,
    outer_bias,
    final_gain,
    final_shift,
):
    vmem = pl.BlockSpec(memory_space=pltpu.VMEM)
    anywhere = pl.BlockSpec(memory_space=pl.ANY)
    scalars = pl.BlockSpec(memory_space=pltpu.SMEM)
    bf = lambda *shape: pltpu.VMEM(shape, BF16)
    fl = lambda *shape: pltpu.VMEM(shape, F32)
    dma = lambda *shape: pltpu.SemaphoreType.DMA(shape)
    shape = lambda dims, dtype: jax.ShapeDtypeStruct(dims, dtype)
    result = pl.pallas_call(
        layer_body,
        out_shape=[
            shape((384, 768), BF16),
            shape((384, 768), BF16),
            shape((9216, 256), BF16),
            shape((96, 192), F32),
            shape((96, 192), F32),
            shape((96, 192), F32),
            shape((96, 192), F32),
            shape((96, 768), F32),
            shape((384, 192), F32),
            shape((16, 768), F32),
        ],
        in_specs=[anywhere] * 8 + [vmem] * 11 + [scalars, scalars],
        out_specs=[anywhere] * 3 + [vmem] * 7,
        scratch_shapes=[
            bf(3072, 768),
            bf(3072, 768),
            bf(768, 768),
            bf(768, 768),
            bf(768, 768),
            bf(768, 768),
            fl(16, 768),
            bf(3, 512, 768),
            bf(3, 512, 768),
            bf(3, 512, 768),
            bf(384, 768),
            bf(384, 768),
            bf(9216, 256),
            bf(384, 768),
            fl(384, 768),
            fl(384, 1),
            fl(384, 768),
            fl(384, 768),
            bf(384, 768),
            bf(384, 768),
            pltpu.VMEM((4, 8, 128), jnp.int32),
            fl(512, 8),
            fl(12, 8, 256),
            fl(3, 8, 256),
            bf(4, 2, 2, 2, 2, 2, 96, 384),
            bf(4, 2, 2, 2, 2, 2, 48, 384),
            bf(SLOTS, 2, 2, 2, 2, 96, 384),
            bf(4, 2, 2, 2, 96, 384),
            bf(4, 2, 2, 96, 384),
            bf(4, 2, 96, 384),
            bf(4, 96, 384),
            bf(2, 96, 384),
            bf(4, 2, 2, 2, 48, 384),
            bf(4, 2, 2, 48, 384),
            bf(4, 2, 48, 384),
            bf(4, 48, 384),
            bf(4, 48, 384),
            bf(2, 384, 768),
            bf(384, 768),
            fl(6, 16, 768),
            fl(5, 16, 768),
            dma(8, 6),
            dma(8, 6),
            dma(4, 3),
            dma(4, 3),
            dma(3),
            dma(3),
            dma(5),
            dma(5),
            dma(19),
            pltpu.SemaphoreType.REGULAR,
        ],
        compiler_params=pltpu.CompilerParams(
            collective_id=1, has_side_effects=True, vmem_limit_bytes=63 * 2**20
        ),
        name="fused_layer",
    )(
        hidden_in,
        cotangent.reshape(384, 768),
        query_weight,
        key_weight,
        value_weight,
        output_weight,
        inner_weight,
        outer_weight,
        span_mask,
        mask_embedding,
        query_bias,
        value_bias,
        output_bias,
        mixing_gain,
        mixing_shift,
        inner_bias,
        outer_bias,
        final_gain,
        final_shift,
        lengths,
        repeats,
    )
    arrays, vectors = [result[0], result[1], *result[3:9]], result[9]
    wide_row = shape((768,), F32)
    handed = pl.pallas_call(
        hand_out,
        out_shape=[shape(v.shape, v.dtype) for v in arrays]
        + [wide_row] * 6
        + [shape((3072,), F32)]
        + [wide_row] * 3,
        in_specs=[vmem] * 9,
        out_specs=[vmem] * 18,
        name="hand_out",
    )(*arrays, vectors)
    layer_out, grad_input, g_query, g_key, g_value, g_output, g_inner, g_outer = handed[:8]
    g_mask, g_q_bias, g_v_bias, g_o_bias, g_gain, g_shift, g_inner_bias, *g_last = handed[8:]
    return (
        layer_out.reshape(3, 128, 768),
        grad_input.reshape(3, 128, 768),
        g_mask,
        g_query,
        g_q_bias,
        g_key,
        g_value,
        g_v_bias,
        g_output,
        g_o_bias,
        g_gain,
        g_shift,
        g_inner,
        g_inner_bias,
        g_outer,
        *g_last,
    )


def with_halo(x, sides, width):
    for axis, dim in sides:
        count, length = (lax.axis_size(axis), x.shape[dim])
        up = [(i, (i + 1) % count) for i in range(count - 1)]
        down = [(j, i) for i, j in up]
        last = lax.slice_in_dim(x, length - width, length, axis=dim)
        initial = lax.slice_in_dim(x, 0, width, axis=dim)
        before = lax.ppermute(last, axis, up)
        after = lax.ppermute(initial, axis, down)
        x = jnp.concatenate([before, x, after], axis=dim)
    return x


def layer_norm(inputs, gain, shift):
    center = inputs - jnp.mean(inputs, -1, keepdims=True)
    spread = jnp.mean(center * center, -1, keepdims=True)
    return center * lax.rsqrt(spread + 1e-05) * gain + shift


def linear(inputs, weight):
    return jnp.dot(inputs, weight, preferred_element_type=jnp.float32)


def linear_back(grads, weight):
    return lax.dot_general(
        grads, weight, (((1,), (1,)), ((), ())), preferred_element_type=jnp.float32
    )


def contract_rows(left, right):
    return lax.dot_general(
        left, right, (((0,), (0,)), ((), ())), preferred_element_type=jnp.float32
    )


def gelu_exact(inputs):
    return jax.nn.gelu(inputs, approximate=False)


def plain_layer(
    hidden_in,
    cotangent,
    span_mask,
    lengths,
    repeats,
    mask_embedding,
    query_weight,
    query_bias,
    key_weight,
    value_weight,
    value_bias,
    output_weight,
    output_bias,
    mixing_gain,
    mixing_shift,
    inner_weight,
    inner_bias,
    outer_weight,
    outer_bias,
    final_gain,
    final_shift,
):
    rows, stretch, width = hidden_in.shape
    whole = stretch * lax.axis_size("seq")
    scale = HEAD_DIM ** (-0.5)
    offset = lax.axis_index("seq") * stretch
    rim = with_halo(span_mask, (("seq", 1),), WIDEN)
    window = rim[:, 0:stretch]
    for shifted in range(1, 2 * WIDEN + 1):
        window = window + rim[:, shifted : shifted + stretch]
    widened = window > 0
    positions = offset + jnp.arange(stretch, dtype=jnp.int32)
    live = positions[None, :] < lengths[:, None]
    key_live = jnp.arange(whole, dtype=jnp.int32)[None, :] < lengths[:, None]
    masked_in = jnp.where(widened[..., None], mask_embedding[None, None, :], hidden_in)
    flat_in = masked_in.reshape(rows * stretch, width)
    queries = (linear(flat_in, query_weight) + query_bias.astype(jnp.float32)).astype(jnp.bfloat16)
    key_rows = linear(flat_in, key_weight).astype(jnp.bfloat16).reshape(rows, stretch, width)
    value_rows = (linear(flat_in, value_weight) + value_bias.astype(jnp.float32)).astype(
        jnp.bfloat16
    )
    value_rows = value_rows.reshape(rows, stretch, width)
    key_all, value_all = (
        lax.all_gather(key_rows, "seq", axis=1, tiled=True),
        lax.all_gather(value_rows, "seq", axis=1, tiled=True),
    )
    query_heads = queries.reshape(rows, stretch, HEADS, HEAD_DIM)

    def scores_of(key_full):
        key_heads = key_full.reshape(rows, whole, HEADS, HEAD_DIM)
        raw = jnp.einsum(
            "rqhd,rkhd->rhqk", query_heads, key_heads, preferred_element_type=jnp.float32
        )
        return jnp.where(key_live[:, None, None, :], raw * scale, -1e30)

    logits = scores_of(key_all)
    highest = jnp.max(logits, -1, keepdims=True)
    expd = jnp.exp(logits - highest)
    totals = jnp.sum(expd, -1, keepdims=True)
    log_total = highest + jnp.log(totals)
    probs_low = (expd / totals).astype(jnp.bfloat16)
    value_heads = value_all.reshape(rows, whole, HEADS, HEAD_DIM)
    mixed = jnp.einsum(
        "rhqk,rkhd->rqhd", probs_low, value_heads, preferred_element_type=jnp.float32
    )
    mixed = mixed.reshape(rows * stretch, width).astype(jnp.bfloat16)
    attended = linear(mixed, output_weight) + output_bias.astype(jnp.float32)
    residual_one = flat_in.astype(jnp.float32) + attended
    first, norm_back_one = jax.vjp(
        layer_norm, residual_one, mixing_gain.astype(jnp.float32), mixing_shift.astype(jnp.float32)
    )
    first_low = first.astype(jnp.bfloat16)
    inner = linear(first_low, inner_weight) + inner_bias.astype(jnp.float32)
    activated, gelu_back = jax.vjp(gelu_exact, inner)
    activated_low = activated.astype(jnp.bfloat16)
    outer = linear(activated_low, outer_weight) + outer_bias.astype(jnp.float32)
    final, norm_back_two = jax.vjp(
        layer_norm, first + outer, final_gain.astype(jnp.float32), final_shift.astype(jnp.float32)
    )
    layer_out = final.astype(jnp.bfloat16).reshape(rows, stretch, width)
    weighting = repeats.astype(jnp.float32)[:, None] * live.astype(jnp.float32)
    d_final = (cotangent.astype(jnp.float32) * weighting[:, :, None]).reshape(rows * stretch, width)
    d_two, d_final_gain, d_final_shift = norm_back_two(d_final)
    d_outer = d_two.astype(jnp.bfloat16)
    g_outer_weight = contract_rows(activated_low, d_outer)
    g_outer_bias = jnp.sum(d_outer.astype(jnp.float32), 0)
    (d_inner,) = gelu_back(linear_back(d_outer, outer_weight))
    d_inner = d_inner.astype(jnp.bfloat16)
    g_inner_weight = contract_rows(first_low, d_inner)
    g_inner_bias = jnp.sum(d_inner.astype(jnp.float32), 0)
    d_first = linear_back(d_inner, inner_weight) + d_two
    d_one, d_mixing_gain, d_mixing_shift = norm_back_one(d_first)
    d_attended = d_one.astype(jnp.bfloat16)
    g_output_weight = contract_rows(mixed, d_attended)
    g_output_bias = jnp.sum(d_attended.astype(jnp.float32), 0)
    d_mixed = linear_back(d_attended, output_weight).astype(jnp.bfloat16)
    d_mixed_heads = d_mixed.reshape(rows, stretch, HEADS, HEAD_DIM)
    key_back, value_back = (
        lax.all_gather(key_rows, "seq", axis=1, tiled=True),
        lax.all_gather(value_rows, "seq", axis=1, tiled=True),
    )
    probs = jnp.exp(scores_of(key_back) - log_total)
    probs_again = probs.astype(jnp.bfloat16)
    key_heads = key_back.reshape(rows, whole, HEADS, HEAD_DIM)
    value_heads = value_back.reshape(rows, whole, HEADS, HEAD_DIM)
    d_probs = jnp.einsum(
        "rqhd,rkhd->rhqk", d_mixed_heads, value_heads, preferred_element_type=jnp.float32
    )
    centered = d_probs - jnp.sum(probs * d_probs, -1, keepdims=True)
    d_raw = (probs * centered * scale).astype(jnp.bfloat16)
    d_queries = jnp.einsum("rhqk,rkhd->rqhd", d_raw, key_heads, preferred_element_type=jnp.float32)
    d_queries = d_queries.reshape(rows * stretch, width).astype(jnp.bfloat16)
    d_key_part = jnp.einsum(
        "rhqk,rqhd->rkhd", d_raw, query_heads, preferred_element_type=jnp.float32
    )
    d_value_part = jnp.einsum(
        "rhqk,rqhd->rkhd", probs_again, d_mixed_heads, preferred_element_type=jnp.float32
    )
    d_key_sum, d_value_sum = (
        lax.psum_scatter(
            d_key_part.reshape(rows, whole, width), "seq", scatter_dimension=1, tiled=True
        ),
        lax.psum_scatter(
            d_value_part.reshape(rows, whole, width), "seq", scatter_dimension=1, tiled=True
        ),
    )
    d_keys = d_key_sum.astype(jnp.bfloat16).reshape(rows * stretch, width)
    d_values = d_value_sum.astype(jnp.bfloat16).reshape(rows * stretch, width)
    g_query_weight = contract_rows(flat_in, d_queries)
    g_key_weight = contract_rows(flat_in, d_keys)
    g_value_weight = contract_rows(flat_in, d_values)
    g_query_bias = jnp.sum(d_queries.astype(jnp.float32), 0)
    g_value_bias = jnp.sum(d_values.astype(jnp.float32), 0)
    d_input = (
        d_one
        + linear_back(d_queries, query_weight)
        + linear_back(d_keys, key_weight)
        + linear_back(d_values, value_weight)
    ).reshape(rows, stretch, width)
    grad_input = jnp.where(widened[..., None], 0.0, d_input).astype(jnp.bfloat16)
    g_mask = jnp.sum(jnp.where(widened[..., None], d_input, 0.0), (0, 1))
    matrices = (
        g_query_weight,
        g_key_weight,
        g_value_weight,
        g_output_weight,
        g_inner_weight,
        g_outer_weight,
    )
    partial_sums = (
        lax.psum_scatter(matrices[0], "batch", scatter_dimension=0, tiled=True),
        lax.psum_scatter(matrices[1], "batch", scatter_dimension=0, tiled=True),
        lax.psum_scatter(matrices[2], "batch", scatter_dimension=0, tiled=True),
        lax.psum_scatter(matrices[3], "batch", scatter_dimension=0, tiled=True),
        lax.psum_scatter(matrices[4], "batch", scatter_dimension=0, tiled=True),
        lax.psum_scatter(matrices[5], "batch", scatter_dimension=0, tiled=True),
    )
    summed = (
        lax.psum_scatter(partial_sums[0], "seq", scatter_dimension=1, tiled=True),
        lax.psum_scatter(partial_sums[1], "seq", scatter_dimension=1, tiled=True),
        lax.psum_scatter(partial_sums[2], "seq", scatter_dimension=1, tiled=True),
        lax.psum_scatter(partial_sums[3], "seq", scatter_dimension=1, tiled=True),
        lax.psum_scatter(partial_sums[4], "seq", scatter_dimension=1, tiled=True),
        lax.psum_scatter(partial_sums[5], "seq", scatter_dimension=1, tiled=True),
    )
    vectors = lax.psum(
        (
            g_mask,
            g_query_bias,
            g_value_bias,
            g_output_bias,
            d_mixing_gain,
            d_mixing_shift,
            g_inner_bias,
            g_outer_bias,
            d_final_gain,
            d_final_shift,
        ),
        ("batch", "seq"),
    )
    return (
        layer_out,
        grad_input,
        vectors[0],
        summed[0],
        vectors[1],
        summed[1],
        summed[2],
        vectors[2],
        summed[3],
        vectors[3],
        vectors[4],
        vectors[5],
        summed[4],
        vectors[6],
        summed[5],
        vectors[7],
        vectors[8],
        vectors[9],
    )


def solution(mesh):
    fused = mesh.shape["batch"] == 8 and mesh.shape["seq"] == 4
    return jax.shard_map(
        fused_layer if fused else plain_layer,
        mesh=mesh,
        in_specs=(
            P("batch", "seq", None),
            P("batch", "seq", None),
            P("batch", "seq"),
            P("batch"),
            P("batch"),
            P(),
            P(),
            P(),
            P(),
            P(),
            P(),
            P(),
            P(),
            P(),
            P(),
            P(),
            P(),
            P(),
            P(),
            P(),
            P(),
        ),
        out_specs=(
            P("batch", "seq", None),
            P("batch", "seq", None),
            P(),
            P("batch", "seq"),
            P(),
            P("batch", "seq"),
            P("batch", "seq"),
            P(),
            P("batch", "seq"),
            P(),
            P(),
            P(),
            P("batch", "seq"),
            P(),
            P("batch", "seq"),
            P(),
            P(),
            P(),
        ),
        check_vma=False,
    )
```

```python
import jax
import jax.numpy as jnp
from jax import lax
from jax.experimental import pallas as pl
from jax.experimental.pallas import tpu as pltpu
from jax.sharding import PartitionSpec as P

HEADS = 12
HEAD_DIM = 64
WIDEN = 5

MESH = pl.DeviceIdType.MESH
F32 = jnp.float32
BF16 = jnp.bfloat16
ROOT_HALF = 0.7071067811865476
DENSITY = 0.3989422804014327


def mm(a, b):
    return jnp.dot(a, b, preferred_element_type=F32)


def mm_t(a, b):
    return lax.dot_general(a, b, (((1,), (1,)), ((), ())), preferred_element_type=F32)


def mm_tl(a, b):
    return lax.dot_general(a, b, (((0,), (0,)), ((), ())), preferred_element_type=F32)


def fold(v):
    return jnp.sum(v.reshape(v.shape[0] // 8, 8, v.shape[1]), 0)


def loop(count, body):
    def step(i, carry):
        body(i)
        return carry

    lax.fori_loop(0, count, step, 0)


def span_loop(first, last, body):
    def step(i, carry):
        body(i)
        return carry

    lax.fori_loop(first, last, step, 0)


def aligned(i, size):
    return pl.ds(pl.multiple_of(i * size, size), size)


def places():
    b, s = lax.axis_index("batch"), lax.axis_index("seq")
    x, zlo, zhi = lax.rem(b, 2), lax.rem(b // 2, 2), b // 4
    core, y = lax.rem(s, 2), s // 2
    spot = {"core": core, "x": x, "y": y, "zlo": zlo, "zhi": zhi}
    peer = {
        "core": (b, s + 1 - 2 * core),
        "y": (b, s + 2 - 4 * y),
        "x": (b + 1 - 2 * x, s),
        "zlo": (b + 2 - 4 * zlo, s),
        "zhi": (b + 4 - 8 * zhi, s),
        "far": (b, 3 - s),
    }
    return spot, peer


class Unit:
    def __init__(self, order, both, inbox, sends, recvs, spot, peer):
        self.order, self.both, self.inbox = order, both, inbox
        self.sends, self.recvs, self.spot, self.peer = sends, recvs, spot, peer
        self.own = both.at[spot["core"]]
        self.phase = 0

    def where(self, phase, stays):
        done, axis = self.order[: phase - 1], self.order[phase - 1]
        place = []
        for name in ("y", "zhi", "zlo", "x"):
            side = self.spot[name]
            if name == axis:
                place.append(side if stays else 1 - side)
            else:
                place.append(side if name in done else slice(None))
        return tuple(place)

    def copy(self, phase):
        if phase == 0:
            axis, source = "core", self.both.at[1 - self.spot["core"]]
        else:
            axis, source = self.order[phase - 1], self.own.at[self.where(phase, False)]
        return pltpu.make_async_remote_copy(
            src_ref=source,
            dst_ref=self.inbox[phase],
            send_sem=self.sends.at[phase],
            recv_sem=self.recvs.at[phase],
            device_id=self.peer[axis],
            device_id_type=MESH,
        )

    def start(self):
        self.copy(0).start()

    def step(self):
        phase = self.phase
        self.copy(phase).wait()
        came = self.inbox[phase]
        target = self.own if phase == 0 else self.own.at[self.where(phase, True)]
        lead = 4 - phase

        def body(n):
            place = tuple(lax.rem(n // 2 ** (lead - 1 - i), 2) for i in range(lead))
            target[place] = target[place] + came[place]

        loop(2**lead, body)
        self.phase = phase + 1
        self.copy(self.phase).start()


STARTS = (
    "outer0", "outer1", "outer2", "outer3", "inner0", "inner1",
    "inner2", "inner3", "output", "key", "query", "value",
)
ORDERS = {
    "outer0": ("y", "zlo", "x", "zhi"),
    "outer1": ("zlo", "x", "y", "zhi"),
    "outer2": ("x", "zlo", "y", "zhi"),
    "outer3": ("zlo", "y", "x", "zhi"),
    "inner0": ("y", "zlo", "x", "zhi"),
    "inner1": ("zlo", "y", "x", "zhi"),
    "inner2": ("y", "x", "zlo", "zhi"),
    "inner3": ("x", "zlo", "y", "zhi"),
    "output": ("x", "y", "zlo", "zhi"),
    "key": ("y", "x", "zlo", "zhi"),
    "query": ("x", "zlo", "zhi", "y"),
    "value": ("x", "zlo", "y", "zhi"),
}
PLAN = (
    "d_hidden", "outer0", "outer1", "outer2", "inner", "outer3", "d_first", "refill",
    "fnb", "inner0", "inner1", "outer1", "outer0", "inner2", "outer2", "V1",
    "dWo", "inner3", "W1", "dmixed", "ab00", "output", "outer1", "inner0",
    "outer3", "ab01", "ab10", "inner1", "inner3", "W1", "ab11", "outer0",
    "inner2", "ab20", "outer1", "ab21", "output", "outer2", "outer3", "dWk",
    "outer0", "inner0", "inner1", "W1", "dWq", "inner2", "inner3", "dWv",
    "key", "outer1", "query", "W1", "output", "inner0", "outer0", "outer2",
    "inner1", "outer3", "outer1", "inner2", "inner3", "din0", "outer0", "din1",
    "value", "W1", "output", "dc0", "din2", "inner0", "key", "outer2",
    "dc1", "query", "vec", "inner1", "outer2", "outer3", "dc2", "W2",
    "outer3", "inner2", "dy0", "inner3", "output", "value", "output", "query",
    "dy1", "key", "W2", "value", "dy2", "W2", "query", "value",
    "key", "W2", "query", "query", "value", "key", "value", "W2",
    "key",
)
SLOTS = 6


def layer_body(
    hidden,
    cotangent,
    query_weight,
    key_weight,
    value_weight,
    output_weight,
    inner_weight,
    outer_weight,
    span,
    mask_embedding,
    query_bias,
    value_bias,
    output_bias,
    mixing_gain,
    mixing_shift,
    inner_bias,
    outer_bias,
    final_gain,
    final_shift,
    lengths,
    repeats,
    layer_out,
    grad_input,
    probs_out,
    out_query,
    out_key,
    out_value,
    out_output,
    out_inner,
    out_outer,
    out_vectors,
    wi,
    wf,
    wq,
    wk,
    wv,
    wo,
    params,
    x_all,
    k_all,
    v_all,
    q_own,
    mixed,
    region,
    first_low,
    norm_one,
    spread_one,
    total,
    d_res,
    d_outer,
    d_att,
    masks,
    wide,
    inner_sums,
    mask_sums,
    grads,
    in0,
    in1,
    in2,
    in3,
    in4,
    in5,
    d_in0,
    d_in1,
    vec,
    vec_came,
    late,
    late_came,
    sends,
    recvs,
    x_send,
    x_recv,
    m_send,
    m_recv,
    v_send,
    v_recv,
    local,
    credit,
):
    spot, peer = places()
    core, y = spot["core"], spot["y"]
    me = 2 * y + core
    sibling = 2 * y + 1 - core
    across = 2 * (1 - y) + core

    weight_loads = {}

    def load(name, number, source, target):
        copy = pltpu.make_async_copy(source, target, local.at[number])
        copy.start()
        weight_loads[name] = copy

    load("hidden", 0, hidden, x_all.at[:, aligned(me, 128)])
    load("key", 1, key_weight, wk)
    load("value", 2, value_weight, wv)
    load("query", 3, query_weight, wq)
    load("output", 4, output_weight, wo)
    for j in range(4):
        load(f"inner{j}", 5 + j, inner_weight.at[:, pl.ds(768 * j, 768)], wi.at[pl.ds(768 * j, 768)])
    load("outer", 9, outer_weight, wf)
    load("cotangent", 10, cotangent, d_outer)

    names = ("core", "x", "y", "zlo", "zhi", "far")
    barrier = pltpu.get_barrier_semaphore()
    for name in names:
        pl.semaphore_signal(barrier, inc=1, device_id=peer[name], device_id_type=MESH)
    pl.semaphore_wait(barrier, len(names))

    vectors = [mask_embedding, query_bias, value_bias, output_bias, mixing_gain, mixing_shift]
    vectors += [inner_bias.at[pl.ds(768 * i, 768)] for i in range(4)]
    vectors += [outer_bias, final_gain, final_shift]
    for i, vector in enumerate(vectors):
        params[i : i + 1] = vector[...].astype(F32).reshape(1, 768)

    masks[me] = jnp.zeros((8, 128), jnp.int32)
    masks[me, 0:3] = span[...]
    mask_copies = []
    for i, name in enumerate(("core", "y", "far")):
        copy = pltpu.make_async_remote_copy(
            src_ref=masks.at[me],
            dst_ref=masks.at[me],
            send_sem=m_send.at[i],
            recv_sem=m_recv.at[i],
            device_id=peer[name],
            device_id_type=MESH,
        )
        copy.start()
        mask_copies.append(copy)

    def x_copy(kind, r):
        source = hidden.at[r] if kind < 2 else x_all.at[r, aligned(across, 128)]
        slot = me if kind < 2 else across
        return pltpu.make_async_remote_copy(
            src_ref=source,
            dst_ref=x_all.at[r, aligned(slot, 128)],
            send_sem=x_send.at[kind, r],
            recv_sem=x_recv.at[kind, r],
            device_id=peer["y" if kind == 0 else "core"],
            device_id_type=MESH,
        )

    for r in range(3):
        x_copy(0, r).start()
        x_copy(1, r).start()

    for copy in mask_copies:
        copy.wait()
    span_all = jnp.concatenate([masks[s].astype(F32) for s in range(4)], axis=1)
    lane = lax.broadcasted_iota(jnp.int32, span_all.shape, 1)
    window = span_all
    for d in range(1, WIDEN + 1):
        window = jnp.maximum(window, jnp.where(lane >= d, pltpu.roll(span_all, d, 1), 0.0))
        window = jnp.maximum(
            window, jnp.where(lane < 512 - d, pltpu.roll(span_all, 512 - d, 1), 0.0)
        )
    wide[...] = window.T

    half = lax.broadcasted_iota(jnp.int32, (128, 128), 1) < HEAD_DIM
    zero = jnp.zeros((128, 128), BF16)

    def stacked(pair):
        return jnp.concatenate([jnp.where(half, pair, zero), jnp.where(half, zero, pair)], 0)

    def unstacked(both):
        return jnp.where(half, both[:128], both[128:])

    mask_row = params[0:1]
    spills = []

    def put_mask(r, slot):
        rows = aligned(slot, 128)
        chosen = wide[rows, r : r + 1] > 0.5
        kept = x_all[r, rows].astype(F32)
        x_all[r, rows] = jnp.where(chosen, mask_row, kept).astype(BF16)

    def project(pieces, with_queries):
        inputs = jnp.concatenate([x_all[r, aligned(slot, 128)] for r, slot in pieces], 0)

        def part(n):
            cols = aligned(n, 256)
            keys = mm(inputs, wk[:, cols]).astype(BF16)
            values = (mm(inputs, wv[:, cols]) + params[2:3, cols]).astype(BF16)
            for i, (r, slot) in enumerate(pieces):
                k_all[r, aligned(slot, 128), cols] = keys[128 * i : 128 * i + 128]
                v_all[r, aligned(slot, 128), cols] = values[128 * i : 128 * i + 128]
            if with_queries:
                q_own[:, cols] = (mm(inputs, wq[:, cols]) + params[1:2, cols]).astype(BF16)

        loop(3, part)

    weight_loads["hidden"].wait()
    for r in range(3):
        put_mask(r, me)
    for name in ("key", "value", "query"):
        weight_loads[name].wait()
    project([(r, me) for r in range(3)], True)
    for r in range(3):
        x_copy(1, r).wait()
        put_mask(r, sibling)
    project([(r, sibling) for r in range(3)], False)
    x_copy(0, 0).wait_recv()
    x_copy(2, 0).start()
    for r in range(3):
        x_copy(2, r).wait()
        put_mask(r, across)
        put_mask(r, 3 - me)
        project([(r, across), (r, 3 - me)], False)
        key_live = lax.broadcasted_iota(jnp.int32, (1, 512), 1) < lengths[r]

        def attend(p):
            cols = aligned(p, 128)
            queries = stacked(q_own[pl.ds(128 * r, 128), cols] * BF16(HEAD_DIM**-0.5))
            logits = mm_t(queries, k_all[r, :, cols])
            logits = jnp.where(key_live, logits, -1e30)
            expd = jnp.exp(logits - jnp.max(logits, -1, keepdims=True))
            probs = (expd / jnp.sum(expd, -1, keepdims=True)).astype(BF16)
            base = r * 6 + p
            region[aligned(2 * base, 256)] = probs[:, :256]
            region[aligned(2 * base + 1, 256)] = probs[:, 256:]
            out = mm(probs, v_all[r, :, cols])
            mixed[pl.ds(128 * r, 128), cols] = unstacked(out).astype(BF16)

        span_loop(0, 3, attend)
        if r < 2:
            x_copy(0, r + 1).wait_recv()
            x_copy(2, r + 1).start()
        span_loop(3, 6, attend)
        rows = pl.ds(3072 * r, 3072)
        spill = pltpu.make_async_copy(region.at[rows], probs_out.at[rows], local.at[11 + r])
        spill.start()
        spills.append(spill)

    for r in range(3):
        x_copy(0, r).wait_send()
    weight_loads["output"].wait()

    def first_norm(i):
        rows = aligned(i, 128)
        attended = mm(mixed[rows], wo[...]) + params[3:4]
        value = x_all[i, aligned(me, 128)].astype(F32) + attended
        center = value - jnp.mean(value, -1, keepdims=True)
        scale = lax.rsqrt(jnp.mean(center * center, -1, keepdims=True) + 1e-5)
        norm = center * scale
        norm_one[rows] = norm
        spread_one[rows] = scale
        first_low[rows] = (norm * params[4:5] + params[5:6]).astype(BF16)

    loop(3, first_norm)
    for spill in spills:
        spill.wait()
    for j in range(4):
        weight_loads[f"inner{j}"].wait()

    def hidden_units(j):
        inner = mm(
            first_low[...], wi[pl.ds((j // 3) * 768, 768), aligned(lax.rem(j, 3), 256)]
        ) + params[pl.ds(6 + j // 3, 1), aligned(lax.rem(j, 3), 256)]
        below = 0.5 * (1.0 + lax.erf(inner * ROOT_HALF))
        slope = below + inner * (DENSITY * jnp.exp(-0.5 * inner * inner))
        region[aligned(j, 384)] = (inner * below).astype(BF16)
        region[aligned(12 + j, 384)] = slope.astype(BF16)

    loop(12, hidden_units)
    weight_loads["outer"].wait()
    weight_loads["cotangent"].wait()

    def panels(first, count):
        return jnp.concatenate(
            [region[pl.ds(384 * j, 384)] for j in range(first, first + count)], axis=1
        )

    def project_out(n):
        cols = aligned(n, 256)
        total[:, cols] = mm(panels(0, 12), wf[:, cols])

    loop(3, project_out)

    def last_norm(i, sums):
        rows = aligned(i, 64)
        first = norm_one[rows] * params[4:5] + params[5:6]
        value = first + (total[rows] + params[10:11])
        center = value - jnp.mean(value, -1, keepdims=True)
        scale = lax.rsqrt(jnp.mean(center * center, -1, keepdims=True) + 1e-5)
        norm = center * scale
        d_att[rows] = (norm * params[11:12] + params[12:13]).astype(BF16)
        r = i // 2
        position = lax.broadcasted_iota(jnp.int32, (64, 1), 0) + lax.rem(i, 2) * 64 + me * 128
        weight = jnp.where(position < lengths[r], repeats[r].astype(F32), 0.0)
        d_final = d_outer[rows].astype(F32) * weight
        d_norm = d_final * params[11:12]
        d_two = scale * (
            d_norm
            - jnp.mean(d_norm, -1, keepdims=True)
            - norm * jnp.mean(d_norm * norm, -1, keepdims=True)
        )
        d_res[rows] = d_two
        low = d_two.astype(BF16)
        d_outer[rows] = low
        return (
            sums[0] + fold(d_final * norm),
            sums[1] + fold(d_final),
            sums[2] + fold(low.astype(F32)),
        )

    nothing = jnp.zeros((8, 768), F32)

    def put_sum(row, value):
        vec[0, row : row + 1] = jnp.sum(value, 0, keepdims=True)

    vec[0] = jnp.zeros((16, 768), F32)
    sums = lax.fori_loop(0, 6, last_norm, (nothing, nothing, nothing))
    put_sum(11, sums[0])
    put_sum(12, sums[1])
    put_sum(10, sums[2])
    out_copy = pltpu.make_async_copy(
        d_att, layer_out, local.at[14]
    )
    out_copy.start()

    units = {}
    for u, name in enumerate(STARTS):
        inbox = [in0.at[u % SLOTS], in1.at[u], in2.at[u], in3.at[u], in4.at[u]]
        units[name] = Unit(ORDERS[name], grads.at[u], inbox, sends.at[u], recvs.at[u], spot, peer)

    def start_unit(name):
        if STARTS.index(name) >= SLOTS:
            claim_slot()
        units[name].start()

    def free_slot():
        pl.semaphore_signal(credit, inc=1, device_id=peer["core"], device_id_type=MESH)

    def claim_slot():
        pl.semaphore_wait(credit, 1)

    def outer_grads(z):
        for x in range(2):
            cols = [region[pl.ds(pl.multiple_of((3 * z + j) * 384, 384), 384)] for j in range(3)]
            part = jnp.concatenate(cols, axis=1)[:, 384 * x : 384 * x + 384]
            grad = mm_tl(part, d_outer[...]).astype(BF16)
            for h in range(2):
                for i in range(4):
                    for side in range(2):
                        rows = (h * 4 + i) * 48
                        grads[STARTS.index(f"outer{i}"), h, side, z // 2, lax.rem(z, 2), x] = grad[
                            rows : rows + 48, side * 384 : side * 384 + 384
                        ]

    loop(4, outer_grads)
    for i in range(4):
        start_unit(f"outer{i}")

    def d_hidden_units(j):
        d_act = mm_t(d_outer[...], wf[aligned(j, 256)])
        place = aligned(12 + j, 384)
        low = (d_act * region[place].astype(F32)).astype(BF16)
        region[place] = low
        inner_sums[j] = fold(low.astype(F32))

    def inner_grads(s):
        cols = [region[pl.ds(pl.multiple_of((12 + 3 * s + j) * 384, 384), 384)] for j in range(3)]
        grad = mm_tl(first_low[...], jnp.concatenate(cols, axis=1)).astype(BF16)
        for b in range(8):
            for i in range(4):
                rows, side = 96 * b + 48 * (i % 2), 384 * (i // 2)
                grads[
                    STARTS.index(f"inner{i}"), lax.rem(s, 2), s // 2, b // 4, (b // 2) % 2, b % 2
                ] = grad[rows : rows + 48, side : side + 384]

    def do_inner_grads():
        loop(4, inner_grads)
        for i in range(4):
            start_unit(f"inner{i}")

    def d_first_part(n):
        cols = aligned(n, 256)
        acc = None
        for s in range(4):
            d_inner = panels(12 + 3 * s, 3)
            term = mm_t(d_inner, wi[pl.ds(pl.multiple_of(s * 768 + n * 256, 256), 256)])
            acc = term if acc is None else acc + term
        total[:, cols] = acc

    refills = []

    def do_d_first():
        loop(3, d_first_part)
        for j in range(12):
            vec[0, 6 + j // 3 : 7 + j // 3, (j % 3) * 256 : (j % 3) * 256 + 256] = jnp.sum(
                inner_sums[j], 0, keepdims=True
            )

    def refill_probs():
        for r in range(3):
            rows = pl.ds(3072 * r, 3072)
            refill = pltpu.make_async_copy(probs_out.at[rows], region.at[rows], local.at[15 + r])
            refill.start()
            refills.append(refill)

    def first_norm_back(i, sums):
        rows = aligned(i, 64)
        d_first = total[rows] + d_res[rows]
        norm = norm_one[rows]
        d_norm = d_first * params[4:5]
        d_one = spread_one[rows] * (
            d_norm
            - jnp.mean(d_norm, -1, keepdims=True)
            - norm * jnp.mean(d_norm * norm, -1, keepdims=True)
        )
        d_res[rows] = d_one
        low = d_one.astype(BF16)
        d_att[rows] = low
        return (
            sums[0] + fold(d_first * norm),
            sums[1] + fold(d_first),
            sums[2] + fold(low.astype(F32)),
        )

    def do_first_norm_back():
        out_copy.wait()
        sums = lax.fori_loop(0, 6, first_norm_back, (nothing, nothing, nothing))
        put_sum(4, sums[0])
        put_sum(5, sums[1])
        put_sum(3, sums[2])

    def square_grads(name, left, right):
        u = STARTS.index(name)
        for m in range(2):
            grad = mm_tl(left(m), right).astype(BF16)
            for b in range(4):
                for h in range(2):
                    for side in range(2):
                        rows = b * 96 + h * 48
                        grads[u, h, side, m, b // 2, b % 2] = grad[
                            rows : rows + 48, side * 384 : side * 384 + 384
                        ]
        start_unit(name)

    def do_output_grads():
        square_grads("output", lambda m: mixed[:, 384 * m : 384 * m + 384], d_att[...])

    def d_mixed_part(i):
        rows = aligned(i, 128)
        mixed[rows] = mm_t(d_att[rows], wo[...]).astype(BF16)

    def do_attend_back(r, first, last):
        if first == 0:
            refills[r].wait()

        def attend_back(p):
            cols = aligned(p, 128)
            own_rows = pl.ds(128 * r, 128)
            base = r * 6 + p
            queries = stacked(q_own[own_rows, cols] * BF16(HEAD_DIM**-0.5))
            d_mix = stacked(mixed[own_rows, cols])
            low_probs = jnp.concatenate(
                [region[aligned(2 * base, 256)], region[aligned(2 * base + 1, 256)]], axis=1
            )
            d_probs = mm_t(d_mix, v_all[r, :, cols])
            probs = low_probs.astype(F32)
            weighted = probs * d_probs
            d_raw = (weighted - probs * jnp.sum(weighted, -1, keepdims=True)).astype(BF16)
            d_query = mm(d_raw, k_all[r, :, cols]) * HEAD_DIM**-0.5
            q_own[own_rows, cols] = unstacked(d_query).astype(BF16)
            wi[pl.ds(512 * r, 512), cols] = mm_tl(d_raw, queries).astype(BF16)
            wi[pl.ds(1536 + 512 * r, 512), cols] = mm_tl(low_probs, d_mix).astype(BF16)

        span_loop(first, last, attend_back)

    def own_inputs(m):
        return jnp.concatenate(
            [x_all[r, aligned(me, 128), pl.ds(384 * m, 384)] for r in range(3)], 0
        )

    def all_inputs(m):
        return jnp.concatenate([x_all[r, :, pl.ds(384 * m, 384)] for r in range(3)], 0)

    def do_query_grads():
        square_grads("query", own_inputs, q_own[...])

    def do_key_grads():
        square_grads("key", all_inputs, wi[pl.ds(0, 1536)])

    def do_value_grads():
        square_grads("value", all_inputs, wi[pl.ds(1536, 1536)])

    def value_sum(i, acc):
        return acc + fold(wi[pl.ds(pl.multiple_of(1536 + i * 128, 128), 128)].astype(F32))

    mask_sums[...] = jnp.zeros((3, 8, 256), F32)

    def d_in_copy(kind, r):
        if kind == 0:
            source = wf.at[aligned(2 * r + 1 - core, 256)]
            target, name = d_in0.at[r], "core"
        else:
            source = wf.at[aligned(4 * r + 2 * core + 1 - y, 128)]
            target, name = d_in1.at[r], "y"
        return pltpu.make_async_remote_copy(
            src_ref=source,
            dst_ref=target,
            send_sem=x_send.at[3 + kind, r],
            recv_sem=x_recv.at[3 + kind, r],
            device_id=peer[name],
            device_id_type=MESH,
        )

    def do_d_in(r):
        def d_in_part(n):
            cols = aligned(n, 256)
            part = mm_t(wi[pl.ds(512 * r, 512)], wk[cols]) + mm_t(
                wi[pl.ds(1536 + 512 * r, 512)], wv[cols]
            )
            for s in range(4):
                block = 4 * r + 2 * (s % 2) + s // 2
                wf[pl.ds(128 * block, 128), cols] = part[128 * s : 128 * s + 128].astype(BF16)
            mask_sums[n] = mask_sums[n] + fold(part * wide[:, r : r + 1])

        loop(3, d_in_part)
        d_in_copy(0, r).start()

    def d_in_pass(r):
        d_in_copy(0, r).wait()
        rows = aligned(4 * r + 2 * core + 1 - y, 128)
        wf[rows] = wf[rows] + d_in0[r, aligned(1 - y, 128)]
        d_in_copy(1, r).start()

    def own_part(i, acc):
        rows = aligned(i, 128)
        part = d_res[rows] + mm_t(q_own[rows], wq[...])
        d_res[rows] = part
        chosen = wide[aligned(me, 128)]
        chosen = jnp.where(i == 0, chosen[:, 0:1], jnp.where(i == 1, chosen[:, 1:2], chosen[:, 2:3]))
        return acc + fold(part * chosen)

    grad_copies = []

    def d_in_close(r):
        d_in_copy(1, r).wait()
        rows = pl.ds(128 * r, 128)
        value = (
            d_res[rows]
            + wf[aligned(4 * r + 2 * core + y, 128)].astype(F32)
            + d_in0[r, aligned(y, 128)].astype(F32)
            + d_in1[r].astype(F32)
        )
        chosen = wide[aligned(me, 128), r : r + 1] > 0.5
        d_att[rows] = jnp.where(chosen, 0.0, value).astype(BF16)
        copy = pltpu.make_async_copy(d_att.at[rows], grad_input.at[rows], local.at[18 + r])
        copy.start()
        grad_copies.append(copy)

    axes = ("core", "x", "y", "zlo", "zhi")

    def vector_copy(group, phase):
        sums, came = (vec, vec_came) if group == 0 else (late, late_came)
        return pltpu.make_async_remote_copy(
            src_ref=sums.at[phase],
            dst_ref=came.at[phase],
            send_sem=v_send.at[group, phase],
            recv_sem=v_recv.at[group, phase],
            device_id=peer[axes[phase]],
            device_id_type=MESH,
        )

    def vector_step(group, phase):
        vector_copy(group, phase).wait()
        sums, came = (vec, vec_came) if group == 0 else (late, late_came)
        sums[phase + 1] = sums[phase] + came[phase]
        if phase < 4:
            vector_copy(group, phase + 1).start()

    def do_late_sums():
        late[0] = jnp.zeros((8, 768), F32)
        mask_sum = jnp.concatenate([mask_sums[n] for n in range(3)], axis=1)
        all_sums = (
            lax.fori_loop(0, 3, own_part, mask_sum),
            fold(q_own[...].astype(F32)),
            lax.fori_loop(0, 12, value_sum, nothing),
        )
        for i, value in enumerate(all_sums):
            late[0, i : i + 1] = jnp.sum(value, 0, keepdims=True)
        vector_copy(1, 0).start()

    mine = (y, spot["zhi"], spot["zlo"], spot["x"])

    def swap_copy(name):
        u = STARTS.index(name)
        return pltpu.make_async_remote_copy(
            src_ref=units[name].own.at[mine],
            dst_ref=in5.at[u],
            send_sem=sends.at[u, 5],
            recv_sem=recvs.at[u, 5],
            device_id=peer["core"],
            device_id_type=MESH,
        )

    def close(name):
        unit = units[name]
        unit.copy(4).wait()
        result = unit.own[mine].astype(F32) + unit.inbox[4][...].astype(F32)
        if name.startswith("inner"):
            i = int(name[5:])
            out_inner[pl.ds(48 * (i % 2), 48), pl.ds(384 * (i // 2), 384)] = result
            return
        unit.own[mine] = result.astype(BF16)
        swap_copy(name).start()
        put_half(name, core, result)

    def put_half(name, side, value):
        value = jnp.where(core == 0, value[:, :192], pltpu.roll(value, 192, 1)[:, :192])
        if name.startswith("outer"):
            rows = side * 192 + int(name[5:]) * 48
            out_outer[pl.ds(pl.multiple_of(rows, 48), 48)] = value
        else:
            target = {
                "output": out_output, "query": out_query, "key": out_key, "value": out_value
            }[name]
            target[pl.ds(pl.multiple_of(side * 48, 48), 48)] = value

    def open_half(name):
        swap_copy(name).wait()
        put_half(name, 1 - core, in5[STARTS.index(name)].astype(F32))

    stages = {
        "d_hidden": lambda: loop(12, d_hidden_units),
        "inner": do_inner_grads,
        "d_first": do_d_first,
        "fnb": do_first_norm_back,
        "V1": lambda: vector_copy(0, 0).start(),
        "dWo": do_output_grads,
        "refill": refill_probs,
        "dmixed": lambda: loop(3, d_mixed_part),
        "dWq": do_query_grads,
        "dWk": do_key_grads,
        "dWv": do_value_grads,
        "vec": do_late_sums,
    }
    for r in range(3):
        stages[f"ab{r}0"] = lambda r=r: do_attend_back(r, 0, 3)
        stages[f"ab{r}1"] = lambda r=r: do_attend_back(r, 3, 6)
        stages[f"din{r}"] = lambda r=r: do_d_in(r)
    count = {}
    for name in PLAN:
        if name in stages:
            stages[name]()
            continue
        turn = count[name] = count.get(name, -1) + 1
        if name in units:
            if turn < 4:
                units[name].step()
                if turn == 0 and STARTS.index(name) < SLOTS:
                    free_slot()
            elif turn == 4:
                close(name)
            else:
                open_half(name)
        elif name in ("W1", "W2"):
            vector_step(int(name[1]) - 1, turn)
        elif name.startswith("dc"):
            d_in_pass(int(name[2]))
        else:
            d_in_close(int(name[2]))
    out_vectors[...] = vec[5]
    out_vectors[0:3] = late[5, 0:3]
    for copy in grad_copies:
        copy.wait()


def hand_out(*refs):
    sources, vectors, targets, rows = refs[:8], refs[8], refs[9:17], refs[17:27]
    for source, target in zip(sources[:7], targets[:7]):
        target[...] = source[...]
    targets[7][...] = sources[7][...].T
    for i, place in enumerate((0, 1, 2, 3, 4, 5, None, 10, 11, 12)):
        if place is not None:
            rows[i][...] = vectors[place]
    for j in range(4):
        rows[6][pl.ds(768 * j, 768)] = vectors[6 + j]


def fused_layer(
    hidden_in,
    cotangent,
    span_mask,
    lengths,
    repeats,
    mask_embedding,
    query_weight,
    query_bias,
    key_weight,
    value_weight,
    value_bias,
    output_weight,
    output_bias,
    mixing_gain,
    mixing_shift,
    inner_weight,
    inner_bias,
    outer_weight,
    outer_bias,
    final_gain,
    final_shift,
):
    vmem = pl.BlockSpec(memory_space=pltpu.VMEM)
    anywhere = pl.BlockSpec(memory_space=pl.ANY)
    scalars = pl.BlockSpec(memory_space=pltpu.SMEM)
    bf = lambda *shape: pltpu.VMEM(shape, BF16)
    fl = lambda *shape: pltpu.VMEM(shape, F32)
    dma = lambda *shape: pltpu.SemaphoreType.DMA(shape)
    shape = lambda dims, dtype: jax.ShapeDtypeStruct(dims, dtype)
    result = pl.pallas_call(
        layer_body,
        out_shape=[
            shape((384, 768), BF16),
            shape((384, 768), BF16),
            shape((9216, 256), BF16),
            shape((96, 192), F32),
            shape((96, 192), F32),
            shape((96, 192), F32),
            shape((96, 192), F32),
            shape((96, 768), F32),
            shape((384, 192), F32),
            shape((16, 768), F32),
        ],
        in_specs=[anywhere] * 8 + [vmem] * 11 + [scalars, scalars],
        out_specs=[anywhere] * 3 + [vmem] * 7,
        scratch_shapes=[
            bf(3072, 768),
            bf(3072, 768),
            bf(768, 768),
            bf(768, 768),
            bf(768, 768),
            bf(768, 768),
            fl(16, 768),
            bf(3, 512, 768),
            bf(3, 512, 768),
            bf(3, 512, 768),
            bf(384, 768),
            bf(384, 768),
            bf(9216, 256),
            bf(384, 768),
            fl(384, 768),
            fl(384, 1),
            fl(384, 768),
            fl(384, 768),
            bf(384, 768),
            bf(384, 768),
            pltpu.VMEM((4, 8, 128), jnp.int32),
            fl(512, 8),
            fl(12, 8, 256),
            fl(3, 8, 256),
            bf(12, 2, 2, 2, 2, 2, 48, 384),
            bf(SLOTS, 2, 2, 2, 2, 48, 384),
            bf(12, 2, 2, 2, 48, 384),
            bf(12, 2, 2, 48, 384),
            bf(12, 2, 48, 384),
            bf(12, 48, 384),
            bf(12, 48, 384),
            bf(3, 256, 768),
            bf(3, 128, 768),
            fl(6, 16, 768),
            fl(5, 16, 768),
            fl(6, 8, 768),
            fl(5, 8, 768),
            dma(12, 6),
            dma(12, 6),
            dma(5, 3),
            dma(5, 3),
            dma(3),
            dma(3),
            dma(2, 5),
            dma(2, 5),
            dma(21),
            pltpu.SemaphoreType.REGULAR,
        ],
        compiler_params=pltpu.CompilerParams(
            collective_id=1, has_side_effects=True, vmem_limit_bytes=63 * 2**20
        ),
        name="fused_layer",
    )(
        hidden_in,
        cotangent.reshape(384, 768),
        query_weight,
        key_weight,
        value_weight,
        output_weight,
        inner_weight,
        outer_weight,
        span_mask,
        mask_embedding,
        query_bias,
        value_bias,
        output_bias,
        mixing_gain,
        mixing_shift,
        inner_bias,
        outer_bias,
        final_gain,
        final_shift,
        lengths,
        repeats,
    )
    arrays, vectors = [result[0], result[1], *result[3:9]], result[9]
    wide_row = shape((768,), F32)
    handed = pl.pallas_call(
        hand_out,
        out_shape=[shape(v.shape, v.dtype) for v in arrays[:7]]
        + [shape((192, 384), F32)]
        + [wide_row] * 6
        + [shape((3072,), F32)]
        + [wide_row] * 3,
        in_specs=[vmem] * 9,
        out_specs=[vmem] * 18,
        name="hand_out",
    )(*arrays, vectors)
    layer_out, grad_input, g_query, g_key, g_value, g_output, g_inner, g_outer = handed[:8]
    g_mask, g_q_bias, g_v_bias, g_o_bias, g_gain, g_shift, g_inner_bias, *g_last = handed[8:]
    return (
        layer_out.reshape(3, 128, 768),
        grad_input.reshape(3, 128, 768),
        g_mask,
        g_query,
        g_q_bias,
        g_key,
        g_value,
        g_v_bias,
        g_output,
        g_o_bias,
        g_gain,
        g_shift,
        g_inner,
        g_inner_bias,
        g_outer.T,
        *g_last,
    )


def with_halo(x, sides, width):
    for axis, dim in sides:
        count, length = (lax.axis_size(axis), x.shape[dim])
        up = [(i, (i + 1) % count) for i in range(count - 1)]
        down = [(j, i) for i, j in up]
        last = lax.slice_in_dim(x, length - width, length, axis=dim)
        initial = lax.slice_in_dim(x, 0, width, axis=dim)
        before = lax.ppermute(last, axis, up)
        after = lax.ppermute(initial, axis, down)
        x = jnp.concatenate([before, x, after], axis=dim)
    return x


def layer_norm(inputs, gain, shift):
    center = inputs - jnp.mean(inputs, -1, keepdims=True)
    spread = jnp.mean(center * center, -1, keepdims=True)
    return center * lax.rsqrt(spread + 1e-05) * gain + shift


def linear(inputs, weight):
    return jnp.dot(inputs, weight, preferred_element_type=jnp.float32)


def linear_back(grads, weight):
    return lax.dot_general(
        grads, weight, (((1,), (1,)), ((), ())), preferred_element_type=jnp.float32
    )


def contract_rows(left, right):
    return lax.dot_general(
        left, right, (((0,), (0,)), ((), ())), preferred_element_type=jnp.float32
    )


def gelu_exact(inputs):
    return jax.nn.gelu(inputs, approximate=False)


def plain_layer(
    hidden_in,
    cotangent,
    span_mask,
    lengths,
    repeats,
    mask_embedding,
    query_weight,
    query_bias,
    key_weight,
    value_weight,
    value_bias,
    output_weight,
    output_bias,
    mixing_gain,
    mixing_shift,
    inner_weight,
    inner_bias,
    outer_weight,
    outer_bias,
    final_gain,
    final_shift,
):
    rows, stretch, width = hidden_in.shape
    whole = stretch * lax.axis_size("seq")
    scale = HEAD_DIM ** (-0.5)
    offset = lax.axis_index("seq") * stretch
    rim = with_halo(span_mask, (("seq", 1),), WIDEN)
    window = rim[:, 0:stretch]
    for shifted in range(1, 2 * WIDEN + 1):
        window = window + rim[:, shifted : shifted + stretch]
    widened = window > 0
    positions = offset + jnp.arange(stretch, dtype=jnp.int32)
    live = positions[None, :] < lengths[:, None]
    key_live = jnp.arange(whole, dtype=jnp.int32)[None, :] < lengths[:, None]
    masked_in = jnp.where(widened[..., None], mask_embedding[None, None, :], hidden_in)
    flat_in = masked_in.reshape(rows * stretch, width)
    queries = (linear(flat_in, query_weight) + query_bias.astype(jnp.float32)).astype(jnp.bfloat16)
    key_rows = linear(flat_in, key_weight).astype(jnp.bfloat16).reshape(rows, stretch, width)
    value_rows = (linear(flat_in, value_weight) + value_bias.astype(jnp.float32)).astype(
        jnp.bfloat16
    )
    value_rows = value_rows.reshape(rows, stretch, width)
    key_all, value_all = (
        lax.all_gather(key_rows, "seq", axis=1, tiled=True),
        lax.all_gather(value_rows, "seq", axis=1, tiled=True),
    )
    query_heads = queries.reshape(rows, stretch, HEADS, HEAD_DIM)

    def scores_of(key_full):
        key_heads = key_full.reshape(rows, whole, HEADS, HEAD_DIM)
        raw = jnp.einsum(
            "rqhd,rkhd->rhqk", query_heads, key_heads, preferred_element_type=jnp.float32
        )
        return jnp.where(key_live[:, None, None, :], raw * scale, -1e30)

    logits = scores_of(key_all)
    highest = jnp.max(logits, -1, keepdims=True)
    expd = jnp.exp(logits - highest)
    totals = jnp.sum(expd, -1, keepdims=True)
    log_total = highest + jnp.log(totals)
    probs_low = (expd / totals).astype(jnp.bfloat16)
    value_heads = value_all.reshape(rows, whole, HEADS, HEAD_DIM)
    mixed = jnp.einsum(
        "rhqk,rkhd->rqhd", probs_low, value_heads, preferred_element_type=jnp.float32
    )
    mixed = mixed.reshape(rows * stretch, width).astype(jnp.bfloat16)
    attended = linear(mixed, output_weight) + output_bias.astype(jnp.float32)
    residual_one = flat_in.astype(jnp.float32) + attended
    first, norm_back_one = jax.vjp(
        layer_norm, residual_one, mixing_gain.astype(jnp.float32), mixing_shift.astype(jnp.float32)
    )
    first_low = first.astype(jnp.bfloat16)
    inner = linear(first_low, inner_weight) + inner_bias.astype(jnp.float32)
    activated, gelu_back = jax.vjp(gelu_exact, inner)
    activated_low = activated.astype(jnp.bfloat16)
    outer = linear(activated_low, outer_weight) + outer_bias.astype(jnp.float32)
    final, norm_back_two = jax.vjp(
        layer_norm, first + outer, final_gain.astype(jnp.float32), final_shift.astype(jnp.float32)
    )
    layer_out = final.astype(jnp.bfloat16).reshape(rows, stretch, width)
    weighting = repeats.astype(jnp.float32)[:, None] * live.astype(jnp.float32)
    d_final = (cotangent.astype(jnp.float32) * weighting[:, :, None]).reshape(rows * stretch, width)
    d_two, d_final_gain, d_final_shift = norm_back_two(d_final)
    d_outer = d_two.astype(jnp.bfloat16)
    g_outer_weight = contract_rows(activated_low, d_outer)
    g_outer_bias = jnp.sum(d_outer.astype(jnp.float32), 0)
    (d_inner,) = gelu_back(linear_back(d_outer, outer_weight))
    d_inner = d_inner.astype(jnp.bfloat16)
    g_inner_weight = contract_rows(first_low, d_inner)
    g_inner_bias = jnp.sum(d_inner.astype(jnp.float32), 0)
    d_first = linear_back(d_inner, inner_weight) + d_two
    d_one, d_mixing_gain, d_mixing_shift = norm_back_one(d_first)
    d_attended = d_one.astype(jnp.bfloat16)
    g_output_weight = contract_rows(mixed, d_attended)
    g_output_bias = jnp.sum(d_attended.astype(jnp.float32), 0)
    d_mixed = linear_back(d_attended, output_weight).astype(jnp.bfloat16)
    d_mixed_heads = d_mixed.reshape(rows, stretch, HEADS, HEAD_DIM)
    key_back, value_back = (
        lax.all_gather(key_rows, "seq", axis=1, tiled=True),
        lax.all_gather(value_rows, "seq", axis=1, tiled=True),
    )
    probs = jnp.exp(scores_of(key_back) - log_total)
    probs_again = probs.astype(jnp.bfloat16)
    key_heads = key_back.reshape(rows, whole, HEADS, HEAD_DIM)
    value_heads = value_back.reshape(rows, whole, HEADS, HEAD_DIM)
    d_probs = jnp.einsum(
        "rqhd,rkhd->rhqk", d_mixed_heads, value_heads, preferred_element_type=jnp.float32
    )
    centered = d_probs - jnp.sum(probs * d_probs, -1, keepdims=True)
    d_raw = (probs * centered * scale).astype(jnp.bfloat16)
    d_queries = jnp.einsum("rhqk,rkhd->rqhd", d_raw, key_heads, preferred_element_type=jnp.float32)
    d_queries = d_queries.reshape(rows * stretch, width).astype(jnp.bfloat16)
    d_key_part = jnp.einsum(
        "rhqk,rqhd->rkhd", d_raw, query_heads, preferred_element_type=jnp.float32
    )
    d_value_part = jnp.einsum(
        "rhqk,rqhd->rkhd", probs_again, d_mixed_heads, preferred_element_type=jnp.float32
    )
    d_key_sum, d_value_sum = (
        lax.psum_scatter(
            d_key_part.reshape(rows, whole, width), "seq", scatter_dimension=1, tiled=True
        ),
        lax.psum_scatter(
            d_value_part.reshape(rows, whole, width), "seq", scatter_dimension=1, tiled=True
        ),
    )
    d_keys = d_key_sum.astype(jnp.bfloat16).reshape(rows * stretch, width)
    d_values = d_value_sum.astype(jnp.bfloat16).reshape(rows * stretch, width)
    g_query_weight = contract_rows(flat_in, d_queries)
    g_key_weight = contract_rows(flat_in, d_keys)
    g_value_weight = contract_rows(flat_in, d_values)
    g_query_bias = jnp.sum(d_queries.astype(jnp.float32), 0)
    g_value_bias = jnp.sum(d_values.astype(jnp.float32), 0)
    d_input = (
        d_one
        + linear_back(d_queries, query_weight)
        + linear_back(d_keys, key_weight)
        + linear_back(d_values, value_weight)
    ).reshape(rows, stretch, width)
    grad_input = jnp.where(widened[..., None], 0.0, d_input).astype(jnp.bfloat16)
    g_mask = jnp.sum(jnp.where(widened[..., None], d_input, 0.0), (0, 1))
    matrices = (
        g_query_weight,
        g_key_weight,
        g_value_weight,
        g_output_weight,
        g_inner_weight,
        g_outer_weight,
    )
    partial_sums = (
        lax.psum_scatter(matrices[0], "batch", scatter_dimension=0, tiled=True),
        lax.psum_scatter(matrices[1], "batch", scatter_dimension=0, tiled=True),
        lax.psum_scatter(matrices[2], "batch", scatter_dimension=0, tiled=True),
        lax.psum_scatter(matrices[3], "batch", scatter_dimension=0, tiled=True),
        lax.psum_scatter(matrices[4], "batch", scatter_dimension=0, tiled=True),
        lax.psum_scatter(matrices[5], "batch", scatter_dimension=0, tiled=True),
    )
    summed = (
        lax.psum_scatter(partial_sums[0], "seq", scatter_dimension=1, tiled=True),
        lax.psum_scatter(partial_sums[1], "seq", scatter_dimension=1, tiled=True),
        lax.psum_scatter(partial_sums[2], "seq", scatter_dimension=1, tiled=True),
        lax.psum_scatter(partial_sums[3], "seq", scatter_dimension=1, tiled=True),
        lax.psum_scatter(partial_sums[4], "seq", scatter_dimension=1, tiled=True),
        lax.psum_scatter(partial_sums[5], "seq", scatter_dimension=1, tiled=True),
    )
    vectors = lax.psum(
        (
            g_mask,
            g_query_bias,
            g_value_bias,
            g_output_bias,
            d_mixing_gain,
            d_mixing_shift,
            g_inner_bias,
            g_outer_bias,
            d_final_gain,
            d_final_shift,
        ),
        ("batch", "seq"),
    )
    return (
        layer_out,
        grad_input,
        vectors[0],
        summed[0],
        vectors[1],
        summed[1],
        summed[2],
        vectors[2],
        summed[3],
        vectors[3],
        vectors[4],
        vectors[5],
        summed[4],
        vectors[6],
        summed[5],
        vectors[7],
        vectors[8],
        vectors[9],
    )


def solution(mesh):
    fused = mesh.shape["batch"] == 8 and mesh.shape["seq"] == 4
    return jax.shard_map(
        fused_layer if fused else plain_layer,
        mesh=mesh,
        in_specs=(
            P("batch", "seq", None),
            P("batch", "seq", None),
            P("batch", "seq"),
            P("batch"),
            P("batch"),
            P(),
            P(),
            P(),
            P(),
            P(),
            P(),
            P(),
            P(),
            P(),
            P(),
            P(),
            P(),
            P(),
            P(),
            P(),
            P(),
        ),
        out_specs=(
            P("batch", "seq", None),
            P("batch", "seq", None),
            P(),
            P("batch", "seq"),
            P(),
            P("batch", "seq"),
            P("batch", "seq"),
            P(),
            P("batch", "seq"),
            P(),
            P(),
            P(),
            P("batch", "seq"),
            P(),
            P("batch", "seq"),
            P(),
            P(),
            P(),
        ),
        check_vma=False,
    )
```

```python
import jax
import jax.numpy as jnp
from jax import lax
from jax.experimental import pallas as pl
from jax.experimental.pallas import tpu as pltpu
from jax.sharding import PartitionSpec as P

HEADS = 12
HEAD_DIM = 64
WIDEN = 5

MESH = pl.DeviceIdType.MESH
F32 = jnp.float32
BF16 = jnp.bfloat16
ROOT_HALF = 0.7071067811865476
DENSITY = 0.3989422804014327


def mm(a, b):
    return jnp.dot(a, b, preferred_element_type=F32)


def mm_t(a, b):
    return lax.dot_general(a, b, (((1,), (1,)), ((), ())), preferred_element_type=F32)


def mm_tl(a, b):
    return lax.dot_general(a, b, (((0,), (0,)), ((), ())), preferred_element_type=F32)


def fold(v):
    return jnp.sum(v.reshape(v.shape[0] // 8, 8, v.shape[1]), 0)


def loop(count, body):
    def step(i, carry):
        body(i)
        return carry

    lax.fori_loop(0, count, step, 0, unroll=count if count <= 4 else 4)


def span_loop(first, last, body):
    def step(i, carry):
        body(i)
        return carry

    lax.fori_loop(first, last, step, 0, unroll=True)


def aligned(i, size):
    return pl.ds(pl.multiple_of(i * size, size), size)


def places():
    b, s = lax.axis_index("batch"), lax.axis_index("seq")
    x, zlo, zhi = lax.rem(b, 2), lax.rem(b // 2, 2), b // 4
    core, y = lax.rem(s, 2), s // 2
    spot = {CORE: core, X: x, Y: y, ZLO: zlo, ZHI: zhi}
    peer = {
        CORE: (b, s + 1 - 2 * core),
        Y: (b, s + 2 - 4 * y),
        X: (b + 1 - 2 * x, s),
        ZLO: (b + 2 - 4 * zlo, s),
        ZHI: (b + 4 - 8 * zhi, s),
        FAR: (b, 3 - s),
    }
    return spot, peer


class Unit:
    def __init__(self, order, both, inbox, sends, recvs, spot, peer):
        self.order, self.both, self.inbox = order, both, inbox
        self.sends, self.recvs, self.spot, self.peer = sends, recvs, spot, peer
        self.own = both.at[spot[CORE]]
        self.phase = 0

    def where(self, phase, stays):
        done, axis = self.order[: phase - 1], self.order[phase - 1]
        place = []
        for name in (Y, ZHI, ZLO, X):
            side = self.spot[name]
            if name == axis:
                place.append(side if stays else 1 - side)
            else:
                place.append(side if name in done else slice(None))
        return tuple(place)

    def copy(self, phase):
        if phase == 0:
            axis, source = CORE, self.both.at[1 - self.spot[CORE]]
        else:
            axis, source = self.order[phase - 1], self.own.at[self.where(phase, False)]
        return pltpu.make_async_remote_copy(
            src_ref=source,
            dst_ref=self.inbox[phase],
            send_sem=self.sends.at[phase],
            recv_sem=self.recvs.at[phase],
            device_id=self.peer[axis],
            device_id_type=MESH,
        )

    def start(self):
        self.copy(0).start()

    def step(self):
        phase = self.phase
        self.copy(phase).wait()
        came = self.inbox[phase]
        target = self.own if phase == 0 else self.own.at[self.where(phase, True)]
        lead = 4 - phase

        def body(n):
            place = tuple(lax.rem(n // 2 ** (lead - 1 - i), 2) for i in range(lead))
            target[place] = target[place] + came[place]

        loop(2**lead, body)
        self.phase = phase + 1
        self.copy(self.phase).start()


CORE, X, Y, ZLO, ZHI, FAR = range(6)
OUTER0, OUTER1, OUTER2, OUTER3, INNER0, INNER1, INNER2, INNER3, OUTPUT, QUERY, KEY, VALUE = range(0, 12)
(
    D_HIDDEN0, D_HIDDEN1, D_HIDDEN2, INNER, D_FIRST, FNB, V1, DWO,
    REFILL, DMIXED, DWQ, DWK, DWV, VEC, AB00, AB01,
    AB10, AB11, AB20, AB21, DIN0, DIN1, DIN2,
) = range(12, 35)
W1, W2, DC0, DC1, DC2, DY0, DY1, DY2 = range(35, 43)
STARTS = (
    OUTER0, OUTER1, OUTER2, OUTER3, INNER0, INNER1,
    INNER2, INNER3, OUTPUT, KEY, QUERY, VALUE,
)
ORDERS = {
    OUTER0: (Y, ZLO, X, ZHI),
    OUTER1: (X, Y, ZLO, ZHI),
    OUTER2: (Y, X, ZLO, ZHI),
    OUTER3: (ZLO, ZHI, Y, X),
    INNER0: (X, ZLO, Y, ZHI),
    INNER1: (Y, ZLO, ZHI, X),
    INNER2: (X, ZLO, Y, ZHI),
    INNER3: (Y, X, ZLO, ZHI),
    OUTPUT: (X, Y, ZLO, ZHI),
    KEY: (X, ZLO, ZHI, Y),
    QUERY: (Y, X, ZLO, ZHI),
    VALUE: (X, ZLO, Y, ZHI),
}
PLAN = (
    D_HIDDEN0, D_HIDDEN1, OUTER0, D_HIDDEN2, OUTER1, OUTER2, INNER, OUTER3,
    D_FIRST, REFILL, OUTER0, INNER0, FNB, INNER1, OUTER1, INNER2,
    V1, DWO, INNER3, W1, DMIXED, OUTER2, OUTER3, AB00,
    OUTPUT, OUTER0, INNER0, AB01, INNER1, AB10, AB11, INNER2,
    OUTER1, W1, OUTER3, INNER0, AB20, OUTER2, AB21, INNER1,
    INNER3, W1, DWK, INNER2, OUTER3, DWQ, INNER0, OUTER1,
    OUTPUT, DWV, KEY, OUTER0, INNER2, QUERY, INNER1, OUTER2,
    DIN0, INNER3, INNER0, W1, OUTER3, OUTPUT, DIN1, VALUE,
    OUTER0, OUTER1, OUTER3, INNER2, DC0, DIN2, OUTER0, OUTER2,
    INNER1, INNER3, OUTER1, DC1, QUERY, KEY, VEC, OUTER2,
    W1, OUTPUT, DC2, W2, DY0, INNER3, VALUE, KEY,
    DY1, OUTPUT, QUERY, W2, OUTPUT, VALUE, DY2, W2,
    KEY, VALUE, QUERY, W2, KEY, KEY, VALUE, QUERY,
    VALUE, W2, QUERY,
)
SLOTS = 6


def layer_body(
    hidden,
    cotangent,
    query_weight,
    key_weight,
    value_weight,
    output_weight,
    inner_weight,
    outer_weight,
    span,
    mask_embedding,
    query_bias,
    value_bias,
    output_bias,
    mixing_gain,
    mixing_shift,
    inner_bias,
    outer_bias,
    final_gain,
    final_shift,
    lengths,
    repeats,
    layer_out,
    grad_input,
    probs_out,
    out_query,
    out_key,
    out_value,
    out_output,
    out_inner,
    out_outer,
    out_vectors,
    wi,
    wf,
    wq,
    wk,
    wv,
    wo,
    packed,
    params,
    x_all,
    k_all,
    v_all,
    q_own,
    mixed,
    region,
    first_low,
    norm_one,
    spread_one,
    total,
    d_res,
    d_outer,
    d_att,
    masks,
    wide,
    inner_sums,
    mask_sums,
    grads,
    in0,
    in1,
    in2,
    in3,
    in4,
    in5,
    d_in0,
    d_in1,
    vec,
    vec_came,
    late,
    late_came,
    sends,
    recvs,
    x_send,
    x_recv,
    m_send,
    m_recv,
    v_send,
    v_recv,
    local,
    credit,
):
    spot, peer = places()
    core, y = spot[CORE], spot[Y]
    me = 2 * y + core
    sibling = 2 * y + 1 - core
    across = 2 * (1 - y) + core

    names = (CORE, X, Y, ZLO, ZHI, FAR)
    barrier = pltpu.get_barrier_semaphore()
    for name in names:
        pl.semaphore_signal(barrier, inc=1, device_id=peer[name], device_id_type=MESH)

    weight_loads = {}

    def load(name, number, source, target):
        copy = pltpu.make_async_copy(source, target, local.at[number])
        copy.start()
        weight_loads[name] = copy

    load("hidden", 0, hidden, x_all.at[:, aligned(me, 128)])
    load("key", 1, key_weight, wk)
    load("value", 2, value_weight, wv)
    load("query", 3, query_weight, wq)

    pl.semaphore_wait(barrier, len(names))

    masks[me] = jnp.zeros((8, 128), jnp.int32)
    masks[me, 0:3] = span[...]
    mask_copies = []
    for i, name in enumerate((CORE, Y, FAR)):
        copy = pltpu.make_async_remote_copy(
            src_ref=masks.at[me],
            dst_ref=masks.at[me],
            send_sem=m_send.at[i],
            recv_sem=m_recv.at[i],
            device_id=peer[name],
            device_id_type=MESH,
        )
        copy.start()
        mask_copies.append(copy)

    def x_copy(kind, r):
        source = hidden.at[r] if kind < 2 else x_all.at[r, aligned(across, 128)]
        slot = me if kind < 2 else across
        return pltpu.make_async_remote_copy(
            src_ref=source,
            dst_ref=x_all.at[r, aligned(slot, 128)],
            send_sem=x_send.at[kind, r],
            recv_sem=x_recv.at[kind, r],
            device_id=peer[Y if kind == 0 else CORE],
            device_id_type=MESH,
        )

    for r in range(3):
        x_copy(0, r).start()
        x_copy(1, r).start()

    vectors = (
        (mask_embedding, 0),
        (query_bias, 1),
        (value_bias, 2),
        (output_bias, 3),
        (mixing_gain, 4),
        (mixing_shift, 5),
        (inner_bias, 6),
        (outer_bias, 10),
        (final_gain, 11),
        (final_shift, 12),
    )
    vector_loads = []
    for i, (vector, place) in enumerate(vectors):
        target = packed.at[pl.ds(768 * place, vector.shape[0])]
        copy = pltpu.make_async_copy(vector, target, local.at[21 + i])
        copy.start()
        vector_loads.append(copy)
    for copy in vector_loads:
        copy.wait()
    for i in range(13):
        params[i : i + 1] = packed[pl.ds(768 * i, 768)].astype(F32).reshape(1, 768)

    for copy in mask_copies:
        copy.wait()
    span_all = jnp.concatenate([masks[s].astype(F32) for s in range(4)], axis=1)
    lane = lax.broadcasted_iota(jnp.int32, span_all.shape, 1)
    window = span_all
    for d in range(1, WIDEN + 1):
        window = jnp.maximum(window, jnp.where(lane >= d, pltpu.roll(span_all, d, 1), 0.0))
        window = jnp.maximum(
            window, jnp.where(lane < 512 - d, pltpu.roll(span_all, 512 - d, 1), 0.0)
        )
    wide[...] = window.T

    half = lax.broadcasted_iota(jnp.int32, (128, 128), 1) < HEAD_DIM
    zero = jnp.zeros((128, 128), BF16)

    def stacked(pair):
        return jnp.concatenate([jnp.where(half, pair, zero), jnp.where(half, zero, pair)], 0)

    def unstacked(both):
        return jnp.where(half, both[:128], both[128:])

    mask_row = params[0:1]
    spills = []

    def put_mask(r, slot):
        rows = aligned(slot, 128)
        chosen = wide[rows, r : r + 1] > 0.5
        kept = x_all[r, rows].astype(F32)
        x_all[r, rows] = jnp.where(chosen, mask_row, kept).astype(BF16)

    def project(pieces, with_queries):
        inputs = jnp.concatenate([x_all[r, aligned(slot, 128)] for r, slot in pieces], 0)

        def part(n):
            cols = aligned(n, 256)
            keys = mm(inputs, wk[:, cols]).astype(BF16)
            values = (mm(inputs, wv[:, cols]) + params[2:3, cols]).astype(BF16)
            for i, (r, slot) in enumerate(pieces):
                k_all[r, aligned(slot, 128), cols] = keys[128 * i : 128 * i + 128]
                v_all[r, aligned(slot, 128), cols] = values[128 * i : 128 * i + 128]
            if with_queries:
                q_own[:, cols] = (mm(inputs, wq[:, cols]) + params[1:2, cols]).astype(BF16)

        loop(3, part)

    weight_loads["hidden"].wait()
    for r in range(3):
        put_mask(r, me)
    for name in ("key", "value", "query"):
        weight_loads[name].wait()
    load("output", 4, output_weight, wo)
    for j in range(4):
        load(j, 5 + j, inner_weight.at[:, pl.ds(768 * j, 768)], wi.at[pl.ds(768 * j, 768)])
    load("outer", 9, outer_weight, wf)
    load("cotangent", 10, cotangent, d_outer)
    project([(r, me) for r in range(3)], True)
    for r in range(3):
        x_copy(1, r).wait()
        put_mask(r, sibling)
    project([(r, sibling) for r in range(3)], False)
    x_copy(0, 0).wait_recv()
    x_copy(2, 0).start()
    for r in range(3):
        x_copy(2, r).wait()
        put_mask(r, across)
        put_mask(r, 3 - me)
        project([(r, across), (r, 3 - me)], False)
        key_live = lax.broadcasted_iota(jnp.int32, (1, 512), 1) < lengths[r]

        def attend(p):
            cols = aligned(p, 128)
            queries = stacked(q_own[pl.ds(128 * r, 128), cols] * BF16(HEAD_DIM**-0.5))
            logits = mm_t(queries, k_all[r, :, cols])
            logits = jnp.where(key_live, logits, -1e30)
            expd = jnp.exp(logits - jnp.max(logits, -1, keepdims=True))
            probs = (expd * (1.0 / jnp.sum(expd, -1, keepdims=True))).astype(BF16)
            base = r * 6 + p
            region[aligned(2 * base, 256)] = probs[:, :256]
            region[aligned(2 * base + 1, 256)] = probs[:, 256:]
            out = mm(probs, v_all[r, :, cols])
            mixed[pl.ds(128 * r, 128), cols] = unstacked(out).astype(BF16)

        span_loop(0, 3, attend)
        if r < 2:
            x_copy(0, r + 1).wait_recv()
            x_copy(2, r + 1).start()
        span_loop(3, 6, attend)
        rows = pl.ds(3072 * r, 3072)
        spill = pltpu.make_async_copy(region.at[rows], probs_out.at[rows], local.at[11 + r])
        spill.start()
        spills.append(spill)

    for r in range(3):
        x_copy(0, r).wait_send()
    weight_loads["output"].wait()

    def first_norm(i):
        rows = aligned(i, 128)
        attended = mm(mixed[rows], wo[...]) + params[3:4]
        value = x_all[i, aligned(me, 128)].astype(F32) + attended
        center = value - jnp.mean(value, -1, keepdims=True)
        scale = lax.rsqrt(jnp.mean(center * center, -1, keepdims=True) + 1e-5)
        norm = center * scale
        norm_one[rows] = norm
        spread_one[rows] = scale
        first_low[rows] = (norm * params[4:5] + params[5:6]).astype(BF16)

    loop(3, first_norm)
    for spill in spills:
        spill.wait()
    for j in range(4):
        weight_loads[j].wait()

    def hidden_units(j):
        inner = mm(
            first_low[...], wi[pl.ds((j // 3) * 768, 768), aligned(lax.rem(j, 3), 256)]
        ) + params[pl.ds(6 + j // 3, 1), aligned(lax.rem(j, 3), 256)]
        below = 0.5 * (1.0 + lax.erf(inner * ROOT_HALF))
        slope = below + inner * (DENSITY * jnp.exp(-0.5 * inner * inner))
        region[aligned(j, 384)] = (inner * below).astype(BF16)
        region[aligned(12 + j, 384)] = slope.astype(BF16)

    loop(12, hidden_units)
    weight_loads["outer"].wait()
    weight_loads["cotangent"].wait()

    def panels(first, count):
        return jnp.concatenate(
            [region[pl.ds(384 * j, 384)] for j in range(first, first + count)], axis=1
        )

    def project_out(n):
        cols = aligned(n, 256)
        total[:, cols] = mm(panels(0, 12), wf[:, cols])

    loop(3, project_out)

    def last_norm(i, sums):
        rows = aligned(i, 64)
        first = norm_one[rows] * params[4:5] + params[5:6]
        value = first + (total[rows] + params[10:11])
        center = value - jnp.mean(value, -1, keepdims=True)
        scale = lax.rsqrt(jnp.mean(center * center, -1, keepdims=True) + 1e-5)
        norm = center * scale
        d_att[rows] = (norm * params[11:12] + params[12:13]).astype(BF16)
        r = i // 2
        position = lax.broadcasted_iota(jnp.int32, (64, 1), 0) + lax.rem(i, 2) * 64 + me * 128
        weight = jnp.where(position < lengths[r], repeats[r].astype(F32), 0.0)
        d_final = d_outer[rows].astype(F32) * weight
        d_norm = d_final * params[11:12]
        d_two = scale * (
            d_norm
            - jnp.mean(d_norm, -1, keepdims=True)
            - norm * jnp.mean(d_norm * norm, -1, keepdims=True)
        )
        d_res[rows] = d_two
        low = d_two.astype(BF16)
        d_outer[rows] = low
        return (
            sums[0] + fold(d_final * norm),
            sums[1] + fold(d_final),
            sums[2] + fold(low.astype(F32)),
        )

    nothing = jnp.zeros((8, 768), F32)

    def put_sum(row, value):
        vec[0, row : row + 1] = jnp.sum(value, 0, keepdims=True)

    vec[0] = jnp.zeros((16, 768), F32)
    sums = lax.fori_loop(0, 6, last_norm, (nothing, nothing, nothing))
    put_sum(11, sums[0])
    put_sum(12, sums[1])
    put_sum(10, sums[2])
    out_copy = pltpu.make_async_copy(
        d_att, layer_out, local.at[14]
    )
    out_copy.start()

    units = [None] * 12
    for turn, u in enumerate(STARTS):
        inbox = [in0.at[turn % SLOTS], in1.at[u], in2.at[u], in3.at[u], in4.at[u]]
        units[u] = Unit(ORDERS[u], grads.at[u], inbox, sends.at[u], recvs.at[u], spot, peer)

    def start_unit(name):
        if STARTS.index(name) >= SLOTS:
            claim_slot()
        units[name].start()

    def free_slot():
        pl.semaphore_signal(credit, inc=1, device_id=peer[CORE], device_id_type=MESH)

    def claim_slot():
        pl.semaphore_wait(credit, 1)

    def outer_grads(z):
        for x in range(2):
            cols = [region[pl.ds(pl.multiple_of((3 * z + j) * 384, 384), 384)] for j in range(3)]
            part = jnp.concatenate(cols, axis=1)[:, 384 * x : 384 * x + 384]
            grad = mm_tl(part, d_outer[...]).astype(BF16)
            for h in range(2):
                for i in range(4):
                    for side in range(2):
                        rows = (h * 4 + i) * 48
                        grads[OUTER0 + i, h, side, z // 2, lax.rem(z, 2), x] = grad[
                            rows : rows + 48, side * 384 : side * 384 + 384
                        ]

    loop(4, outer_grads)
    for i in range(4):
        start_unit(OUTER0 + i)

    def d_hidden_units(j):
        d_act = mm_t(d_outer[...], wf[aligned(j, 256)])
        place = aligned(12 + j, 384)
        low = (d_act * region[place].astype(F32)).astype(BF16)
        region[place] = low
        inner_sums[j] = fold(low.astype(F32))

    def inner_grads(s):
        cols = [region[pl.ds(pl.multiple_of((12 + 3 * s + j) * 384, 384), 384)] for j in range(3)]
        grad = mm_tl(first_low[...], jnp.concatenate(cols, axis=1)).astype(BF16)
        for b in range(8):
            for i in range(4):
                rows, side = 96 * b + 48 * (i % 2), 384 * (i // 2)
                grads[
                    INNER0 + i, lax.rem(s, 2), s // 2, b // 4, (b // 2) % 2, b % 2
                ] = grad[rows : rows + 48, side : side + 384]

    def do_inner_grads():
        loop(4, inner_grads)
        for i in range(4):
            start_unit(INNER0 + i)

    def d_first_part(n):
        cols = aligned(n, 256)
        acc = None
        for s in range(4):
            d_inner = panels(12 + 3 * s, 3)
            term = mm_t(d_inner, wi[pl.ds(pl.multiple_of(s * 768 + n * 256, 256), 256)])
            acc = term if acc is None else acc + term
        total[:, cols] = acc

    refills = []

    def do_d_first():
        loop(3, d_first_part)
        for j in range(12):
            vec[0, 6 + j // 3 : 7 + j // 3, (j % 3) * 256 : (j % 3) * 256 + 256] = jnp.sum(
                inner_sums[j], 0, keepdims=True
            )

    def refill_probs():
        for r in range(3):
            rows = pl.ds(3072 * r, 3072)
            refill = pltpu.make_async_copy(probs_out.at[rows], region.at[rows], local.at[15 + r])
            refill.start()
            refills.append(refill)

    def first_norm_back(i, sums):
        rows = aligned(i, 64)
        d_first = total[rows] + d_res[rows]
        norm = norm_one[rows]
        d_norm = d_first * params[4:5]
        d_one = spread_one[rows] * (
            d_norm
            - jnp.mean(d_norm, -1, keepdims=True)
            - norm * jnp.mean(d_norm * norm, -1, keepdims=True)
        )
        d_res[rows] = d_one
        low = d_one.astype(BF16)
        d_att[rows] = low
        return (
            sums[0] + fold(d_first * norm),
            sums[1] + fold(d_first),
            sums[2] + fold(low.astype(F32)),
        )

    def do_first_norm_back():
        out_copy.wait()
        sums = lax.fori_loop(0, 6, first_norm_back, (nothing, nothing, nothing))
        put_sum(4, sums[0])
        put_sum(5, sums[1])
        put_sum(3, sums[2])

    def square_grads(u, left, right):
        for m in range(2):
            grad = mm_tl(left(m), right).astype(BF16)
            for b in range(4):
                for h in range(2):
                    for side in range(2):
                        rows = b * 96 + h * 48
                        grads[u, h, side, m, b // 2, b % 2] = grad[
                            rows : rows + 48, side * 384 : side * 384 + 384
                        ]
        start_unit(u)

    def do_output_grads():
        square_grads(OUTPUT, lambda m: mixed[:, 384 * m : 384 * m + 384], d_att[...])

    def d_mixed_part(i):
        rows = aligned(i, 128)
        mixed[rows] = mm_t(d_att[rows], wo[...]).astype(BF16)

    def do_attend_back(r, first, last):
        if first == 0:
            refills[r].wait()

        def attend_back(p):
            cols = aligned(p, 128)
            own_rows = pl.ds(128 * r, 128)
            base = r * 6 + p
            queries = stacked(q_own[own_rows, cols] * BF16(HEAD_DIM**-0.5))
            d_mix = stacked(mixed[own_rows, cols])
            low_probs = jnp.concatenate(
                [region[aligned(2 * base, 256)], region[aligned(2 * base + 1, 256)]], axis=1
            )
            d_probs = mm_t(d_mix, v_all[r, :, cols])
            probs = low_probs.astype(F32)
            weighted = probs * d_probs
            d_raw = (weighted - probs * jnp.sum(weighted, -1, keepdims=True)).astype(BF16)
            d_query = mm(d_raw, k_all[r, :, cols]) * HEAD_DIM**-0.5
            q_own[own_rows, cols] = unstacked(d_query).astype(BF16)
            wi[pl.ds(512 * r, 512), cols] = mm_tl(d_raw, queries).astype(BF16)
            wi[pl.ds(1536 + 512 * r, 512), cols] = mm_tl(low_probs, d_mix).astype(BF16)

        span_loop(first, last, attend_back)

    def own_inputs(m):
        return jnp.concatenate(
            [x_all[r, aligned(me, 128), pl.ds(384 * m, 384)] for r in range(3)], 0
        )

    def all_inputs(m):
        return jnp.concatenate([x_all[r, :, pl.ds(384 * m, 384)] for r in range(3)], 0)

    def do_query_grads():
        square_grads(QUERY, own_inputs, q_own[...])

    def do_key_grads():
        square_grads(KEY, all_inputs, wi[pl.ds(0, 1536)])

    def do_value_grads():
        square_grads(VALUE, all_inputs, wi[pl.ds(1536, 1536)])

    def value_sum(i, acc):
        return acc + fold(wi[pl.ds(pl.multiple_of(1536 + i * 128, 128), 128)].astype(F32))

    mask_sums[...] = jnp.zeros((3, 8, 256), F32)

    def d_in_copy(kind, r):
        if kind == 0:
            source = wf.at[aligned(2 * r + 1 - core, 256)]
            target, name = d_in0.at[r], CORE
        else:
            source = wf.at[aligned(4 * r + 2 * core + 1 - y, 128)]
            target, name = d_in1.at[r], Y
        return pltpu.make_async_remote_copy(
            src_ref=source,
            dst_ref=target,
            send_sem=x_send.at[3 + kind, r],
            recv_sem=x_recv.at[3 + kind, r],
            device_id=peer[name],
            device_id_type=MESH,
        )

    def do_d_in(r):
        def d_in_part(n):
            cols = aligned(n, 256)
            part = mm_t(wi[pl.ds(512 * r, 512)], wk[cols]) + mm_t(
                wi[pl.ds(1536 + 512 * r, 512)], wv[cols]
            )
            for s in range(4):
                block = 4 * r + 2 * (s % 2) + s // 2
                wf[pl.ds(128 * block, 128), cols] = part[128 * s : 128 * s + 128].astype(BF16)
            mask_sums[n] = mask_sums[n] + fold(part * wide[:, r : r + 1])

        loop(3, d_in_part)
        d_in_copy(0, r).start()

    def d_in_pass(r):
        d_in_copy(0, r).wait()
        rows = aligned(4 * r + 2 * core + 1 - y, 128)
        wf[rows] = wf[rows] + d_in0[r, aligned(1 - y, 128)]
        d_in_copy(1, r).start()

    def own_part(i, acc):
        rows = aligned(i, 128)
        part = d_res[rows] + mm_t(q_own[rows], wq[...])
        d_res[rows] = part
        chosen = wide[aligned(me, 128)]
        chosen = jnp.where(i == 0, chosen[:, 0:1], jnp.where(i == 1, chosen[:, 1:2], chosen[:, 2:3]))
        return acc + fold(part * chosen)

    grad_copies = []

    def d_in_close(r):
        d_in_copy(1, r).wait()
        rows = pl.ds(128 * r, 128)
        value = (
            d_res[rows]
            + wf[aligned(4 * r + 2 * core + y, 128)].astype(F32)
            + d_in0[r, aligned(y, 128)].astype(F32)
            + d_in1[r].astype(F32)
        )
        chosen = wide[aligned(me, 128), r : r + 1] > 0.5
        d_att[rows] = jnp.where(chosen, 0.0, value).astype(BF16)
        copy = pltpu.make_async_copy(d_att.at[rows], grad_input.at[rows], local.at[18 + r])
        copy.start()
        grad_copies.append(copy)

    axes = (CORE, X, Y, ZLO, ZHI)

    def vector_copy(group, phase):
        sums, came = (vec, vec_came) if group == 0 else (late, late_came)
        return pltpu.make_async_remote_copy(
            src_ref=sums.at[phase],
            dst_ref=came.at[phase],
            send_sem=v_send.at[group, phase],
            recv_sem=v_recv.at[group, phase],
            device_id=peer[axes[phase]],
            device_id_type=MESH,
        )

    def vector_step(group, phase):
        vector_copy(group, phase).wait()
        sums, came = (vec, vec_came) if group == 0 else (late, late_came)
        sums[phase + 1] = sums[phase] + came[phase]
        if phase < 4:
            vector_copy(group, phase + 1).start()

    def do_late_sums():
        late[0] = jnp.zeros((8, 768), F32)
        mask_sum = jnp.concatenate([mask_sums[n] for n in range(3)], axis=1)
        all_sums = (
            lax.fori_loop(0, 3, own_part, mask_sum),
            fold(q_own[...].astype(F32)),
            lax.fori_loop(0, 12, value_sum, nothing),
        )
        for i, value in enumerate(all_sums):
            late[0, i : i + 1] = jnp.sum(value, 0, keepdims=True)
        vector_copy(1, 0).start()

    mine = (y, spot[ZHI], spot[ZLO], spot[X])

    def swap_copy(u):
        return pltpu.make_async_remote_copy(
            src_ref=units[u].own.at[mine],
            dst_ref=in5.at[u],
            send_sem=sends.at[u, 5],
            recv_sem=recvs.at[u, 5],
            device_id=peer[CORE],
            device_id_type=MESH,
        )

    def close(u):
        unit = units[u]
        unit.copy(4).wait()
        result = unit.own[mine].astype(F32) + unit.inbox[4][...].astype(F32)
        if INNER0 <= u < OUTPUT:
            i = u - INNER0
            out_inner[pl.ds(48 * (i % 2), 48), pl.ds(384 * (i // 2), 384)] = result
            return
        unit.own[mine] = result.astype(BF16)
        swap_copy(u).start()
        put_half(u, core, result)

    def put_half(u, side, value):
        value = jnp.where(core == 0, value[:, :192], pltpu.roll(value, 192, 1)[:, :192])
        if u < INNER0:
            out_outer[pl.ds(pl.multiple_of(side * 192 + u * 48, 48), 48)] = value
        else:
            target = (out_output, out_query, out_key, out_value)[u - OUTPUT]
            target[pl.ds(pl.multiple_of(side * 48, 48), 48)] = value

    def open_half(u):
        swap_copy(u).wait()
        put_half(u, 1 - core, in5[u].astype(F32))

    stages = {
        INNER: do_inner_grads,
        D_FIRST: do_d_first,
        FNB: do_first_norm_back,
        V1: lambda: vector_copy(0, 0).start(),
        DWO: do_output_grads,
        REFILL: refill_probs,
        DMIXED: lambda: loop(3, d_mixed_part),
        DWQ: do_query_grads,
        DWK: do_key_grads,
        DWV: do_value_grads,
        VEC: do_late_sums,
    }
    for r in range(3):
        stages[AB00 + 2 * r] = lambda r=r: do_attend_back(r, 0, 3)
        stages[AB01 + 2 * r] = lambda r=r: do_attend_back(r, 3, 6)
        stages[D_HIDDEN0 + r] = lambda r=r: span_loop(4 * r, 4 * r + 4, d_hidden_units)
        stages[DIN0 + r] = lambda r=r: do_d_in(r)
    count = {}
    for name in PLAN:
        if name in stages:
            stages[name]()
            continue
        turn = count[name] = count.get(name, -1) + 1
        if name <= VALUE:
            if turn < 4:
                units[name].step()
                if turn == 0 and STARTS.index(name) < SLOTS:
                    free_slot()
            elif turn == 4:
                close(name)
            else:
                open_half(name)
        elif name in (W1, W2):
            vector_step(name - W1, turn)
        elif name < DY0:
            d_in_pass(name - DC0)
        else:
            d_in_close(name - DY0)
    out_vectors[...] = vec[5]
    out_vectors[0:3] = late[5, 0:3]
    for copy in grad_copies:
        copy.wait()


def hand_out(*refs):
    sources, vectors, targets, rows = refs[:8], refs[8], refs[9:17], refs[17:27]
    for source, target in zip(sources[:7], targets[:7]):
        target[...] = source[...]
    targets[7][...] = sources[7][...].T
    for i, place in enumerate((0, 1, 2, 3, 4, 5, None, 10, 11, 12)):
        if place is not None:
            rows[i][...] = vectors[place]
    for j in range(4):
        rows[6][pl.ds(768 * j, 768)] = vectors[6 + j]


def fused_layer(
    hidden_in,
    cotangent,
    span_mask,
    lengths,
    repeats,
    mask_embedding,
    query_weight,
    query_bias,
    key_weight,
    value_weight,
    value_bias,
    output_weight,
    output_bias,
    mixing_gain,
    mixing_shift,
    inner_weight,
    inner_bias,
    outer_weight,
    outer_bias,
    final_gain,
    final_shift,
):
    vmem = pl.BlockSpec(memory_space=pltpu.VMEM)
    anywhere = pl.BlockSpec(memory_space=pl.ANY)
    scalars = pl.BlockSpec(memory_space=pltpu.SMEM)
    bf = lambda *shape: pltpu.VMEM(shape, BF16)
    fl = lambda *shape: pltpu.VMEM(shape, F32)
    dma = lambda *shape: pltpu.SemaphoreType.DMA(shape)
    shape = lambda dims, dtype: jax.ShapeDtypeStruct(dims, dtype)
    result = pl.pallas_call(
        layer_body,
        out_shape=[
            shape((384, 768), BF16),
            shape((384, 768), BF16),
            shape((9216, 256), BF16),
            shape((96, 192), F32),
            shape((96, 192), F32),
            shape((96, 192), F32),
            shape((96, 192), F32),
            shape((96, 768), F32),
            shape((384, 192), F32),
            shape((16, 768), F32),
        ],
        in_specs=[anywhere] * 8 + [vmem] + [anywhere] * 10 + [scalars, scalars],
        out_specs=[anywhere] * 3 + [vmem] * 7,
        scratch_shapes=[
            bf(3072, 768),
            bf(3072, 768),
            bf(768, 768),
            bf(768, 768),
            bf(768, 768),
            bf(768, 768),
            bf(13 * 768),
            fl(16, 768),
            bf(3, 512, 768),
            bf(3, 512, 768),
            bf(3, 512, 768),
            bf(384, 768),
            bf(384, 768),
            bf(9216, 256),
            bf(384, 768),
            fl(384, 768),
            fl(384, 1),
            fl(384, 768),
            fl(384, 768),
            bf(384, 768),
            bf(384, 768),
            pltpu.VMEM((4, 8, 128), jnp.int32),
            fl(512, 8),
            fl(12, 8, 256),
            fl(3, 8, 256),
            bf(12, 2, 2, 2, 2, 2, 48, 384),
            bf(SLOTS, 2, 2, 2, 2, 48, 384),
            bf(12, 2, 2, 2, 48, 384),
            bf(12, 2, 2, 48, 384),
            bf(12, 2, 48, 384),
            bf(12, 48, 384),
            bf(12, 48, 384),
            bf(3, 256, 768),
            bf(3, 128, 768),
            fl(6, 16, 768),
            fl(5, 16, 768),
            fl(6, 8, 768),
            fl(5, 8, 768),
            dma(12, 6),
            dma(12, 6),
            dma(5, 3),
            dma(5, 3),
            dma(3),
            dma(3),
            dma(2, 5),
            dma(2, 5),
            dma(31),
            pltpu.SemaphoreType.REGULAR,
        ],
        compiler_params=pltpu.CompilerParams(
            collective_id=1, has_side_effects=True, vmem_limit_bytes=63 * 2**20
        ),
        name="fused_layer",
    )(
        hidden_in,
        cotangent.reshape(384, 768),
        query_weight,
        key_weight,
        value_weight,
        output_weight,
        inner_weight,
        outer_weight,
        span_mask,
        mask_embedding,
        query_bias,
        value_bias,
        output_bias,
        mixing_gain,
        mixing_shift,
        inner_bias,
        outer_bias,
        final_gain,
        final_shift,
        lengths,
        repeats,
    )
    arrays, vectors = [result[0], result[1], *result[3:9]], result[9]
    wide_row = shape((768,), F32)
    handed = pl.pallas_call(
        hand_out,
        out_shape=[shape(v.shape, v.dtype) for v in arrays[:7]]
        + [shape((192, 384), F32)]
        + [wide_row] * 6
        + [shape((3072,), F32)]
        + [wide_row] * 3,
        in_specs=[vmem] * 9,
        out_specs=[vmem] * 18,
        name="hand_out",
    )(*arrays, vectors)
    layer_out, grad_input, g_query, g_key, g_value, g_output, g_inner, g_outer = handed[:8]
    g_mask, g_q_bias, g_v_bias, g_o_bias, g_gain, g_shift, g_inner_bias, *g_last = handed[8:]
    return (
        layer_out.reshape(3, 128, 768),
        grad_input.reshape(3, 128, 768),
        g_mask,
        g_query,
        g_q_bias,
        g_key,
        g_value,
        g_v_bias,
        g_output,
        g_o_bias,
        g_gain,
        g_shift,
        g_inner,
        g_inner_bias,
        g_outer.T,
        *g_last,
    )


def with_halo(x, sides, width):
    for axis, dim in sides:
        count, length = (lax.axis_size(axis), x.shape[dim])
        up = [(i, (i + 1) % count) for i in range(count - 1)]
        down = [(j, i) for i, j in up]
        last = lax.slice_in_dim(x, length - width, length, axis=dim)
        initial = lax.slice_in_dim(x, 0, width, axis=dim)
        before = lax.ppermute(last, axis, up)
        after = lax.ppermute(initial, axis, down)
        x = jnp.concatenate([before, x, after], axis=dim)
    return x


def layer_norm(inputs, gain, shift):
    center = inputs - jnp.mean(inputs, -1, keepdims=True)
    spread = jnp.mean(center * center, -1, keepdims=True)
    return center * lax.rsqrt(spread + 1e-05) * gain + shift


def linear(inputs, weight):
    return jnp.dot(inputs, weight, preferred_element_type=jnp.float32)


def linear_back(grads, weight):
    return lax.dot_general(
        grads, weight, (((1,), (1,)), ((), ())), preferred_element_type=jnp.float32
    )


def contract_rows(left, right):
    return lax.dot_general(
        left, right, (((0,), (0,)), ((), ())), preferred_element_type=jnp.float32
    )


def gelu_exact(inputs):
    return jax.nn.gelu(inputs, approximate=False)


def plain_layer(
    hidden_in,
    cotangent,
    span_mask,
    lengths,
    repeats,
    mask_embedding,
    query_weight,
    query_bias,
    key_weight,
    value_weight,
    value_bias,
    output_weight,
    output_bias,
    mixing_gain,
    mixing_shift,
    inner_weight,
    inner_bias,
    outer_weight,
    outer_bias,
    final_gain,
    final_shift,
):
    rows, stretch, width = hidden_in.shape
    whole = stretch * lax.axis_size("seq")
    scale = HEAD_DIM ** (-0.5)
    offset = lax.axis_index("seq") * stretch
    rim = with_halo(span_mask, (("seq", 1),), WIDEN)
    window = rim[:, 0:stretch]
    for shifted in range(1, 2 * WIDEN + 1):
        window = window + rim[:, shifted : shifted + stretch]
    widened = window > 0
    positions = offset + jnp.arange(stretch, dtype=jnp.int32)
    live = positions[None, :] < lengths[:, None]
    key_live = jnp.arange(whole, dtype=jnp.int32)[None, :] < lengths[:, None]
    masked_in = jnp.where(widened[..., None], mask_embedding[None, None, :], hidden_in)
    flat_in = masked_in.reshape(rows * stretch, width)
    queries = (linear(flat_in, query_weight) + query_bias.astype(jnp.float32)).astype(jnp.bfloat16)
    key_rows = linear(flat_in, key_weight).astype(jnp.bfloat16).reshape(rows, stretch, width)
    value_rows = (linear(flat_in, value_weight) + value_bias.astype(jnp.float32)).astype(
        jnp.bfloat16
    )
    value_rows = value_rows.reshape(rows, stretch, width)
    key_all, value_all = (
        lax.all_gather(key_rows, "seq", axis=1, tiled=True),
        lax.all_gather(value_rows, "seq", axis=1, tiled=True),
    )
    query_heads = queries.reshape(rows, stretch, HEADS, HEAD_DIM)

    def scores_of(key_full):
        key_heads = key_full.reshape(rows, whole, HEADS, HEAD_DIM)
        raw = jnp.einsum(
            "rqhd,rkhd->rhqk", query_heads, key_heads, preferred_element_type=jnp.float32
        )
        return jnp.where(key_live[:, None, None, :], raw * scale, -1e30)

    logits = scores_of(key_all)
    highest = jnp.max(logits, -1, keepdims=True)
    expd = jnp.exp(logits - highest)
    totals = jnp.sum(expd, -1, keepdims=True)
    log_total = highest + jnp.log(totals)
    probs_low = (expd / totals).astype(jnp.bfloat16)
    value_heads = value_all.reshape(rows, whole, HEADS, HEAD_DIM)
    mixed = jnp.einsum(
        "rhqk,rkhd->rqhd", probs_low, value_heads, preferred_element_type=jnp.float32
    )
    mixed = mixed.reshape(rows * stretch, width).astype(jnp.bfloat16)
    attended = linear(mixed, output_weight) + output_bias.astype(jnp.float32)
    residual_one = flat_in.astype(jnp.float32) + attended
    first, norm_back_one = jax.vjp(
        layer_norm, residual_one, mixing_gain.astype(jnp.float32), mixing_shift.astype(jnp.float32)
    )
    first_low = first.astype(jnp.bfloat16)
    inner = linear(first_low, inner_weight) + inner_bias.astype(jnp.float32)
    activated, gelu_back = jax.vjp(gelu_exact, inner)
    activated_low = activated.astype(jnp.bfloat16)
    outer = linear(activated_low, outer_weight) + outer_bias.astype(jnp.float32)
    final, norm_back_two = jax.vjp(
        layer_norm, first + outer, final_gain.astype(jnp.float32), final_shift.astype(jnp.float32)
    )
    layer_out = final.astype(jnp.bfloat16).reshape(rows, stretch, width)
    weighting = repeats.astype(jnp.float32)[:, None] * live.astype(jnp.float32)
    d_final = (cotangent.astype(jnp.float32) * weighting[:, :, None]).reshape(rows * stretch, width)
    d_two, d_final_gain, d_final_shift = norm_back_two(d_final)
    d_outer = d_two.astype(jnp.bfloat16)
    g_outer_weight = contract_rows(activated_low, d_outer)
    g_outer_bias = jnp.sum(d_outer.astype(jnp.float32), 0)
    (d_inner,) = gelu_back(linear_back(d_outer, outer_weight))
    d_inner = d_inner.astype(jnp.bfloat16)
    g_inner_weight = contract_rows(first_low, d_inner)
    g_inner_bias = jnp.sum(d_inner.astype(jnp.float32), 0)
    d_first = linear_back(d_inner, inner_weight) + d_two
    d_one, d_mixing_gain, d_mixing_shift = norm_back_one(d_first)
    d_attended = d_one.astype(jnp.bfloat16)
    g_output_weight = contract_rows(mixed, d_attended)
    g_output_bias = jnp.sum(d_attended.astype(jnp.float32), 0)
    d_mixed = linear_back(d_attended, output_weight).astype(jnp.bfloat16)
    d_mixed_heads = d_mixed.reshape(rows, stretch, HEADS, HEAD_DIM)
    key_back, value_back = (
        lax.all_gather(key_rows, "seq", axis=1, tiled=True),
        lax.all_gather(value_rows, "seq", axis=1, tiled=True),
    )
    probs = jnp.exp(scores_of(key_back) - log_total)
    probs_again = probs.astype(jnp.bfloat16)
    key_heads = key_back.reshape(rows, whole, HEADS, HEAD_DIM)
    value_heads = value_back.reshape(rows, whole, HEADS, HEAD_DIM)
    d_probs = jnp.einsum(
        "rqhd,rkhd->rhqk", d_mixed_heads, value_heads, preferred_element_type=jnp.float32
    )
    centered = d_probs - jnp.sum(probs * d_probs, -1, keepdims=True)
    d_raw = (probs * centered * scale).astype(jnp.bfloat16)
    d_queries = jnp.einsum("rhqk,rkhd->rqhd", d_raw, key_heads, preferred_element_type=jnp.float32)
    d_queries = d_queries.reshape(rows * stretch, width).astype(jnp.bfloat16)
    d_key_part = jnp.einsum(
        "rhqk,rqhd->rkhd", d_raw, query_heads, preferred_element_type=jnp.float32
    )
    d_value_part = jnp.einsum(
        "rhqk,rqhd->rkhd", probs_again, d_mixed_heads, preferred_element_type=jnp.float32
    )
    d_key_sum, d_value_sum = (
        lax.psum_scatter(
            d_key_part.reshape(rows, whole, width), "seq", scatter_dimension=1, tiled=True
        ),
        lax.psum_scatter(
            d_value_part.reshape(rows, whole, width), "seq", scatter_dimension=1, tiled=True
        ),
    )
    d_keys = d_key_sum.astype(jnp.bfloat16).reshape(rows * stretch, width)
    d_values = d_value_sum.astype(jnp.bfloat16).reshape(rows * stretch, width)
    g_query_weight = contract_rows(flat_in, d_queries)
    g_key_weight = contract_rows(flat_in, d_keys)
    g_value_weight = contract_rows(flat_in, d_values)
    g_query_bias = jnp.sum(d_queries.astype(jnp.float32), 0)
    g_value_bias = jnp.sum(d_values.astype(jnp.float32), 0)
    d_input = (
        d_one
        + linear_back(d_queries, query_weight)
        + linear_back(d_keys, key_weight)
        + linear_back(d_values, value_weight)
    ).reshape(rows, stretch, width)
    grad_input = jnp.where(widened[..., None], 0.0, d_input).astype(jnp.bfloat16)
    g_mask = jnp.sum(jnp.where(widened[..., None], d_input, 0.0), (0, 1))
    matrices = (
        g_query_weight,
        g_key_weight,
        g_value_weight,
        g_output_weight,
        g_inner_weight,
        g_outer_weight,
    )
    partial_sums = (
        lax.psum_scatter(matrices[0], "batch", scatter_dimension=0, tiled=True),
        lax.psum_scatter(matrices[1], "batch", scatter_dimension=0, tiled=True),
        lax.psum_scatter(matrices[2], "batch", scatter_dimension=0, tiled=True),
        lax.psum_scatter(matrices[3], "batch", scatter_dimension=0, tiled=True),
        lax.psum_scatter(matrices[4], "batch", scatter_dimension=0, tiled=True),
        lax.psum_scatter(matrices[5], "batch", scatter_dimension=0, tiled=True),
    )
    summed = (
        lax.psum_scatter(partial_sums[0], "seq", scatter_dimension=1, tiled=True),
        lax.psum_scatter(partial_sums[1], "seq", scatter_dimension=1, tiled=True),
        lax.psum_scatter(partial_sums[2], "seq", scatter_dimension=1, tiled=True),
        lax.psum_scatter(partial_sums[3], "seq", scatter_dimension=1, tiled=True),
        lax.psum_scatter(partial_sums[4], "seq", scatter_dimension=1, tiled=True),
        lax.psum_scatter(partial_sums[5], "seq", scatter_dimension=1, tiled=True),
    )
    vectors = lax.psum(
        (
            g_mask,
            g_query_bias,
            g_value_bias,
            g_output_bias,
            d_mixing_gain,
            d_mixing_shift,
            g_inner_bias,
            g_outer_bias,
            d_final_gain,
            d_final_shift,
        ),
        ("batch", "seq"),
    )
    return (
        layer_out,
        grad_input,
        vectors[0],
        summed[0],
        vectors[1],
        summed[1],
        summed[2],
        vectors[2],
        summed[3],
        vectors[3],
        vectors[4],
        vectors[5],
        summed[4],
        vectors[6],
        summed[5],
        vectors[7],
        vectors[8],
        vectors[9],
    )


def solution(mesh):
    fused = mesh.shape["batch"] == 8 and mesh.shape["seq"] == 4
    return jax.shard_map(
        fused_layer if fused else plain_layer,
        mesh=mesh,
        in_specs=(
            P("batch", "seq", None),
            P("batch", "seq", None),
            P("batch", "seq"),
            P("batch"),
            P("batch"),
            P(),
            P(),
            P(),
            P(),
            P(),
            P(),
            P(),
            P(),
            P(),
            P(),
            P(),
            P(),
            P(),
            P(),
            P(),
            P(),
        ),
        out_specs=(
            P("batch", "seq", None),
            P("batch", "seq", None),
            P(),
            P("batch", "seq"),
            P(),
            P("batch", "seq"),
            P("batch", "seq"),
            P(),
            P("batch", "seq"),
            P(),
            P(),
            P(),
            P("batch", "seq"),
            P(),
            P("batch", "seq"),
            P(),
            P(),
            P(),
        ),
        check_vma=False,
    )
```

```python
import jax
import jax.numpy as jnp
from jax import lax
from jax.experimental import pallas as pl
from jax.experimental.pallas import tpu as pltpu
from jax.sharding import PartitionSpec as P

HEADS = 12
HEAD_DIM = 64
WIDEN = 5

MESH = pl.DeviceIdType.MESH
F32 = jnp.float32
BF16 = jnp.bfloat16
ROOT_HALF = 0.7071067811865476
DENSITY = 0.3989422804014327


def mm(a, b):
    return jnp.dot(a, b, preferred_element_type=F32)


def mm_t(a, b):
    return lax.dot_general(a, b, (((1,), (1,)), ((), ())), preferred_element_type=F32)


def mm_tl(a, b):
    return lax.dot_general(a, b, (((0,), (0,)), ((), ())), preferred_element_type=F32)


def fold(v):
    return jnp.sum(v.reshape(v.shape[0] // 8, 8, v.shape[1]), 0)


def loop(count, body, unroll=1):
    def step(i, carry):
        body(i)
        return carry

    lax.fori_loop(0, count, step, 0, unroll=unroll)


def span_loop(first, last, body, unroll=1):
    def step(i, carry):
        body(i)
        return carry

    lax.fori_loop(first, last, step, 0, unroll=unroll)


def aligned(i, size):
    return pl.ds(pl.multiple_of(i * size, size), size)


def places():
    b, s = lax.axis_index("batch"), lax.axis_index("seq")
    x, zlo, zhi = lax.rem(b, 2), lax.rem(b // 2, 2), b // 4
    core, y = lax.rem(s, 2), s // 2
    spot = {CORE: core, X: x, Y: y, ZLO: zlo, ZHI: zhi}
    peer = {
        CORE: (b, s + 1 - 2 * core),
        Y: (b, s + 2 - 4 * y),
        X: (b + 1 - 2 * x, s),
        ZLO: (b + 2 - 4 * zlo, s),
        ZHI: (b + 4 - 8 * zhi, s),
        FAR: (b, 3 - s),
    }
    return spot, peer


class Unit:
    def __init__(self, order, both, inbox, sends, recvs, spot, peer):
        self.order, self.both, self.inbox = order, both, inbox
        self.sends, self.recvs, self.spot, self.peer = sends, recvs, spot, peer
        self.own = both.at[spot[CORE]]
        self.phase = 0

    def where(self, phase, stays):
        done, axis = self.order[: phase - 1], self.order[phase - 1]
        place = []
        for name in (Y, ZHI, ZLO, X):
            side = self.spot[name]
            if name == axis:
                place.append(side if stays else 1 - side)
            else:
                place.append(side if name in done else slice(None))
        return tuple(place)

    def copy(self, phase):
        if phase == 0:
            axis, source = CORE, self.both.at[1 - self.spot[CORE]]
        else:
            axis, source = self.order[phase - 1], self.own.at[self.where(phase, False)]
        return pltpu.make_async_remote_copy(
            src_ref=source,
            dst_ref=self.inbox[phase],
            send_sem=self.sends.at[phase],
            recv_sem=self.recvs.at[phase],
            device_id=self.peer[axis],
            device_id_type=MESH,
        )

    def start(self):
        self.copy(0).start()

    def step(self):
        phase = self.phase
        self.copy(phase).wait()
        came = self.inbox[phase]
        target = self.own if phase == 0 else self.own.at[self.where(phase, True)]
        lead = 4 - phase

        def body(n):
            place = tuple(lax.rem(n // 2 ** (lead - 1 - i), 2) for i in range(lead))
            target[place] = target[place] + came[place]

        loop(2**lead, body, 4 if phase == 0 else 1)
        self.phase = phase + 1
        self.copy(self.phase).start()


CORE, X, Y, ZLO, ZHI, FAR = range(6)
OUTER0, OUTER1, OUTER2, OUTER3, INNER0, INNER1, INNER2, INNER3, OUTPUT, QUERY, KEY, VALUE = range(0, 12)
(
    D_HIDDEN0, D_HIDDEN1, D_HIDDEN2, INNER, D_FIRST, FNB, V1, DWO,
    REFILL, DMIXED, DWQ, DWK, DWV, VEC, AB00, AB01,
    AB10, AB11, AB20, AB21, DIN0, DIN1, DIN2,
) = range(12, 35)
W1, W2, DC0, DC1, DC2, DY0, DY1, DY2 = range(35, 43)
STARTS = (
    OUTER0, OUTER1, OUTER2, OUTER3, INNER0, INNER1,
    INNER2, INNER3, OUTPUT, KEY, QUERY, VALUE,
)
ORDERS = {
    OUTER0: (Y, ZLO, X, ZHI),
    OUTER1: (X, Y, ZLO, ZHI),
    OUTER2: (Y, X, ZLO, ZHI),
    OUTER3: (ZLO, ZHI, Y, X),
    INNER0: (X, ZLO, Y, ZHI),
    INNER1: (Y, ZLO, ZHI, X),
    INNER2: (X, ZLO, Y, ZHI),
    INNER3: (Y, X, ZLO, ZHI),
    OUTPUT: (X, Y, ZLO, ZHI),
    KEY: (X, ZLO, ZHI, Y),
    QUERY: (Y, X, ZLO, ZHI),
    VALUE: (X, ZLO, Y, ZHI),
}
PLAN = (
    D_HIDDEN0, D_HIDDEN1, OUTER0, D_HIDDEN2, OUTER1, OUTER2, INNER, OUTER3,
    D_FIRST, REFILL, OUTER0, INNER0, FNB, INNER1, OUTER1, INNER2,
    V1, DWO, INNER3, W1, DMIXED, OUTER2, OUTER3, AB00,
    OUTPUT, OUTER0, INNER0, AB01, INNER1, AB10, AB11, INNER2,
    OUTER1, W1, OUTER3, INNER0, AB20, OUTER2, AB21, INNER1,
    INNER3, W1, DWK, INNER2, OUTER3, DWQ, INNER0, OUTER1,
    OUTPUT, DWV, KEY, OUTER0, INNER2, QUERY, INNER1, OUTER2,
    DIN0, INNER3, INNER0, W1, OUTER3, OUTPUT, DIN1, VALUE,
    OUTER0, OUTER1, OUTER3, INNER2, DC0, DIN2, OUTER0, OUTER2,
    INNER1, INNER3, OUTER1, DC1, QUERY, KEY, VEC, OUTER2,
    W1, OUTPUT, DC2, W2, DY0, INNER3, VALUE, KEY,
    DY1, OUTPUT, QUERY, W2, OUTPUT, VALUE, DY2, W2,
    KEY, VALUE, QUERY, W2, KEY, KEY, VALUE, QUERY,
    VALUE, W2, QUERY,
)
SLOTS = 6
ROOMS = (0, 2, 1)


def layer_body(
    hidden,
    cotangent,
    query_weight,
    key_weight,
    value_weight,
    output_weight,
    inner_weight,
    outer_weight,
    span,
    mask_embedding,
    query_bias,
    value_bias,
    output_bias,
    mixing_gain,
    mixing_shift,
    inner_bias,
    outer_bias,
    final_gain,
    final_shift,
    lengths,
    repeats,
    layer_out,
    grad_input,
    probs_out,
    out_query,
    out_key,
    out_value,
    out_output,
    out_inner,
    out_outer,
    out_vectors,
    wi,
    wf,
    wq,
    wk,
    wv,
    wo,
    packed,
    params,
    x_all,
    k_all,
    v_all,
    q_own,
    mixed,
    region,
    first_low,
    norm_one,
    spread_one,
    total,
    d_res,
    d_outer,
    d_att,
    masks,
    wide,
    inner_sums,
    mask_sums,
    grads,
    in0,
    in1,
    in2,
    in3,
    in4,
    in5,
    d_in0,
    d_in1,
    vec,
    vec_came,
    late,
    late_came,
    sends,
    recvs,
    x_send,
    x_recv,
    m_send,
    m_recv,
    v_send,
    v_recv,
    local,
    credit,
):
    spot, peer = places()
    core, y = spot[CORE], spot[Y]
    me = 2 * y + core
    sibling = 2 * y + 1 - core
    across = 2 * (1 - y) + core

    names = (CORE, X, Y, ZLO, ZHI, FAR)
    barrier = pltpu.get_barrier_semaphore()
    for name in names:
        pl.semaphore_signal(barrier, inc=1, device_id=peer[name], device_id_type=MESH)

    weight_loads = {}

    def load(name, number, source, target):
        copy = pltpu.make_async_copy(source, target, local.at[number])
        copy.start()
        weight_loads[name] = copy

    load("hidden", 0, hidden, x_all.at[:, aligned(me, 128)])
    load("key", 1, key_weight, wk)
    load("value", 2, value_weight, wv)
    load("query", 3, query_weight, wq)

    pl.semaphore_wait(barrier, len(names))

    masks[me] = jnp.zeros((8, 128), jnp.int32)
    masks[me, 0:3] = span[...]
    mask_copies = []
    for i, name in enumerate((CORE, Y, FAR)):
        copy = pltpu.make_async_remote_copy(
            src_ref=masks.at[me],
            dst_ref=masks.at[me],
            send_sem=m_send.at[i],
            recv_sem=m_recv.at[i],
            device_id=peer[name],
            device_id_type=MESH,
        )
        copy.start()
        mask_copies.append(copy)

    def x_copy(kind, r):
        source = hidden.at[r] if kind < 2 else x_all.at[r, aligned(across, 128)]
        slot = me if kind < 2 else across
        return pltpu.make_async_remote_copy(
            src_ref=source,
            dst_ref=x_all.at[r, aligned(slot, 128)],
            send_sem=x_send.at[kind, r],
            recv_sem=x_recv.at[kind, r],
            device_id=peer[Y if kind == 0 else CORE],
            device_id_type=MESH,
        )

    for r in range(3):
        x_copy(0, r).start()
        x_copy(1, r).start()

    vectors = (
        (mask_embedding, 0),
        (query_bias, 1),
        (value_bias, 2),
        (output_bias, 3),
        (mixing_gain, 4),
        (mixing_shift, 5),
        (inner_bias, 6),
        (outer_bias, 10),
        (final_gain, 11),
        (final_shift, 12),
    )
    vector_loads = []
    for i, (vector, place) in enumerate(vectors):
        target = packed.at[pl.ds(768 * place, vector.shape[0])]
        copy = pltpu.make_async_copy(vector, target, local.at[21 + i])
        copy.start()
        vector_loads.append(copy)
    for copy in vector_loads:
        copy.wait()
    for i in range(13):
        params[i : i + 1] = packed[pl.ds(768 * i, 768)].astype(F32).reshape(1, 768)

    for copy in mask_copies:
        copy.wait()
    span_all = jnp.concatenate([masks[s].astype(F32) for s in range(4)], axis=1)
    lane = lax.broadcasted_iota(jnp.int32, span_all.shape, 1)
    window = span_all
    for d in range(1, WIDEN + 1):
        window = jnp.maximum(window, jnp.where(lane >= d, pltpu.roll(span_all, d, 1), 0.0))
        window = jnp.maximum(
            window, jnp.where(lane < 512 - d, pltpu.roll(span_all, 512 - d, 1), 0.0)
        )
    wide[...] = window.T

    half = lax.broadcasted_iota(jnp.int32, (128, 128), 1) < HEAD_DIM
    zero = jnp.zeros((128, 128), BF16)

    def stacked(pair):
        return jnp.concatenate([jnp.where(half, pair, zero), jnp.where(half, zero, pair)], 0)

    def unstacked(both):
        return jnp.where(half, both[:128], both[128:])

    mask_row = params[0:1]
    spills = []

    def put_mask(r, slot):
        rows = aligned(slot, 128)
        chosen = wide[rows, r : r + 1] > 0.5
        kept = x_all[r, rows].astype(F32)
        x_all[r, rows] = jnp.where(chosen, mask_row, kept).astype(BF16)

    def project(pieces, with_queries):
        inputs = jnp.concatenate([x_all[r, aligned(slot, 128)] for r, slot in pieces], 0)

        def part(n):
            cols = aligned(n, 256)
            keys = mm(inputs, wk[:, cols]).astype(BF16)
            values = (mm(inputs, wv[:, cols]) + params[2:3, cols]).astype(BF16)
            for i, (r, slot) in enumerate(pieces):
                k_all[r, aligned(slot, 128), cols] = keys[128 * i : 128 * i + 128]
                v_all[r, aligned(slot, 128), cols] = values[128 * i : 128 * i + 128]
            if with_queries:
                q_own[:, cols] = (mm(inputs, wq[:, cols]) + params[1:2, cols]).astype(BF16)

        loop(3, part)

    weight_loads["hidden"].wait()
    for r in range(3):
        put_mask(r, me)
    for name in ("key", "value", "query"):
        weight_loads[name].wait()
    load("output", 4, output_weight, wo)
    for j in range(4):
        load(j, 5 + j, inner_weight.at[:, pl.ds(768 * j, 768)], wi.at[pl.ds(768 * j, 768)])
    load("outer", 9, outer_weight, wf)
    load("cotangent", 10, cotangent, d_outer)
    project([(r, me) for r in range(3)], True)
    for r in range(3):
        x_copy(1, r).wait()
        put_mask(r, sibling)
    project([(r, sibling) for r in range(3)], False)
    x_copy(0, 0).wait_recv()
    x_copy(2, 0).start()
    for r in range(3):
        x_copy(2, r).wait()
        put_mask(r, across)
        put_mask(r, 3 - me)
        project([(r, across), (r, 3 - me)], False)
        key_live = lax.broadcasted_iota(jnp.int32, (1, 512), 1) < lengths[r]

        def attend(p):
            cols = aligned(p, 128)
            queries = stacked(q_own[pl.ds(128 * r, 128), cols] * BF16(HEAD_DIM**-0.5))
            logits = mm_t(queries, k_all[r, :, cols])
            logits = jnp.where(key_live, logits, -1e30)
            expd = jnp.exp(logits - jnp.max(logits, -1, keepdims=True))
            probs = (expd * (1.0 / jnp.sum(expd, -1, keepdims=True))).astype(BF16)
            base = ROOMS[r] * 6 + p
            region[aligned(2 * base, 256)] = probs[:, :256]
            region[aligned(2 * base + 1, 256)] = probs[:, 256:]
            out = mm(probs, v_all[r, :, cols])
            mixed[pl.ds(128 * r, 128), cols] = unstacked(out).astype(BF16)

        def attend_three(i):
            for p in range(3):
                attend(3 * i + p)
            if r < 2:

                @pl.when(i == 0)
                def _():
                    x_copy(0, r + 1).wait_recv()
                    x_copy(2, r + 1).start()

        loop(2, attend_three)
        rows = pl.ds(3072 * ROOMS[r], 3072)
        spill = pltpu.make_async_copy(region.at[rows], probs_out.at[rows], local.at[11 + r])
        spill.start()
        spills.append(spill)

    for r in range(3):
        x_copy(0, r).wait_send()
    weight_loads["output"].wait()

    def first_norm(i):
        rows = aligned(i, 128)
        attended = mm(mixed[rows], wo[...]) + params[3:4]
        value = x_all[i, aligned(me, 128)].astype(F32) + attended
        center = value - jnp.mean(value, -1, keepdims=True)
        scale = lax.rsqrt(jnp.mean(center * center, -1, keepdims=True) + 1e-5)
        norm = center * scale
        norm_one[rows] = norm
        spread_one[rows] = scale
        first_low[rows] = (norm * params[4:5] + params[5:6]).astype(BF16)

    loop(3, first_norm)
    spills[0].wait()
    spills[1].wait()
    for j in range(4):
        weight_loads[j].wait()

    def hidden_units(j):
        inner = mm(
            first_low[...], wi[pl.ds((j // 3) * 768, 768), aligned(lax.rem(j, 3), 256)]
        ) + params[pl.ds(6 + j // 3, 1), aligned(lax.rem(j, 3), 256)]
        below = 0.5 * (1.0 + lax.erf(inner * ROOT_HALF))
        slope = below + inner * (DENSITY * jnp.exp(-0.5 * inner * inner))
        region[aligned(j, 384)] = (inner * below).astype(BF16)
        region[aligned(23 - j, 384)] = slope.astype(BF16)

    span_loop(0, 8, hidden_units, 2)
    spills[2].wait()
    span_loop(8, 12, hidden_units, 2)
    weight_loads["outer"].wait()
    weight_loads["cotangent"].wait()

    def panels(which):
        return jnp.concatenate([region[pl.ds(384 * j, 384)] for j in which], axis=1)

    def project_out(n):
        cols = aligned(n, 256)
        total[:, cols] = mm(panels(range(12)), wf[:, cols])

    loop(3, project_out, 3)

    def last_norm(i, sums):
        rows = aligned(i, 64)
        first = norm_one[rows] * params[4:5] + params[5:6]
        value = first + (total[rows] + params[10:11])
        center = value - jnp.mean(value, -1, keepdims=True)
        scale = lax.rsqrt(jnp.mean(center * center, -1, keepdims=True) + 1e-5)
        norm = center * scale
        d_att[rows] = (norm * params[11:12] + params[12:13]).astype(BF16)
        r = i // 2
        position = lax.broadcasted_iota(jnp.int32, (64, 1), 0) + lax.rem(i, 2) * 64 + me * 128
        weight = jnp.where(position < lengths[r], repeats[r].astype(F32), 0.0)
        d_final = d_outer[rows].astype(F32) * weight
        d_norm = d_final * params[11:12]
        d_two = scale * (
            d_norm
            - jnp.mean(d_norm, -1, keepdims=True)
            - norm * jnp.mean(d_norm * norm, -1, keepdims=True)
        )
        d_res[rows] = d_two
        low = d_two.astype(BF16)
        d_outer[rows] = low
        return (
            sums[0] + fold(d_final * norm),
            sums[1] + fold(d_final),
            sums[2] + fold(low.astype(F32)),
        )

    nothing = jnp.zeros((8, 768), F32)

    def put_sum(row, value):
        vec[0, row : row + 1] = jnp.sum(value, 0, keepdims=True)

    vec[0] = jnp.zeros((16, 768), F32)
    sums = lax.fori_loop(0, 6, last_norm, (nothing, nothing, nothing))
    put_sum(11, sums[0])
    put_sum(12, sums[1])
    put_sum(10, sums[2])
    out_copy = pltpu.make_async_copy(
        d_att, layer_out, local.at[14]
    )
    out_copy.start()

    units = [None] * 12
    for turn, u in enumerate(STARTS):
        inbox = [in0.at[turn % SLOTS], in1.at[u], in2.at[u], in3.at[u], in4.at[u]]
        units[u] = Unit(ORDERS[u], grads.at[u], inbox, sends.at[u], recvs.at[u], spot, peer)

    def start_unit(name):
        if STARTS.index(name) >= SLOTS:
            claim_slot()
        units[name].start()

    def free_slot():
        pl.semaphore_signal(credit, inc=1, device_id=peer[CORE], device_id_type=MESH)

    def claim_slot():
        pl.semaphore_wait(credit, 1)

    def outer_grads(z):
        for x in range(2):
            cols = [region[pl.ds(pl.multiple_of((3 * z + j) * 384, 384), 384)] for j in range(3)]
            part = jnp.concatenate(cols, axis=1)[:, 384 * x : 384 * x + 384]
            grad = mm_tl(part, d_outer[...]).astype(BF16)
            for h in range(2):
                for i in range(4):
                    for side in range(2):
                        rows = (h * 4 + i) * 48
                        grads[OUTER0 + i, h, side, z // 2, lax.rem(z, 2), x] = grad[
                            rows : rows + 48, side * 384 : side * 384 + 384
                        ]

    loop(4, outer_grads)
    for i in range(4):
        start_unit(OUTER0 + i)

    def d_hidden_units(j):
        d_act = mm_t(d_outer[...], wf[aligned(j, 256)])
        place = aligned(23 - j, 384)
        low = (d_act * region[place].astype(F32)).astype(BF16)
        region[place] = low
        inner_sums[j] = fold(low.astype(F32))

    def inner_grads(s):
        cols = [region[pl.ds(pl.multiple_of((23 - 3 * s - j) * 384, 384), 384)] for j in range(3)]
        grad = mm_tl(first_low[...], jnp.concatenate(cols, axis=1)).astype(BF16)
        for b in range(8):
            for i in range(4):
                rows, side = 96 * b + 48 * (i % 2), 384 * (i // 2)
                grads[
                    INNER0 + i, lax.rem(s, 2), s // 2, b // 4, (b // 2) % 2, b % 2
                ] = grad[rows : rows + 48, side : side + 384]

    def do_inner_grads():
        loop(4, inner_grads)
        for i in range(4):
            start_unit(INNER0 + i)

    def d_first_part(n):
        cols = aligned(n, 256)
        acc = None
        for s in range(4):
            d_inner = panels(range(23 - 3 * s, 20 - 3 * s, -1))
            term = mm_t(d_inner, wi[pl.ds(pl.multiple_of(s * 768 + n * 256, 256), 256)])
            acc = term if acc is None else acc + term
        total[:, cols] = acc

    refills = []

    def do_d_first():
        loop(3, d_first_part)
        for j in range(12):
            vec[0, 6 + j // 3 : 7 + j // 3, (j % 3) * 256 : (j % 3) * 256 + 256] = jnp.sum(
                inner_sums[j], 0, keepdims=True
            )

    def refill_probs():
        for r in range(3):
            rows = pl.ds(3072 * ROOMS[r], 3072)
            refill = pltpu.make_async_copy(probs_out.at[rows], region.at[rows], local.at[15 + r])
            refill.start()
            refills.append(refill)

    def first_norm_back(i, sums):
        rows = aligned(i, 64)
        d_first = total[rows] + d_res[rows]
        norm = norm_one[rows]
        d_norm = d_first * params[4:5]
        d_one = spread_one[rows] * (
            d_norm
            - jnp.mean(d_norm, -1, keepdims=True)
            - norm * jnp.mean(d_norm * norm, -1, keepdims=True)
        )
        d_res[rows] = d_one
        low = d_one.astype(BF16)
        d_att[rows] = low
        return (
            sums[0] + fold(d_first * norm),
            sums[1] + fold(d_first),
            sums[2] + fold(low.astype(F32)),
        )

    def do_first_norm_back():
        out_copy.wait()
        sums = lax.fori_loop(0, 6, first_norm_back, (nothing, nothing, nothing))
        put_sum(4, sums[0])
        put_sum(5, sums[1])
        put_sum(3, sums[2])

    def square_grads(u, left, right):
        for m in range(2):
            grad = mm_tl(left(m), right).astype(BF16)
            for b in range(4):
                for h in range(2):
                    for side in range(2):
                        rows = b * 96 + h * 48
                        grads[u, h, side, m, b // 2, b % 2] = grad[
                            rows : rows + 48, side * 384 : side * 384 + 384
                        ]
        start_unit(u)

    def do_output_grads():
        square_grads(OUTPUT, lambda m: mixed[:, 384 * m : 384 * m + 384], d_att[...])

    def d_mixed_part(i):
        rows = aligned(i, 128)
        mixed[rows] = mm_t(d_att[rows], wo[...]).astype(BF16)

    def do_attend_back(r, first, last):
        if first == 0:
            refills[r].wait()

        def attend_back(p):
            cols = aligned(p, 128)
            own_rows = pl.ds(128 * r, 128)
            base = ROOMS[r] * 6 + p
            queries = stacked(q_own[own_rows, cols] * BF16(HEAD_DIM**-0.5))
            d_mix = stacked(mixed[own_rows, cols])
            low_probs = jnp.concatenate(
                [region[aligned(2 * base, 256)], region[aligned(2 * base + 1, 256)]], axis=1
            )
            d_probs = mm_t(d_mix, v_all[r, :, cols])
            probs = low_probs.astype(F32)
            weighted = probs * d_probs
            d_raw = (weighted - probs * jnp.sum(weighted, -1, keepdims=True)).astype(BF16)
            d_query = mm(d_raw, k_all[r, :, cols]) * HEAD_DIM**-0.5
            q_own[own_rows, cols] = unstacked(d_query).astype(BF16)
            wi[pl.ds(512 * r, 512), cols] = mm_tl(d_raw, queries).astype(BF16)
            wi[pl.ds(1536 + 512 * r, 512), cols] = mm_tl(low_probs, d_mix).astype(BF16)

        span_loop(first, last, attend_back)

    def own_inputs(m):
        return jnp.concatenate(
            [x_all[r, aligned(me, 128), pl.ds(384 * m, 384)] for r in range(3)], 0
        )

    def all_inputs(m):
        return jnp.concatenate([x_all[r, :, pl.ds(384 * m, 384)] for r in range(3)], 0)

    def do_query_grads():
        square_grads(QUERY, own_inputs, q_own[...])

    def do_key_grads():
        square_grads(KEY, all_inputs, wi[pl.ds(0, 1536)])

    def do_value_grads():
        square_grads(VALUE, all_inputs, wi[pl.ds(1536, 1536)])

    def value_sum(i, acc):
        return acc + fold(wi[pl.ds(pl.multiple_of(1536 + i * 128, 128), 128)].astype(F32))

    mask_sums[...] = jnp.zeros((3, 8, 256), F32)

    def d_in_copy(kind, r):
        if kind == 0:
            source = wf.at[aligned(2 * r + 1 - core, 256)]
            target, name = d_in0.at[r], CORE
        else:
            source = wf.at[aligned(4 * r + 2 * core + 1 - y, 128)]
            target, name = d_in1.at[r], Y
        return pltpu.make_async_remote_copy(
            src_ref=source,
            dst_ref=target,
            send_sem=x_send.at[3 + kind, r],
            recv_sem=x_recv.at[3 + kind, r],
            device_id=peer[name],
            device_id_type=MESH,
        )

    def do_d_in(r):
        def d_in_part(n):
            cols = aligned(n, 256)
            part = mm_t(wi[pl.ds(512 * r, 512)], wk[cols]) + mm_t(
                wi[pl.ds(1536 + 512 * r, 512)], wv[cols]
            )
            for s in range(4):
                block = 4 * r + 2 * (s % 2) + s // 2
                wf[pl.ds(128 * block, 128), cols] = part[128 * s : 128 * s + 128].astype(BF16)
            mask_sums[n] = mask_sums[n] + fold(part * wide[:, r : r + 1])

        loop(3, d_in_part)
        d_in_copy(0, r).start()

    def d_in_pass(r):
        d_in_copy(0, r).wait()
        rows = aligned(4 * r + 2 * core + 1 - y, 128)
        wf[rows] = wf[rows] + d_in0[r, aligned(1 - y, 128)]
        d_in_copy(1, r).start()

    def own_part(i, acc):
        rows = aligned(i, 128)
        part = d_res[rows] + mm_t(q_own[rows], wq[...])
        d_res[rows] = part
        chosen = wide[aligned(me, 128)]
        chosen = jnp.where(i == 0, chosen[:, 0:1], jnp.where(i == 1, chosen[:, 1:2], chosen[:, 2:3]))
        return acc + fold(part * chosen)

    grad_copies = []

    def d_in_close(r):
        d_in_copy(1, r).wait()
        rows = pl.ds(128 * r, 128)
        value = (
            d_res[rows]
            + wf[aligned(4 * r + 2 * core + y, 128)].astype(F32)
            + d_in0[r, aligned(y, 128)].astype(F32)
            + d_in1[r].astype(F32)
        )
        chosen = wide[aligned(me, 128), r : r + 1] > 0.5
        d_att[rows] = jnp.where(chosen, 0.0, value).astype(BF16)
        copy = pltpu.make_async_copy(d_att.at[rows], grad_input.at[rows], local.at[18 + r])
        copy.start()
        grad_copies.append(copy)

    axes = (CORE, X, Y, ZLO, ZHI)

    def vector_copy(group, phase):
        sums, came = (vec, vec_came) if group == 0 else (late, late_came)
        return pltpu.make_async_remote_copy(
            src_ref=sums.at[phase],
            dst_ref=came.at[phase],
            send_sem=v_send.at[group, phase],
            recv_sem=v_recv.at[group, phase],
            device_id=peer[axes[phase]],
            device_id_type=MESH,
        )

    def vector_step(group, phase):
        vector_copy(group, phase).wait()
        sums, came = (vec, vec_came) if group == 0 else (late, late_came)
        sums[phase + 1] = sums[phase] + came[phase]
        if phase < 4:
            vector_copy(group, phase + 1).start()

    def do_late_sums():
        late[0] = jnp.zeros((8, 768), F32)
        mask_sum = jnp.concatenate([mask_sums[n] for n in range(3)], axis=1)
        all_sums = (
            lax.fori_loop(0, 3, own_part, mask_sum),
            fold(q_own[...].astype(F32)),
            lax.fori_loop(0, 12, value_sum, nothing),
        )
        for i, value in enumerate(all_sums):
            late[0, i : i + 1] = jnp.sum(value, 0, keepdims=True)
        vector_copy(1, 0).start()

    mine = (y, spot[ZHI], spot[ZLO], spot[X])

    def swap_copy(u):
        return pltpu.make_async_remote_copy(
            src_ref=units[u].own.at[mine],
            dst_ref=in5.at[u],
            send_sem=sends.at[u, 5],
            recv_sem=recvs.at[u, 5],
            device_id=peer[CORE],
            device_id_type=MESH,
        )

    def close(u):
        unit = units[u]
        unit.copy(4).wait()
        result = unit.own[mine].astype(F32) + unit.inbox[4][...].astype(F32)
        if INNER0 <= u < OUTPUT:
            i = u - INNER0
            out_inner[pl.ds(48 * (i % 2), 48), pl.ds(384 * (i // 2), 384)] = result
            return
        unit.own[mine] = result.astype(BF16)
        swap_copy(u).start()
        put_half(u, core, result)

    def put_half(u, side, value):
        value = jnp.where(core == 0, value[:, :192], pltpu.roll(value, 192, 1)[:, :192])
        if u < INNER0:
            out_outer[pl.ds(pl.multiple_of(side * 192 + u * 48, 48), 48)] = value
        else:
            target = (out_output, out_query, out_key, out_value)[u - OUTPUT]
            target[pl.ds(pl.multiple_of(side * 48, 48), 48)] = value

    def open_half(u):
        swap_copy(u).wait()
        put_half(u, 1 - core, in5[u].astype(F32))

    stages = {
        INNER: do_inner_grads,
        D_FIRST: do_d_first,
        FNB: do_first_norm_back,
        V1: lambda: vector_copy(0, 0).start(),
        DWO: do_output_grads,
        REFILL: refill_probs,
        DMIXED: lambda: loop(3, d_mixed_part),
        DWQ: do_query_grads,
        DWK: do_key_grads,
        DWV: do_value_grads,
        VEC: do_late_sums,
    }
    for r in range(3):
        stages[AB00 + 2 * r] = lambda r=r: do_attend_back(r, 0, 3)
        stages[AB01 + 2 * r] = lambda r=r: do_attend_back(r, 3, 6)
        stages[D_HIDDEN0 + r] = lambda r=r: span_loop(4 * r, 4 * r + 4, d_hidden_units)
        stages[DIN0 + r] = lambda r=r: do_d_in(r)
    count = {}
    for name in PLAN:
        if name in stages:
            stages[name]()
            continue
        turn = count[name] = count.get(name, -1) + 1
        if name <= VALUE:
            if turn < 4:
                units[name].step()
                if turn == 0 and STARTS.index(name) < SLOTS:
                    free_slot()
            elif turn == 4:
                close(name)
            else:
                open_half(name)
        elif name in (W1, W2):
            vector_step(name - W1, turn)
        elif name < DY0:
            d_in_pass(name - DC0)
        else:
            d_in_close(name - DY0)
    out_vectors[...] = vec[5]
    out_vectors[0:3] = late[5, 0:3]
    for copy in grad_copies:
        copy.wait()


def hand_out(*refs):
    sources, vectors, targets, rows = refs[:8], refs[8], refs[9:17], refs[17:27]
    for source, target in zip(sources[:7], targets[:7]):
        target[...] = source[...]
    targets[7][...] = sources[7][...].T
    for i, place in enumerate((0, 1, 2, 3, 4, 5, None, 10, 11, 12)):
        if place is not None:
            rows[i][...] = vectors[place]
    for j in range(4):
        rows[6][pl.ds(768 * j, 768)] = vectors[6 + j]


def fused_layer(
    hidden_in,
    cotangent,
    span_mask,
    lengths,
    repeats,
    mask_embedding,
    query_weight,
    query_bias,
    key_weight,
    value_weight,
    value_bias,
    output_weight,
    output_bias,
    mixing_gain,
    mixing_shift,
    inner_weight,
    inner_bias,
    outer_weight,
    outer_bias,
    final_gain,
    final_shift,
):
    vmem = pl.BlockSpec(memory_space=pltpu.VMEM)
    anywhere = pl.BlockSpec(memory_space=pl.ANY)
    scalars = pl.BlockSpec(memory_space=pltpu.SMEM)
    bf = lambda *shape: pltpu.VMEM(shape, BF16)
    fl = lambda *shape: pltpu.VMEM(shape, F32)
    dma = lambda *shape: pltpu.SemaphoreType.DMA(shape)
    shape = lambda dims, dtype: jax.ShapeDtypeStruct(dims, dtype)
    result = pl.pallas_call(
        layer_body,
        out_shape=[
            shape((384, 768), BF16),
            shape((384, 768), BF16),
            shape((9216, 256), BF16),
            shape((96, 192), F32),
            shape((96, 192), F32),
            shape((96, 192), F32),
            shape((96, 192), F32),
            shape((96, 768), F32),
            shape((384, 192), F32),
            shape((16, 768), F32),
        ],
        in_specs=[anywhere] * 8 + [vmem] + [anywhere] * 10 + [scalars, scalars],
        out_specs=[anywhere] * 3 + [vmem] * 7,
        scratch_shapes=[
            bf(3072, 768),
            bf(3072, 768),
            bf(768, 768),
            bf(768, 768),
            bf(768, 768),
            bf(768, 768),
            bf(13 * 768),
            fl(16, 768),
            bf(3, 512, 768),
            bf(3, 512, 768),
            bf(3, 512, 768),
            bf(384, 768),
            bf(384, 768),
            bf(9216, 256),
            bf(384, 768),
            fl(384, 768),
            fl(384, 1),
            fl(384, 768),
            fl(384, 768),
            bf(384, 768),
            bf(384, 768),
            pltpu.VMEM((4, 8, 128), jnp.int32),
            fl(512, 8),
            fl(12, 8, 256),
            fl(3, 8, 256),
            bf(12, 2, 2, 2, 2, 2, 48, 384),
            bf(SLOTS, 2, 2, 2, 2, 48, 384),
            bf(12, 2, 2, 2, 48, 384),
            bf(12, 2, 2, 48, 384),
            bf(12, 2, 48, 384),
            bf(12, 48, 384),
            bf(12, 48, 384),
            bf(3, 256, 768),
            bf(3, 128, 768),
            fl(6, 16, 768),
            fl(5, 16, 768),
            fl(6, 8, 768),
            fl(5, 8, 768),
            dma(12, 6),
            dma(12, 6),
            dma(5, 3),
            dma(5, 3),
            dma(3),
            dma(3),
            dma(2, 5),
            dma(2, 5),
            dma(31),
            pltpu.SemaphoreType.REGULAR,
        ],
        compiler_params=pltpu.CompilerParams(
            collective_id=1, has_side_effects=True, vmem_limit_bytes=63 * 2**20
        ),
        name="fused_layer",
    )(
        hidden_in,
        cotangent.reshape(384, 768),
        query_weight,
        key_weight,
        value_weight,
        output_weight,
        inner_weight,
        outer_weight,
        span_mask,
        mask_embedding,
        query_bias,
        value_bias,
        output_bias,
        mixing_gain,
        mixing_shift,
        inner_bias,
        outer_bias,
        final_gain,
        final_shift,
        lengths,
        repeats,
    )
    arrays, vectors = [result[0], result[1], *result[3:9]], result[9]
    wide_row = shape((768,), F32)
    handed = pl.pallas_call(
        hand_out,
        out_shape=[shape(v.shape, v.dtype) for v in arrays[:7]]
        + [shape((192, 384), F32)]
        + [wide_row] * 6
        + [shape((3072,), F32)]
        + [wide_row] * 3,
        in_specs=[vmem] * 9,
        out_specs=[vmem] * 18,
        name="hand_out",
    )(*arrays, vectors)
    layer_out, grad_input, g_query, g_key, g_value, g_output, g_inner, g_outer = handed[:8]
    g_mask, g_q_bias, g_v_bias, g_o_bias, g_gain, g_shift, g_inner_bias, *g_last = handed[8:]
    return (
        layer_out.reshape(3, 128, 768),
        grad_input.reshape(3, 128, 768),
        g_mask,
        g_query,
        g_q_bias,
        g_key,
        g_value,
        g_v_bias,
        g_output,
        g_o_bias,
        g_gain,
        g_shift,
        g_inner,
        g_inner_bias,
        g_outer.T,
        *g_last,
    )


def with_halo(x, sides, width):
    for axis, dim in sides:
        count, length = (lax.axis_size(axis), x.shape[dim])
        up = [(i, (i + 1) % count) for i in range(count - 1)]
        down = [(j, i) for i, j in up]
        last = lax.slice_in_dim(x, length - width, length, axis=dim)
        initial = lax.slice_in_dim(x, 0, width, axis=dim)
        before = lax.ppermute(last, axis, up)
        after = lax.ppermute(initial, axis, down)
        x = jnp.concatenate([before, x, after], axis=dim)
    return x


def layer_norm(inputs, gain, shift):
    center = inputs - jnp.mean(inputs, -1, keepdims=True)
    spread = jnp.mean(center * center, -1, keepdims=True)
    return center * lax.rsqrt(spread + 1e-05) * gain + shift


def linear(inputs, weight):
    return jnp.dot(inputs, weight, preferred_element_type=jnp.float32)


def linear_back(grads, weight):
    return lax.dot_general(
        grads, weight, (((1,), (1,)), ((), ())), preferred_element_type=jnp.float32
    )


def contract_rows(left, right):
    return lax.dot_general(
        left, right, (((0,), (0,)), ((), ())), preferred_element_type=jnp.float32
    )


def gelu_exact(inputs):
    return jax.nn.gelu(inputs, approximate=False)


def plain_layer(
    hidden_in,
    cotangent,
    span_mask,
    lengths,
    repeats,
    mask_embedding,
    query_weight,
    query_bias,
    key_weight,
    value_weight,
    value_bias,
    output_weight,
    output_bias,
    mixing_gain,
    mixing_shift,
    inner_weight,
    inner_bias,
    outer_weight,
    outer_bias,
    final_gain,
    final_shift,
):
    rows, stretch, width = hidden_in.shape
    whole = stretch * lax.axis_size("seq")
    scale = HEAD_DIM ** (-0.5)
    offset = lax.axis_index("seq") * stretch
    rim = with_halo(span_mask, (("seq", 1),), WIDEN)
    window = rim[:, 0:stretch]
    for shifted in range(1, 2 * WIDEN + 1):
        window = window + rim[:, shifted : shifted + stretch]
    widened = window > 0
    positions = offset + jnp.arange(stretch, dtype=jnp.int32)
    live = positions[None, :] < lengths[:, None]
    key_live = jnp.arange(whole, dtype=jnp.int32)[None, :] < lengths[:, None]
    masked_in = jnp.where(widened[..., None], mask_embedding[None, None, :], hidden_in)
    flat_in = masked_in.reshape(rows * stretch, width)
    queries = (linear(flat_in, query_weight) + query_bias.astype(jnp.float32)).astype(jnp.bfloat16)
    key_rows = linear(flat_in, key_weight).astype(jnp.bfloat16).reshape(rows, stretch, width)
    value_rows = (linear(flat_in, value_weight) + value_bias.astype(jnp.float32)).astype(
        jnp.bfloat16
    )
    value_rows = value_rows.reshape(rows, stretch, width)
    key_all, value_all = (
        lax.all_gather(key_rows, "seq", axis=1, tiled=True),
        lax.all_gather(value_rows, "seq", axis=1, tiled=True),
    )
    query_heads = queries.reshape(rows, stretch, HEADS, HEAD_DIM)

    def scores_of(key_full):
        key_heads = key_full.reshape(rows, whole, HEADS, HEAD_DIM)
        raw = jnp.einsum(
            "rqhd,rkhd->rhqk", query_heads, key_heads, preferred_element_type=jnp.float32
        )
        return jnp.where(key_live[:, None, None, :], raw * scale, -1e30)

    logits = scores_of(key_all)
    highest = jnp.max(logits, -1, keepdims=True)
    expd = jnp.exp(logits - highest)
    totals = jnp.sum(expd, -1, keepdims=True)
    log_total = highest + jnp.log(totals)
    probs_low = (expd / totals).astype(jnp.bfloat16)
    value_heads = value_all.reshape(rows, whole, HEADS, HEAD_DIM)
    mixed = jnp.einsum(
        "rhqk,rkhd->rqhd", probs_low, value_heads, preferred_element_type=jnp.float32
    )
    mixed = mixed.reshape(rows * stretch, width).astype(jnp.bfloat16)
    attended = linear(mixed, output_weight) + output_bias.astype(jnp.float32)
    residual_one = flat_in.astype(jnp.float32) + attended
    first, norm_back_one = jax.vjp(
        layer_norm, residual_one, mixing_gain.astype(jnp.float32), mixing_shift.astype(jnp.float32)
    )
    first_low = first.astype(jnp.bfloat16)
    inner = linear(first_low, inner_weight) + inner_bias.astype(jnp.float32)
    activated, gelu_back = jax.vjp(gelu_exact, inner)
    activated_low = activated.astype(jnp.bfloat16)
    outer = linear(activated_low, outer_weight) + outer_bias.astype(jnp.float32)
    final, norm_back_two = jax.vjp(
        layer_norm, first + outer, final_gain.astype(jnp.float32), final_shift.astype(jnp.float32)
    )
    layer_out = final.astype(jnp.bfloat16).reshape(rows, stretch, width)
    weighting = repeats.astype(jnp.float32)[:, None] * live.astype(jnp.float32)
    d_final = (cotangent.astype(jnp.float32) * weighting[:, :, None]).reshape(rows * stretch, width)
    d_two, d_final_gain, d_final_shift = norm_back_two(d_final)
    d_outer = d_two.astype(jnp.bfloat16)
    g_outer_weight = contract_rows(activated_low, d_outer)
    g_outer_bias = jnp.sum(d_outer.astype(jnp.float32), 0)
    (d_inner,) = gelu_back(linear_back(d_outer, outer_weight))
    d_inner = d_inner.astype(jnp.bfloat16)
    g_inner_weight = contract_rows(first_low, d_inner)
    g_inner_bias = jnp.sum(d_inner.astype(jnp.float32), 0)
    d_first = linear_back(d_inner, inner_weight) + d_two
    d_one, d_mixing_gain, d_mixing_shift = norm_back_one(d_first)
    d_attended = d_one.astype(jnp.bfloat16)
    g_output_weight = contract_rows(mixed, d_attended)
    g_output_bias = jnp.sum(d_attended.astype(jnp.float32), 0)
    d_mixed = linear_back(d_attended, output_weight).astype(jnp.bfloat16)
    d_mixed_heads = d_mixed.reshape(rows, stretch, HEADS, HEAD_DIM)
    key_back, value_back = (
        lax.all_gather(key_rows, "seq", axis=1, tiled=True),
        lax.all_gather(value_rows, "seq", axis=1, tiled=True),
    )
    probs = jnp.exp(scores_of(key_back) - log_total)
    probs_again = probs.astype(jnp.bfloat16)
    key_heads = key_back.reshape(rows, whole, HEADS, HEAD_DIM)
    value_heads = value_back.reshape(rows, whole, HEADS, HEAD_DIM)
    d_probs = jnp.einsum(
        "rqhd,rkhd->rhqk", d_mixed_heads, value_heads, preferred_element_type=jnp.float32
    )
    centered = d_probs - jnp.sum(probs * d_probs, -1, keepdims=True)
    d_raw = (probs * centered * scale).astype(jnp.bfloat16)
    d_queries = jnp.einsum("rhqk,rkhd->rqhd", d_raw, key_heads, preferred_element_type=jnp.float32)
    d_queries = d_queries.reshape(rows * stretch, width).astype(jnp.bfloat16)
    d_key_part = jnp.einsum(
        "rhqk,rqhd->rkhd", d_raw, query_heads, preferred_element_type=jnp.float32
    )
    d_value_part = jnp.einsum(
        "rhqk,rqhd->rkhd", probs_again, d_mixed_heads, preferred_element_type=jnp.float32
    )
    d_key_sum, d_value_sum = (
        lax.psum_scatter(
            d_key_part.reshape(rows, whole, width), "seq", scatter_dimension=1, tiled=True
        ),
        lax.psum_scatter(
            d_value_part.reshape(rows, whole, width), "seq", scatter_dimension=1, tiled=True
        ),
    )
    d_keys = d_key_sum.astype(jnp.bfloat16).reshape(rows * stretch, width)
    d_values = d_value_sum.astype(jnp.bfloat16).reshape(rows * stretch, width)
    g_query_weight = contract_rows(flat_in, d_queries)
    g_key_weight = contract_rows(flat_in, d_keys)
    g_value_weight = contract_rows(flat_in, d_values)
    g_query_bias = jnp.sum(d_queries.astype(jnp.float32), 0)
    g_value_bias = jnp.sum(d_values.astype(jnp.float32), 0)
    d_input = (
        d_one
        + linear_back(d_queries, query_weight)
        + linear_back(d_keys, key_weight)
        + linear_back(d_values, value_weight)
    ).reshape(rows, stretch, width)
    grad_input = jnp.where(widened[..., None], 0.0, d_input).astype(jnp.bfloat16)
    g_mask = jnp.sum(jnp.where(widened[..., None], d_input, 0.0), (0, 1))
    matrices = (
        g_query_weight,
        g_key_weight,
        g_value_weight,
        g_output_weight,
        g_inner_weight,
        g_outer_weight,
    )
    partial_sums = (
        lax.psum_scatter(matrices[0], "batch", scatter_dimension=0, tiled=True),
        lax.psum_scatter(matrices[1], "batch", scatter_dimension=0, tiled=True),
        lax.psum_scatter(matrices[2], "batch", scatter_dimension=0, tiled=True),
        lax.psum_scatter(matrices[3], "batch", scatter_dimension=0, tiled=True),
        lax.psum_scatter(matrices[4], "batch", scatter_dimension=0, tiled=True),
        lax.psum_scatter(matrices[5], "batch", scatter_dimension=0, tiled=True),
    )
    summed = (
        lax.psum_scatter(partial_sums[0], "seq", scatter_dimension=1, tiled=True),
        lax.psum_scatter(partial_sums[1], "seq", scatter_dimension=1, tiled=True),
        lax.psum_scatter(partial_sums[2], "seq", scatter_dimension=1, tiled=True),
        lax.psum_scatter(partial_sums[3], "seq", scatter_dimension=1, tiled=True),
        lax.psum_scatter(partial_sums[4], "seq", scatter_dimension=1, tiled=True),
        lax.psum_scatter(partial_sums[5], "seq", scatter_dimension=1, tiled=True),
    )
    vectors = lax.psum(
        (
            g_mask,
            g_query_bias,
            g_value_bias,
            g_output_bias,
            d_mixing_gain,
            d_mixing_shift,
            g_inner_bias,
            g_outer_bias,
            d_final_gain,
            d_final_shift,
        ),
        ("batch", "seq"),
    )
    return (
        layer_out,
        grad_input,
        vectors[0],
        summed[0],
        vectors[1],
        summed[1],
        summed[2],
        vectors[2],
        summed[3],
        vectors[3],
        vectors[4],
        vectors[5],
        summed[4],
        vectors[6],
        summed[5],
        vectors[7],
        vectors[8],
        vectors[9],
    )


def solution(mesh):
    fused = mesh.shape["batch"] == 8 and mesh.shape["seq"] == 4
    return jax.shard_map(
        fused_layer if fused else plain_layer,
        mesh=mesh,
        in_specs=(
            P("batch", "seq", None),
            P("batch", "seq", None),
            P("batch", "seq"),
            P("batch"),
            P("batch"),
            P(),
            P(),
            P(),
            P(),
            P(),
            P(),
            P(),
            P(),
            P(),
            P(),
            P(),
            P(),
            P(),
            P(),
            P(),
            P(),
        ),
        out_specs=(
            P("batch", "seq", None),
            P("batch", "seq", None),
            P(),
            P("batch", "seq"),
            P(),
            P("batch", "seq"),
            P("batch", "seq"),
            P(),
            P("batch", "seq"),
            P(),
            P(),
            P(),
            P("batch", "seq"),
            P(),
            P("batch", "seq"),
            P(),
            P(),
            P(),
        ),
        check_vma=False,
    )
```

```python
import jax
import jax.numpy as jnp
from jax import lax
from jax.experimental import pallas as pl
from jax.experimental.pallas import tpu as pltpu
from jax.sharding import PartitionSpec as P

HEADS = 12
HEAD_DIM = 64
WIDEN = 5

MESH = pl.DeviceIdType.MESH
F32 = jnp.float32
BF16 = jnp.bfloat16
ROOT_HALF = 0.7071067811865476
DENSITY = 0.3989422804014327


def mm(a, b):
    return jnp.dot(a, b, preferred_element_type=F32)


def mm_t(a, b):
    return lax.dot_general(a, b, (((1,), (1,)), ((), ())), preferred_element_type=F32)


def mm_tl(a, b):
    return lax.dot_general(a, b, (((0,), (0,)), ((), ())), preferred_element_type=F32)


def fold(v):
    return jnp.sum(v.reshape(v.shape[0] // 8, 8, v.shape[1]), 0)


def loop(count, body, unroll=1):
    def step(i, carry):
        body(i)
        return carry

    lax.fori_loop(0, count, step, 0, unroll=unroll)


def span_loop(first, last, body, unroll=1):
    def step(i, carry):
        body(i)
        return carry

    lax.fori_loop(first, last, step, 0, unroll=unroll)


def aligned(i, size):
    return pl.ds(pl.multiple_of(i * size, size), size)


def places():
    b, s = lax.axis_index("batch"), lax.axis_index("seq")
    x, zlo, zhi = lax.rem(b, 2), lax.rem(b // 2, 2), b // 4
    core, y = lax.rem(s, 2), s // 2
    spot = {CORE: core, X: x, Y: y, ZLO: zlo, ZHI: zhi}
    peer = {
        CORE: (b, s + 1 - 2 * core),
        Y: (b, s + 2 - 4 * y),
        X: (b + 1 - 2 * x, s),
        ZLO: (b + 2 - 4 * zlo, s),
        ZHI: (b + 4 - 8 * zhi, s),
        FAR: (b, 3 - s),
    }
    return spot, peer


class Unit:
    def __init__(self, order, both, inbox, sends, recvs, spot, peer):
        self.order, self.both, self.inbox = order, both, inbox
        self.sends, self.recvs, self.spot, self.peer = sends, recvs, spot, peer
        self.own = both.at[spot[CORE]]
        self.phase = 0

    def where(self, phase, stays):
        done, axis = self.order[: phase - 1], self.order[phase - 1]
        place = []
        for name in (Y, ZHI, ZLO, X):
            side = self.spot[name]
            if name == axis:
                place.append(side if stays else 1 - side)
            else:
                place.append(side if name in done else slice(None))
        return tuple(place)

    def copy(self, phase):
        if phase == 0:
            axis, source = CORE, self.both.at[1 - self.spot[CORE]]
        else:
            axis, source = self.order[phase - 1], self.own.at[self.where(phase, False)]
        return pltpu.make_async_remote_copy(
            src_ref=source,
            dst_ref=self.inbox[phase],
            send_sem=self.sends.at[phase],
            recv_sem=self.recvs.at[phase],
            device_id=self.peer[axis],
            device_id_type=MESH,
        )

    def start(self):
        self.copy(0).start()

    def step(self):
        phase = self.phase
        self.copy(phase).wait()
        came = self.inbox[phase]
        target = self.own if phase == 0 else self.own.at[self.where(phase, True)]
        lead = 4 - phase

        def body(n):
            place = tuple(lax.rem(n // 2 ** (lead - 1 - i), 2) for i in range(lead))
            target[place] = target[place] + came[place]

        loop(2**lead, body, min(4, 2**lead))
        self.phase = phase + 1
        self.copy(self.phase).start()


CORE, X, Y, ZLO, ZHI, FAR = range(6)
OUTER0, OUTER1, OUTER2, OUTER3, INNER0, INNER1, INNER2, INNER3, OUTPUT, QUERY, KEY, VALUE = range(0, 12)
(
    D_HIDDEN0, D_HIDDEN1, D_HIDDEN2, INNER, D_FIRST, FNB, V1, DWO,
    REFILL, DMIXED, DWQ, DWK, DWV, VEC, AB00, AB01,
    AB10, AB11, AB20, AB21, DIN0, DIN1, DIN2,
) = range(12, 35)
W1, W2, DC0, DC1, DC2, DY0, DY1, DY2 = range(35, 43)
STARTS = (
    OUTER0, OUTER1, OUTER2, OUTER3, INNER0, INNER1,
    INNER2, INNER3, OUTPUT, KEY, QUERY, VALUE,
)
ORDERS = {
    OUTER0: (Y, ZLO, X, ZHI),
    OUTER1: (X, Y, ZLO, ZHI),
    OUTER2: (Y, X, ZLO, ZHI),
    OUTER3: (ZLO, ZHI, Y, X),
    INNER0: (X, ZLO, Y, ZHI),
    INNER1: (Y, ZLO, ZHI, X),
    INNER2: (X, ZLO, Y, ZHI),
    INNER3: (Y, X, ZLO, ZHI),
    OUTPUT: (X, Y, ZLO, ZHI),
    KEY: (X, ZLO, ZHI, Y),
    QUERY: (Y, X, ZLO, ZHI),
    VALUE: (X, ZLO, Y, ZHI),
}
PLAN = (
    D_HIDDEN0, D_HIDDEN1, OUTER0, D_HIDDEN2, OUTER1, OUTER2, INNER, OUTER3,
    D_FIRST, REFILL, OUTER0, INNER0, FNB, INNER1, OUTER1, INNER2,
    V1, DWO, INNER3, W1, DMIXED, OUTER2, OUTER3, AB00,
    OUTPUT, OUTER0, INNER0, AB01, INNER1, AB10, AB11, INNER2,
    OUTER1, W1, OUTER3, INNER0, AB20, OUTER2, AB21, INNER1,
    INNER3, W1, DWK, INNER2, OUTER3, DWQ, INNER0, OUTER1,
    OUTPUT, DWV, KEY, OUTER0, INNER2, QUERY, INNER1, OUTER2,
    DIN0, INNER3, INNER0, W1, OUTER3, OUTPUT, DIN1, VALUE,
    OUTER0, OUTER1, OUTER3, INNER2, DC0, DIN2, OUTER0, OUTER2,
    INNER1, INNER3, OUTER1, DC1, QUERY, KEY, VEC, OUTER2,
    W1, OUTPUT, DC2, W2, DY0, INNER3, VALUE, KEY,
    DY1, OUTPUT, QUERY, W2, OUTPUT, VALUE, DY2, W2,
    KEY, VALUE, QUERY, W2, KEY, KEY, VALUE, QUERY,
    VALUE, W2, QUERY,
)
SLOTS = 6
ROOMS = (0, 2, 1)


def layer_body(
    hidden,
    cotangent,
    query_weight,
    key_weight,
    value_weight,
    output_weight,
    inner_weight,
    outer_weight,
    span,
    mask_embedding,
    query_bias,
    value_bias,
    output_bias,
    mixing_gain,
    mixing_shift,
    inner_bias,
    outer_bias,
    final_gain,
    final_shift,
    lengths,
    repeats,
    layer_out,
    grad_input,
    probs_out,
    out_query,
    out_key,
    out_value,
    out_output,
    out_inner,
    out_outer,
    out_vectors,
    wi,
    wf,
    wq,
    wk,
    wv,
    wo,
    packed,
    params,
    x_all,
    k_all,
    v_all,
    q_own,
    mixed,
    region,
    first_low,
    norm_one,
    spread_one,
    total,
    d_res,
    d_outer,
    d_att,
    masks,
    wide,
    inner_sums,
    mask_sums,
    grads,
    in0,
    in1,
    in2,
    in3,
    in4,
    in5,
    d_in0,
    d_in1,
    vec,
    vec_came,
    late,
    late_came,
    sends,
    recvs,
    x_send,
    x_recv,
    m_send,
    m_recv,
    v_send,
    v_recv,
    local,
    credit,
):
    spot, peer = places()
    core, y = spot[CORE], spot[Y]
    me = 2 * y + core
    sibling = 2 * y + 1 - core
    across = 2 * (1 - y) + core

    names = (CORE, X, Y, ZLO, ZHI, FAR)
    barrier = pltpu.get_barrier_semaphore()
    for name in names:
        pl.semaphore_signal(barrier, inc=1, device_id=peer[name], device_id_type=MESH)

    weight_loads = {}

    def load(name, number, source, target):
        copy = pltpu.make_async_copy(source, target, local.at[number])
        copy.start()
        weight_loads[name] = copy

    load("hidden", 0, hidden, x_all.at[:, aligned(me, 128)])
    load("key", 1, key_weight, wk)
    load("value", 2, value_weight, wv)
    load("query", 3, query_weight, wq)

    pl.semaphore_wait(barrier, len(names))

    masks[me] = jnp.zeros((8, 128), jnp.int32)
    masks[me, 0:3] = span[...]
    mask_copies = []
    for i, name in enumerate((CORE, Y, FAR)):
        copy = pltpu.make_async_remote_copy(
            src_ref=masks.at[me],
            dst_ref=masks.at[me],
            send_sem=m_send.at[i],
            recv_sem=m_recv.at[i],
            device_id=peer[name],
            device_id_type=MESH,
        )
        copy.start()
        mask_copies.append(copy)

    def x_copy(kind, r):
        source = hidden.at[r] if kind < 2 else x_all.at[r, aligned(across, 128)]
        slot = me if kind < 2 else across
        return pltpu.make_async_remote_copy(
            src_ref=source,
            dst_ref=x_all.at[r, aligned(slot, 128)],
            send_sem=x_send.at[kind, r],
            recv_sem=x_recv.at[kind, r],
            device_id=peer[Y if kind == 0 else CORE],
            device_id_type=MESH,
        )

    for r in range(3):
        x_copy(0, r).start()
        x_copy(1, r).start()

    vectors = (
        (mask_embedding, 0),
        (query_bias, 1),
        (value_bias, 2),
        (output_bias, 3),
        (mixing_gain, 4),
        (mixing_shift, 5),
        (inner_bias, 6),
        (outer_bias, 10),
        (final_gain, 11),
        (final_shift, 12),
    )
    vector_loads = []
    for i, (vector, place) in enumerate(vectors):
        target = packed.at[pl.ds(768 * place, vector.shape[0])]
        copy = pltpu.make_async_copy(vector, target, local.at[21 + i])
        copy.start()
        vector_loads.append(copy)
    for copy in vector_loads:
        copy.wait()
    for i in range(13):
        params[i : i + 1] = packed[pl.ds(768 * i, 768)].astype(F32).reshape(1, 768)

    for copy in mask_copies:
        copy.wait()
    span_all = jnp.concatenate([masks[s].astype(F32) for s in range(4)], axis=1)
    lane = lax.broadcasted_iota(jnp.int32, span_all.shape, 1)
    window = span_all
    for d in range(1, WIDEN + 1):
        window = jnp.maximum(window, jnp.where(lane >= d, pltpu.roll(span_all, d, 1), 0.0))
        window = jnp.maximum(
            window, jnp.where(lane < 512 - d, pltpu.roll(span_all, 512 - d, 1), 0.0)
        )
    wide[...] = window.T

    half = lax.broadcasted_iota(jnp.int32, (128, 128), 1) < HEAD_DIM
    zero = jnp.zeros((128, 128), BF16)

    def stacked(pair):
        return jnp.concatenate([jnp.where(half, pair, zero), jnp.where(half, zero, pair)], 0)

    def unstacked(both):
        return jnp.where(half, both[:128], both[128:])

    mask_row = params[0:1]
    spills = []

    def put_mask(r, slot):
        rows = aligned(slot, 128)
        chosen = wide[rows, r : r + 1] > 0.5
        kept = x_all[r, rows].astype(F32)
        x_all[r, rows] = jnp.where(chosen, mask_row, kept).astype(BF16)

    def project(pieces, with_queries):
        inputs = jnp.concatenate([x_all[r, aligned(slot, 128)] for r, slot in pieces], 0)

        def part(n):
            cols = aligned(n, 256)
            keys = mm(inputs, wk[:, cols]).astype(BF16)
            values = (mm(inputs, wv[:, cols]) + params[2:3, cols]).astype(BF16)
            for i, (r, slot) in enumerate(pieces):
                k_all[r, aligned(slot, 128), cols] = keys[128 * i : 128 * i + 128]
                v_all[r, aligned(slot, 128), cols] = values[128 * i : 128 * i + 128]
            if with_queries:
                q_own[:, cols] = (mm(inputs, wq[:, cols]) + params[1:2, cols]).astype(BF16)

        loop(3, part, 3)

    weight_loads["hidden"].wait()
    for r in range(3):
        put_mask(r, me)
    for name in ("key", "value", "query"):
        weight_loads[name].wait()
    load("output", 4, output_weight, wo)
    for j in range(4):
        load(j, 5 + j, inner_weight.at[:, pl.ds(768 * j, 768)], wi.at[pl.ds(768 * j, 768)])
    load("outer", 9, outer_weight, wf)
    load("cotangent", 10, cotangent, d_outer)
    project([(r, me) for r in range(3)], True)
    for r in range(3):
        x_copy(1, r).wait()
        put_mask(r, sibling)
    project([(r, sibling) for r in range(3)], False)
    x_copy(0, 0).wait_recv()
    x_copy(2, 0).start()
    for r in range(3):
        x_copy(2, r).wait()
        put_mask(r, across)
        put_mask(r, 3 - me)
        project([(r, across), (r, 3 - me)], False)
        key_live = lax.broadcasted_iota(jnp.int32, (1, 512), 1) < lengths[r]

        def attend(p):
            cols = aligned(p, 128)
            queries = stacked(q_own[pl.ds(128 * r, 128), cols] * BF16(HEAD_DIM**-0.5))
            logits = mm_t(queries, k_all[r, :, cols])
            logits = jnp.where(key_live, logits, -1e30)
            expd = jnp.exp(logits - jnp.max(logits, -1, keepdims=True))
            probs = (expd * (1.0 / jnp.sum(expd, -1, keepdims=True))).astype(BF16)
            base = ROOMS[r] * 6 + p
            region[aligned(2 * base, 256)] = probs[:, :256]
            region[aligned(2 * base + 1, 256)] = probs[:, 256:]
            out = mm(probs, v_all[r, :, cols])
            mixed[pl.ds(128 * r, 128), cols] = unstacked(out).astype(BF16)

        def attend_three(i):
            for p in range(3):
                attend(3 * i + p)
            if r < 2:

                @pl.when(i == 0)
                def _():
                    x_copy(0, r + 1).wait_recv()
                    x_copy(2, r + 1).start()

        loop(2, attend_three)
        rows = pl.ds(3072 * ROOMS[r], 3072)
        spill = pltpu.make_async_copy(region.at[rows], probs_out.at[rows], local.at[11 + r])
        spill.start()
        spills.append(spill)

    for r in range(3):
        x_copy(0, r).wait_send()
    weight_loads["output"].wait()

    def first_norm(i):
        rows = aligned(i, 128)
        attended = mm(mixed[rows], wo[...]) + params[3:4]
        value = x_all[i, aligned(me, 128)].astype(F32) + attended
        center = value - jnp.mean(value, -1, keepdims=True)
        scale = lax.rsqrt(jnp.mean(center * center, -1, keepdims=True) + 1e-5)
        norm = center * scale
        norm_one[rows] = norm
        spread_one[rows] = scale
        first_low[rows] = (norm * params[4:5] + params[5:6]).astype(BF16)

    loop(3, first_norm, 3)
    spills[0].wait()
    spills[1].wait()
    for j in range(4):
        weight_loads[j].wait()

    def hidden_units(j):
        inner = mm(
            first_low[...], wi[pl.ds((j // 3) * 768, 768), aligned(lax.rem(j, 3), 256)]
        ) + params[pl.ds(6 + j // 3, 1), aligned(lax.rem(j, 3), 256)]
        below = 0.5 * (1.0 + lax.erf(inner * ROOT_HALF))
        slope = below + inner * (DENSITY * jnp.exp(-0.5 * inner * inner))
        region[aligned(j, 384)] = (inner * below).astype(BF16)
        region[aligned(23 - j, 384)] = slope.astype(BF16)

    span_loop(0, 8, hidden_units, 4)
    spills[2].wait()
    span_loop(8, 12, hidden_units, 2)
    weight_loads["outer"].wait()
    weight_loads["cotangent"].wait()

    def panels(which):
        return jnp.concatenate([region[pl.ds(384 * j, 384)] for j in which], axis=1)

    def project_out(n):
        cols = aligned(n, 256)
        total[:, cols] = mm(panels(range(12)), wf[:, cols])

    loop(3, project_out, 3)

    def last_norm(i, sums):
        rows = aligned(i, 64)
        first = norm_one[rows] * params[4:5] + params[5:6]
        value = first + (total[rows] + params[10:11])
        center = value - jnp.mean(value, -1, keepdims=True)
        scale = lax.rsqrt(jnp.mean(center * center, -1, keepdims=True) + 1e-5)
        norm = center * scale
        d_att[rows] = (norm * params[11:12] + params[12:13]).astype(BF16)
        r = i // 2
        position = lax.broadcasted_iota(jnp.int32, (64, 1), 0) + lax.rem(i, 2) * 64 + me * 128
        weight = jnp.where(position < lengths[r], repeats[r].astype(F32), 0.0)
        d_final = d_outer[rows].astype(F32) * weight
        d_norm = d_final * params[11:12]
        d_two = scale * (
            d_norm
            - jnp.mean(d_norm, -1, keepdims=True)
            - norm * jnp.mean(d_norm * norm, -1, keepdims=True)
        )
        d_res[rows] = d_two
        low = d_two.astype(BF16)
        d_outer[rows] = low
        return (
            sums[0] + fold(d_final * norm),
            sums[1] + fold(d_final),
            sums[2] + fold(low.astype(F32)),
        )

    nothing = jnp.zeros((8, 768), F32)

    def put_sum(row, value):
        vec[0, row : row + 1] = jnp.sum(value, 0, keepdims=True)

    vec[0] = jnp.zeros((16, 768), F32)
    sums = lax.fori_loop(0, 6, last_norm, (nothing, nothing, nothing))
    put_sum(11, sums[0])
    put_sum(12, sums[1])
    put_sum(10, sums[2])
    out_copy = pltpu.make_async_copy(
        d_att, layer_out, local.at[14]
    )
    out_copy.start()

    units = [None] * 12
    for turn, u in enumerate(STARTS):
        inbox = [in0.at[turn % SLOTS], in1.at[u], in2.at[u], in3.at[u], in4.at[u]]
        units[u] = Unit(ORDERS[u], grads.at[u], inbox, sends.at[u], recvs.at[u], spot, peer)

    def start_unit(name):
        if STARTS.index(name) >= SLOTS:
            claim_slot()
        units[name].start()

    def free_slot():
        pl.semaphore_signal(credit, inc=1, device_id=peer[CORE], device_id_type=MESH)

    def claim_slot():
        pl.semaphore_wait(credit, 1)

    def outer_grads(z):
        for x in range(2):
            cols = [region[pl.ds(pl.multiple_of((3 * z + j) * 384, 384), 384)] for j in range(3)]
            part = jnp.concatenate(cols, axis=1)[:, 384 * x : 384 * x + 384]
            grad = mm_tl(part, d_outer[...]).astype(BF16)
            for h in range(2):
                for i in range(4):
                    for side in range(2):
                        rows = (h * 4 + i) * 48
                        grads[OUTER0 + i, h, side, z // 2, lax.rem(z, 2), x] = grad[
                            rows : rows + 48, side * 384 : side * 384 + 384
                        ]

    loop(4, outer_grads, 2)
    for i in range(4):
        start_unit(OUTER0 + i)

    def d_hidden_units(j):
        d_act = mm_t(d_outer[...], wf[aligned(j, 256)])
        place = aligned(23 - j, 384)
        low = (d_act * region[place].astype(F32)).astype(BF16)
        region[place] = low
        inner_sums[j] = fold(low.astype(F32))

    def inner_grads(s):
        cols = [region[pl.ds(pl.multiple_of((23 - 3 * s - j) * 384, 384), 384)] for j in range(3)]
        grad = mm_tl(first_low[...], jnp.concatenate(cols, axis=1)).astype(BF16)
        for b in range(8):
            for i in range(4):
                rows, side = 96 * b + 48 * (i % 2), 384 * (i // 2)
                grads[
                    INNER0 + i, lax.rem(s, 2), s // 2, b // 4, (b // 2) % 2, b % 2
                ] = grad[rows : rows + 48, side : side + 384]

    def do_inner_grads():
        loop(4, inner_grads, 2)
        for i in range(4):
            start_unit(INNER0 + i)

    def d_first_part(n):
        cols = aligned(n, 256)
        acc = None
        for s in range(4):
            d_inner = panels(range(23 - 3 * s, 20 - 3 * s, -1))
            term = mm_t(d_inner, wi[pl.ds(pl.multiple_of(s * 768 + n * 256, 256), 256)])
            acc = term if acc is None else acc + term
        total[:, cols] = acc

    refills = []

    def do_d_first():
        loop(3, d_first_part)
        for j in range(12):
            vec[0, 6 + j // 3 : 7 + j // 3, (j % 3) * 256 : (j % 3) * 256 + 256] = jnp.sum(
                inner_sums[j], 0, keepdims=True
            )

    def refill_probs():
        for r in range(3):
            rows = pl.ds(3072 * ROOMS[r], 3072)
            refill = pltpu.make_async_copy(probs_out.at[rows], region.at[rows], local.at[15 + r])
            refill.start()
            refills.append(refill)

    def first_norm_back(i, sums):
        rows = aligned(i, 64)
        d_first = total[rows] + d_res[rows]
        norm = norm_one[rows]
        d_norm = d_first * params[4:5]
        d_one = spread_one[rows] * (
            d_norm
            - jnp.mean(d_norm, -1, keepdims=True)
            - norm * jnp.mean(d_norm * norm, -1, keepdims=True)
        )
        d_res[rows] = d_one
        low = d_one.astype(BF16)
        d_att[rows] = low
        return (
            sums[0] + fold(d_first * norm),
            sums[1] + fold(d_first),
            sums[2] + fold(low.astype(F32)),
        )

    def do_first_norm_back():
        out_copy.wait()
        sums = lax.fori_loop(0, 6, first_norm_back, (nothing, nothing, nothing))
        put_sum(4, sums[0])
        put_sum(5, sums[1])
        put_sum(3, sums[2])

    def square_grads(u, left, right):
        for m in range(2):
            grad = mm_tl(left(m), right).astype(BF16)
            for b in range(4):
                for h in range(2):
                    for side in range(2):
                        rows = b * 96 + h * 48
                        grads[u, h, side, m, b // 2, b % 2] = grad[
                            rows : rows + 48, side * 384 : side * 384 + 384
                        ]
        start_unit(u)

    def do_output_grads():
        square_grads(OUTPUT, lambda m: mixed[:, 384 * m : 384 * m + 384], d_att[...])

    def d_mixed_part(i):
        rows = aligned(i, 128)
        mixed[rows] = mm_t(d_att[rows], wo[...]).astype(BF16)

    def do_attend_back(r, first, last):
        if first == 0:
            refills[r].wait()

        def attend_back(p):
            cols = aligned(p, 128)
            own_rows = pl.ds(128 * r, 128)
            base = ROOMS[r] * 6 + p
            queries = stacked(q_own[own_rows, cols] * BF16(HEAD_DIM**-0.5))
            d_mix = stacked(mixed[own_rows, cols])
            low_probs = jnp.concatenate(
                [region[aligned(2 * base, 256)], region[aligned(2 * base + 1, 256)]], axis=1
            )
            d_probs = mm_t(d_mix, v_all[r, :, cols])
            probs = low_probs.astype(F32)
            weighted = probs * d_probs
            d_raw = (weighted - probs * jnp.sum(weighted, -1, keepdims=True)).astype(BF16)
            d_query = mm(d_raw, k_all[r, :, cols]) * HEAD_DIM**-0.5
            q_own[own_rows, cols] = unstacked(d_query).astype(BF16)
            wi[pl.ds(512 * r, 512), cols] = mm_tl(d_raw, queries).astype(BF16)
            wi[pl.ds(1536 + 512 * r, 512), cols] = mm_tl(low_probs, d_mix).astype(BF16)

        span_loop(first, last, attend_back)

    def own_inputs(m):
        return jnp.concatenate(
            [x_all[r, aligned(me, 128), pl.ds(384 * m, 384)] for r in range(3)], 0
        )

    def all_inputs(m):
        return jnp.concatenate([x_all[r, :, pl.ds(384 * m, 384)] for r in range(3)], 0)

    def do_query_grads():
        square_grads(QUERY, own_inputs, q_own[...])

    def do_key_grads():
        square_grads(KEY, all_inputs, wi[pl.ds(0, 1536)])

    def do_value_grads():
        square_grads(VALUE, all_inputs, wi[pl.ds(1536, 1536)])

    def value_sum(i, acc):
        return acc + fold(wi[pl.ds(pl.multiple_of(1536 + i * 128, 128), 128)].astype(F32))

    mask_sums[...] = jnp.zeros((3, 8, 256), F32)

    def d_in_copy(kind, r):
        if kind == 0:
            source = wf.at[aligned(2 * r + 1 - core, 256)]
            target, name = d_in0.at[r], CORE
        else:
            source = wf.at[aligned(4 * r + 2 * core + 1 - y, 128)]
            target, name = d_in1.at[r], Y
        return pltpu.make_async_remote_copy(
            src_ref=source,
            dst_ref=target,
            send_sem=x_send.at[3 + kind, r],
            recv_sem=x_recv.at[3 + kind, r],
            device_id=peer[name],
            device_id_type=MESH,
        )

    def do_d_in(r):
        def d_in_part(n):
            cols = aligned(n, 256)
            part = mm_t(wi[pl.ds(512 * r, 512)], wk[cols]) + mm_t(
                wi[pl.ds(1536 + 512 * r, 512)], wv[cols]
            )
            for s in range(4):
                block = 4 * r + 2 * (s % 2) + s // 2
                wf[pl.ds(128 * block, 128), cols] = part[128 * s : 128 * s + 128].astype(BF16)
            mask_sums[n] = mask_sums[n] + fold(part * wide[:, r : r + 1])

        loop(3, d_in_part)
        d_in_copy(0, r).start()

    def d_in_pass(r):
        d_in_copy(0, r).wait()
        rows = aligned(4 * r + 2 * core + 1 - y, 128)
        wf[rows] = wf[rows] + d_in0[r, aligned(1 - y, 128)]
        d_in_copy(1, r).start()

    def own_part(i, acc):
        rows = aligned(i, 128)
        part = d_res[rows] + mm_t(q_own[rows], wq[...])
        d_res[rows] = part
        chosen = wide[aligned(me, 128)]
        chosen = jnp.where(i == 0, chosen[:, 0:1], jnp.where(i == 1, chosen[:, 1:2], chosen[:, 2:3]))
        return acc + fold(part * chosen)

    grad_copies = []

    def d_in_close(r):
        d_in_copy(1, r).wait()
        rows = pl.ds(128 * r, 128)
        value = (
            d_res[rows]
            + wf[aligned(4 * r + 2 * core + y, 128)].astype(F32)
            + d_in0[r, aligned(y, 128)].astype(F32)
            + d_in1[r].astype(F32)
        )
        chosen = wide[aligned(me, 128), r : r + 1] > 0.5
        d_att[rows] = jnp.where(chosen, 0.0, value).astype(BF16)
        copy = pltpu.make_async_copy(d_att.at[rows], grad_input.at[rows], local.at[18 + r])
        copy.start()
        grad_copies.append(copy)

    axes = (CORE, X, Y, ZLO, ZHI)

    def vector_copy(group, phase):
        sums, came = (vec, vec_came) if group == 0 else (late, late_came)
        return pltpu.make_async_remote_copy(
            src_ref=sums.at[phase],
            dst_ref=came.at[phase],
            send_sem=v_send.at[group, phase],
            recv_sem=v_recv.at[group, phase],
            device_id=peer[axes[phase]],
            device_id_type=MESH,
        )

    def vector_step(group, phase):
        vector_copy(group, phase).wait()
        sums, came = (vec, vec_came) if group == 0 else (late, late_came)
        sums[phase + 1] = sums[phase] + came[phase]
        if phase < 4:
            vector_copy(group, phase + 1).start()

    def do_late_sums():
        late[0] = jnp.zeros((8, 768), F32)
        mask_sum = jnp.concatenate([mask_sums[n] for n in range(3)], axis=1)
        all_sums = (
            lax.fori_loop(0, 3, own_part, mask_sum),
            fold(q_own[...].astype(F32)),
            lax.fori_loop(0, 12, value_sum, nothing),
        )
        for i, value in enumerate(all_sums):
            late[0, i : i + 1] = jnp.sum(value, 0, keepdims=True)
        vector_copy(1, 0).start()

    mine = (y, spot[ZHI], spot[ZLO], spot[X])

    def swap_copy(u):
        return pltpu.make_async_remote_copy(
            src_ref=units[u].own.at[mine],
            dst_ref=in5.at[u],
            send_sem=sends.at[u, 5],
            recv_sem=recvs.at[u, 5],
            device_id=peer[CORE],
            device_id_type=MESH,
        )

    def close(u):
        unit = units[u]
        unit.copy(4).wait()
        result = unit.own[mine].astype(F32) + unit.inbox[4][...].astype(F32)
        if INNER0 <= u < OUTPUT:
            i = u - INNER0
            out_inner[pl.ds(48 * (i % 2), 48), pl.ds(384 * (i // 2), 384)] = result
            return
        unit.own[mine] = result.astype(BF16)
        swap_copy(u).start()
        put_half(u, core, result)

    def put_half(u, side, value):
        value = jnp.where(core == 0, value[:, :192], pltpu.roll(value, 192, 1)[:, :192])
        if u < INNER0:
            out_outer[pl.ds(pl.multiple_of(side * 192 + u * 48, 48), 48)] = value
        else:
            target = (out_output, out_query, out_key, out_value)[u - OUTPUT]
            target[pl.ds(pl.multiple_of(side * 48, 48), 48)] = value

    def open_half(u):
        swap_copy(u).wait()
        put_half(u, 1 - core, in5[u].astype(F32))

    stages = {
        INNER: do_inner_grads,
        D_FIRST: do_d_first,
        FNB: do_first_norm_back,
        V1: lambda: vector_copy(0, 0).start(),
        DWO: do_output_grads,
        REFILL: refill_probs,
        DMIXED: lambda: loop(3, d_mixed_part),
        DWQ: do_query_grads,
        DWK: do_key_grads,
        DWV: do_value_grads,
        VEC: do_late_sums,
    }
    for r in range(3):
        stages[AB00 + 2 * r] = lambda r=r: do_attend_back(r, 0, 3)
        stages[AB01 + 2 * r] = lambda r=r: do_attend_back(r, 3, 6)
        stages[D_HIDDEN0 + r] = lambda r=r: span_loop(4 * r, 4 * r + 4, d_hidden_units)
        stages[DIN0 + r] = lambda r=r: do_d_in(r)
    count = {}
    for name in PLAN:
        if name in stages:
            stages[name]()
            continue
        turn = count[name] = count.get(name, -1) + 1
        if name <= VALUE:
            if turn < 4:
                units[name].step()
                if turn == 0 and STARTS.index(name) < SLOTS:
                    free_slot()
            elif turn == 4:
                close(name)
            else:
                open_half(name)
        elif name in (W1, W2):
            vector_step(name - W1, turn)
        elif name < DY0:
            d_in_pass(name - DC0)
        else:
            d_in_close(name - DY0)
    out_vectors[...] = vec[5]
    out_vectors[0:3] = late[5, 0:3]
    for copy in grad_copies:
        copy.wait()


def hand_out(*refs):
    sources, vectors, targets, rows = refs[:8], refs[8], refs[9:17], refs[17:27]
    for source, target in zip(sources[:7], targets[:7]):
        target[...] = source[...]
    targets[7][...] = sources[7][...].T
    for i, place in enumerate((0, 1, 2, 3, 4, 5, None, 10, 11, 12)):
        if place is not None:
            rows[i][...] = vectors[place]
    for j in range(4):
        rows[6][pl.ds(768 * j, 768)] = vectors[6 + j]


def fused_layer(
    hidden_in,
    cotangent,
    span_mask,
    lengths,
    repeats,
    mask_embedding,
    query_weight,
    query_bias,
    key_weight,
    value_weight,
    value_bias,
    output_weight,
    output_bias,
    mixing_gain,
    mixing_shift,
    inner_weight,
    inner_bias,
    outer_weight,
    outer_bias,
    final_gain,
    final_shift,
):
    vmem = pl.BlockSpec(memory_space=pltpu.VMEM)
    anywhere = pl.BlockSpec(memory_space=pl.ANY)
    scalars = pl.BlockSpec(memory_space=pltpu.SMEM)
    bf = lambda *shape: pltpu.VMEM(shape, BF16)
    fl = lambda *shape: pltpu.VMEM(shape, F32)
    dma = lambda *shape: pltpu.SemaphoreType.DMA(shape)
    shape = lambda dims, dtype: jax.ShapeDtypeStruct(dims, dtype)
    result = pl.pallas_call(
        layer_body,
        out_shape=[
            shape((384, 768), BF16),
            shape((384, 768), BF16),
            shape((9216, 256), BF16),
            shape((96, 192), F32),
            shape((96, 192), F32),
            shape((96, 192), F32),
            shape((96, 192), F32),
            shape((96, 768), F32),
            shape((384, 192), F32),
            shape((16, 768), F32),
        ],
        in_specs=[anywhere] * 8 + [vmem] + [anywhere] * 10 + [scalars, scalars],
        out_specs=[anywhere] * 3 + [vmem] * 7,
        scratch_shapes=[
            bf(3072, 768),
            bf(3072, 768),
            bf(768, 768),
            bf(768, 768),
            bf(768, 768),
            bf(768, 768),
            bf(13 * 768),
            fl(16, 768),
            bf(3, 512, 768),
            bf(3, 512, 768),
            bf(3, 512, 768),
            bf(384, 768),
            bf(384, 768),
            bf(9216, 256),
            bf(384, 768),
            fl(384, 768),
            fl(384, 1),
            fl(384, 768),
            fl(384, 768),
            bf(384, 768),
            bf(384, 768),
            pltpu.VMEM((4, 8, 128), jnp.int32),
            fl(512, 8),
            fl(12, 8, 256),
            fl(3, 8, 256),
            bf(12, 2, 2, 2, 2, 2, 48, 384),
            bf(SLOTS, 2, 2, 2, 2, 48, 384),
            bf(12, 2, 2, 2, 48, 384),
            bf(12, 2, 2, 48, 384),
            bf(12, 2, 48, 384),
            bf(12, 48, 384),
            bf(12, 48, 384),
            bf(3, 256, 768),
            bf(3, 128, 768),
            fl(6, 16, 768),
            fl(5, 16, 768),
            fl(6, 8, 768),
            fl(5, 8, 768),
            dma(12, 6),
            dma(12, 6),
            dma(5, 3),
            dma(5, 3),
            dma(3),
            dma(3),
            dma(2, 5),
            dma(2, 5),
            dma(31),
            pltpu.SemaphoreType.REGULAR,
        ],
        compiler_params=pltpu.CompilerParams(
            collective_id=1, has_side_effects=True, vmem_limit_bytes=63 * 2**20
        ),
        name="fused_layer",
    )(
        hidden_in,
        cotangent.reshape(384, 768),
        query_weight,
        key_weight,
        value_weight,
        output_weight,
        inner_weight,
        outer_weight,
        span_mask,
        mask_embedding,
        query_bias,
        value_bias,
        output_bias,
        mixing_gain,
        mixing_shift,
        inner_bias,
        outer_bias,
        final_gain,
        final_shift,
        lengths,
        repeats,
    )
    arrays, vectors = [result[0], result[1], *result[3:9]], result[9]
    wide_row = shape((768,), F32)
    handed = pl.pallas_call(
        hand_out,
        out_shape=[shape(v.shape, v.dtype) for v in arrays[:7]]
        + [shape((192, 384), F32)]
        + [wide_row] * 6
        + [shape((3072,), F32)]
        + [wide_row] * 3,
        in_specs=[vmem] * 9,
        out_specs=[vmem] * 18,
        name="hand_out",
    )(*arrays, vectors)
    layer_out, grad_input, g_query, g_key, g_value, g_output, g_inner, g_outer = handed[:8]
    g_mask, g_q_bias, g_v_bias, g_o_bias, g_gain, g_shift, g_inner_bias, *g_last = handed[8:]
    return (
        layer_out.reshape(3, 128, 768),
        grad_input.reshape(3, 128, 768),
        g_mask,
        g_query,
        g_q_bias,
        g_key,
        g_value,
        g_v_bias,
        g_output,
        g_o_bias,
        g_gain,
        g_shift,
        g_inner,
        g_inner_bias,
        g_outer.T,
        *g_last,
    )


def with_halo(x, sides, width):
    for axis, dim in sides:
        count, length = (lax.axis_size(axis), x.shape[dim])
        up = [(i, (i + 1) % count) for i in range(count - 1)]
        down = [(j, i) for i, j in up]
        last = lax.slice_in_dim(x, length - width, length, axis=dim)
        initial = lax.slice_in_dim(x, 0, width, axis=dim)
        before = lax.ppermute(last, axis, up)
        after = lax.ppermute(initial, axis, down)
        x = jnp.concatenate([before, x, after], axis=dim)
    return x


def layer_norm(inputs, gain, shift):
    center = inputs - jnp.mean(inputs, -1, keepdims=True)
    spread = jnp.mean(center * center, -1, keepdims=True)
    return center * lax.rsqrt(spread + 1e-05) * gain + shift


def linear(inputs, weight):
    return jnp.dot(inputs, weight, preferred_element_type=jnp.float32)


def linear_back(grads, weight):
    return lax.dot_general(
        grads, weight, (((1,), (1,)), ((), ())), preferred_element_type=jnp.float32
    )


def contract_rows(left, right):
    return lax.dot_general(
        left, right, (((0,), (0,)), ((), ())), preferred_element_type=jnp.float32
    )


def gelu_exact(inputs):
    return jax.nn.gelu(inputs, approximate=False)


def plain_layer(
    hidden_in,
    cotangent,
    span_mask,
    lengths,
    repeats,
    mask_embedding,
    query_weight,
    query_bias,
    key_weight,
    value_weight,
    value_bias,
    output_weight,
    output_bias,
    mixing_gain,
    mixing_shift,
    inner_weight,
    inner_bias,
    outer_weight,
    outer_bias,
    final_gain,
    final_shift,
):
    rows, stretch, width = hidden_in.shape
    whole = stretch * lax.axis_size("seq")
    scale = HEAD_DIM ** (-0.5)
    offset = lax.axis_index("seq") * stretch
    rim = with_halo(span_mask, (("seq", 1),), WIDEN)
    window = rim[:, 0:stretch]
    for shifted in range(1, 2 * WIDEN + 1):
        window = window + rim[:, shifted : shifted + stretch]
    widened = window > 0
    positions = offset + jnp.arange(stretch, dtype=jnp.int32)
    live = positions[None, :] < lengths[:, None]
    key_live = jnp.arange(whole, dtype=jnp.int32)[None, :] < lengths[:, None]
    masked_in = jnp.where(widened[..., None], mask_embedding[None, None, :], hidden_in)
    flat_in = masked_in.reshape(rows * stretch, width)
    queries = (linear(flat_in, query_weight) + query_bias.astype(jnp.float32)).astype(jnp.bfloat16)
    key_rows = linear(flat_in, key_weight).astype(jnp.bfloat16).reshape(rows, stretch, width)
    value_rows = (linear(flat_in, value_weight) + value_bias.astype(jnp.float32)).astype(
        jnp.bfloat16
    )
    value_rows = value_rows.reshape(rows, stretch, width)
    key_all, value_all = (
        lax.all_gather(key_rows, "seq", axis=1, tiled=True),
        lax.all_gather(value_rows, "seq", axis=1, tiled=True),
    )
    query_heads = queries.reshape(rows, stretch, HEADS, HEAD_DIM)

    def scores_of(key_full):
        key_heads = key_full.reshape(rows, whole, HEADS, HEAD_DIM)
        raw = jnp.einsum(
            "rqhd,rkhd->rhqk", query_heads, key_heads, preferred_element_type=jnp.float32
        )
        return jnp.where(key_live[:, None, None, :], raw * scale, -1e30)

    logits = scores_of(key_all)
    highest = jnp.max(logits, -1, keepdims=True)
    expd = jnp.exp(logits - highest)
    totals = jnp.sum(expd, -1, keepdims=True)
    log_total = highest + jnp.log(totals)
    probs_low = (expd / totals).astype(jnp.bfloat16)
    value_heads = value_all.reshape(rows, whole, HEADS, HEAD_DIM)
    mixed = jnp.einsum(
        "rhqk,rkhd->rqhd", probs_low, value_heads, preferred_element_type=jnp.float32
    )
    mixed = mixed.reshape(rows * stretch, width).astype(jnp.bfloat16)
    attended = linear(mixed, output_weight) + output_bias.astype(jnp.float32)
    residual_one = flat_in.astype(jnp.float32) + attended
    first, norm_back_one = jax.vjp(
        layer_norm, residual_one, mixing_gain.astype(jnp.float32), mixing_shift.astype(jnp.float32)
    )
    first_low = first.astype(jnp.bfloat16)
    inner = linear(first_low, inner_weight) + inner_bias.astype(jnp.float32)
    activated, gelu_back = jax.vjp(gelu_exact, inner)
    activated_low = activated.astype(jnp.bfloat16)
    outer = linear(activated_low, outer_weight) + outer_bias.astype(jnp.float32)
    final, norm_back_two = jax.vjp(
        layer_norm, first + outer, final_gain.astype(jnp.float32), final_shift.astype(jnp.float32)
    )
    layer_out = final.astype(jnp.bfloat16).reshape(rows, stretch, width)
    weighting = repeats.astype(jnp.float32)[:, None] * live.astype(jnp.float32)
    d_final = (cotangent.astype(jnp.float32) * weighting[:, :, None]).reshape(rows * stretch, width)
    d_two, d_final_gain, d_final_shift = norm_back_two(d_final)
    d_outer = d_two.astype(jnp.bfloat16)
    g_outer_weight = contract_rows(activated_low, d_outer)
    g_outer_bias = jnp.sum(d_outer.astype(jnp.float32), 0)
    (d_inner,) = gelu_back(linear_back(d_outer, outer_weight))
    d_inner = d_inner.astype(jnp.bfloat16)
    g_inner_weight = contract_rows(first_low, d_inner)
    g_inner_bias = jnp.sum(d_inner.astype(jnp.float32), 0)
    d_first = linear_back(d_inner, inner_weight) + d_two
    d_one, d_mixing_gain, d_mixing_shift = norm_back_one(d_first)
    d_attended = d_one.astype(jnp.bfloat16)
    g_output_weight = contract_rows(mixed, d_attended)
    g_output_bias = jnp.sum(d_attended.astype(jnp.float32), 0)
    d_mixed = linear_back(d_attended, output_weight).astype(jnp.bfloat16)
    d_mixed_heads = d_mixed.reshape(rows, stretch, HEADS, HEAD_DIM)
    key_back, value_back = (
        lax.all_gather(key_rows, "seq", axis=1, tiled=True),
        lax.all_gather(value_rows, "seq", axis=1, tiled=True),
    )
    probs = jnp.exp(scores_of(key_back) - log_total)
    probs_again = probs.astype(jnp.bfloat16)
    key_heads = key_back.reshape(rows, whole, HEADS, HEAD_DIM)
    value_heads = value_back.reshape(rows, whole, HEADS, HEAD_DIM)
    d_probs = jnp.einsum(
        "rqhd,rkhd->rhqk", d_mixed_heads, value_heads, preferred_element_type=jnp.float32
    )
    centered = d_probs - jnp.sum(probs * d_probs, -1, keepdims=True)
    d_raw = (probs * centered * scale).astype(jnp.bfloat16)
    d_queries = jnp.einsum("rhqk,rkhd->rqhd", d_raw, key_heads, preferred_element_type=jnp.float32)
    d_queries = d_queries.reshape(rows * stretch, width).astype(jnp.bfloat16)
    d_key_part = jnp.einsum(
        "rhqk,rqhd->rkhd", d_raw, query_heads, preferred_element_type=jnp.float32
    )
    d_value_part = jnp.einsum(
        "rhqk,rqhd->rkhd", probs_again, d_mixed_heads, preferred_element_type=jnp.float32
    )
    d_key_sum, d_value_sum = (
        lax.psum_scatter(
            d_key_part.reshape(rows, whole, width), "seq", scatter_dimension=1, tiled=True
        ),
        lax.psum_scatter(
            d_value_part.reshape(rows, whole, width), "seq", scatter_dimension=1, tiled=True
        ),
    )
    d_keys = d_key_sum.astype(jnp.bfloat16).reshape(rows * stretch, width)
    d_values = d_value_sum.astype(jnp.bfloat16).reshape(rows * stretch, width)
    g_query_weight = contract_rows(flat_in, d_queries)
    g_key_weight = contract_rows(flat_in, d_keys)
    g_value_weight = contract_rows(flat_in, d_values)
    g_query_bias = jnp.sum(d_queries.astype(jnp.float32), 0)
    g_value_bias = jnp.sum(d_values.astype(jnp.float32), 0)
    d_input = (
        d_one
        + linear_back(d_queries, query_weight)
        + linear_back(d_keys, key_weight)
        + linear_back(d_values, value_weight)
    ).reshape(rows, stretch, width)
    grad_input = jnp.where(widened[..., None], 0.0, d_input).astype(jnp.bfloat16)
    g_mask = jnp.sum(jnp.where(widened[..., None], d_input, 0.0), (0, 1))
    matrices = (
        g_query_weight,
        g_key_weight,
        g_value_weight,
        g_output_weight,
        g_inner_weight,
        g_outer_weight,
    )
    partial_sums = (
        lax.psum_scatter(matrices[0], "batch", scatter_dimension=0, tiled=True),
        lax.psum_scatter(matrices[1], "batch", scatter_dimension=0, tiled=True),
        lax.psum_scatter(matrices[2], "batch", scatter_dimension=0, tiled=True),
        lax.psum_scatter(matrices[3], "batch", scatter_dimension=0, tiled=True),
        lax.psum_scatter(matrices[4], "batch", scatter_dimension=0, tiled=True),
        lax.psum_scatter(matrices[5], "batch", scatter_dimension=0, tiled=True),
    )
    summed = (
        lax.psum_scatter(partial_sums[0], "seq", scatter_dimension=1, tiled=True),
        lax.psum_scatter(partial_sums[1], "seq", scatter_dimension=1, tiled=True),
        lax.psum_scatter(partial_sums[2], "seq", scatter_dimension=1, tiled=True),
        lax.psum_scatter(partial_sums[3], "seq", scatter_dimension=1, tiled=True),
        lax.psum_scatter(partial_sums[4], "seq", scatter_dimension=1, tiled=True),
        lax.psum_scatter(partial_sums[5], "seq", scatter_dimension=1, tiled=True),
    )
    vectors = lax.psum(
        (
            g_mask,
            g_query_bias,
            g_value_bias,
            g_output_bias,
            d_mixing_gain,
            d_mixing_shift,
            g_inner_bias,
            g_outer_bias,
            d_final_gain,
            d_final_shift,
        ),
        ("batch", "seq"),
    )
    return (
        layer_out,
        grad_input,
        vectors[0],
        summed[0],
        vectors[1],
        summed[1],
        summed[2],
        vectors[2],
        summed[3],
        vectors[3],
        vectors[4],
        vectors[5],
        summed[4],
        vectors[6],
        summed[5],
        vectors[7],
        vectors[8],
        vectors[9],
    )


def solution(mesh):
    fused = mesh.shape["batch"] == 8 and mesh.shape["seq"] == 4
    return jax.shard_map(
        fused_layer if fused else plain_layer,
        mesh=mesh,
        in_specs=(
            P("batch", "seq", None),
            P("batch", "seq", None),
            P("batch", "seq"),
            P("batch"),
            P("batch"),
            P(),
            P(),
            P(),
            P(),
            P(),
            P(),
            P(),
            P(),
            P(),
            P(),
            P(),
            P(),
            P(),
            P(),
            P(),
            P(),
        ),
        out_specs=(
            P("batch", "seq", None),
            P("batch", "seq", None),
            P(),
            P("batch", "seq"),
            P(),
            P("batch", "seq"),
            P("batch", "seq"),
            P(),
            P("batch", "seq"),
            P(),
            P(),
            P(),
            P("batch", "seq"),
            P(),
            P("batch", "seq"),
            P(),
            P(),
            P(),
        ),
        check_vma=False,
    )
```

```python
import jax
import jax.numpy as jnp
from jax import lax
from jax.experimental import pallas as pl
from jax.experimental.pallas import tpu as pltpu
from jax.sharding import PartitionSpec as P

HEADS = 12
HEAD_DIM = 64
WIDEN = 5

MESH = pl.DeviceIdType.MESH
F32 = jnp.float32
BF16 = jnp.bfloat16
ROOT_HALF = 0.7071067811865476
DENSITY = 0.3989422804014327


def mm(a, b):
    return jnp.dot(a, b, preferred_element_type=F32)


def mm_t(a, b):
    return lax.dot_general(a, b, (((1,), (1,)), ((), ())), preferred_element_type=F32)


def mm_tl(a, b):
    return lax.dot_general(a, b, (((0,), (0,)), ((), ())), preferred_element_type=F32)


def fold(v):
    return jnp.sum(v.reshape(v.shape[0] // 8, 8, v.shape[1]), 0)


def loop(count, body, unroll=1):
    def step(i, carry):
        body(i)
        return carry

    lax.fori_loop(0, count, step, 0, unroll=unroll)


def span_loop(first, last, body, unroll=1):
    def step(i, carry):
        body(i)
        return carry

    lax.fori_loop(first, last, step, 0, unroll=unroll)


def aligned(i, size):
    return pl.ds(pl.multiple_of(i * size, size), size)


def places():
    b, s = lax.axis_index("batch"), lax.axis_index("seq")
    x, zlo, zhi = lax.rem(b, 2), lax.rem(b // 2, 2), b // 4
    core, y = lax.rem(s, 2), s // 2
    spot = {CORE: core, X: x, Y: y, ZLO: zlo, ZHI: zhi}
    peer = {
        CORE: (b, s + 1 - 2 * core),
        Y: (b, s + 2 - 4 * y),
        X: (b + 1 - 2 * x, s),
        ZLO: (b + 2 - 4 * zlo, s),
        ZHI: (b + 4 - 8 * zhi, s),
        FAR: (b, 3 - s),
    }
    return spot, peer


class Unit:
    def __init__(self, order, both, inbox, sends, recvs, spot, peer):
        self.order, self.both, self.inbox = order, both, inbox
        self.sends, self.recvs, self.spot, self.peer = sends, recvs, spot, peer
        self.own = both.at[spot[CORE]]
        self.phase = 0

    def where(self, phase, stays):
        done, axis = self.order[: phase - 1], self.order[phase - 1]
        place = []
        for name in (Y, ZHI, ZLO, X):
            side = self.spot[name]
            if name == axis:
                place.append(side if stays else 1 - side)
            else:
                place.append(side if name in done else slice(None))
        return tuple(place)

    def copy(self, phase):
        if phase == 0:
            axis, source = CORE, self.both.at[1 - self.spot[CORE]]
        else:
            axis, source = self.order[phase - 1], self.own.at[self.where(phase, False)]
        return pltpu.make_async_remote_copy(
            src_ref=source,
            dst_ref=self.inbox[phase],
            send_sem=self.sends.at[phase],
            recv_sem=self.recvs.at[phase],
            device_id=self.peer[axis],
            device_id_type=MESH,
        )

    def start(self):
        self.copy(0).start()

    def step(self):
        phase = self.phase
        self.copy(phase).wait()
        came = self.inbox[phase]
        target = self.own if phase == 0 else self.own.at[self.where(phase, True)]
        lead = 4 - phase

        def body(n):
            place = tuple(lax.rem(n // 2 ** (lead - 1 - i), 2) for i in range(lead))
            target[place] = target[place] + came[place]

        loop(2**lead, body, min(4, 2**lead))
        self.phase = phase + 1
        self.copy(self.phase).start()


CORE, X, Y, ZLO, ZHI, FAR = range(6)
OUTER0, OUTER1, OUTER2, OUTER3, INNER0, INNER1, INNER2, INNER3, OUTPUT, QUERY, KEY, VALUE = range(0, 12)
(
    D_HIDDEN0, D_HIDDEN1, D_HIDDEN2, INNER, D_FIRST, FNB, V1, DWO,
    REFILL, DMIXED, DWQ, DWK, DWV, VEC, AB00, AB01,
    AB10, AB11, AB20, AB21, DIN0, DIN1, DIN2,
) = range(12, 35)
W1, W2, DC0, DC1, DC2, DY0, DY1, DY2 = range(35, 43)
STARTS = (
    OUTER0, OUTER1, OUTER2, OUTER3, INNER0, INNER1,
    INNER2, INNER3, OUTPUT, KEY, QUERY, VALUE,
)
ORDERS = {
    OUTER0: (ZLO, Y, ZHI, X),
    OUTER1: (Y, X, ZLO, ZHI),
    OUTER2: (X, ZLO, Y, ZHI),
    OUTER3: (ZLO, Y, ZHI, X),
    INNER0: (X, Y, ZLO, ZHI),
    INNER1: (ZLO, Y, X, ZHI),
    INNER2: (X, Y, ZLO, ZHI),
    INNER3: (Y, ZLO, ZHI, X),
    OUTPUT: (X, Y, ZLO, ZHI),
    KEY: (X, ZLO, ZHI, Y),
    QUERY: (Y, X, ZLO, ZHI),
    VALUE: (X, ZLO, Y, ZHI),
}
PLAN = (
    D_HIDDEN0, D_HIDDEN1, OUTER0, D_HIDDEN2, OUTER1, OUTER2, INNER, OUTER3,
    D_FIRST, REFILL, FNB, INNER0, OUTER0, INNER1, OUTER1, OUTER2,
    INNER2, V1, DWO, INNER3, W1, DMIXED, OUTER3, OUTER0,
    AB00, OUTPUT, AB01, INNER0, AB10, OUTER1, INNER3, INNER1,
    AB11, OUTER2, AB20, OUTER3, AB21, INNER2, OUTER0, W1,
    OUTER1, INNER0, DWK, INNER3, INNER1, DWQ, DWV, KEY,
    OUTER2, OUTPUT, OUTER1, QUERY, INNER2, OUTER0, OUTER3, INNER0,
    DIN0, OUTER0, W1, OUTER1, INNER1, DIN1, VALUE, INNER3,
    OUTER2, INNER2, DC0, OUTPUT, DIN2, OUTER2, W1, KEY,
    INNER0, DC1, OUTER3, VEC, INNER1, INNER2, OUTER3, QUERY,
    DC2, OUTPUT, W2, W1, VALUE, DY0, INNER3, KEY,
    OUTPUT, QUERY, W2, OUTPUT, DY1, VALUE, KEY, DY2,
    W2, QUERY, VALUE, W2, KEY, KEY, QUERY, VALUE,
    QUERY, W2, VALUE,
)
SLOTS = 6
ROOMS = (0, 2, 1)


def layer_body(
    hidden,
    cotangent,
    query_weight,
    key_weight,
    value_weight,
    output_weight,
    inner_weight,
    outer_weight,
    span,
    mask_embedding,
    query_bias,
    value_bias,
    output_bias,
    mixing_gain,
    mixing_shift,
    inner_bias,
    outer_bias,
    final_gain,
    final_shift,
    lengths,
    repeats,
    layer_out,
    grad_input,
    probs_out,
    out_query,
    out_key,
    out_value,
    out_output,
    out_inner,
    out_outer,
    out_vectors,
    wi,
    wf,
    wq,
    wk,
    wv,
    wo,
    packed,
    params,
    x_all,
    k_all,
    v_all,
    q_own,
    mixed,
    region,
    first_low,
    norm_one,
    spread_one,
    total,
    d_res,
    d_outer,
    d_att,
    masks,
    wide,
    inner_sums,
    mask_sums,
    grads,
    in0,
    in1,
    in2,
    in3,
    in4,
    in5,
    d_in0,
    d_in1,
    vec,
    vec_came,
    late,
    late_came,
    sends,
    recvs,
    x_send,
    x_recv,
    m_send,
    m_recv,
    v_send,
    v_recv,
    local,
    credit,
):
    spot, peer = places()
    core, y = spot[CORE], spot[Y]
    me = 2 * y + core
    sibling = 2 * y + 1 - core
    across = 2 * (1 - y) + core

    names = (CORE, X, Y, ZLO, ZHI, FAR)
    barrier = pltpu.get_barrier_semaphore()
    for name in names:
        pl.semaphore_signal(barrier, inc=1, device_id=peer[name], device_id_type=MESH)

    weight_loads = {}

    def load(name, number, source, target):
        copy = pltpu.make_async_copy(source, target, local.at[number])
        copy.start()
        weight_loads[name] = copy

    load("hidden", 0, hidden, x_all.at[:, aligned(me, 128)])
    load("key", 1, key_weight, wk)
    load("value", 2, value_weight, wv)
    load("query", 3, query_weight, wq)

    pl.semaphore_wait(barrier, len(names))

    masks[me] = jnp.zeros((8, 128), jnp.int32)
    masks[me, 0:3] = span[...]
    mask_copies = []
    for i, name in enumerate((CORE, Y, FAR)):
        copy = pltpu.make_async_remote_copy(
            src_ref=masks.at[me],
            dst_ref=masks.at[me],
            send_sem=m_send.at[i],
            recv_sem=m_recv.at[i],
            device_id=peer[name],
            device_id_type=MESH,
        )
        copy.start()
        mask_copies.append(copy)

    def x_copy(kind, r):
        source = hidden.at[r] if kind < 2 else x_all.at[r, aligned(across, 128)]
        slot = me if kind < 2 else across
        return pltpu.make_async_remote_copy(
            src_ref=source,
            dst_ref=x_all.at[r, aligned(slot, 128)],
            send_sem=x_send.at[kind, r],
            recv_sem=x_recv.at[kind, r],
            device_id=peer[Y if kind == 0 else CORE],
            device_id_type=MESH,
        )

    for r in range(3):
        x_copy(0, r).start()
        x_copy(1, r).start()

    vectors = (
        (mask_embedding, 0),
        (query_bias, 1),
        (value_bias, 2),
        (output_bias, 3),
        (mixing_gain, 4),
        (mixing_shift, 5),
        (inner_bias, 6),
        (outer_bias, 10),
        (final_gain, 11),
        (final_shift, 12),
    )
    vector_loads = []
    for i, (vector, place) in enumerate(vectors):
        target = packed.at[pl.ds(768 * place, vector.shape[0])]
        copy = pltpu.make_async_copy(vector, target, local.at[21 + i])
        copy.start()
        vector_loads.append(copy)
    for copy in vector_loads:
        copy.wait()
    for i in range(13):
        params[i : i + 1] = packed[pl.ds(768 * i, 768)].astype(F32).reshape(1, 768)

    for copy in mask_copies:
        copy.wait()
    span_all = jnp.concatenate([masks[s].astype(F32) for s in range(4)], axis=1)
    lane = lax.broadcasted_iota(jnp.int32, span_all.shape, 1)
    window = span_all
    for d in range(1, WIDEN + 1):
        window = jnp.maximum(window, jnp.where(lane >= d, pltpu.roll(span_all, d, 1), 0.0))
        window = jnp.maximum(
            window, jnp.where(lane < 512 - d, pltpu.roll(span_all, 512 - d, 1), 0.0)
        )
    wide[...] = window.T

    half = lax.broadcasted_iota(jnp.int32, (128, 128), 1) < HEAD_DIM
    zero = jnp.zeros((128, 128), BF16)

    def stacked(pair):
        return jnp.concatenate([jnp.where(half, pair, zero), jnp.where(half, zero, pair)], 0)

    def unstacked(both):
        return jnp.where(half, both[:128], both[128:])

    mask_row = params[0:1]
    spills = []

    def put_mask(r, slot):
        rows = aligned(slot, 128)
        chosen = wide[rows, r : r + 1] > 0.5
        kept = x_all[r, rows].astype(F32)
        x_all[r, rows] = jnp.where(chosen, mask_row, kept).astype(BF16)

    def project(pieces, with_queries):
        inputs = jnp.concatenate([x_all[r, aligned(slot, 128)] for r, slot in pieces], 0)

        def part(n):
            cols = aligned(n, 256)
            keys = mm(inputs, wk[:, cols]).astype(BF16)
            values = (mm(inputs, wv[:, cols]) + params[2:3, cols]).astype(BF16)
            for i, (r, slot) in enumerate(pieces):
                k_all[r, aligned(slot, 128), cols] = keys[128 * i : 128 * i + 128]
                v_all[r, aligned(slot, 128), cols] = values[128 * i : 128 * i + 128]
            if with_queries:
                q_own[:, cols] = (mm(inputs, wq[:, cols]) + params[1:2, cols]).astype(BF16)

        loop(3, part, 3)

    weight_loads["hidden"].wait()
    for r in range(3):
        put_mask(r, me)
    for name in ("key", "value", "query"):
        weight_loads[name].wait()
    load("output", 4, output_weight, wo)
    for j in range(4):
        load(j, 5 + j, inner_weight.at[:, pl.ds(768 * j, 768)], wi.at[pl.ds(768 * j, 768)])
    load("outer", 9, outer_weight, wf)
    load("cotangent", 10, cotangent, d_outer)
    project([(r, me) for r in range(3)], True)
    for r in range(3):
        x_copy(1, r).wait()
        put_mask(r, sibling)
    project([(r, sibling) for r in range(3)], False)
    x_copy(0, 0).wait_recv()
    x_copy(2, 0).start()
    for r in range(3):
        x_copy(2, r).wait()
        put_mask(r, across)
        put_mask(r, 3 - me)
        project([(r, across), (r, 3 - me)], False)
        key_live = lax.broadcasted_iota(jnp.int32, (1, 512), 1) < lengths[r]

        def attend(p):
            cols = aligned(p, 128)
            queries = stacked(q_own[pl.ds(128 * r, 128), cols] * BF16(HEAD_DIM**-0.5))
            logits = mm_t(queries, k_all[r, :, cols])
            logits = jnp.where(key_live, logits, -1e30)
            expd = jnp.exp(logits - jnp.max(logits, -1, keepdims=True))
            probs = (expd * (1.0 / jnp.sum(expd, -1, keepdims=True))).astype(BF16)
            base = ROOMS[r] * 6 + p
            region[aligned(2 * base, 256)] = probs[:, :256]
            region[aligned(2 * base + 1, 256)] = probs[:, 256:]
            out = mm(probs, v_all[r, :, cols])
            mixed[pl.ds(128 * r, 128), cols] = unstacked(out).astype(BF16)

        def attend_three(i):
            for p in range(3):
                attend(3 * i + p)
            if r < 2:

                @pl.when(i == 0)
                def _():
                    x_copy(0, r + 1).wait_recv()
                    x_copy(2, r + 1).start()

        loop(2, attend_three)
        rows = pl.ds(3072 * ROOMS[r], 3072)
        spill = pltpu.make_async_copy(region.at[rows], probs_out.at[rows], local.at[11 + r])
        spill.start()
        spills.append(spill)

    for r in range(3):
        x_copy(0, r).wait_send()
    weight_loads["output"].wait()

    def first_norm(i):
        rows = aligned(i, 128)
        attended = mm(mixed[rows], wo[...]) + params[3:4]
        value = x_all[i, aligned(me, 128)].astype(F32) + attended
        center = value - jnp.mean(value, -1, keepdims=True)
        scale = lax.rsqrt(jnp.mean(center * center, -1, keepdims=True) + 1e-5)
        norm = center * scale
        norm_one[rows] = norm
        spread_one[rows] = scale
        first_low[rows] = (norm * params[4:5] + params[5:6]).astype(BF16)

    loop(3, first_norm, 3)
    spills[0].wait()
    spills[1].wait()
    for j in range(4):
        weight_loads[j].wait()

    def hidden_units(j):
        inner = mm(
            first_low[...], wi[pl.ds((j // 3) * 768, 768), aligned(lax.rem(j, 3), 256)]
        ) + params[pl.ds(6 + j // 3, 1), aligned(lax.rem(j, 3), 256)]
        below = 0.5 * (1.0 + lax.erf(inner * ROOT_HALF))
        slope = below + inner * (DENSITY * jnp.exp(-0.5 * inner * inner))
        region[aligned(j, 384)] = (inner * below).astype(BF16)
        region[aligned(23 - j, 384)] = slope.astype(BF16)

    span_loop(0, 8, hidden_units, 4)
    spills[2].wait()
    span_loop(8, 12, hidden_units, 2)
    weight_loads["outer"].wait()
    weight_loads["cotangent"].wait()

    def panels(which):
        return jnp.concatenate([region[pl.ds(384 * j, 384)] for j in which], axis=1)

    def project_out(n):
        cols = aligned(n, 256)
        total[:, cols] = mm(panels(range(12)), wf[:, cols])

    loop(3, project_out, 3)

    def last_norm(i, sums):
        rows = aligned(i, 64)
        first = norm_one[rows] * params[4:5] + params[5:6]
        value = first + (total[rows] + params[10:11])
        center = value - jnp.mean(value, -1, keepdims=True)
        scale = lax.rsqrt(jnp.mean(center * center, -1, keepdims=True) + 1e-5)
        norm = center * scale
        d_att[rows] = (norm * params[11:12] + params[12:13]).astype(BF16)
        r = i // 2
        position = lax.broadcasted_iota(jnp.int32, (64, 1), 0) + lax.rem(i, 2) * 64 + me * 128
        weight = jnp.where(position < lengths[r], repeats[r].astype(F32), 0.0)
        d_final = d_outer[rows].astype(F32) * weight
        d_norm = d_final * params[11:12]
        d_two = scale * (
            d_norm
            - jnp.mean(d_norm, -1, keepdims=True)
            - norm * jnp.mean(d_norm * norm, -1, keepdims=True)
        )
        d_res[rows] = d_two
        low = d_two.astype(BF16)
        d_outer[rows] = low
        return (
            sums[0] + fold(d_final * norm),
            sums[1] + fold(d_final),
            sums[2] + fold(low.astype(F32)),
        )

    nothing = jnp.zeros((8, 768), F32)

    def put_sum(row, value):
        vec[0, row : row + 1] = jnp.sum(value, 0, keepdims=True)

    vec[0] = jnp.zeros((16, 768), F32)
    sums = lax.fori_loop(0, 6, last_norm, (nothing, nothing, nothing))
    put_sum(11, sums[0])
    put_sum(12, sums[1])
    put_sum(10, sums[2])
    out_copy = pltpu.make_async_copy(
        d_att, layer_out, local.at[14]
    )
    out_copy.start()

    units = [None] * 12
    for turn, u in enumerate(STARTS):
        inbox = [in0.at[turn % SLOTS], in1.at[u], in2.at[u], in3.at[u], in4.at[u]]
        units[u] = Unit(ORDERS[u], grads.at[u], inbox, sends.at[u], recvs.at[u], spot, peer)

    def start_unit(name):
        if STARTS.index(name) >= SLOTS:
            claim_slot()
        units[name].start()

    def free_slot():
        pl.semaphore_signal(credit, inc=1, device_id=peer[CORE], device_id_type=MESH)

    def claim_slot():
        pl.semaphore_wait(credit, 1)

    def outer_grads(z):
        for x in range(2):
            cols = [region[pl.ds(pl.multiple_of((3 * z + j) * 384, 384), 384)] for j in range(3)]
            part = jnp.concatenate(cols, axis=1)[:, 384 * x : 384 * x + 384]
            grad = mm_tl(part, d_outer[...]).astype(BF16)
            for h in range(2):
                for i in range(4):
                    for side in range(2):
                        rows = (h * 4 + i) * 48
                        grads[OUTER0 + i, h, side, z // 2, lax.rem(z, 2), x] = grad[
                            rows : rows + 48, side * 384 : side * 384 + 384
                        ]

    loop(4, outer_grads, 2)
    for i in range(4):
        start_unit(OUTER0 + i)

    def d_hidden_units(j):
        d_act = mm_t(d_outer[...], wf[aligned(j, 256)])
        place = aligned(23 - j, 384)
        low = (d_act * region[place].astype(F32)).astype(BF16)
        region[place] = low
        inner_sums[j] = fold(low.astype(F32))

    def inner_grads(s):
        cols = [region[pl.ds(pl.multiple_of((23 - 3 * s - j) * 384, 384), 384)] for j in range(3)]
        grad = mm_tl(first_low[...], jnp.concatenate(cols, axis=1)).astype(BF16)
        for b in range(8):
            for i in range(4):
                rows, side = 96 * b + 48 * (i % 2), 384 * (i // 2)
                grads[
                    INNER0 + i, lax.rem(s, 2), s // 2, b // 4, (b // 2) % 2, b % 2
                ] = grad[rows : rows + 48, side : side + 384]

    def do_inner_grads():
        loop(4, inner_grads, 2)
        for i in range(4):
            start_unit(INNER0 + i)

    def d_first_part(n):
        cols = aligned(n, 256)
        acc = None
        for s in range(4):
            d_inner = panels(range(23 - 3 * s, 20 - 3 * s, -1))
            term = mm_t(d_inner, wi[pl.ds(pl.multiple_of(s * 768 + n * 256, 256), 256)])
            acc = term if acc is None else acc + term
        total[:, cols] = acc

    refills = []

    def do_d_first():
        loop(3, d_first_part)
        for j in range(12):
            vec[0, 6 + j // 3 : 7 + j // 3, (j % 3) * 256 : (j % 3) * 256 + 256] = jnp.sum(
                inner_sums[j], 0, keepdims=True
            )

    def refill_probs():
        for r in range(3):
            rows = pl.ds(3072 * ROOMS[r], 3072)
            refill = pltpu.make_async_copy(probs_out.at[rows], region.at[rows], local.at[15 + r])
            refill.start()
            refills.append(refill)

    def first_norm_back(i, sums):
        rows = aligned(i, 64)
        d_first = total[rows] + d_res[rows]
        norm = norm_one[rows]
        d_norm = d_first * params[4:5]
        d_one = spread_one[rows] * (
            d_norm
            - jnp.mean(d_norm, -1, keepdims=True)
            - norm * jnp.mean(d_norm * norm, -1, keepdims=True)
        )
        d_res[rows] = d_one
        low = d_one.astype(BF16)
        d_att[rows] = low
        return (
            sums[0] + fold(d_first * norm),
            sums[1] + fold(d_first),
            sums[2] + fold(low.astype(F32)),
        )

    def do_first_norm_back():
        out_copy.wait()
        sums = lax.fori_loop(0, 6, first_norm_back, (nothing, nothing, nothing))
        put_sum(4, sums[0])
        put_sum(5, sums[1])
        put_sum(3, sums[2])

    def square_grads(u, left, right):
        for m in range(2):
            grad = mm_tl(left(m), right).astype(BF16)
            for b in range(4):
                for h in range(2):
                    for side in range(2):
                        rows = b * 96 + h * 48
                        grads[u, h, side, m, b // 2, b % 2] = grad[
                            rows : rows + 48, side * 384 : side * 384 + 384
                        ]
        start_unit(u)

    def do_output_grads():
        square_grads(OUTPUT, lambda m: mixed[:, 384 * m : 384 * m + 384], d_att[...])

    def d_mixed_part(i):
        rows = aligned(i, 128)
        mixed[rows] = mm_t(d_att[rows], wo[...]).astype(BF16)

    def do_attend_back(r, first, last):
        if first == 0:
            refills[r].wait()

        def attend_back(p):
            cols = aligned(p, 128)
            own_rows = pl.ds(128 * r, 128)
            base = ROOMS[r] * 6 + p
            queries = stacked(q_own[own_rows, cols] * BF16(HEAD_DIM**-0.5))
            d_mix = stacked(mixed[own_rows, cols])
            low_probs = jnp.concatenate(
                [region[aligned(2 * base, 256)], region[aligned(2 * base + 1, 256)]], axis=1
            )
            d_probs = mm_t(d_mix, v_all[r, :, cols])
            probs = low_probs.astype(F32)
            weighted = probs * d_probs
            d_raw = (weighted - probs * jnp.sum(weighted, -1, keepdims=True)).astype(BF16)
            d_query = mm(d_raw, k_all[r, :, cols]) * HEAD_DIM**-0.5
            q_own[own_rows, cols] = unstacked(d_query).astype(BF16)
            wi[pl.ds(512 * r, 512), cols] = mm_tl(d_raw, queries).astype(BF16)
            wi[pl.ds(1536 + 512 * r, 512), cols] = mm_tl(low_probs, d_mix).astype(BF16)

        span_loop(first, last, attend_back)

    def own_inputs(m):
        return jnp.concatenate(
            [x_all[r, aligned(me, 128), pl.ds(384 * m, 384)] for r in range(3)], 0
        )

    def all_inputs(m):
        return jnp.concatenate([x_all[r, :, pl.ds(384 * m, 384)] for r in range(3)], 0)

    def do_query_grads():
        square_grads(QUERY, own_inputs, q_own[...])

    def do_key_grads():
        square_grads(KEY, all_inputs, wi[pl.ds(0, 1536)])

    def do_value_grads():
        square_grads(VALUE, all_inputs, wi[pl.ds(1536, 1536)])

    def value_sum(i, acc):
        return acc + fold(wi[pl.ds(pl.multiple_of(1536 + i * 128, 128), 128)].astype(F32))

    mask_sums[...] = jnp.zeros((3, 8, 256), F32)

    def d_in_copy(kind, r):
        if kind == 0:
            source = wf.at[aligned(2 * r + 1 - core, 256)]
            target, name = d_in0.at[r], CORE
        else:
            source = wf.at[aligned(4 * r + 2 * core + 1 - y, 128)]
            target, name = d_in1.at[r], Y
        return pltpu.make_async_remote_copy(
            src_ref=source,
            dst_ref=target,
            send_sem=x_send.at[3 + kind, r],
            recv_sem=x_recv.at[3 + kind, r],
            device_id=peer[name],
            device_id_type=MESH,
        )

    def do_d_in(r):
        def d_in_part(n):
            cols = aligned(n, 256)
            part = mm_t(wi[pl.ds(512 * r, 512)], wk[cols]) + mm_t(
                wi[pl.ds(1536 + 512 * r, 512)], wv[cols]
            )
            for s in range(4):
                block = 4 * r + 2 * (s % 2) + s // 2
                wf[pl.ds(128 * block, 128), cols] = part[128 * s : 128 * s + 128].astype(BF16)
            mask_sums[n] = mask_sums[n] + fold(part * wide[:, r : r + 1])

        loop(3, d_in_part)
        d_in_copy(0, r).start()

    def d_in_pass(r):
        d_in_copy(0, r).wait()
        rows = aligned(4 * r + 2 * core + 1 - y, 128)
        wf[rows] = wf[rows] + d_in0[r, aligned(1 - y, 128)]
        d_in_copy(1, r).start()

    def own_part(i, acc):
        rows = aligned(i, 128)
        part = d_res[rows] + mm_t(q_own[rows], wq[...])
        d_res[rows] = part
        chosen = wide[aligned(me, 128)]
        chosen = jnp.where(i == 0, chosen[:, 0:1], jnp.where(i == 1, chosen[:, 1:2], chosen[:, 2:3]))
        return acc + fold(part * chosen)

    grad_copies = []

    def d_in_close(r):
        d_in_copy(1, r).wait()
        rows = pl.ds(128 * r, 128)
        value = (
            d_res[rows]
            + wf[aligned(4 * r + 2 * core + y, 128)].astype(F32)
            + d_in0[r, aligned(y, 128)].astype(F32)
            + d_in1[r].astype(F32)
        )
        chosen = wide[aligned(me, 128), r : r + 1] > 0.5
        d_att[rows] = jnp.where(chosen, 0.0, value).astype(BF16)
        copy = pltpu.make_async_copy(d_att.at[rows], grad_input.at[rows], local.at[18 + r])
        copy.start()
        grad_copies.append(copy)

    axes = (CORE, X, Y, ZLO, ZHI)

    def vector_copy(group, phase):
        sums, came = (vec, vec_came) if group == 0 else (late, late_came)
        return pltpu.make_async_remote_copy(
            src_ref=sums.at[phase],
            dst_ref=came.at[phase],
            send_sem=v_send.at[group, phase],
            recv_sem=v_recv.at[group, phase],
            device_id=peer[axes[phase]],
            device_id_type=MESH,
        )

    def vector_step(group, phase):
        vector_copy(group, phase).wait()
        sums, came = (vec, vec_came) if group == 0 else (late, late_came)
        sums[phase + 1] = sums[phase] + came[phase]
        if phase < 4:
            vector_copy(group, phase + 1).start()

    def do_late_sums():
        late[0] = jnp.zeros((8, 768), F32)
        mask_sum = jnp.concatenate([mask_sums[n] for n in range(3)], axis=1)
        all_sums = (
            lax.fori_loop(0, 3, own_part, mask_sum),
            fold(q_own[...].astype(F32)),
            lax.fori_loop(0, 12, value_sum, nothing),
        )
        for i, value in enumerate(all_sums):
            late[0, i : i + 1] = jnp.sum(value, 0, keepdims=True)
        vector_copy(1, 0).start()

    mine = (y, spot[ZHI], spot[ZLO], spot[X])

    def swap_copy(u):
        return pltpu.make_async_remote_copy(
            src_ref=units[u].own.at[mine],
            dst_ref=in5.at[u],
            send_sem=sends.at[u, 5],
            recv_sem=recvs.at[u, 5],
            device_id=peer[CORE],
            device_id_type=MESH,
        )

    def close(u):
        unit = units[u]
        unit.copy(4).wait()
        result = unit.own[mine].astype(F32) + unit.inbox[4][...].astype(F32)
        if INNER0 <= u < OUTPUT:
            i = u - INNER0
            out_inner[pl.ds(48 * (i % 2), 48), pl.ds(384 * (i // 2), 384)] = result
            return
        unit.own[mine] = result.astype(BF16)
        swap_copy(u).start()
        put_half(u, core, result)

    def put_half(u, side, value):
        value = jnp.where(core == 0, value[:, :192], pltpu.roll(value, 192, 1)[:, :192])
        if u < INNER0:
            out_outer[pl.ds(pl.multiple_of(side * 192 + u * 48, 48), 48)] = value
        else:
            target = (out_output, out_query, out_key, out_value)[u - OUTPUT]
            target[pl.ds(pl.multiple_of(side * 48, 48), 48)] = value

    def open_half(u):
        swap_copy(u).wait()
        put_half(u, 1 - core, in5[u].astype(F32))

    stages = {
        INNER: do_inner_grads,
        D_FIRST: do_d_first,
        FNB: do_first_norm_back,
        V1: lambda: vector_copy(0, 0).start(),
        DWO: do_output_grads,
        REFILL: refill_probs,
        DMIXED: lambda: loop(3, d_mixed_part),
        DWQ: do_query_grads,
        DWK: do_key_grads,
        DWV: do_value_grads,
        VEC: do_late_sums,
    }
    for r in range(3):
        stages[AB00 + 2 * r] = lambda r=r: do_attend_back(r, 0, 3)
        stages[AB01 + 2 * r] = lambda r=r: do_attend_back(r, 3, 6)
        stages[D_HIDDEN0 + r] = lambda r=r: span_loop(4 * r, 4 * r + 4, d_hidden_units)
        stages[DIN0 + r] = lambda r=r: do_d_in(r)
    count = {}
    for name in PLAN:
        if name in stages:
            stages[name]()
            continue
        turn = count[name] = count.get(name, -1) + 1
        if name <= VALUE:
            if turn < 4:
                units[name].step()
                if turn == 0 and STARTS.index(name) < SLOTS:
                    free_slot()
            elif turn == 4:
                close(name)
            else:
                open_half(name)
        elif name in (W1, W2):
            vector_step(name - W1, turn)
        elif name < DY0:
            d_in_pass(name - DC0)
        else:
            d_in_close(name - DY0)
    out_vectors[...] = vec[5]
    out_vectors[0:3] = late[5, 0:3]
    for copy in grad_copies:
        copy.wait()


def hand_out(*refs):
    sources, vectors, targets, rows = refs[:8], refs[8], refs[9:17], refs[17:27]
    for source, target in zip(sources[:7], targets[:7]):
        target[...] = source[...]
    targets[7][...] = sources[7][...].T
    for i, place in enumerate((0, 1, 2, 3, 4, 5, None, 10, 11, 12)):
        if place is not None:
            rows[i][...] = vectors[place]
    for j in range(4):
        rows[6][pl.ds(768 * j, 768)] = vectors[6 + j]


def fused_layer(
    hidden_in,
    cotangent,
    span_mask,
    lengths,
    repeats,
    mask_embedding,
    query_weight,
    query_bias,
    key_weight,
    value_weight,
    value_bias,
    output_weight,
    output_bias,
    mixing_gain,
    mixing_shift,
    inner_weight,
    inner_bias,
    outer_weight,
    outer_bias,
    final_gain,
    final_shift,
):
    vmem = pl.BlockSpec(memory_space=pltpu.VMEM)
    anywhere = pl.BlockSpec(memory_space=pl.ANY)
    scalars = pl.BlockSpec(memory_space=pltpu.SMEM)
    bf = lambda *shape: pltpu.VMEM(shape, BF16)
    fl = lambda *shape: pltpu.VMEM(shape, F32)
    dma = lambda *shape: pltpu.SemaphoreType.DMA(shape)
    shape = lambda dims, dtype: jax.ShapeDtypeStruct(dims, dtype)
    result = pl.pallas_call(
        layer_body,
        out_shape=[
            shape((384, 768), BF16),
            shape((384, 768), BF16),
            shape((9216, 256), BF16),
            shape((96, 192), F32),
            shape((96, 192), F32),
            shape((96, 192), F32),
            shape((96, 192), F32),
            shape((96, 768), F32),
            shape((384, 192), F32),
            shape((16, 768), F32),
        ],
        in_specs=[anywhere] * 8 + [vmem] + [anywhere] * 10 + [scalars, scalars],
        out_specs=[anywhere] * 3 + [vmem] * 7,
        scratch_shapes=[
            bf(3072, 768),
            bf(3072, 768),
            bf(768, 768),
            bf(768, 768),
            bf(768, 768),
            bf(768, 768),
            bf(13 * 768),
            fl(16, 768),
            bf(3, 512, 768),
            bf(3, 512, 768),
            bf(3, 512, 768),
            bf(384, 768),
            bf(384, 768),
            bf(9216, 256),
            bf(384, 768),
            fl(384, 768),
            fl(384, 1),
            fl(384, 768),
            fl(384, 768),
            bf(384, 768),
            bf(384, 768),
            pltpu.VMEM((4, 8, 128), jnp.int32),
            fl(512, 8),
            fl(12, 8, 256),
            fl(3, 8, 256),
            bf(12, 2, 2, 2, 2, 2, 48, 384),
            bf(SLOTS, 2, 2, 2, 2, 48, 384),
            bf(12, 2, 2, 2, 48, 384),
            bf(12, 2, 2, 48, 384),
            bf(12, 2, 48, 384),
            bf(12, 48, 384),
            bf(12, 48, 384),
            bf(3, 256, 768),
            bf(3, 128, 768),
            fl(6, 16, 768),
            fl(5, 16, 768),
            fl(6, 8, 768),
            fl(5, 8, 768),
            dma(12, 6),
            dma(12, 6),
            dma(5, 3),
            dma(5, 3),
            dma(3),
            dma(3),
            dma(2, 5),
            dma(2, 5),
            dma(31),
            pltpu.SemaphoreType.REGULAR,
        ],
        compiler_params=pltpu.CompilerParams(
            collective_id=1, has_side_effects=True, vmem_limit_bytes=63 * 2**20
        ),
        name="fused_layer",
    )(
        hidden_in,
        cotangent.reshape(384, 768),
        query_weight,
        key_weight,
        value_weight,
        output_weight,
        inner_weight,
        outer_weight,
        span_mask,
        mask_embedding,
        query_bias,
        value_bias,
        output_bias,
        mixing_gain,
        mixing_shift,
        inner_bias,
        outer_bias,
        final_gain,
        final_shift,
        lengths,
        repeats,
    )
    arrays, vectors = [result[0], result[1], *result[3:9]], result[9]
    wide_row = shape((768,), F32)
    handed = pl.pallas_call(
        hand_out,
        out_shape=[shape(v.shape, v.dtype) for v in arrays[:7]]
        + [shape((192, 384), F32)]
        + [wide_row] * 6
        + [shape((3072,), F32)]
        + [wide_row] * 3,
        in_specs=[vmem] * 9,
        out_specs=[vmem] * 18,
        name="hand_out",
    )(*arrays, vectors)
    layer_out, grad_input, g_query, g_key, g_value, g_output, g_inner, g_outer = handed[:8]
    g_mask, g_q_bias, g_v_bias, g_o_bias, g_gain, g_shift, g_inner_bias, *g_last = handed[8:]
    return (
        layer_out.reshape(3, 128, 768),
        grad_input.reshape(3, 128, 768),
        g_mask,
        g_query,
        g_q_bias,
        g_key,
        g_value,
        g_v_bias,
        g_output,
        g_o_bias,
        g_gain,
        g_shift,
        g_inner,
        g_inner_bias,
        g_outer.T,
        *g_last,
    )


def with_halo(x, sides, width):
    for axis, dim in sides:
        count, length = (lax.axis_size(axis), x.shape[dim])
        up = [(i, (i + 1) % count) for i in range(count - 1)]
        down = [(j, i) for i, j in up]
        last = lax.slice_in_dim(x, length - width, length, axis=dim)
        initial = lax.slice_in_dim(x, 0, width, axis=dim)
        before = lax.ppermute(last, axis, up)
        after = lax.ppermute(initial, axis, down)
        x = jnp.concatenate([before, x, after], axis=dim)
    return x


def layer_norm(inputs, gain, shift):
    center = inputs - jnp.mean(inputs, -1, keepdims=True)
    spread = jnp.mean(center * center, -1, keepdims=True)
    return center * lax.rsqrt(spread + 1e-05) * gain + shift


def linear(inputs, weight):
    return jnp.dot(inputs, weight, preferred_element_type=jnp.float32)


def linear_back(grads, weight):
    return lax.dot_general(
        grads, weight, (((1,), (1,)), ((), ())), preferred_element_type=jnp.float32
    )


def contract_rows(left, right):
    return lax.dot_general(
        left, right, (((0,), (0,)), ((), ())), preferred_element_type=jnp.float32
    )


def gelu_exact(inputs):
    return jax.nn.gelu(inputs, approximate=False)


def plain_layer(
    hidden_in,
    cotangent,
    span_mask,
    lengths,
    repeats,
    mask_embedding,
    query_weight,
    query_bias,
    key_weight,
    value_weight,
    value_bias,
    output_weight,
    output_bias,
    mixing_gain,
    mixing_shift,
    inner_weight,
    inner_bias,
    outer_weight,
    outer_bias,
    final_gain,
    final_shift,
):
    rows, stretch, width = hidden_in.shape
    whole = stretch * lax.axis_size("seq")
    scale = HEAD_DIM ** (-0.5)
    offset = lax.axis_index("seq") * stretch
    rim = with_halo(span_mask, (("seq", 1),), WIDEN)
    window = rim[:, 0:stretch]
    for shifted in range(1, 2 * WIDEN + 1):
        window = window + rim[:, shifted : shifted + stretch]
    widened = window > 0
    positions = offset + jnp.arange(stretch, dtype=jnp.int32)
    live = positions[None, :] < lengths[:, None]
    key_live = jnp.arange(whole, dtype=jnp.int32)[None, :] < lengths[:, None]
    masked_in = jnp.where(widened[..., None], mask_embedding[None, None, :], hidden_in)
    flat_in = masked_in.reshape(rows * stretch, width)
    queries = (linear(flat_in, query_weight) + query_bias.astype(jnp.float32)).astype(jnp.bfloat16)
    key_rows = linear(flat_in, key_weight).astype(jnp.bfloat16).reshape(rows, stretch, width)
    value_rows = (linear(flat_in, value_weight) + value_bias.astype(jnp.float32)).astype(
        jnp.bfloat16
    )
    value_rows = value_rows.reshape(rows, stretch, width)
    key_all, value_all = (
        lax.all_gather(key_rows, "seq", axis=1, tiled=True),
        lax.all_gather(value_rows, "seq", axis=1, tiled=True),
    )
    query_heads = queries.reshape(rows, stretch, HEADS, HEAD_DIM)

    def scores_of(key_full):
        key_heads = key_full.reshape(rows, whole, HEADS, HEAD_DIM)
        raw = jnp.einsum(
            "rqhd,rkhd->rhqk", query_heads, key_heads, preferred_element_type=jnp.float32
        )
        return jnp.where(key_live[:, None, None, :], raw * scale, -1e30)

    logits = scores_of(key_all)
    highest = jnp.max(logits, -1, keepdims=True)
    expd = jnp.exp(logits - highest)
    totals = jnp.sum(expd, -1, keepdims=True)
    log_total = highest + jnp.log(totals)
    probs_low = (expd / totals).astype(jnp.bfloat16)
    value_heads = value_all.reshape(rows, whole, HEADS, HEAD_DIM)
    mixed = jnp.einsum(
        "rhqk,rkhd->rqhd", probs_low, value_heads, preferred_element_type=jnp.float32
    )
    mixed = mixed.reshape(rows * stretch, width).astype(jnp.bfloat16)
    attended = linear(mixed, output_weight) + output_bias.astype(jnp.float32)
    residual_one = flat_in.astype(jnp.float32) + attended
    first, norm_back_one = jax.vjp(
        layer_norm, residual_one, mixing_gain.astype(jnp.float32), mixing_shift.astype(jnp.float32)
    )
    first_low = first.astype(jnp.bfloat16)
    inner = linear(first_low, inner_weight) + inner_bias.astype(jnp.float32)
    activated, gelu_back = jax.vjp(gelu_exact, inner)
    activated_low = activated.astype(jnp.bfloat16)
    outer = linear(activated_low, outer_weight) + outer_bias.astype(jnp.float32)
    final, norm_back_two = jax.vjp(
        layer_norm, first + outer, final_gain.astype(jnp.float32), final_shift.astype(jnp.float32)
    )
    layer_out = final.astype(jnp.bfloat16).reshape(rows, stretch, width)
    weighting = repeats.astype(jnp.float32)[:, None] * live.astype(jnp.float32)
    d_final = (cotangent.astype(jnp.float32) * weighting[:, :, None]).reshape(rows * stretch, width)
    d_two, d_final_gain, d_final_shift = norm_back_two(d_final)
    d_outer = d_two.astype(jnp.bfloat16)
    g_outer_weight = contract_rows(activated_low, d_outer)
    g_outer_bias = jnp.sum(d_outer.astype(jnp.float32), 0)
    (d_inner,) = gelu_back(linear_back(d_outer, outer_weight))
    d_inner = d_inner.astype(jnp.bfloat16)
    g_inner_weight = contract_rows(first_low, d_inner)
    g_inner_bias = jnp.sum(d_inner.astype(jnp.float32), 0)
    d_first = linear_back(d_inner, inner_weight) + d_two
    d_one, d_mixing_gain, d_mixing_shift = norm_back_one(d_first)
    d_attended = d_one.astype(jnp.bfloat16)
    g_output_weight = contract_rows(mixed, d_attended)
    g_output_bias = jnp.sum(d_attended.astype(jnp.float32), 0)
    d_mixed = linear_back(d_attended, output_weight).astype(jnp.bfloat16)
    d_mixed_heads = d_mixed.reshape(rows, stretch, HEADS, HEAD_DIM)
    key_back, value_back = (
        lax.all_gather(key_rows, "seq", axis=1, tiled=True),
        lax.all_gather(value_rows, "seq", axis=1, tiled=True),
    )
    probs = jnp.exp(scores_of(key_back) - log_total)
    probs_again = probs.astype(jnp.bfloat16)
    key_heads = key_back.reshape(rows, whole, HEADS, HEAD_DIM)
    value_heads = value_back.reshape(rows, whole, HEADS, HEAD_DIM)
    d_probs = jnp.einsum(
        "rqhd,rkhd->rhqk", d_mixed_heads, value_heads, preferred_element_type=jnp.float32
    )
    centered = d_probs - jnp.sum(probs * d_probs, -1, keepdims=True)
    d_raw = (probs * centered * scale).astype(jnp.bfloat16)
    d_queries = jnp.einsum("rhqk,rkhd->rqhd", d_raw, key_heads, preferred_element_type=jnp.float32)
    d_queries = d_queries.reshape(rows * stretch, width).astype(jnp.bfloat16)
    d_key_part = jnp.einsum(
        "rhqk,rqhd->rkhd", d_raw, query_heads, preferred_element_type=jnp.float32
    )
    d_value_part = jnp.einsum(
        "rhqk,rqhd->rkhd", probs_again, d_mixed_heads, preferred_element_type=jnp.float32
    )
    d_key_sum, d_value_sum = (
        lax.psum_scatter(
            d_key_part.reshape(rows, whole, width), "seq", scatter_dimension=1, tiled=True
        ),
        lax.psum_scatter(
            d_value_part.reshape(rows, whole, width), "seq", scatter_dimension=1, tiled=True
        ),
    )
    d_keys = d_key_sum.astype(jnp.bfloat16).reshape(rows * stretch, width)
    d_values = d_value_sum.astype(jnp.bfloat16).reshape(rows * stretch, width)
    g_query_weight = contract_rows(flat_in, d_queries)
    g_key_weight = contract_rows(flat_in, d_keys)
    g_value_weight = contract_rows(flat_in, d_values)
    g_query_bias = jnp.sum(d_queries.astype(jnp.float32), 0)
    g_value_bias = jnp.sum(d_values.astype(jnp.float32), 0)
    d_input = (
        d_one
        + linear_back(d_queries, query_weight)
        + linear_back(d_keys, key_weight)
        + linear_back(d_values, value_weight)
    ).reshape(rows, stretch, width)
    grad_input = jnp.where(widened[..., None], 0.0, d_input).astype(jnp.bfloat16)
    g_mask = jnp.sum(jnp.where(widened[..., None], d_input, 0.0), (0, 1))
    matrices = (
        g_query_weight,
        g_key_weight,
        g_value_weight,
        g_output_weight,
        g_inner_weight,
        g_outer_weight,
    )
    partial_sums = (
        lax.psum_scatter(matrices[0], "batch", scatter_dimension=0, tiled=True),
        lax.psum_scatter(matrices[1], "batch", scatter_dimension=0, tiled=True),
        lax.psum_scatter(matrices[2], "batch", scatter_dimension=0, tiled=True),
        lax.psum_scatter(matrices[3], "batch", scatter_dimension=0, tiled=True),
        lax.psum_scatter(matrices[4], "batch", scatter_dimension=0, tiled=True),
        lax.psum_scatter(matrices[5], "batch", scatter_dimension=0, tiled=True),
    )
    summed = (
        lax.psum_scatter(partial_sums[0], "seq", scatter_dimension=1, tiled=True),
        lax.psum_scatter(partial_sums[1], "seq", scatter_dimension=1, tiled=True),
        lax.psum_scatter(partial_sums[2], "seq", scatter_dimension=1, tiled=True),
        lax.psum_scatter(partial_sums[3], "seq", scatter_dimension=1, tiled=True),
        lax.psum_scatter(partial_sums[4], "seq", scatter_dimension=1, tiled=True),
        lax.psum_scatter(partial_sums[5], "seq", scatter_dimension=1, tiled=True),
    )
    vectors = lax.psum(
        (
            g_mask,
            g_query_bias,
            g_value_bias,
            g_output_bias,
            d_mixing_gain,
            d_mixing_shift,
            g_inner_bias,
            g_outer_bias,
            d_final_gain,
            d_final_shift,
        ),
        ("batch", "seq"),
    )
    return (
        layer_out,
        grad_input,
        vectors[0],
        summed[0],
        vectors[1],
        summed[1],
        summed[2],
        vectors[2],
        summed[3],
        vectors[3],
        vectors[4],
        vectors[5],
        summed[4],
        vectors[6],
        summed[5],
        vectors[7],
        vectors[8],
        vectors[9],
    )


def solution(mesh):
    fused = mesh.shape["batch"] == 8 and mesh.shape["seq"] == 4
    return jax.shard_map(
        fused_layer if fused else plain_layer,
        mesh=mesh,
        in_specs=(
            P("batch", "seq", None),
            P("batch", "seq", None),
            P("batch", "seq"),
            P("batch"),
            P("batch"),
            P(),
            P(),
            P(),
            P(),
            P(),
            P(),
            P(),
            P(),
            P(),
            P(),
            P(),
            P(),
            P(),
            P(),
            P(),
            P(),
        ),
        out_specs=(
            P("batch", "seq", None),
            P("batch", "seq", None),
            P(),
            P("batch", "seq"),
            P(),
            P("batch", "seq"),
            P("batch", "seq"),
            P(),
            P("batch", "seq"),
            P(),
            P(),
            P(),
            P("batch", "seq"),
            P(),
            P("batch", "seq"),
            P(),
            P(),
            P(),
        ),
        check_vma=False,
    )
```

```python
import jax
import jax.numpy as jnp
from jax import lax
from jax.experimental import pallas as pl
from jax.experimental.pallas import tpu as pltpu
from jax.sharding import PartitionSpec as P

HEADS = 12
HEAD_DIM = 64
WIDEN = 5

MESH = pl.DeviceIdType.MESH
F32 = jnp.float32
BF16 = jnp.bfloat16
ROOT_HALF = 0.7071067811865476
DENSITY = 0.3989422804014327


def mm(a, b):
    return jnp.dot(a, b, preferred_element_type=F32)


def mm_t(a, b):
    return lax.dot_general(a, b, (((1,), (1,)), ((), ())), preferred_element_type=F32)


def mm_tl(a, b):
    return lax.dot_general(a, b, (((0,), (0,)), ((), ())), preferred_element_type=F32)


def fold(v):
    return jnp.sum(v.reshape(v.shape[0] // 8, 8, v.shape[1]), 0)


def loop(count, body, unroll=1):
    def step(i, carry):
        body(i)
        return carry

    lax.fori_loop(0, count, step, 0, unroll=unroll)


def span_loop(first, last, body, unroll=1):
    def step(i, carry):
        body(i)
        return carry

    lax.fori_loop(first, last, step, 0, unroll=unroll)


def aligned(i, size):
    return pl.ds(pl.multiple_of(i * size, size), size)


def places():
    b, s = lax.axis_index("batch"), lax.axis_index("seq")
    x, zlo, zhi = lax.rem(b, 2), lax.rem(b // 2, 2), b // 4
    core, y = lax.rem(s, 2), s // 2
    spot = {CORE: core, X: x, Y: y, ZLO: zlo, ZHI: zhi}
    peer = {
        CORE: (b, s + 1 - 2 * core),
        Y: (b, s + 2 - 4 * y),
        X: (b + 1 - 2 * x, s),
        ZLO: (b + 2 - 4 * zlo, s),
        ZHI: (b + 4 - 8 * zhi, s),
        FAR: (b, 3 - s),
    }
    return spot, peer


class Unit:
    def __init__(self, order, both, inbox, sends, recvs, spot, peer):
        self.order, self.both, self.inbox = order, both, inbox
        self.sends, self.recvs, self.spot, self.peer = sends, recvs, spot, peer
        self.own = both.at[spot[CORE]]
        self.phase = 0

    def where(self, phase, stays):
        done, axis = self.order[: phase - 1], self.order[phase - 1]
        place = []
        for name in (Y, ZHI, ZLO, X):
            side = self.spot[name]
            if name == axis:
                place.append(side if stays else 1 - side)
            else:
                place.append(side if name in done else slice(None))
        return tuple(place)

    def copy(self, phase):
        if phase == 0:
            axis, source = CORE, self.both.at[1 - self.spot[CORE]]
        else:
            axis, source = self.order[phase - 1], self.own.at[self.where(phase, False)]
        return pltpu.make_async_remote_copy(
            src_ref=source,
            dst_ref=self.inbox[phase],
            send_sem=self.sends.at[phase],
            recv_sem=self.recvs.at[phase],
            device_id=self.peer[axis],
            device_id_type=MESH,
        )

    def start(self):
        self.copy(0).start()

    def step(self):
        phase = self.phase
        self.copy(phase).wait()
        came = self.inbox[phase]
        target = self.own if phase == 0 else self.own.at[self.where(phase, True)]
        lead = 4 - phase

        def body(n):
            place = tuple(lax.rem(n // 2 ** (lead - 1 - i), 2) for i in range(lead))
            target[place] = target[place] + came[place]

        loop(2**lead, body, min(4, 2**lead))
        self.phase = phase + 1
        self.copy(self.phase).start()


CORE, X, Y, ZLO, ZHI, FAR = range(6)
OUTER0, OUTER1, OUTER2, OUTER3, INNER0, INNER1, INNER2, INNER3, OUTPUT, QUERY, KEY, VALUE = range(0, 12)
(
    D_HIDDEN0, D_HIDDEN1, D_HIDDEN2, INNER, D_FIRST, FNB, V1, DWO,
    REFILL, DMIXED, DWQ, DWK, DWV, VEC, AB00, AB01,
    AB10, AB11, AB20, AB21, DIN0, DIN1, DIN2,
) = range(12, 35)
W1, W2, DC0, DC1, DC2, DY0, DY1, DY2 = range(35, 43)
STARTS = (
    OUTER0, OUTER1, OUTER2, OUTER3, INNER0, INNER1,
    INNER2, INNER3, OUTPUT, KEY, QUERY, VALUE,
)
ORDERS = {
    OUTER0: (ZLO, Y, ZHI, X),
    OUTER1: (Y, X, ZLO, ZHI),
    OUTER2: (X, ZLO, Y, ZHI),
    OUTER3: (ZLO, Y, ZHI, X),
    INNER0: (X, Y, ZLO, ZHI),
    INNER1: (ZLO, Y, X, ZHI),
    INNER2: (X, Y, ZLO, ZHI),
    INNER3: (Y, ZLO, ZHI, X),
    OUTPUT: (X, Y, ZLO, ZHI),
    KEY: (X, ZLO, ZHI, Y),
    QUERY: (Y, X, ZLO, ZHI),
    VALUE: (X, ZLO, Y, ZHI),
}
PLAN = (
    D_HIDDEN0, D_HIDDEN1, OUTER0, D_HIDDEN2, OUTER1, OUTER2, INNER, OUTER3,
    D_FIRST, REFILL, FNB, INNER0, OUTER0, INNER1, OUTER1, OUTER2,
    INNER2, V1, DWO, INNER3, W1, DMIXED, OUTER3, OUTER0,
    AB00, OUTPUT, AB01, INNER0, AB10, OUTER1, INNER3, INNER1,
    AB11, OUTER2, AB20, OUTER3, AB21, INNER2, OUTER0, W1,
    OUTER1, INNER0, DWK, INNER3, INNER1, DWQ, DWV, KEY,
    OUTER2, OUTPUT, OUTER1, QUERY, INNER2, OUTER0, OUTER3, INNER0,
    DIN0, OUTER0, W1, OUTER1, INNER1, DIN1, VALUE, INNER3,
    OUTER2, INNER2, DC0, OUTPUT, DIN2, OUTER2, W1, KEY,
    INNER0, DC1, OUTER3, VEC, INNER1, INNER2, OUTER3, QUERY,
    DC2, OUTPUT, W2, W1, VALUE, DY0, INNER3, KEY,
    OUTPUT, QUERY, W2, OUTPUT, DY1, VALUE, KEY, DY2,
    W2, QUERY, VALUE, W2, KEY, KEY, QUERY, VALUE,
    QUERY, W2, VALUE,
)
SLOTS = 6
ROOMS = (0, 2, 1)


def layer_body(
    hidden,
    cotangent,
    query_weight,
    key_weight,
    value_weight,
    output_weight,
    inner_weight,
    outer_weight,
    span,
    mask_embedding,
    query_bias,
    value_bias,
    output_bias,
    mixing_gain,
    mixing_shift,
    inner_bias,
    outer_bias,
    final_gain,
    final_shift,
    lengths,
    repeats,
    layer_out,
    grad_input,
    probs_out,
    out_query,
    out_key,
    out_value,
    out_output,
    out_inner,
    out_outer,
    out_vectors,
    wi,
    wf,
    wq,
    wk,
    wv,
    wo,
    packed,
    params,
    x_all,
    k_all,
    v_all,
    q_own,
    mixed,
    region,
    first_low,
    norm_one,
    spread_one,
    total,
    d_res,
    d_outer,
    d_att,
    masks,
    wide,
    inner_sums,
    mask_sums,
    grads,
    in0,
    in1,
    in2,
    in3,
    in4,
    in5,
    d_in0,
    d_in1,
    vec,
    vec_came,
    late,
    late_came,
    sends,
    recvs,
    x_send,
    x_recv,
    m_send,
    m_recv,
    v_send,
    v_recv,
    local,
    credit,
):
    spot, peer = places()
    core, y = spot[CORE], spot[Y]
    me = 2 * y + core
    sibling = 2 * y + 1 - core
    across = 2 * (1 - y) + core

    names = (CORE, X, Y, ZLO, ZHI, FAR)
    barrier = pltpu.get_barrier_semaphore()
    for name in names:
        pl.semaphore_signal(barrier, inc=1, device_id=peer[name], device_id_type=MESH)

    weight_loads = {}

    def load(name, number, source, target):
        copy = pltpu.make_async_copy(source, target, local.at[number])
        copy.start()
        weight_loads[name] = copy

    load("hidden", 0, hidden, x_all.at[:, aligned(me, 128)])
    load("key", 1, key_weight, wk)
    load("value", 2, value_weight, wv)
    load("query", 3, query_weight, wq)

    pl.semaphore_wait(barrier, len(names))

    masks[me] = jnp.zeros((8, 128), jnp.int32)
    masks[me, 0:3] = span[...]
    mask_copies = []
    for i, name in enumerate((CORE, Y, FAR)):
        copy = pltpu.make_async_remote_copy(
            src_ref=masks.at[me],
            dst_ref=masks.at[me],
            send_sem=m_send.at[i],
            recv_sem=m_recv.at[i],
            device_id=peer[name],
            device_id_type=MESH,
        )
        copy.start()
        mask_copies.append(copy)

    def x_copy(kind, r):
        source = hidden.at[r] if kind < 2 else x_all.at[r, aligned(across, 128)]
        slot = me if kind < 2 else across
        return pltpu.make_async_remote_copy(
            src_ref=source,
            dst_ref=x_all.at[r, aligned(slot, 128)],
            send_sem=x_send.at[kind, r],
            recv_sem=x_recv.at[kind, r],
            device_id=peer[Y if kind == 0 else CORE],
            device_id_type=MESH,
        )

    for r in range(3):
        x_copy(0, r).start()
        x_copy(1, r).start()

    vectors = (
        (mask_embedding, 0),
        (query_bias, 1),
        (value_bias, 2),
        (output_bias, 3),
        (mixing_gain, 4),
        (mixing_shift, 5),
        (inner_bias, 6),
        (outer_bias, 10),
        (final_gain, 11),
        (final_shift, 12),
    )
    vector_loads = []
    for i, (vector, place) in enumerate(vectors):
        target = packed.at[pl.ds(768 * place, vector.shape[0])]
        copy = pltpu.make_async_copy(vector, target, local.at[21 + i])
        copy.start()
        vector_loads.append(copy)
    for copy in vector_loads:
        copy.wait()
    for i in range(13):
        params[i : i + 1] = packed[pl.ds(768 * i, 768)].astype(F32).reshape(1, 768)

    for copy in mask_copies:
        copy.wait()
    span_all = jnp.concatenate([masks[s].astype(F32) for s in range(4)], axis=1)
    lane = lax.broadcasted_iota(jnp.int32, span_all.shape, 1)
    window = span_all
    for d in range(1, WIDEN + 1):
        window = jnp.maximum(window, jnp.where(lane >= d, pltpu.roll(span_all, d, 1), 0.0))
        window = jnp.maximum(
            window, jnp.where(lane < 512 - d, pltpu.roll(span_all, 512 - d, 1), 0.0)
        )
    wide[...] = window.T

    half = lax.broadcasted_iota(jnp.int32, (128, 128), 1) < HEAD_DIM
    zero = jnp.zeros((128, 128), BF16)

    def stacked(pair):
        return jnp.concatenate([jnp.where(half, pair, zero), jnp.where(half, zero, pair)], 0)

    def unstacked(both):
        return jnp.where(half, both[:128], both[128:])

    mask_row = params[0:1]
    spills = []

    def put_mask(r, slot):
        rows = aligned(slot, 128)
        chosen = wide[rows, r : r + 1] > 0.5
        kept = x_all[r, rows].astype(F32)
        x_all[r, rows] = jnp.where(chosen, mask_row, kept).astype(BF16)

    def project(pieces, with_queries):
        inputs = jnp.concatenate([x_all[r, aligned(slot, 128)] for r, slot in pieces], 0)

        def part(n):
            cols = aligned(n, 256)
            keys = mm(inputs, wk[:, cols]).astype(BF16)
            values = (mm(inputs, wv[:, cols]) + params[2:3, cols]).astype(BF16)
            for i, (r, slot) in enumerate(pieces):
                k_all[r, aligned(slot, 128), cols] = keys[128 * i : 128 * i + 128]
                v_all[r, aligned(slot, 128), cols] = values[128 * i : 128 * i + 128]
            if with_queries:
                q_own[:, cols] = (mm(inputs, wq[:, cols]) + params[1:2, cols]).astype(BF16)

        loop(3, part, 3)

    weight_loads["hidden"].wait()
    for r in range(3):
        put_mask(r, me)
    for name in ("key", "value", "query"):
        weight_loads[name].wait()
    load("output", 4, output_weight, wo)
    for j in range(4):
        load(j, 5 + j, inner_weight.at[:, pl.ds(768 * j, 768)], wi.at[pl.ds(768 * j, 768)])
    load("outer", 9, outer_weight, wf)
    load("cotangent", 10, cotangent, d_outer)
    project([(r, me) for r in range(3)], True)
    for r in range(3):
        x_copy(1, r).wait()
        put_mask(r, sibling)
    project([(r, sibling) for r in range(3)], False)
    x_copy(0, 0).wait_recv()
    x_copy(2, 0).start()
    for r in range(3):
        x_copy(2, r).wait()
        put_mask(r, across)
        put_mask(r, 3 - me)
        project([(r, across), (r, 3 - me)], False)
        key_live = lax.broadcasted_iota(jnp.int32, (1, 512), 1) < lengths[r]

        def attend(p):
            cols = aligned(p, 128)
            queries = stacked(q_own[pl.ds(128 * r, 128), cols] * BF16(HEAD_DIM**-0.5))
            logits = mm_t(queries, k_all[r, :, cols])
            logits = jnp.where(key_live, logits, -1e30)
            expd = jnp.exp(logits - jnp.max(logits, -1, keepdims=True))
            probs = (expd * (1.0 / jnp.sum(expd, -1, keepdims=True))).astype(BF16)
            base = ROOMS[r] * 6 + p
            region[aligned(2 * base, 256)] = probs[:, :256]
            region[aligned(2 * base + 1, 256)] = probs[:, 256:]
            out = mm(probs, v_all[r, :, cols])
            mixed[pl.ds(128 * r, 128), cols] = unstacked(out).astype(BF16)

        def attend_three(i):
            for p in range(3):
                attend(3 * i + p)
            if r < 2:

                @pl.when(i == 0)
                def _():
                    x_copy(0, r + 1).wait_recv()
                    x_copy(2, r + 1).start()

        loop(2, attend_three)
        rows = pl.ds(3072 * ROOMS[r], 3072)
        spill = pltpu.make_async_copy(region.at[rows], probs_out.at[rows], local.at[11 + r])
        spill.start()
        spills.append(spill)

    for r in range(3):
        x_copy(0, r).wait_send()
    weight_loads["output"].wait()

    def first_norm(i):
        rows = aligned(i, 128)
        attended = mm(mixed[rows], wo[...]) + params[3:4]
        value = x_all[i, aligned(me, 128)].astype(F32) + attended
        center = value - jnp.mean(value, -1, keepdims=True)
        scale = lax.rsqrt(jnp.mean(center * center, -1, keepdims=True) + 1e-5)
        norm = center * scale
        norm_one[rows] = norm
        spread_one[rows] = scale
        first_low[rows] = (norm * params[4:5] + params[5:6]).astype(BF16)

    loop(3, first_norm, 3)
    spills[0].wait()
    spills[1].wait()
    for j in range(4):
        weight_loads[j].wait()

    def hidden_units(j):
        inner = mm(
            first_low[...], wi[pl.ds((j // 3) * 768, 768), aligned(lax.rem(j, 3), 256)]
        ) + params[pl.ds(6 + j // 3, 1), aligned(lax.rem(j, 3), 256)]
        below = 0.5 * (1.0 + lax.erf(inner * ROOT_HALF))
        slope = below + inner * (DENSITY * jnp.exp(-0.5 * inner * inner))
        region[aligned(j, 384)] = (inner * below).astype(BF16)
        region[aligned(23 - j, 384)] = slope.astype(BF16)

    span_loop(0, 8, hidden_units, 4)
    spills[2].wait()
    span_loop(8, 12, hidden_units, 4)
    weight_loads["outer"].wait()
    weight_loads["cotangent"].wait()

    def panels(which):
        return jnp.concatenate([region[pl.ds(384 * j, 384)] for j in which], axis=1)

    def project_out(n):
        cols = aligned(n, 256)
        total[:, cols] = mm(panels(range(12)), wf[:, cols])

    loop(3, project_out, 3)

    def last_norm(i, sums):
        rows = aligned(i, 64)
        first = norm_one[rows] * params[4:5] + params[5:6]
        value = first + (total[rows] + params[10:11])
        center = value - jnp.mean(value, -1, keepdims=True)
        scale = lax.rsqrt(jnp.mean(center * center, -1, keepdims=True) + 1e-5)
        norm = center * scale
        d_att[rows] = (norm * params[11:12] + params[12:13]).astype(BF16)
        r = i // 2
        position = lax.broadcasted_iota(jnp.int32, (64, 1), 0) + lax.rem(i, 2) * 64 + me * 128
        weight = jnp.where(position < lengths[r], repeats[r].astype(F32), 0.0)
        d_final = d_outer[rows].astype(F32) * weight
        d_norm = d_final * params[11:12]
        d_two = scale * (
            d_norm
            - jnp.mean(d_norm, -1, keepdims=True)
            - norm * jnp.mean(d_norm * norm, -1, keepdims=True)
        )
        d_res[rows] = d_two
        low = d_two.astype(BF16)
        d_outer[rows] = low
        return (
            sums[0] + fold(d_final * norm),
            sums[1] + fold(d_final),
            sums[2] + fold(low.astype(F32)),
        )

    nothing = jnp.zeros((8, 768), F32)

    def put_sum(row, value):
        vec[0, row : row + 1] = jnp.sum(value, 0, keepdims=True)

    vec[0] = jnp.zeros((16, 768), F32)
    sums = lax.fori_loop(0, 6, last_norm, (nothing, nothing, nothing), unroll=2)
    put_sum(11, sums[0])
    put_sum(12, sums[1])
    put_sum(10, sums[2])
    out_copy = pltpu.make_async_copy(
        d_att, layer_out, local.at[14]
    )
    out_copy.start()

    units = [None] * 12
    for turn, u in enumerate(STARTS):
        inbox = [in0.at[turn % SLOTS], in1.at[u], in2.at[u], in3.at[u], in4.at[u]]
        units[u] = Unit(ORDERS[u], grads.at[u], inbox, sends.at[u], recvs.at[u], spot, peer)

    def start_unit(name):
        if STARTS.index(name) >= SLOTS:
            claim_slot()
        units[name].start()

    def free_slot():
        pl.semaphore_signal(credit, inc=1, device_id=peer[CORE], device_id_type=MESH)

    def claim_slot():
        pl.semaphore_wait(credit, 1)

    def outer_grads(z):
        for x in range(2):
            cols = [region[pl.ds(pl.multiple_of((3 * z + j) * 384, 384), 384)] for j in range(3)]
            part = jnp.concatenate(cols, axis=1)[:, 384 * x : 384 * x + 384]
            grad = mm_tl(part, d_outer[...]).astype(BF16)
            for h in range(2):
                for i in range(4):
                    for side in range(2):
                        rows = (h * 4 + i) * 48
                        grads[OUTER0 + i, h, side, z // 2, lax.rem(z, 2), x] = grad[
                            rows : rows + 48, side * 384 : side * 384 + 384
                        ]

    loop(4, outer_grads, 4)
    for i in range(4):
        start_unit(OUTER0 + i)

    def d_hidden_units(j):
        d_act = mm_t(d_outer[...], wf[aligned(j, 256)])
        place = aligned(23 - j, 384)
        low = (d_act * region[place].astype(F32)).astype(BF16)
        region[place] = low
        inner_sums[j] = fold(low.astype(F32))

    def inner_grads(s):
        cols = [region[pl.ds(pl.multiple_of((23 - 3 * s - j) * 384, 384), 384)] for j in range(3)]
        grad = mm_tl(first_low[...], jnp.concatenate(cols, axis=1)).astype(BF16)
        for b in range(8):
            for i in range(4):
                rows, side = 96 * b + 48 * (i % 2), 384 * (i // 2)
                grads[
                    INNER0 + i, lax.rem(s, 2), s // 2, b // 4, (b // 2) % 2, b % 2
                ] = grad[rows : rows + 48, side : side + 384]

    def do_inner_grads():
        loop(4, inner_grads, 2)
        for i in range(4):
            start_unit(INNER0 + i)

    def d_first_part(n):
        cols = aligned(n, 256)
        acc = None
        for s in range(4):
            d_inner = panels(range(23 - 3 * s, 20 - 3 * s, -1))
            term = mm_t(d_inner, wi[pl.ds(pl.multiple_of(s * 768 + n * 256, 256), 256)])
            acc = term if acc is None else acc + term
        total[:, cols] = acc

    refills = []

    def do_d_first():
        loop(3, d_first_part, 3)
        for j in range(12):
            vec[0, 6 + j // 3 : 7 + j // 3, (j % 3) * 256 : (j % 3) * 256 + 256] = jnp.sum(
                inner_sums[j], 0, keepdims=True
            )

    def refill_probs():
        for r in range(3):
            rows = pl.ds(3072 * ROOMS[r], 3072)
            refill = pltpu.make_async_copy(probs_out.at[rows], region.at[rows], local.at[15 + r])
            refill.start()
            refills.append(refill)

    def first_norm_back(i, sums):
        rows = aligned(i, 64)
        d_first = total[rows] + d_res[rows]
        norm = norm_one[rows]
        d_norm = d_first * params[4:5]
        d_one = spread_one[rows] * (
            d_norm
            - jnp.mean(d_norm, -1, keepdims=True)
            - norm * jnp.mean(d_norm * norm, -1, keepdims=True)
        )
        d_res[rows] = d_one
        low = d_one.astype(BF16)
        d_att[rows] = low
        return (
            sums[0] + fold(d_first * norm),
            sums[1] + fold(d_first),
            sums[2] + fold(low.astype(F32)),
        )

    def do_first_norm_back():
        out_copy.wait()
        sums = lax.fori_loop(0, 6, first_norm_back, (nothing, nothing, nothing), unroll=2)
        put_sum(4, sums[0])
        put_sum(5, sums[1])
        put_sum(3, sums[2])

    def square_grads(u, left, right):
        for m in range(2):
            grad = mm_tl(left(m), right).astype(BF16)
            for b in range(4):
                for h in range(2):
                    for side in range(2):
                        rows = b * 96 + h * 48
                        grads[u, h, side, m, b // 2, b % 2] = grad[
                            rows : rows + 48, side * 384 : side * 384 + 384
                        ]
        start_unit(u)

    def do_output_grads():
        square_grads(OUTPUT, lambda m: mixed[:, 384 * m : 384 * m + 384], d_att[...])

    def d_mixed_part(i):
        rows = aligned(i, 128)
        mixed[rows] = mm_t(d_att[rows], wo[...]).astype(BF16)

    def do_attend_back(r, first, last):
        if first == 0:
            refills[r].wait()

        def attend_back(p):
            cols = aligned(p, 128)
            own_rows = pl.ds(128 * r, 128)
            base = ROOMS[r] * 6 + p
            queries = stacked(q_own[own_rows, cols] * BF16(HEAD_DIM**-0.5))
            d_mix = stacked(mixed[own_rows, cols])
            low_probs = jnp.concatenate(
                [region[aligned(2 * base, 256)], region[aligned(2 * base + 1, 256)]], axis=1
            )
            d_probs = mm_t(d_mix, v_all[r, :, cols])
            probs = low_probs.astype(F32)
            weighted = probs * d_probs
            d_raw = (weighted - probs * jnp.sum(weighted, -1, keepdims=True)).astype(BF16)
            d_query = mm(d_raw, k_all[r, :, cols]) * HEAD_DIM**-0.5
            q_own[own_rows, cols] = unstacked(d_query).astype(BF16)
            wi[pl.ds(512 * r, 512), cols] = mm_tl(d_raw, queries).astype(BF16)
            wi[pl.ds(1536 + 512 * r, 512), cols] = mm_tl(low_probs, d_mix).astype(BF16)

        span_loop(first, last, attend_back)

    def own_inputs(m):
        return jnp.concatenate(
            [x_all[r, aligned(me, 128), pl.ds(384 * m, 384)] for r in range(3)], 0
        )

    def all_inputs(m):
        return jnp.concatenate([x_all[r, :, pl.ds(384 * m, 384)] for r in range(3)], 0)

    def do_query_grads():
        square_grads(QUERY, own_inputs, q_own[...])

    def do_key_grads():
        square_grads(KEY, all_inputs, wi[pl.ds(0, 1536)])

    def do_value_grads():
        square_grads(VALUE, all_inputs, wi[pl.ds(1536, 1536)])

    def value_sum(i, acc):
        return acc + fold(wi[pl.ds(pl.multiple_of(1536 + i * 128, 128), 128)].astype(F32))

    mask_sums[...] = jnp.zeros((3, 8, 256), F32)

    def d_in_copy(kind, r):
        if kind == 0:
            source = wf.at[aligned(2 * r + 1 - core, 256)]
            target, name = d_in0.at[r], CORE
        else:
            source = wf.at[aligned(4 * r + 2 * core + 1 - y, 128)]
            target, name = d_in1.at[r], Y
        return pltpu.make_async_remote_copy(
            src_ref=source,
            dst_ref=target,
            send_sem=x_send.at[3 + kind, r],
            recv_sem=x_recv.at[3 + kind, r],
            device_id=peer[name],
            device_id_type=MESH,
        )

    def do_d_in(r):
        def d_in_part(n):
            cols = aligned(n, 256)
            part = mm_t(wi[pl.ds(512 * r, 512)], wk[cols]) + mm_t(
                wi[pl.ds(1536 + 512 * r, 512)], wv[cols]
            )
            for s in range(4):
                block = 4 * r + 2 * (s % 2) + s // 2
                wf[pl.ds(128 * block, 128), cols] = part[128 * s : 128 * s + 128].astype(BF16)
            mask_sums[n] = mask_sums[n] + fold(part * wide[:, r : r + 1])

        loop(3, d_in_part)
        d_in_copy(0, r).start()

    def d_in_pass(r):
        d_in_copy(0, r).wait()
        rows = aligned(4 * r + 2 * core + 1 - y, 128)
        wf[rows] = wf[rows] + d_in0[r, aligned(1 - y, 128)]
        d_in_copy(1, r).start()

    def own_part(i, acc):
        rows = aligned(i, 128)
        part = d_res[rows] + mm_t(q_own[rows], wq[...])
        d_res[rows] = part
        chosen = wide[aligned(me, 128)]
        chosen = jnp.where(i == 0, chosen[:, 0:1], jnp.where(i == 1, chosen[:, 1:2], chosen[:, 2:3]))
        return acc + fold(part * chosen)

    grad_copies = []

    def d_in_close(r):
        d_in_copy(1, r).wait()
        rows = pl.ds(128 * r, 128)
        value = (
            d_res[rows]
            + wf[aligned(4 * r + 2 * core + y, 128)].astype(F32)
            + d_in0[r, aligned(y, 128)].astype(F32)
            + d_in1[r].astype(F32)
        )
        chosen = wide[aligned(me, 128), r : r + 1] > 0.5
        d_att[rows] = jnp.where(chosen, 0.0, value).astype(BF16)
        copy = pltpu.make_async_copy(d_att.at[rows], grad_input.at[rows], local.at[18 + r])
        copy.start()
        grad_copies.append(copy)

    axes = (CORE, X, Y, ZLO, ZHI)

    def vector_copy(group, phase):
        sums, came = (vec, vec_came) if group == 0 else (late, late_came)
        return pltpu.make_async_remote_copy(
            src_ref=sums.at[phase],
            dst_ref=came.at[phase],
            send_sem=v_send.at[group, phase],
            recv_sem=v_recv.at[group, phase],
            device_id=peer[axes[phase]],
            device_id_type=MESH,
        )

    def vector_step(group, phase):
        vector_copy(group, phase).wait()
        sums, came = (vec, vec_came) if group == 0 else (late, late_came)
        sums[phase + 1] = sums[phase] + came[phase]
        if phase < 4:
            vector_copy(group, phase + 1).start()

    def do_late_sums():
        late[0] = jnp.zeros((8, 768), F32)
        mask_sum = jnp.concatenate([mask_sums[n] for n in range(3)], axis=1)
        all_sums = (
            lax.fori_loop(0, 3, own_part, mask_sum),
            fold(q_own[...].astype(F32)),
            lax.fori_loop(0, 12, value_sum, nothing),
        )
        for i, value in enumerate(all_sums):
            late[0, i : i + 1] = jnp.sum(value, 0, keepdims=True)
        vector_copy(1, 0).start()

    mine = (y, spot[ZHI], spot[ZLO], spot[X])

    def swap_copy(u):
        return pltpu.make_async_remote_copy(
            src_ref=units[u].own.at[mine],
            dst_ref=in5.at[u],
            send_sem=sends.at[u, 5],
            recv_sem=recvs.at[u, 5],
            device_id=peer[CORE],
            device_id_type=MESH,
        )

    def close(u):
        unit = units[u]
        unit.copy(4).wait()
        result = unit.own[mine].astype(F32) + unit.inbox[4][...].astype(F32)
        if INNER0 <= u < OUTPUT:
            i = u - INNER0
            out_inner[pl.ds(48 * (i % 2), 48), pl.ds(384 * (i // 2), 384)] = result
            return
        unit.own[mine] = result.astype(BF16)
        swap_copy(u).start()
        put_half(u, core, result)

    def put_half(u, side, value):
        value = jnp.where(core == 0, value[:, :192], pltpu.roll(value, 192, 1)[:, :192])
        if u < INNER0:
            out_outer[pl.ds(pl.multiple_of(side * 192 + u * 48, 48), 48)] = value
        else:
            target = (out_output, out_query, out_key, out_value)[u - OUTPUT]
            target[pl.ds(pl.multiple_of(side * 48, 48), 48)] = value

    def open_half(u):
        swap_copy(u).wait()
        put_half(u, 1 - core, in5[u].astype(F32))

    stages = {
        INNER: do_inner_grads,
        D_FIRST: do_d_first,
        FNB: do_first_norm_back,
        V1: lambda: vector_copy(0, 0).start(),
        DWO: do_output_grads,
        REFILL: refill_probs,
        DMIXED: lambda: loop(3, d_mixed_part),
        DWQ: do_query_grads,
        DWK: do_key_grads,
        DWV: do_value_grads,
        VEC: do_late_sums,
    }
    for r in range(3):
        stages[AB00 + 2 * r] = lambda r=r: do_attend_back(r, 0, 3)
        stages[AB01 + 2 * r] = lambda r=r: do_attend_back(r, 3, 6)
        stages[D_HIDDEN0 + r] = lambda r=r: span_loop(4 * r, 4 * r + 4, d_hidden_units, 2)
        stages[DIN0 + r] = lambda r=r: do_d_in(r)
    count = {}
    for name in PLAN:
        if name in stages:
            stages[name]()
            continue
        turn = count[name] = count.get(name, -1) + 1
        if name <= VALUE:
            if turn < 4:
                units[name].step()
                if turn == 0 and STARTS.index(name) < SLOTS:
                    free_slot()
            elif turn == 4:
                close(name)
            else:
                open_half(name)
        elif name in (W1, W2):
            vector_step(name - W1, turn)
        elif name < DY0:
            d_in_pass(name - DC0)
        else:
            d_in_close(name - DY0)
    out_vectors[...] = vec[5]
    out_vectors[0:3] = late[5, 0:3]
    for copy in grad_copies:
        copy.wait()


def hand_out(*refs):
    sources, vectors, targets, rows = refs[:8], refs[8], refs[9:17], refs[17:27]
    for source, target in zip(sources[:7], targets[:7]):
        target[...] = source[...]
    targets[7][...] = sources[7][...].T
    for i, place in enumerate((0, 1, 2, 3, 4, 5, None, 10, 11, 12)):
        if place is not None:
            rows[i][...] = vectors[place]
    for j in range(4):
        rows[6][pl.ds(768 * j, 768)] = vectors[6 + j]


def fused_layer(
    hidden_in,
    cotangent,
    span_mask,
    lengths,
    repeats,
    mask_embedding,
    query_weight,
    query_bias,
    key_weight,
    value_weight,
    value_bias,
    output_weight,
    output_bias,
    mixing_gain,
    mixing_shift,
    inner_weight,
    inner_bias,
    outer_weight,
    outer_bias,
    final_gain,
    final_shift,
):
    vmem = pl.BlockSpec(memory_space=pltpu.VMEM)
    anywhere = pl.BlockSpec(memory_space=pl.ANY)
    scalars = pl.BlockSpec(memory_space=pltpu.SMEM)
    bf = lambda *shape: pltpu.VMEM(shape, BF16)
    fl = lambda *shape: pltpu.VMEM(shape, F32)
    dma = lambda *shape: pltpu.SemaphoreType.DMA(shape)
    shape = lambda dims, dtype: jax.ShapeDtypeStruct(dims, dtype)
    result = pl.pallas_call(
        layer_body,
        out_shape=[
            shape((384, 768), BF16),
            shape((384, 768), BF16),
            shape((9216, 256), BF16),
            shape((96, 192), F32),
            shape((96, 192), F32),
            shape((96, 192), F32),
            shape((96, 192), F32),
            shape((96, 768), F32),
            shape((384, 192), F32),
            shape((16, 768), F32),
        ],
        in_specs=[anywhere] * 8 + [vmem] + [anywhere] * 10 + [scalars, scalars],
        out_specs=[anywhere] * 3 + [vmem] * 7,
        scratch_shapes=[
            bf(3072, 768),
            bf(3072, 768),
            bf(768, 768),
            bf(768, 768),
            bf(768, 768),
            bf(768, 768),
            bf(13 * 768),
            fl(16, 768),
            bf(3, 512, 768),
            bf(3, 512, 768),
            bf(3, 512, 768),
            bf(384, 768),
            bf(384, 768),
            bf(9216, 256),
            bf(384, 768),
            fl(384, 768),
            fl(384, 1),
            fl(384, 768),
            fl(384, 768),
            bf(384, 768),
            bf(384, 768),
            pltpu.VMEM((4, 8, 128), jnp.int32),
            fl(512, 8),
            fl(12, 8, 256),
            fl(3, 8, 256),
            bf(12, 2, 2, 2, 2, 2, 48, 384),
            bf(SLOTS, 2, 2, 2, 2, 48, 384),
            bf(12, 2, 2, 2, 48, 384),
            bf(12, 2, 2, 48, 384),
            bf(12, 2, 48, 384),
            bf(12, 48, 384),
            bf(12, 48, 384),
            bf(3, 256, 768),
            bf(3, 128, 768),
            fl(6, 16, 768),
            fl(5, 16, 768),
            fl(6, 8, 768),
            fl(5, 8, 768),
            dma(12, 6),
            dma(12, 6),
            dma(5, 3),
            dma(5, 3),
            dma(3),
            dma(3),
            dma(2, 5),
            dma(2, 5),
            dma(31),
            pltpu.SemaphoreType.REGULAR,
        ],
        compiler_params=pltpu.CompilerParams(
            collective_id=1, has_side_effects=True, vmem_limit_bytes=63 * 2**20
        ),
        name="fused_layer",
    )(
        hidden_in,
        cotangent.reshape(384, 768),
        query_weight,
        key_weight,
        value_weight,
        output_weight,
        inner_weight,
        outer_weight,
        span_mask,
        mask_embedding,
        query_bias,
        value_bias,
        output_bias,
        mixing_gain,
        mixing_shift,
        inner_bias,
        outer_bias,
        final_gain,
        final_shift,
        lengths,
        repeats,
    )
    arrays, vectors = [result[0], result[1], *result[3:9]], result[9]
    wide_row = shape((768,), F32)
    handed = pl.pallas_call(
        hand_out,
        out_shape=[shape(v.shape, v.dtype) for v in arrays[:7]]
        + [shape((192, 384), F32)]
        + [wide_row] * 6
        + [shape((3072,), F32)]
        + [wide_row] * 3,
        in_specs=[vmem] * 9,
        out_specs=[vmem] * 18,
        name="hand_out",
    )(*arrays, vectors)
    layer_out, grad_input, g_query, g_key, g_value, g_output, g_inner, g_outer = handed[:8]
    g_mask, g_q_bias, g_v_bias, g_o_bias, g_gain, g_shift, g_inner_bias, *g_last = handed[8:]
    return (
        layer_out.reshape(3, 128, 768),
        grad_input.reshape(3, 128, 768),
        g_mask,
        g_query,
        g_q_bias,
        g_key,
        g_value,
        g_v_bias,
        g_output,
        g_o_bias,
        g_gain,
        g_shift,
        g_inner,
        g_inner_bias,
        g_outer.T,
        *g_last,
    )


def with_halo(x, sides, width):
    for axis, dim in sides:
        count, length = (lax.axis_size(axis), x.shape[dim])
        up = [(i, (i + 1) % count) for i in range(count - 1)]
        down = [(j, i) for i, j in up]
        last = lax.slice_in_dim(x, length - width, length, axis=dim)
        initial = lax.slice_in_dim(x, 0, width, axis=dim)
        before = lax.ppermute(last, axis, up)
        after = lax.ppermute(initial, axis, down)
        x = jnp.concatenate([before, x, after], axis=dim)
    return x


def layer_norm(inputs, gain, shift):
    center = inputs - jnp.mean(inputs, -1, keepdims=True)
    spread = jnp.mean(center * center, -1, keepdims=True)
    return center * lax.rsqrt(spread + 1e-05) * gain + shift


def linear(inputs, weight):
    return jnp.dot(inputs, weight, preferred_element_type=jnp.float32)


def linear_back(grads, weight):
    return lax.dot_general(
        grads, weight, (((1,), (1,)), ((), ())), preferred_element_type=jnp.float32
    )


def contract_rows(left, right):
    return lax.dot_general(
        left, right, (((0,), (0,)), ((), ())), preferred_element_type=jnp.float32
    )


def gelu_exact(inputs):
    return jax.nn.gelu(inputs, approximate=False)


def plain_layer(
    hidden_in,
    cotangent,
    span_mask,
    lengths,
    repeats,
    mask_embedding,
    query_weight,
    query_bias,
    key_weight,
    value_weight,
    value_bias,
    output_weight,
    output_bias,
    mixing_gain,
    mixing_shift,
    inner_weight,
    inner_bias,
    outer_weight,
    outer_bias,
    final_gain,
    final_shift,
):
    rows, stretch, width = hidden_in.shape
    whole = stretch * lax.axis_size("seq")
    scale = HEAD_DIM ** (-0.5)
    offset = lax.axis_index("seq") * stretch
    rim = with_halo(span_mask, (("seq", 1),), WIDEN)
    window = rim[:, 0:stretch]
    for shifted in range(1, 2 * WIDEN + 1):
        window = window + rim[:, shifted : shifted + stretch]
    widened = window > 0
    positions = offset + jnp.arange(stretch, dtype=jnp.int32)
    live = positions[None, :] < lengths[:, None]
    key_live = jnp.arange(whole, dtype=jnp.int32)[None, :] < lengths[:, None]
    masked_in = jnp.where(widened[..., None], mask_embedding[None, None, :], hidden_in)
    flat_in = masked_in.reshape(rows * stretch, width)
    queries = (linear(flat_in, query_weight) + query_bias.astype(jnp.float32)).astype(jnp.bfloat16)
    key_rows = linear(flat_in, key_weight).astype(jnp.bfloat16).reshape(rows, stretch, width)
    value_rows = (linear(flat_in, value_weight) + value_bias.astype(jnp.float32)).astype(
        jnp.bfloat16
    )
    value_rows = value_rows.reshape(rows, stretch, width)
    key_all, value_all = (
        lax.all_gather(key_rows, "seq", axis=1, tiled=True),
        lax.all_gather(value_rows, "seq", axis=1, tiled=True),
    )
    query_heads = queries.reshape(rows, stretch, HEADS, HEAD_DIM)

    def scores_of(key_full):
        key_heads = key_full.reshape(rows, whole, HEADS, HEAD_DIM)
        raw = jnp.einsum(
            "rqhd,rkhd->rhqk", query_heads, key_heads, preferred_element_type=jnp.float32
        )
        return jnp.where(key_live[:, None, None, :], raw * scale, -1e30)

    logits = scores_of(key_all)
    highest = jnp.max(logits, -1, keepdims=True)
    expd = jnp.exp(logits - highest)
    totals = jnp.sum(expd, -1, keepdims=True)
    log_total = highest + jnp.log(totals)
    probs_low = (expd / totals).astype(jnp.bfloat16)
    value_heads = value_all.reshape(rows, whole, HEADS, HEAD_DIM)
    mixed = jnp.einsum(
        "rhqk,rkhd->rqhd", probs_low, value_heads, preferred_element_type=jnp.float32
    )
    mixed = mixed.reshape(rows * stretch, width).astype(jnp.bfloat16)
    attended = linear(mixed, output_weight) + output_bias.astype(jnp.float32)
    residual_one = flat_in.astype(jnp.float32) + attended
    first, norm_back_one = jax.vjp(
        layer_norm, residual_one, mixing_gain.astype(jnp.float32), mixing_shift.astype(jnp.float32)
    )
    first_low = first.astype(jnp.bfloat16)
    inner = linear(first_low, inner_weight) + inner_bias.astype(jnp.float32)
    activated, gelu_back = jax.vjp(gelu_exact, inner)
    activated_low = activated.astype(jnp.bfloat16)
    outer = linear(activated_low, outer_weight) + outer_bias.astype(jnp.float32)
    final, norm_back_two = jax.vjp(
        layer_norm, first + outer, final_gain.astype(jnp.float32), final_shift.astype(jnp.float32)
    )
    layer_out = final.astype(jnp.bfloat16).reshape(rows, stretch, width)
    weighting = repeats.astype(jnp.float32)[:, None] * live.astype(jnp.float32)
    d_final = (cotangent.astype(jnp.float32) * weighting[:, :, None]).reshape(rows * stretch, width)
    d_two, d_final_gain, d_final_shift = norm_back_two(d_final)
    d_outer = d_two.astype(jnp.bfloat16)
    g_outer_weight = contract_rows(activated_low, d_outer)
    g_outer_bias = jnp.sum(d_outer.astype(jnp.float32), 0)
    (d_inner,) = gelu_back(linear_back(d_outer, outer_weight))
    d_inner = d_inner.astype(jnp.bfloat16)
    g_inner_weight = contract_rows(first_low, d_inner)
    g_inner_bias = jnp.sum(d_inner.astype(jnp.float32), 0)
    d_first = linear_back(d_inner, inner_weight) + d_two
    d_one, d_mixing_gain, d_mixing_shift = norm_back_one(d_first)
    d_attended = d_one.astype(jnp.bfloat16)
    g_output_weight = contract_rows(mixed, d_attended)
    g_output_bias = jnp.sum(d_attended.astype(jnp.float32), 0)
    d_mixed = linear_back(d_attended, output_weight).astype(jnp.bfloat16)
    d_mixed_heads = d_mixed.reshape(rows, stretch, HEADS, HEAD_DIM)
    key_back, value_back = (
        lax.all_gather(key_rows, "seq", axis=1, tiled=True),
        lax.all_gather(value_rows, "seq", axis=1, tiled=True),
    )
    probs = jnp.exp(scores_of(key_back) - log_total)
    probs_again = probs.astype(jnp.bfloat16)
    key_heads = key_back.reshape(rows, whole, HEADS, HEAD_DIM)
    value_heads = value_back.reshape(rows, whole, HEADS, HEAD_DIM)
    d_probs = jnp.einsum(
        "rqhd,rkhd->rhqk", d_mixed_heads, value_heads, preferred_element_type=jnp.float32
    )
    centered = d_probs - jnp.sum(probs * d_probs, -1, keepdims=True)
    d_raw = (probs * centered * scale).astype(jnp.bfloat16)
    d_queries = jnp.einsum("rhqk,rkhd->rqhd", d_raw, key_heads, preferred_element_type=jnp.float32)
    d_queries = d_queries.reshape(rows * stretch, width).astype(jnp.bfloat16)
    d_key_part = jnp.einsum(
        "rhqk,rqhd->rkhd", d_raw, query_heads, preferred_element_type=jnp.float32
    )
    d_value_part = jnp.einsum(
        "rhqk,rqhd->rkhd", probs_again, d_mixed_heads, preferred_element_type=jnp.float32
    )
    d_key_sum, d_value_sum = (
        lax.psum_scatter(
            d_key_part.reshape(rows, whole, width), "seq", scatter_dimension=1, tiled=True
        ),
        lax.psum_scatter(
            d_value_part.reshape(rows, whole, width), "seq", scatter_dimension=1, tiled=True
        ),
    )
    d_keys = d_key_sum.astype(jnp.bfloat16).reshape(rows * stretch, width)
    d_values = d_value_sum.astype(jnp.bfloat16).reshape(rows * stretch, width)
    g_query_weight = contract_rows(flat_in, d_queries)
    g_key_weight = contract_rows(flat_in, d_keys)
    g_value_weight = contract_rows(flat_in, d_values)
    g_query_bias = jnp.sum(d_queries.astype(jnp.float32), 0)
    g_value_bias = jnp.sum(d_values.astype(jnp.float32), 0)
    d_input = (
        d_one
        + linear_back(d_queries, query_weight)
        + linear_back(d_keys, key_weight)
        + linear_back(d_values, value_weight)
    ).reshape(rows, stretch, width)
    grad_input = jnp.where(widened[..., None], 0.0, d_input).astype(jnp.bfloat16)
    g_mask = jnp.sum(jnp.where(widened[..., None], d_input, 0.0), (0, 1))
    matrices = (
        g_query_weight,
        g_key_weight,
        g_value_weight,
        g_output_weight,
        g_inner_weight,
        g_outer_weight,
    )
    partial_sums = (
        lax.psum_scatter(matrices[0], "batch", scatter_dimension=0, tiled=True),
        lax.psum_scatter(matrices[1], "batch", scatter_dimension=0, tiled=True),
        lax.psum_scatter(matrices[2], "batch", scatter_dimension=0, tiled=True),
        lax.psum_scatter(matrices[3], "batch", scatter_dimension=0, tiled=True),
        lax.psum_scatter(matrices[4], "batch", scatter_dimension=0, tiled=True),
        lax.psum_scatter(matrices[5], "batch", scatter_dimension=0, tiled=True),
    )
    summed = (
        lax.psum_scatter(partial_sums[0], "seq", scatter_dimension=1, tiled=True),
        lax.psum_scatter(partial_sums[1], "seq", scatter_dimension=1, tiled=True),
        lax.psum_scatter(partial_sums[2], "seq", scatter_dimension=1, tiled=True),
        lax.psum_scatter(partial_sums[3], "seq", scatter_dimension=1, tiled=True),
        lax.psum_scatter(partial_sums[4], "seq", scatter_dimension=1, tiled=True),
        lax.psum_scatter(partial_sums[5], "seq", scatter_dimension=1, tiled=True),
    )
    vectors = lax.psum(
        (
            g_mask,
            g_query_bias,
            g_value_bias,
            g_output_bias,
            d_mixing_gain,
            d_mixing_shift,
            g_inner_bias,
            g_outer_bias,
            d_final_gain,
            d_final_shift,
        ),
        ("batch", "seq"),
    )
    return (
        layer_out,
        grad_input,
        vectors[0],
        summed[0],
        vectors[1],
        summed[1],
        summed[2],
        vectors[2],
        summed[3],
        vectors[3],
        vectors[4],
        vectors[5],
        summed[4],
        vectors[6],
        summed[5],
        vectors[7],
        vectors[8],
        vectors[9],
    )


def solution(mesh):
    fused = mesh.shape["batch"] == 8 and mesh.shape["seq"] == 4
    return jax.shard_map(
        fused_layer if fused else plain_layer,
        mesh=mesh,
        in_specs=(
            P("batch", "seq", None),
            P("batch", "seq", None),
            P("batch", "seq"),
            P("batch"),
            P("batch"),
            P(),
            P(),
            P(),
            P(),
            P(),
            P(),
            P(),
            P(),
            P(),
            P(),
            P(),
            P(),
            P(),
            P(),
            P(),
            P(),
        ),
        out_specs=(
            P("batch", "seq", None),
            P("batch", "seq", None),
            P(),
            P("batch", "seq"),
            P(),
            P("batch", "seq"),
            P("batch", "seq"),
            P(),
            P("batch", "seq"),
            P(),
            P(),
            P(),
            P("batch", "seq"),
            P(),
            P("batch", "seq"),
            P(),
            P(),
            P(),
        ),
        check_vma=False,
    )
```
